32 devices in a mesh: seq: 4 (over y, core), fsdp: 8 (over z, x).
Axes of the slice: x: 2, y: 2, z: 4, core: 2. Of those that a mesh axis runs over, the one named last changes fastest.
Arguments:
- tokens: bfloat16 [8, 1024, 1536], P('fsdp', 'seq'), may hold values from -6 to 6
- cotangent: bfloat16 [8, 1024, 1536], P('fsdp', 'seq'), may hold values from -6 to 6
- segments: int32 [8, 1024], P('fsdp'), may hold values from 0 to 3, as said below
- in_weight: float32 [1536, 6448], P('fsdp'), may hold values from -0.15625 to 0.15625
- out_weight: float32 [1536, 3072], P('fsdp'), may hold values from -0.109375 to 0.109375
- small_params: float32 [21392], replicated
- in_first: float32 [1536, 6448], P('fsdp')
- in_second: float32 [1536, 6448], P('fsdp'), as said below
- out_first: float32 [1536, 3072], P('fsdp')
- out_second: float32 [1536, 3072], P('fsdp'), as said below
- small_first: float32 [21392], replicated
- small_second: float32 [21392], replicated, as said below
Outputs:
- output: bfloat16 [8, 1024, 1536], P('fsdp', 'seq')
- input_grad: float32 [8, 1024, 1536], P('fsdp', 'seq')
- in_grad: float32 [1536, 6448], P('fsdp')
- in_new: float32 [1536, 6448], P('fsdp')
- in_first_new: float32 [1536, 6448], P('fsdp')
- in_second_new: float32 [1536, 6448], P('fsdp')
- out_grad: float32 [1536, 3072], P('fsdp')
- out_new: float32 [1536, 3072], P('fsdp')
- out_first_new: float32 [1536, 3072], P('fsdp')
- out_second_new: float32 [1536, 3072], P('fsdp')
- small_grad: float32 [21392], replicated
- small_new: float32 [21392], replicated
- small_first_new: float32 [21392], replicated
- small_second_new: float32 [21392], replicated
- norms: float32 [4], replicated
The draws below stay inside these ranges and needn't reach their ends.
Inputs may be any that keep to these rules, and one draw needn't show every extreme that they name: `segments`: ids start at 0 at each sequence's first position and rise by one at each new document's first position; a document is a run of equal ids. `in_second`: positive. `out_second`: positive. `small_second`: positive.
All inputs are finite; a program needn't handle non-finite values.
Results may differ from the reference program's by a relative error of at most 0.018.
Values may be sent and summed in bfloat16 or wider, within the bound.
A program may use at most 512 MiB of HBM per device.

```python
import math
from functools import partial
import jax
import jax.numpy as jnp
from jax import lax

D = 1536
HEADS = 48
HEAD = 64
STATE = 128
KERNEL = 4
STRETCH = 256
STEP = 5
TOK_DEV = 256
INNER = 3072
CONV = 3328
PROJ = 6448
SMALL = 21392
LENGTH = 1024
SEQS = 8


def small_scales():
    grad_root = math.sqrt(SEQS * LENGTH)
    return jnp.concatenate([jnp.full((D,), 0.3 * grad_root, jnp.float32), jnp.full((KERNEL * CONV + CONV,), 0.1 * grad_root, jnp.float32), jnp.full((3 * HEADS,), 0.5 * grad_root, jnp.float32), jnp.full((INNER,), 0.3 * grad_root, jnp.float32)])


def first_state(key, shape, scale):
    return jax.random.normal(key, shape, jnp.float32) * scale * (0.1 / 0.9)


def second_state(key, shape, scale):
    factor = jnp.exp(jax.random.uniform(key, shape, jnp.float32, math.log(0.5), math.log(8.0)))
    return scale * scale * (0.001 / 0.999) * factor


def draw_segments(key, part):
    key = jax.random.fold_in(key, 5)
    subkeys = jax.random.split(key, 9)
    shortest = min(LENGTH * 25 // 256, TOK_DEV - 4)
    widest = TOK_DEV - shortest
    edge_count = LENGTH // TOK_DEV - 1
    rows = jnp.arange(SEQS, dtype=jnp.int32)
    picked = jax.random.randint(subkeys[0], (), 0, SEQS)
    other = (picked + jax.random.randint(subkeys[1], (), 1, SEQS)) % SEQS
    spanning = jax.random.randint(subkeys[2], (SEQS,), 0, 2)
    spanning = jnp.where(rows == picked, 1, jnp.where(rows == other, 0, spanning))
    position = jnp.arange(LENGTH, dtype=jnp.int32)[None, :]
    opening = jax.random.randint(subkeys[3], (SEQS, 1), shortest, TOK_DEV)
    closing = jax.random.randint(subkeys[4], (SEQS, 1), LENGTH - TOK_DEV + 1, LENGTH - shortest + 1)
    long_ids = (position >= opening).astype(jnp.int32) + (position >= closing).astype(jnp.int32)
    kind = jax.random.randint(subkeys[5], (SEQS, edge_count), 0, 4)
    near = jax.random.randint(subkeys[6], (SEQS, edge_count), 1, 4)
    spread = jax.random.randint(subkeys[7], (SEQS, edge_count), 0, widest + 1)
    offset = jnp.where(kind == 0, 0, jnp.where(kind == 1, near, spread))
    cut_on = jax.random.randint(subkeys[8], (SEQS, edge_count), 0, 2)
    cut_on = jnp.where(rows[:, None] == other, 1, cut_on)
    edge_index = jnp.arange(edge_count, dtype=jnp.int32)[None, :]
    nothing = jnp.sum(cut_on, axis=1, keepdims=True) == 0
    cut_on = jnp.where(nothing & (edge_index == 0), 1, cut_on)
    cuts = (edge_index + 1) * TOK_DEV + offset
    passed = (position[:, :, None] >= cuts[:, None, :]) & (cut_on[:, None, :] == 1)
    short_ids = jnp.sum(passed.astype(jnp.int32), axis=2)
    return jnp.where(spanning[:, None] == 1, long_ids, short_ids).astype(jnp.int32)


def draw_small_params(key, part):
    key = jax.random.fold_in(key, 3)
    subkeys = jax.random.split(key, 7)
    in_gain = (0.5 + jnp.arange(D, dtype=jnp.float32) / D) * jax.random.uniform(subkeys[0], (D,), jnp.float32, 0.8, 1.25)
    conv_weight = 0.5 * jax.random.normal(subkeys[1], (KERNEL * CONV,), jnp.float32)
    conv_bias = 0.3 * jax.random.normal(subkeys[2], (CONV,), jnp.float32)
    dt_bias = jax.random.uniform(subkeys[3], (HEADS,), jnp.float32, -2.0, 0.0)
    a_log = jax.random.uniform(subkeys[4], (HEADS,), jnp.float32, math.log(0.1 / LENGTH), math.log(0.1))
    skip_gain = jax.random.uniform(subkeys[5], (HEADS,), jnp.float32, 0.5, 1.5)
    out_gain = (0.5 + jnp.arange(INNER, dtype=jnp.float32) / INNER) * jax.random.uniform(subkeys[6], (INNER,), jnp.float32, 0.8, 1.25)
    return jnp.concatenate([in_gain, conv_weight, conv_bias, dt_bias, a_log, skip_gain, out_gain])


def draw_in_first(key, part):
    key = jax.random.fold_in(key, 21)
    return first_state(key, (D, PROJ), 0.3 * math.sqrt(SEQS * LENGTH))


def draw_in_second(key, part):
    key = jax.random.fold_in(key, 22)
    return second_state(key, (D, PROJ), 0.3 * math.sqrt(SEQS * LENGTH))


def draw_out_first(key, part):
    key = jax.random.fold_in(key, 23)
    return first_state(key, (D, INNER), math.sqrt(SEQS * LENGTH))


def draw_out_second(key, part):
    key = jax.random.fold_in(key, 24)
    return second_state(key, (D, INNER), math.sqrt(SEQS * LENGTH))


def draw_small_first(key, part):
    key = jax.random.fold_in(key, 25)
    return first_state(key, (SMALL,), small_scales())


def draw_small_second(key, part):
    key = jax.random.fold_in(key, 26)
    return second_state(key, (SMALL,), small_scales())


def block_scale(own_key, dims, shards, least, largest):
    gain, own = 1.0, jax.random.fold_in(own_key, 6)
    for axis_at, blocks in shards:
        draws = jnp.exp(jax.random.uniform(jax.random.fold_in(own, axis_at), (blocks,), jnp.float32, least / len(shards), largest / len(shards)))
        gain = gain * jnp.repeat(draws, dims[axis_at] // blocks).reshape([-1 if axis == axis_at else 1 for axis in range(len(dims))])
    return gain


def normal_values(key, shape, scale, reach, cuts=(), kind=jnp.bfloat16):
    gain = block_scale(key, shape, cuts, -0.22, 0.18) if cuts else 1.0
    values = jax.random.normal(key, shape, jnp.float32) * scale * gain
    return jnp.minimum(jnp.maximum(values, -reach), reach).astype(kind)


def setup_inputs(seed: int = 0) -> dict:
    seeds = jax.random.split(jax.random.key(seed), 13)
    tokens = normal_values(seeds[0], (SEQS, LENGTH, D), 1.0, 6.0, ((0, 8), (1, 4)))
    cotangent = normal_values(seeds[1], (SEQS, LENGTH, D), 1.0, 6.0, ((0, 8), (1, 4)))
    segments = draw_segments(jax.random.fold_in(seeds[12], 71), 0)
    in_weight = normal_values(seeds[3], (D, PROJ), D ** -0.5, 0.15625, ((0, 8),), jnp.float32)
    out_weight = normal_values(seeds[4], (D, INNER), INNER ** -0.5, 0.109375, ((0, 8),), jnp.float32)
    small_params = draw_small_params(jax.random.fold_in(seeds[12], 71), 0)
    in_first = draw_in_first(jax.random.fold_in(seeds[12], 71), 0)
    in_second = draw_in_second(jax.random.fold_in(seeds[12], 71), 0)
    out_first = draw_out_first(jax.random.fold_in(seeds[12], 71), 0)
    out_second = draw_out_second(jax.random.fold_in(seeds[12], 71), 0)
    small_first = draw_small_first(jax.random.fold_in(seeds[12], 71), 0)
    small_second = draw_small_second(jax.random.fold_in(seeds[12], 71), 0)
    return {"tokens": tokens, "cotangent": cotangent, "segments": segments, "in_weight": in_weight, "out_weight": out_weight, "small_params": small_params, "in_first": in_first, "in_second": in_second, "out_first": out_first, "out_second": out_second, "small_first": small_first, "small_second": small_second}


NORM_EPS = 1e-05
FIRST_DECAY = 0.9
SECOND_DECAY = 0.999
ADAM_EPSILON = 1e-06
WEIGHT_DECAY = 0.01
LEARN_RATE = 0.5

@jax.custom_vjp
def low(v):
    return lax.optimization_barrier(v.astype(jnp.bfloat16)).astype(jnp.float32)

@jax.custom_vjp
def low_back(v):
    return v

def low_keep(v):
    return (low(v), None)

def low_pass(kept, grad):
    return (grad,)

def back_keep(v):
    return (v, None)

def back_low(kept, grad):
    return (low(grad),)
low.defvjp(low_keep, low_pass)
low_back.defvjp(back_keep, back_low)

def split_params(vector):
    offset = 0
    in_gain = vector[offset:offset + D]
    offset = offset + D
    conv_weight = vector[offset:offset + KERNEL * CONV].reshape(KERNEL, CONV)
    offset = offset + KERNEL * CONV
    conv_bias = vector[offset:offset + CONV]
    offset = offset + CONV
    dt_bias = vector[offset:offset + HEADS]
    offset = offset + HEADS
    a_log = vector[offset:offset + HEADS]
    offset = offset + HEADS
    skip_gain = vector[offset:offset + HEADS]
    offset = offset + HEADS
    out_gain = vector[offset:offset + INNER]
    return (in_gain, conv_weight, conv_bias, dt_bias, a_log, skip_gain, out_gain)

def in_norm(inputs, in_gain):
    return inputs * lax.rsqrt(lax.optimization_barrier(jnp.mean(inputs * inputs, axis=-1, keepdims=True)) + NORM_EPS) * in_gain

def convolve(padded, weight, conv_bias, segment_pad):
    row_count = padded.shape[0] - (KERNEL - 1)
    summed = conv_bias[None, :] + jnp.zeros((row_count, padded.shape[1]), jnp.float32)
    for tap_index in range(KERNEL):
        same_doc = (segment_pad[tap_index:tap_index + row_count] == segment_pad[KERNEL - 1:]).astype(jnp.float32)
        summed = summed + weight[tap_index][None, :] * padded[tap_index:tap_index + row_count] * same_doc[:, None]
    return jax.nn.silu(summed)

def gated_norm(scanned, gate_z, out_gain):
    gated = scanned * jax.nn.silu(gate_z)
    return gated * lax.rsqrt(lax.optimization_barrier(jnp.mean(gated * gated, axis=-1, keepdims=True)) + NORM_EPS) * out_gain

def state_scan(values, step_sizes, inputs_b, readout_c, a_log, skip_gain, segment):
    length = values.shape[0]
    head_count = values.shape[1]
    blocks = length // STRETCH
    decay_rate = -jnp.exp(a_log)
    seg_blocks = segment.reshape(blocks, STRETCH)
    prior_seg = jnp.concatenate([segment[:1], seg_blocks[:-1, -1]])
    row_index = jnp.arange(STRETCH)
    causal = row_index[:, None] >= row_index[None, :]
    highest = lax.Precision.HIGHEST

    def block_step(carried, pieces):
        block_x, block_dt, block_b, block_c, block_seg, block_prior = pieces
        cumulative = jnp.cumsum(block_dt * decay_rate[None, :], axis=0)
        within = causal & (block_seg[:, None] == block_seg[None, :])
        spread = cumulative.T[:, :, None] - cumulative.T[:, None, :]
        weights = jnp.where(within[None], jnp.exp(jnp.where(within[None], spread, 0.0)), 0.0)
        scores = jnp.einsum('tn,sn->ts', block_c, block_b, precision=highest)
        scaled = block_x * block_dt[:, :, None]
        result = jnp.einsum('hts,shp->thp', weights * scores[None], scaled, precision=highest)
        carry_in = (block_seg == block_prior).astype(jnp.float32)[:, None] * jnp.exp(cumulative)
        result = result + jnp.einsum('tn,hnp->thp', block_c, carried, precision=highest) * carry_in[:, :, None]
        last_sum = cumulative[-1]
        tail_decay = jnp.exp(last_sum[None, :] - cumulative) * (block_seg == block_seg[-1]).astype(jnp.float32)[:, None]
        keep_factor = jnp.exp(last_sum) * (block_seg[-1] == block_prior).astype(jnp.float32)
        updated = carried * keep_factor[:, None, None] + jnp.einsum('sn,shp->hnp', block_b, scaled * tail_decay[:, :, None], precision=highest)
        return (updated, result + skip_gain[None, :, None] * block_x)
    initial = jnp.zeros((head_count, inputs_b.shape[1], values.shape[2]), jnp.float32)
    final_state, outputs = lax.scan(jax.checkpoint(block_step), initial, (values.reshape(blocks, STRETCH, head_count, values.shape[2]), step_sizes.reshape(blocks, STRETCH, head_count), inputs_b.reshape(blocks, STRETCH, inputs_b.shape[1]), readout_c.reshape(blocks, STRETCH, readout_c.shape[1]), seg_blocks, prior_seg))
    return outputs.reshape(length, head_count, values.shape[2])

def branch_of(inputs, in_full, out_full, small_vector, segment):
    in_gain, conv_weight, conv_bias, dt_bias, a_log, skip_gain, out_gain = split_params(small_vector)
    highest = lax.Precision.HIGHEST
    normed = low(in_norm(inputs, in_gain))
    projected = low_back(jnp.dot(normed, low(in_full), precision=highest))
    gate_z = projected[:, :INNER]
    conv_in = low(projected[:, INNER:INNER + CONV])
    dt_raw = projected[:, INNER + CONV:]
    padded = jnp.concatenate([jnp.zeros((KERNEL - 1, CONV), jnp.float32), conv_in], axis=0)
    segment_pad = jnp.concatenate([jnp.full((KERNEL - 1,), -1, jnp.int32), segment.astype(jnp.int32)])
    activated = convolve(padded, conv_weight, conv_bias, segment_pad)
    conv_values = low_back(low(activated[:, :INNER]))
    inputs_b = low(activated[:, INNER:INNER + STATE])
    readout_c = low(activated[:, INNER + STATE:])
    step_sizes = low_back(low(jax.nn.softplus(dt_raw + dt_bias[None, :])))
    scanned = state_scan(conv_values.reshape(-1, HEADS, HEAD), step_sizes, inputs_b, readout_c, a_log, skip_gain, segment)
    scanned = low_back(low(scanned.reshape(-1, INNER)))
    mixed_low = low(gated_norm(scanned, gate_z, out_gain))
    return lax.dot_general(mixed_low, low(out_full), (((1,), (1,)), ((), ())), precision=highest)

def adam_parts(gradient, first_old, second_old):
    first_new = FIRST_DECAY * first_old + (1.0 - FIRST_DECAY) * gradient
    second_new = SECOND_DECAY * second_old + (1.0 - SECOND_DECAY) * gradient * gradient
    direction = first_new / (1.0 - FIRST_DECAY ** STEP) / (jnp.sqrt(second_new / (1.0 - SECOND_DECAY ** STEP)) + ADAM_EPSILON)
    return (first_new, second_new, direction)

def reference(tokens, cotangent, segments, in_weight, out_weight, small_params, in_first, in_second, out_first, out_second, small_first, small_second):

    def per_sequence(totals, pieces):
        seq_tokens, seq_cot, seq_segments = pieces
        inputs = seq_tokens.astype(jnp.float32)
        returned = seq_cot.astype(jnp.float32)
        branch, pullback = jax.vjp(partial(branch_of, segment=seq_segments), inputs, in_weight, out_weight, small_params)
        d_inputs, d_in, d_out, d_small = pullback(returned)
        output = (inputs + branch).astype(jnp.bfloat16)
        return ((totals[0] + d_in, totals[1] + d_out, totals[2] + d_small), (output, returned + d_inputs))
    initial = (jnp.zeros(in_weight.shape, jnp.float32), jnp.zeros(out_weight.shape, jnp.float32), jnp.zeros(small_params.shape, jnp.float32))
    grads, stacked = lax.scan(per_sequence, initial, (tokens, cotangent, segments))
    in_grad, out_grad, small_grad = grads
    output, input_grad = stacked
    in_first_new, in_second_new, in_dir = adam_parts(in_grad, in_first, in_second)
    in_dir = in_dir + WEIGHT_DECAY * in_weight
    out_first_new, out_second_new, out_dir = adam_parts(out_grad, out_first, out_second)
    out_dir = out_dir + WEIGHT_DECAY * out_weight
    small_first_new, small_second_new, small_dir = adam_parts(small_grad, small_first, small_second)
    norms = jnp.sqrt(jnp.stack([jnp.sum(in_weight * in_weight), jnp.sum(in_dir * in_dir), jnp.sum(out_weight * out_weight), jnp.sum(out_dir * out_dir)]))
    in_new = in_weight - LEARN_RATE * (norms[0] / norms[1]) * in_dir
    out_new = out_weight - LEARN_RATE * (norms[2] / norms[3]) * out_dir
    small_new = small_params - LEARN_RATE * small_dir
    return (output, input_grad, in_grad, in_new, in_first_new, in_second_new, out_grad, out_new, out_first_new, out_second_new, small_grad, small_new, small_first_new, small_second_new, norms)
```

```python
from functools import partial

import jax
import jax.numpy as jnp
from jax import lax
from jax.sharding import PartitionSpec as P

D = 1536
HEADS = 48
HEAD = 64
STATE = 128
KERNEL = 4
STRETCH = 256
STEP = 5
INNER = 3072
CONV = 3328
PROJ = 6448
DT_PAD = 128

NORM_EPS = 1e-05
FIRST_DECAY = 0.9
SECOND_DECAY = 0.999
ADAM_EPSILON = 1e-06
WEIGHT_DECAY = 0.01
LEARN_RATE = 0.5
SCAN_PRECISION = lax.Precision.DEFAULT
F32 = jnp.float32
BF16 = jnp.bfloat16


def split_params(vector):
    offset = 0
    in_gain = vector[offset : offset + D]
    offset = offset + D
    conv_weight = vector[offset : offset + KERNEL * CONV].reshape(KERNEL, CONV)
    offset = offset + KERNEL * CONV
    conv_bias = vector[offset : offset + CONV]
    offset = offset + CONV
    dt_bias = vector[offset : offset + HEADS]
    offset = offset + HEADS
    a_log = vector[offset : offset + HEADS]
    offset = offset + HEADS
    skip_gain = vector[offset : offset + HEADS]
    offset = offset + HEADS
    out_gain = vector[offset : offset + INNER]
    return (in_gain, conv_weight, conv_bias, dt_bias, a_log, skip_gain, out_gain)


def state_scan(values, step_sizes, inputs_b, readout_c, a_log, skip_gain, segment):
    length = values.shape[0]
    head_count = values.shape[1]
    blocks = length // STRETCH
    decay_rate = -jnp.exp(a_log)
    seg_blocks = segment.reshape(blocks, STRETCH)
    prior_seg = jnp.concatenate([segment[:1], seg_blocks[:-1, -1]])
    row_index = jnp.arange(STRETCH)
    causal = row_index[:, None] >= row_index[None, :]

    def block_step(carried, pieces):
        block_x, block_dt, block_b, block_c, block_seg, block_prior = pieces
        cumulative = jnp.cumsum(block_dt * decay_rate[None, :], axis=0)
        within = causal & (block_seg[:, None] == block_seg[None, :])
        spread = cumulative.T[:, :, None] - cumulative.T[:, None, :]
        weights = jnp.where(within[None], jnp.exp(jnp.where(within[None], spread, 0.0)), 0.0)
        scores = jnp.einsum("tn,sn->ts", block_c, block_b, precision=SCAN_PRECISION)
        scaled = block_x * block_dt[:, :, None]
        result = jnp.einsum(
            "hts,shp->thp", weights * scores[None], scaled, precision=SCAN_PRECISION
        )
        carry_in = (block_seg == block_prior).astype(jnp.float32)[:, None] * jnp.exp(cumulative)
        result = (
            result
            + jnp.einsum("tn,hnp->thp", block_c, carried, precision=SCAN_PRECISION)
            * carry_in[:, :, None]
        )
        last_sum = cumulative[-1]
        tail_decay = (
            jnp.exp(last_sum[None, :] - cumulative)
            * (block_seg == block_seg[-1]).astype(jnp.float32)[:, None]
        )
        keep_factor = jnp.exp(last_sum) * (block_seg[-1] == block_prior).astype(jnp.float32)
        updated = carried * keep_factor[:, None, None] + jnp.einsum(
            "sn,shp->hnp", block_b, scaled * tail_decay[:, :, None], precision=SCAN_PRECISION
        )
        return (updated, result + skip_gain[None, :, None] * block_x)

    initial = jnp.zeros((head_count, inputs_b.shape[1], values.shape[2]), jnp.float32)
    final_state, outputs = lax.scan(
        jax.checkpoint(block_step),
        initial,
        (
            values.reshape(blocks, STRETCH, head_count, values.shape[2]),
            step_sizes.reshape(blocks, STRETCH, head_count),
            inputs_b.reshape(blocks, STRETCH, inputs_b.shape[1]),
            readout_c.reshape(blocks, STRETCH, readout_c.shape[1]),
            seg_blocks,
            prior_seg,
        ),
    )
    return outputs.reshape(length, head_count, values.shape[2])


def adam_parts(gradient, first_old, second_old):
    first_new = FIRST_DECAY * first_old + (1.0 - FIRST_DECAY) * gradient
    second_new = SECOND_DECAY * second_old + (1.0 - SECOND_DECAY) * gradient * gradient
    direction = (
        first_new
        / (1.0 - FIRST_DECAY**STEP)
        / (jnp.sqrt(second_new / (1.0 - SECOND_DECAY**STEP)) + ADAM_EPSILON)
    )
    return (first_new, second_new, direction)


def later(x, by):
    if by == 0:
        return x
    return jnp.pad(x[:-by], ((by, 0), (0, 0)))


def sooner(x, by):
    if by == 0:
        return x
    return jnp.pad(x[by:], ((0, by), (0, 0)))


def shards(
    tokens,
    cotangent,
    segments,
    in_weight,
    out_weight,
    small_params,
    in_first,
    in_second,
    out_first,
    out_second,
    small_first,
    small_second,
):
    in_gain, conv_weight, conv_bias, dt_bias, a_log, skip_gain, out_gain = split_params(
        small_params
    )
    groups = lax.axis_size("seq")
    where_seq = lax.axis_index("seq")
    seq_length = segments.shape[1]
    heads = HEADS // groups
    wide = INNER // groups
    segment_row = segments[0]

    def own(vector, axis=-1):
        size = vector.shape[axis] // groups
        return lax.dynamic_slice_in_dim(vector, where_seq * size, size, axis)

    in_low = in_weight.astype(BF16)
    in_own = jnp.concatenate(
        [
            own(in_low[:, :INNER]),
            own(in_low[:, INNER : 2 * INNER]),
            in_low[:, 2 * INNER : INNER + CONV],
            jnp.pad(own(in_low[:, INNER + CONV :]), ((0, 0), (0, DT_PAD - heads))),
        ],
        axis=1,
    )
    out_own = own(out_weight).astype(BF16)
    in_cols = lax.all_gather(in_own, "fsdp", axis=0, tiled=True)
    out_cols = lax.all_gather(out_own, "fsdp", axis=0, tiled=True)

    inputs = tokens[0].astype(F32)
    in_rms = lax.rsqrt(jnp.mean(inputs * inputs, axis=-1, keepdims=True) + NORM_EPS)
    normed_own = (inputs * in_rms * in_gain).astype(BF16)
    normed = lax.all_gather(normed_own, "seq", axis=0, tiled=True)
    returned = lax.all_gather(cotangent[0], "seq", axis=0, tiled=True)

    projected = jnp.dot(normed, in_cols, preferred_element_type=F32)
    gate_z = projected[:, :wide]
    conv_in = projected[:, wide : 2 * wide + 2 * STATE].astype(BF16).astype(F32)
    dt_raw = projected[:, 2 * wide + 2 * STATE : 2 * wide + 2 * STATE + heads]
    conv_own = jnp.concatenate([own(conv_weight[:, :INNER]), conv_weight[:, INNER:]], axis=1)
    bias_own = jnp.concatenate([own(conv_bias[:INNER]), conv_bias[INNER:]])
    same = []
    for tap in range(KERNEL):
        by = KERNEL - 1 - tap
        before = jnp.concatenate([jnp.full((by,), -1, jnp.int32), segment_row[: seq_length - by]])
        same.append((before == segment_row).astype(F32)[:, None])
    pre = bias_own[None, :]
    for tap in range(KERNEL):
        pre = pre + conv_own[tap][None, :] * later(conv_in, KERNEL - 1 - tap) * same[tap]
    sig = jax.nn.sigmoid(pre)
    act = (pre * sig).astype(BF16).astype(F32)
    dt_pre = dt_raw + own(dt_bias)[None, :]
    steps = jax.nn.softplus(dt_pre).astype(BF16).astype(F32)
    head_y, scan_pull = jax.vjp(
        partial(state_scan, segment=segment_row),
        act[:, :wide].reshape(seq_length, heads, HEAD),
        steps,
        act[:, wide : wide + STATE],
        act[:, wide + STATE :],
        own(a_log),
        own(skip_gain),
    )
    y = head_y.reshape(seq_length, wide).astype(BF16).astype(F32)
    gate_sig = jax.nn.sigmoid(gate_z)
    silu_z = gate_z * gate_sig
    gated = y * silu_z
    gain_own = own(out_gain)
    d_mixed = jnp.dot(returned, out_cols, preferred_element_type=F32)
    weighted = d_mixed * gain_own[None, :]
    stats = lax.psum(
        jnp.stack([jnp.sum(gated * gated, axis=1), jnp.sum(weighted * gated, axis=1)]), "seq"
    )
    out_rms = lax.rsqrt(stats[0] / INNER + NORM_EPS)[:, None]
    mixed = (gated * out_rms * gain_own[None, :]).astype(BF16)
    branch = lax.dot_general(
        mixed, out_cols, (((1,), (1,)), ((), ())), preferred_element_type=F32
    ).astype(BF16)
    d_gated = weighted * out_rms - gated * (out_rms**3 / INNER) * stats[1][:, None]
    d_out_gain = jnp.sum(d_mixed * gated * out_rms, axis=0)
    d_y = (d_gated * silu_z).astype(BF16)
    d_gate = d_gated * y * (gate_sig * (1.0 + gate_z * (1.0 - gate_sig)))
    dx_heads, ddt, d_b, d_c, d_a, d_skip = scan_pull(
        d_y.astype(F32).reshape(seq_length, heads, HEAD)
    )
    d_act = jnp.concatenate([dx_heads.reshape(seq_length, wide), d_b, d_c], axis=1)
    d_pre = d_act * (sig * (1.0 + pre * (1.0 - sig)))
    d_conv_in = 0.0
    d_taps = []
    for tap in range(KERNEL):
        by = KERNEL - 1 - tap
        masked = d_pre * same[tap]
        d_conv_in = d_conv_in + conv_own[tap][None, :] * sooner(masked, by)
        d_taps.append(jnp.sum(masked * later(conv_in, by), axis=0))
    d_conv = jnp.stack(d_taps + [jnp.sum(d_pre, axis=0)])
    d_dt_raw = ddt * jax.nn.sigmoid(dt_pre)
    d_dt_bias = jnp.sum(d_dt_raw, axis=0)
    d_projected = jnp.concatenate(
        [d_gate, d_conv_in, jnp.pad(d_dt_raw, ((0, 0), (0, DT_PAD - heads)))], axis=1
    ).astype(BF16)
    d_normed_part = lax.dot_general(
        d_projected, in_cols, (((1,), (1,)), ((), ())), preferred_element_type=F32
    ).astype(BF16)
    both = lax.psum_scatter(
        jnp.concatenate([branch, d_normed_part], axis=1), "seq", scatter_dimension=0, tiled=True
    ).astype(F32)
    output = (inputs + both[:, :D]).astype(BF16)[None]
    d_normed = both[:, D:]
    slope = d_normed * in_gain[None, :]
    d_inputs = slope * in_rms - inputs * (in_rms**3 / D) * jnp.sum(
        slope * inputs, axis=1, keepdims=True
    )
    input_grad = (cotangent[0].astype(F32) + d_inputs)[None]
    d_in_gain = jnp.sum(d_normed * inputs * in_rms, axis=0)

    contract_rows = (((0,), (0,)), ((), ()))
    grad_part = jnp.concatenate(
        [
            lax.dot_general(normed, d_projected, contract_rows, preferred_element_type=F32),
            lax.dot_general(returned, mixed, contract_rows, preferred_element_type=F32),
        ],
        axis=1,
    ).astype(BF16)
    grad_own = lax.psum_scatter(grad_part, "fsdp", scatter_dimension=0, tiled=True)
    pieces = lax.all_gather(grad_own, "seq", axis=0, tiled=False).astype(F32)

    def spread(start, size):
        part = pieces[:, :, start : start + size]
        return jnp.transpose(part, (1, 0, 2)).reshape(part.shape[1], groups * size)

    edge = 2 * wide + 2 * STATE
    in_grad = jnp.concatenate(
        [
            spread(0, wide),
            spread(wide, wide),
            jnp.sum(pieces[:, :, 2 * wide : edge], axis=0),
            spread(edge, heads),
        ],
        axis=1,
    )
    out_grad = spread(edge + DT_PAD, wide)

    def placed(part, size):
        return lax.dynamic_update_slice_in_dim(
            jnp.zeros(part.shape[:-1] + (size,), F32), part, where_seq * part.shape[-1], -1
        )

    d_conv_full = jnp.concatenate([placed(d_conv[:, :wide], INNER), d_conv[:, wide:]], axis=1)
    small_part = jnp.concatenate(
        [
            d_in_gain,
            d_conv_full.reshape(-1),
            placed(d_dt_bias, HEADS),
            placed(d_a, HEADS),
            placed(d_skip, HEADS),
            placed(d_out_gain, INNER),
        ]
    )
    in_first_new, in_second_new, in_dir = adam_parts(in_grad, in_first, in_second)
    in_dir = in_dir + WEIGHT_DECAY * in_weight
    out_first_new, out_second_new, out_dir = adam_parts(out_grad, out_first, out_second)
    out_dir = out_dir + WEIGHT_DECAY * out_weight

    partial_sums = jnp.stack(
        [
            jnp.sum(in_weight * in_weight),
            jnp.sum(in_dir * in_dir),
            jnp.sum(out_weight * out_weight),
            jnp.sum(out_dir * out_dir),
        ]
    )
    totals = lax.psum(partial_sums, "fsdp")
    small_grad = lax.psum(small_part, ("seq", "fsdp"))
    norms = jnp.sqrt(totals)
    in_new = in_weight - LEARN_RATE * (norms[0] / norms[1]) * in_dir
    out_new = out_weight - LEARN_RATE * (norms[2] / norms[3]) * out_dir
    small_first_new, small_second_new, small_dir = adam_parts(small_grad, small_first, small_second)
    small_new = small_params - LEARN_RATE * small_dir
    return (
        output,
        input_grad,
        in_grad,
        in_new,
        in_first_new,
        in_second_new,
        out_grad,
        out_new,
        out_first_new,
        out_second_new,
        small_grad,
        small_new,
        small_first_new,
        small_second_new,
        norms,
    )


def solution(mesh):
    matrix = P("fsdp", None)
    rows = P("fsdp", "seq", None)
    return jax.shard_map(
        shards,
        mesh=mesh,
        in_specs=(rows, rows, matrix, matrix, matrix, P(), matrix, matrix, matrix, matrix, P(), P()),
        out_specs=(rows, rows) + (matrix,) * 8 + (P(),) * 5,
        check_vma=False,
    )
```

```python
from functools import partial

import jax
import jax.numpy as jnp
from jax import lax
from jax.experimental import pallas as pl
from jax.experimental.pallas import tpu as pltpu
from jax.sharding import PartitionSpec as P

D = 1536
HEADS = 48
HEAD = 64
STATE = 128
KERNEL = 4
STRETCH = 256
STEP = 5
INNER = 3072
CONV = 3328
PROJ = 6448
DT_PAD = 128

NORM_EPS = 1e-05
FIRST_DECAY = 0.9
SECOND_DECAY = 0.999
ADAM_EPSILON = 1e-06
WEIGHT_DECAY = 0.01
LEARN_RATE = 0.5
F32 = jnp.float32
BF16 = jnp.bfloat16


def split_params(vector):
    offset = 0
    in_gain = vector[offset : offset + D]
    offset = offset + D
    conv_weight = vector[offset : offset + KERNEL * CONV].reshape(KERNEL, CONV)
    offset = offset + KERNEL * CONV
    conv_bias = vector[offset : offset + CONV]
    offset = offset + CONV
    dt_bias = vector[offset : offset + HEADS]
    offset = offset + HEADS
    a_log = vector[offset : offset + HEADS]
    offset = offset + HEADS
    skip_gain = vector[offset : offset + HEADS]
    offset = offset + HEADS
    out_gain = vector[offset : offset + INNER]
    return (in_gain, conv_weight, conv_bias, dt_bias, a_log, skip_gain, out_gain)


def dot(a, b, dims=((1,), (0,))):
    return lax.dot_general(a, b, (dims, ((), ())), preferred_element_type=F32)


def split_dot(value, ones):
    high = value.astype(BF16)
    low = (value - high.astype(F32)).astype(BF16)
    return dot(high, ones) + dot(low, ones)


def tri_dot(ones, value):
    high = value.astype(BF16)
    rest = value - high.astype(F32)
    middle = rest.astype(BF16)
    low = (rest - middle.astype(F32)).astype(BF16)
    return dot(ones, high) + dot(ones, middle) + dot(ones, low)


def sigmoid(v):
    return 1.0 / (1.0 + jnp.exp(-v))


def softplus(v):
    return jnp.maximum(v, 0.0) + jnp.log1p(jnp.exp(-jnp.abs(v)))


def row_at_least():
    rows = lax.broadcasted_iota(jnp.int32, (STRETCH, STRETCH), 0)
    columns = lax.broadcasted_iota(jnp.int32, (STRETCH, STRETCH), 1)
    return rows >= columns


def decays(dt, rate, masks, spread):
    lower = jnp.where(row_at_least(), 1.0, 0.0).astype(BF16)
    cumulative = dot(lower, dt.astype(BF16)) * rate
    last = cumulative[STRETCH - 1 :, :]
    carry = split_dot(jnp.exp(cumulative) * masks[:, 3:4], spread)
    tail = split_dot(jnp.exp(last - cumulative) * masks[:, 4:5], spread)
    keep = split_dot(jnp.broadcast_to(jnp.exp(last) * masks[:1, 5:6], (8, 128)), spread)[:1]
    return cumulative, jnp.transpose(cumulative), carry, tail, keep


def barred(seg_col, seg_row):
    within = row_at_least() & (seg_col == seg_row)
    return jnp.where(within, 0.0, -1e30)


def forward_kernel(
    heads,
    normed,
    w_in,
    returned,
    w_out,
    seg_col,
    seg_row,
    masks_ref,
    conv_pack,
    head_pack,
    chan_pack,
    spread_ref,
    pre_out,
    conv_out,
    z_out,
    dt_out,
    y_out,
    mixed_out,
    states_out,
    stats_out,
    extended,
    state,
):
    wide = heads * HEAD
    edge = wide + 2 * STATE

    @pl.when(pl.program_id(0) == 0)
    def _():
        state[...] = jnp.zeros_like(state)
        extended[0:8, :] = jnp.zeros((8, edge), F32)

    masks = masks_ref[...]
    spread = spread_ref[...]
    z = dot(normed[...], w_in[:, :wide])
    z_out[...] = z
    conv_low = dot(normed[...], w_in[:, wide : wide + edge]).astype(BF16)
    conv_out[...] = conv_low
    conv_in = conv_low.astype(F32)
    extended[8 : 8 + STRETCH, :] = conv_in
    pre = conv_pack[4:5, :] + conv_pack[3:4, :] * conv_in
    for by in range(1, KERNEL):
        pre = pre + conv_pack[3 - by : 4 - by, :] * (
            extended[8 - by : 8 - by + STRETCH, :] * masks[:, 3 - by : 4 - by]
        )
    extended[0:8, :] = extended[STRETCH : STRETCH + 8, :]
    pre_out[...] = pre
    act = (pre * sigmoid(pre)).astype(BF16)
    xs = act[:, :wide].astype(F32)
    b_mat = act[:, wide : wide + STATE]
    c_mat = act[:, wide + STATE :]
    dt_pre = dot(normed[...], w_in[:, wide + edge :]) + head_pack[0:1, :]
    dt_out[...] = dt_pre
    dt = softplus(dt_pre).astype(BF16)
    cumulative, cum_rows, carry, tail, keep = decays(dt, head_pack[1:2, :], masks, spread)
    scaled = xs * dot(dt, spread)
    scaled_low = scaled.astype(BF16)
    bar = barred(seg_col[...], seg_row[...])
    scores = dot(c_mat, b_mat, ((1,), (1,)))
    old = state[...]
    states_out[0] = old
    y_all = dot(c_mat, old.astype(BF16)) * carry + chan_pack[0:1, :] * xs
    state[...] = old * keep + dot(b_mat, (scaled * tail).astype(BF16), ((0,), (0,)))
    first_half = lax.broadcasted_iota(jnp.int32, (STRETCH, 2 * HEAD), 1) < HEAD
    pieces = []
    for pair in range(heads // 2):
        columns = slice(pair * 2 * HEAD, (pair + 1) * 2 * HEAD)
        halves = []
        for h in (2 * pair, 2 * pair + 1):
            weights = scores * jnp.exp(cumulative[:, h : h + 1] - cum_rows[h : h + 1, :] + bar)
            halves.append(dot(weights.astype(BF16), scaled_low[:, columns]))
        pieces.append(jnp.where(first_half, halves[0], halves[1]))
    y_low = (y_all + jnp.concatenate(pieces, axis=1)).astype(BF16)
    y_out[...] = y_low
    gated = y_low.astype(F32) * (z * sigmoid(z))
    d_mixed = dot(returned[...], w_out[...])
    mixed_out[...] = d_mixed
    squares = jnp.sum(gated * gated, axis=1, keepdims=True)
    products = jnp.sum(d_mixed * chan_pack[1:2, :] * gated, axis=1, keepdims=True)
    lane = lax.broadcasted_iota(jnp.int32, (STRETCH, 128), 1)
    both = jnp.where(lane == 0, squares, jnp.where(lane == 1, products, 0.0))
    stats_out[...] = jnp.transpose(both)[0:8, :]


def middle_kernel(
    y_ref, z_ref, d_mixed_ref, stats, chan_pack, mixed_out, d_y_out, d_z_out, d_gain_out
):
    @pl.when(pl.program_id(0) == 0)
    def _():
        d_gain_out[...] = jnp.zeros_like(d_gain_out)

    columns = jnp.transpose(jnp.concatenate([stats[...], jnp.zeros((120, STRETCH), F32)], axis=0))
    rms = lax.rsqrt(columns[:, 0:1] / INNER + NORM_EPS)
    gain = chan_pack[1:2, :]
    y = y_ref[...].astype(F32)
    z = z_ref[...]
    sig = sigmoid(z)
    silu = z * sig
    gated = y * silu
    unit = gated * rms
    d_mixed = d_mixed_ref[...]
    mixed_out[...] = (unit * gain).astype(BF16)
    d_gain_out[0:1, :] += jnp.sum(d_mixed * unit, axis=0, keepdims=True)
    d_gated = d_mixed * gain * rms - unit * (rms * rms / INNER * columns[:, 1:2])
    d_y_out[...] = (d_gated * silu).astype(BF16)
    d_z_out[...] = (d_gated * y * (sig * (1.0 + z * (1.0 - sig)))).astype(BF16)


def backward_kernel(
    heads,
    d_y_ref,
    d_z_ref,
    pre_ref,
    conv_ref,
    dt_ref,
    states,
    seg_col,
    seg_row,
    masks_ref,
    conv_pack,
    head_pack,
    chan_pack,
    spread_ref,
    gather_ref,
    d_proj_out,
    d_conv_out,
    d_head_out,
    extended,
    d_state,
):
    wide = heads * HEAD
    edge = wide + 2 * STATE

    @pl.when(pl.program_id(0) == 0)
    def _():
        d_state[...] = jnp.zeros_like(d_state)
        extended[STRETCH : STRETCH + 8, :] = jnp.zeros((8, edge), F32)
        d_conv_out[...] = jnp.zeros_like(d_conv_out)
        d_head_out[...] = jnp.zeros_like(d_head_out)

    masks = masks_ref[...]
    spread = spread_ref[...]
    gather = gather_ref[...]
    pre = pre_ref[...]
    sig = sigmoid(pre)
    act = (pre * sig).astype(BF16)
    xs = act[:, :wide].astype(F32)
    b_mat = act[:, wide : wide + STATE]
    c_mat = act[:, wide + STATE :]
    dt_pre = dt_ref[...]
    dt = softplus(dt_pre).astype(BF16)
    rate = head_pack[1:2, :]
    cumulative, cum_rows, carry, tail, keep = decays(dt, rate, masks, spread)
    dt_wide = dot(dt, spread)
    scaled = xs * dt_wide
    scaled_low = scaled.astype(BF16)
    bar = barred(seg_col[...], seg_row[...])
    scores = dot(c_mat, b_mat, ((1,), (1,)))
    old = states[0]
    old_low = old.astype(BF16)
    d_new = d_state[...]
    d_new_low = d_new.astype(BF16)
    d_y_low = d_y_ref[...]
    d_y = d_y_low.astype(F32)

    d_carried = d_y * carry
    d_carried_low = d_carried.astype(BF16)
    d_c = dot(d_carried_low, old_low, ((1,), (1,)))
    d_cum = split_dot(d_carried * dot(c_mat, old_low), gather)
    weighed = scaled * tail
    into = dot(b_mat, d_new_low)
    d_b = dot(weighed.astype(BF16), d_new_low, ((1,), (1,)))
    d_scaled = into * tail
    tail_part = split_dot(weighed * into, gather)
    d_cum = d_cum - tail_part
    kept = jnp.sum(d_new * old, axis=0, keepdims=True) * keep
    kept = split_dot(jnp.broadcast_to(kept, (8, wide)), gather)[:1]
    d_last = jnp.sum(tail_part, axis=0, keepdims=True) + kept
    d_state[...] = d_new * keep + dot(c_mat, d_carried_low, ((0,), (0,)))

    lane = lax.broadcasted_iota(jnp.int32, (STRETCH, 128), 1)
    first_half = lane < HEAD
    d_scores = jnp.zeros((STRETCH, STRETCH), F32)
    column_sums = []
    pieces = []
    for pair in range(heads // 2):
        columns = slice(pair * 2 * HEAD, (pair + 1) * 2 * HEAD)
        halves = []
        d_y_pair = d_y_low[:, columns]
        scaled_pair = scaled_low[:, columns]
        zero = jnp.zeros_like(d_y_pair)
        for h in (2 * pair, 2 * pair + 1):
            decay = jnp.exp(cumulative[:, h : h + 1] - cum_rows[h : h + 1, :] + bar)
            weights = scores * decay
            halves.append(dot(weights.astype(BF16), d_y_pair, ((0,), (0,))))
            d_y_head = jnp.where(first_half == (h % 2 == 0), d_y_pair, zero)
            d_weights = dot(d_y_head, scaled_pair, ((1,), (1,)))
            d_scores = d_scores + d_weights * decay
            product = d_weights * weights
            d_cum = d_cum + jnp.where(lane == h, jnp.sum(product, axis=1, keepdims=True), 0.0)
            column_sums.append(jnp.sum(product, axis=0, keepdims=True))
        pieces.append(jnp.where(first_half, halves[0], halves[1]))
    column_sums.append(jnp.zeros((128 - heads, STRETCH), F32))
    d_cum = d_cum - jnp.transpose(jnp.concatenate(column_sums, axis=0))
    row = lax.broadcasted_iota(jnp.int32, (STRETCH, 128), 0)
    d_cum = d_cum + jnp.where(row == STRETCH - 1, d_last, 0.0)
    d_scaled = d_scaled + jnp.concatenate(pieces, axis=1)
    d_scores_low = d_scores.astype(BF16)
    d_c = d_c + dot(d_scores_low, b_mat)
    d_b = d_b + dot(d_scores_low, c_mat, ((0,), (0,)))

    d_xs = d_scaled * dt_wide + chan_pack[0:1, :] * d_y
    rows = lax.broadcasted_iota(jnp.int32, (STRETCH, STRETCH), 0)
    upper = jnp.where(rows <= lax.broadcasted_iota(jnp.int32, (STRETCH, STRETCH), 1), 1.0, 0.0)
    d_dt = split_dot(d_scaled * xs, gather) + rate * tri_dot(upper.astype(BF16), d_cum)
    d_dt_raw = d_dt.astype(BF16).astype(F32) * sigmoid(dt_pre)
    d_head_out[0:1, :] += jnp.sum(d_dt_raw, axis=0, keepdims=True)
    d_head_out[1:2, :] += jnp.sum(d_cum * cumulative, axis=0, keepdims=True)
    d_skip = jnp.sum(d_y * xs, axis=0, keepdims=True)
    d_head_out[2:3, :] += split_dot(jnp.broadcast_to(d_skip, (8, wide)), gather)[:1]

    d_act = jnp.concatenate([d_xs.astype(BF16).astype(F32), d_b, d_c], axis=1)
    d_pre = d_act * (sig * (1.0 + pre * (1.0 - sig)))
    extended[0:STRETCH, :] = d_pre
    conv_in = conv_ref[...].astype(F32)
    d_conv_in = conv_pack[3:4, :] * d_pre
    d_conv_out[3:4, :] += jnp.sum(d_pre * conv_in, axis=0, keepdims=True)
    d_conv_out[4:5, :] += jnp.sum(d_pre, axis=0, keepdims=True)
    for by in range(1, KERNEL):
        moved = extended[by : by + STRETCH, :] * masks[:, 8 + by : 9 + by]
        d_conv_in = d_conv_in + conv_pack[3 - by : 4 - by, :] * moved
        d_conv_out[3 - by : 4 - by, :] += jnp.sum(moved * conv_in, axis=0, keepdims=True)
    extended[STRETCH : STRETCH + 8, :] = extended[0:8, :]
    d_proj_out[:, :wide] = d_z_ref[...]
    d_proj_out[:, wide : wide + edge] = d_conv_in.astype(BF16)
    d_proj_out[:, wide + edge :] = jnp.where(lane < heads, d_dt_raw, 0.0).astype(BF16)


VMEM_BYTES = 56 * 1024 * 1024


def block_masks(segment):
    length = segment.shape[0]
    blocks = segment.reshape(-1, STRETCH)
    prior = jnp.concatenate([segment[:1], blocks[:-1, -1]])[:, None]
    last = blocks[:, -1:]
    columns = [None] * 12
    for by in range(1, KERNEL):
        gap = jnp.full((by,), -1, jnp.int32)
        columns[3 - by] = segment == jnp.concatenate([gap, segment[:-by]])
        columns[8 + by] = segment == jnp.concatenate([segment[by:], gap])
    columns[3] = (blocks == prior).reshape(length)
    columns[4] = (blocks == last).reshape(length)
    columns[5] = jnp.broadcast_to(last == prior, blocks.shape).reshape(length)
    nothing = jnp.zeros((length,), bool)
    packed = jnp.stack([nothing if c is None else c for c in columns], axis=1)
    return jnp.pad(packed.astype(F32), ((0, 0), (0, 116)))


def block(columns, reverse=0):
    if reverse:
        return pl.BlockSpec((STRETCH, columns), lambda i: (reverse - 1 - i, 0))
    return pl.BlockSpec((STRETCH, columns), lambda i: (i, 0))


def whole(*shape):
    return pl.BlockSpec(shape, lambda i: (0,) * len(shape))


def compiler_params():
    return pltpu.CompilerParams(
        vmem_limit_bytes=VMEM_BYTES, dimension_semantics=("arbitrary",)
    )


def run_forward(heads, normed, w_in, returned, w_out, seg, masks, packs, spread):
    length = normed.shape[0]
    blocks = length // STRETCH
    wide = heads * HEAD
    edge = wide + 2 * STATE
    columns = w_in.shape[1]
    flops = 2 * length * D * (columns + wide) + 2 * length * heads * STRETCH * 128
    return pl.pallas_call(
        partial(forward_kernel, heads),
        grid=(blocks,),
        in_specs=[
            block(D),
            whole(D, columns),
            block(D),
            whole(D, wide),
            block(1),
            pl.BlockSpec((1, STRETCH), lambda i: (0, i)),
            block(128),
            whole(8, edge),
            whole(8, 128),
            whole(8, wide),
            whole(128, wide),
        ],
        out_specs=[
            block(edge),
            block(edge),
            block(wide),
            block(128),
            block(wide),
            block(wide),
            pl.BlockSpec((1, STATE, wide), lambda i: (i, 0, 0)),
            pl.BlockSpec((8, STRETCH), lambda i: (0, i)),
        ],
        out_shape=[
            jax.ShapeDtypeStruct((length, edge), F32),
            jax.ShapeDtypeStruct((length, edge), BF16),
            jax.ShapeDtypeStruct((length, wide), F32),
            jax.ShapeDtypeStruct((length, 128), F32),
            jax.ShapeDtypeStruct((length, wide), BF16),
            jax.ShapeDtypeStruct((length, wide), F32),
            jax.ShapeDtypeStruct((blocks, STATE, wide), F32),
            jax.ShapeDtypeStruct((8, length), F32),
        ],
        scratch_shapes=[pltpu.VMEM((STRETCH + 8, edge), F32), pltpu.VMEM((STATE, wide), F32)],
        compiler_params=compiler_params(),
        cost_estimate=pl.CostEstimate(
            flops=flops, bytes_accessed=40 * 1024 * 1024, transcendentals=length * heads * STRETCH
        ),
        name="forward_scan",
    )(normed, w_in, returned, w_out, seg[:, None], seg[None, :], masks, *packs, spread)


def run_middle(heads, y, z, d_mixed, stats, chan_pack):
    length, wide = y.shape
    low = jax.ShapeDtypeStruct((length, wide), BF16)
    return pl.pallas_call(
        middle_kernel,
        grid=(length // STRETCH,),
        in_specs=[
            block(wide),
            block(wide),
            block(wide),
            pl.BlockSpec((8, STRETCH), lambda i: (0, i)),
            whole(8, wide),
        ],
        out_specs=[block(wide), block(wide), block(wide), whole(8, wide)],
        out_shape=[low, low, low, jax.ShapeDtypeStruct((8, wide), F32)],
        compiler_params=compiler_params(),
        cost_estimate=pl.CostEstimate(
            flops=20 * length * wide, bytes_accessed=16 * length * wide, transcendentals=length * wide
        ),
        name="gate_gradients",
    )(y, z, d_mixed, stats, chan_pack)


def run_backward(heads, d_y, d_z, pre, conv, dt_pre, states, seg, masks, packs, spread):
    length = d_y.shape[0]
    blocks = length // STRETCH
    wide = heads * HEAD
    edge = wide + 2 * STATE
    columns = wide + edge + DT_PAD
    flops = 8 * length * heads * STRETCH * 256
    return pl.pallas_call(
        partial(backward_kernel, heads),
        grid=(blocks,),
        in_specs=[
            block(wide, blocks),
            block(wide, blocks),
            block(edge, blocks),
            block(edge, blocks),
            block(128, blocks),
            pl.BlockSpec((1, STATE, wide), lambda i: (blocks - 1 - i, 0, 0)),
            block(1, blocks),
            pl.BlockSpec((1, STRETCH), lambda i: (0, blocks - 1 - i)),
            block(128, blocks),
            whole(8, edge),
            whole(8, 128),
            whole(8, wide),
            whole(128, wide),
            whole(wide, 128),
        ],
        out_specs=[block(columns, blocks), whole(8, edge), whole(8, 128)],
        out_shape=[
            jax.ShapeDtypeStruct((length, columns), BF16),
            jax.ShapeDtypeStruct((8, edge), F32),
            jax.ShapeDtypeStruct((8, 128), F32),
        ],
        scratch_shapes=[pltpu.VMEM((STRETCH + 8, edge), F32), pltpu.VMEM((STATE, wide), F32)],
        compiler_params=compiler_params(),
        cost_estimate=pl.CostEstimate(
            flops=flops, bytes_accessed=40 * 1024 * 1024, transcendentals=length * heads * STRETCH
        ),
        name="backward_scan",
    )(
        d_y, d_z, pre, conv, dt_pre, states, seg[:, None], seg[None, :], masks, *packs, spread, spread.T
    )


def adam_parts(gradient, first_old, second_old):
    first_new = FIRST_DECAY * first_old + (1.0 - FIRST_DECAY) * gradient
    second_new = SECOND_DECAY * second_old + (1.0 - SECOND_DECAY) * gradient * gradient
    direction = (
        first_new
        / (1.0 - FIRST_DECAY**STEP)
        / (jnp.sqrt(second_new / (1.0 - SECOND_DECAY**STEP)) + ADAM_EPSILON)
    )
    return (first_new, second_new, direction)


def shards(
    tokens,
    cotangent,
    segments,
    in_weight,
    out_weight,
    small_params,
    in_first,
    in_second,
    out_first,
    out_second,
    small_first,
    small_second,
):
    in_gain, conv_weight, conv_bias, dt_bias, a_log, skip_gain, out_gain = split_params(
        small_params
    )
    groups = lax.axis_size("seq")
    where_seq = lax.axis_index("seq")
    seq_length = segments.shape[1]
    heads = HEADS // groups
    wide = INNER // groups
    segment_row = segments[0]

    def own(vector, axis=-1):
        size = vector.shape[axis] // groups
        return lax.dynamic_slice_in_dim(vector, where_seq * size, size, axis)

    in_low = in_weight.astype(BF16)
    in_own = jnp.concatenate(
        [
            own(in_low[:, :INNER]),
            own(in_low[:, INNER : 2 * INNER]),
            in_low[:, 2 * INNER : INNER + CONV],
            jnp.pad(own(in_low[:, INNER + CONV :]), ((0, 0), (0, DT_PAD - heads))),
        ],
        axis=1,
    )
    out_own = own(out_weight).astype(BF16)
    in_cols = lax.all_gather(in_own, "fsdp", axis=0, tiled=True)
    out_cols = lax.all_gather(out_own, "fsdp", axis=0, tiled=True)

    inputs = tokens[0].astype(F32)
    in_rms = lax.rsqrt(jnp.mean(inputs * inputs, axis=-1, keepdims=True) + NORM_EPS)
    normed_own = (inputs * in_rms * in_gain).astype(BF16)
    normed = lax.all_gather(normed_own, "seq", axis=0, tiled=True)
    returned = lax.all_gather(cotangent[0], "seq", axis=0, tiled=True)

    conv_own = jnp.concatenate([own(conv_weight[:, :INNER]), conv_weight[:, INNER:]], axis=1)
    bias_own = jnp.concatenate([own(conv_bias[:INNER]), conv_bias[INNER:]])
    conv_pack = jnp.pad(jnp.concatenate([conv_own, bias_own[None]], axis=0), ((0, 3), (0, 0)))
    head_pack = jnp.pad(
        jnp.stack([own(dt_bias), -jnp.exp(own(a_log))]), ((0, 6), (0, 128 - heads))
    )
    chan_pack = jnp.pad(
        jnp.stack([jnp.repeat(own(skip_gain), HEAD), own(out_gain)]), ((0, 6), (0, 0))
    )
    packs = (conv_pack, head_pack, chan_pack)
    spread_heads = (
        jnp.arange(128)[:, None] == jnp.arange(wide)[None, :] // HEAD
    ).astype(BF16)
    masks = block_masks(segment_row)

    pre, conv_in, gate_z, dt_pre, y, d_mixed, states, stats = run_forward(
        heads, normed, in_cols, returned, out_cols, segment_row, masks, packs, spread_heads
    )
    stats = lax.psum(stats, "seq")
    mixed, d_y, d_z, d_out_gain = run_middle(heads, y, gate_z, d_mixed, stats, chan_pack)
    d_out_gain = d_out_gain[0]
    contract_rows = (((0,), (0,)), ((), ()))
    contract_columns = (((1,), (1,)), ((), ()))

    def summed(matrix, axis):
        return lax.psum_scatter(matrix.astype(BF16), axis, scatter_dimension=0, tiled=True)

    out_own_grad = summed(
        lax.dot_general(returned, mixed, contract_rows, preferred_element_type=F32), "fsdp"
    )
    z_own_grad = summed(
        lax.dot_general(normed, d_z, contract_rows, preferred_element_type=F32), "fsdp"
    )
    branch = summed(
        lax.dot_general(mixed, out_cols, contract_columns, preferred_element_type=F32), "seq"
    )
    output = (inputs + branch.astype(F32)).astype(BF16)[None]
    d_projected, d_conv, d_head = run_backward(
        heads, d_y, d_z, pre, conv_in, dt_pre, states, segment_row, masks, packs, spread_heads
    )
    d_conv = d_conv[: KERNEL + 1]
    d_dt_bias, d_a, d_skip = d_head[0, :heads], d_head[1, :heads], d_head[2, :heads]
    rest_own_grad = summed(
        lax.dot_general(normed, d_projected[:, wide:], contract_rows, preferred_element_type=F32),
        "fsdp",
    )
    d_normed = summed(
        lax.dot_general(d_projected, in_cols, contract_columns, preferred_element_type=F32), "seq"
    ).astype(F32)
    slope = d_normed * in_gain[None, :]
    d_inputs = slope * in_rms - inputs * (in_rms**3 / D) * jnp.sum(
        slope * inputs, axis=1, keepdims=True
    )
    input_grad = (cotangent[0].astype(F32) + d_inputs)[None]
    d_in_gain = jnp.sum(d_normed * inputs * in_rms, axis=0)

    early = lax.all_gather(
        jnp.concatenate([z_own_grad, out_own_grad], axis=1), "seq", axis=0, tiled=False
    ).astype(F32)
    late = lax.all_gather(rest_own_grad, "seq", axis=0, tiled=False).astype(F32)

    def spread(pieces, start, size):
        part = pieces[:, :, start : start + size]
        return jnp.transpose(part, (1, 0, 2)).reshape(part.shape[1], groups * size)

    edge = wide + 2 * STATE
    in_grad = jnp.concatenate(
        [
            spread(early, 0, wide),
            spread(late, 0, wide),
            jnp.sum(late[:, :, wide:edge], axis=0),
            spread(late, edge, heads),
        ],
        axis=1,
    )
    out_grad = spread(early, wide, wide)

    def placed(part, size):
        return lax.dynamic_update_slice_in_dim(
            jnp.zeros(part.shape[:-1] + (size,), F32), part, where_seq * part.shape[-1], -1
        )

    d_conv_full = jnp.concatenate([placed(d_conv[:, :wide], INNER), d_conv[:, wide:]], axis=1)
    small_part = jnp.concatenate(
        [
            d_in_gain,
            d_conv_full.reshape(-1),
            placed(d_dt_bias, HEADS),
            placed(d_a, HEADS),
            placed(d_skip, HEADS),
            placed(d_out_gain, INNER),
        ]
    )
    in_first_new, in_second_new, in_dir = adam_parts(in_grad, in_first, in_second)
    in_dir = in_dir + WEIGHT_DECAY * in_weight
    out_first_new, out_second_new, out_dir = adam_parts(out_grad, out_first, out_second)
    out_dir = out_dir + WEIGHT_DECAY * out_weight

    partial_sums = jnp.stack(
        [
            jnp.sum(in_weight * in_weight),
            jnp.sum(in_dir * in_dir),
            jnp.sum(out_weight * out_weight),
            jnp.sum(out_dir * out_dir),
        ]
    )
    totals = lax.psum(partial_sums, "fsdp")
    small_grad = lax.psum(small_part, ("seq", "fsdp"))
    norms = jnp.sqrt(totals)
    in_new = in_weight - LEARN_RATE * (norms[0] / norms[1]) * in_dir
    out_new = out_weight - LEARN_RATE * (norms[2] / norms[3]) * out_dir
    small_first_new, small_second_new, small_dir = adam_parts(small_grad, small_first, small_second)
    small_new = small_params - LEARN_RATE * small_dir
    return (
        output,
        input_grad,
        in_grad,
        in_new,
        in_first_new,
        in_second_new,
        out_grad,
        out_new,
        out_first_new,
        out_second_new,
        small_grad,
        small_new,
        small_first_new,
        small_second_new,
        norms,
    )


def solution(mesh):
    matrix = P("fsdp", None)
    rows = P("fsdp", "seq", None)
    return jax.shard_map(
        shards,
        mesh=mesh,
        in_specs=(rows, rows, matrix, matrix, matrix, P(), matrix, matrix, matrix, matrix, P(), P()),
        out_specs=(rows, rows) + (matrix,) * 8 + (P(),) * 5,
        check_vma=False,
    )
```

```python
from functools import partial

import jax
import jax.numpy as jnp
from jax import lax
from jax.experimental import pallas as pl
from jax.experimental.pallas import tpu as pltpu
from jax.sharding import PartitionSpec as P

D = 1536
HEADS = 48
HEAD = 64
STATE = 128
KERNEL = 4
STRETCH = 256
STEP = 5
INNER = 3072
CONV = 3328
PROJ = 6448
DT_PAD = 128

NORM_EPS = 1e-05
FIRST_DECAY = 0.9
SECOND_DECAY = 0.999
ADAM_EPSILON = 1e-06
WEIGHT_DECAY = 0.01
LEARN_RATE = 0.5
F32 = jnp.float32
BF16 = jnp.bfloat16


def split_params(vector):
    offset = 0
    in_gain = vector[offset : offset + D]
    offset = offset + D
    conv_weight = vector[offset : offset + KERNEL * CONV].reshape(KERNEL, CONV)
    offset = offset + KERNEL * CONV
    conv_bias = vector[offset : offset + CONV]
    offset = offset + CONV
    dt_bias = vector[offset : offset + HEADS]
    offset = offset + HEADS
    a_log = vector[offset : offset + HEADS]
    offset = offset + HEADS
    skip_gain = vector[offset : offset + HEADS]
    offset = offset + HEADS
    out_gain = vector[offset : offset + INNER]
    return (in_gain, conv_weight, conv_bias, dt_bias, a_log, skip_gain, out_gain)


def dot(a, b, dims=((1,), (0,))):
    return lax.dot_general(a, b, (dims, ((), ())), preferred_element_type=F32)


def split_dot(value, ones):
    high = value.astype(BF16)
    low = (value - high.astype(F32)).astype(BF16)
    return dot(high, ones) + dot(low, ones)


def tri_dot(ones, value):
    high = value.astype(BF16)
    rest = value - high.astype(F32)
    middle = rest.astype(BF16)
    low = (rest - middle.astype(F32)).astype(BF16)
    return dot(ones, high) + dot(ones, middle) + dot(ones, low)


def sigmoid(v):
    return 1.0 / (1.0 + jnp.exp(-v))


def softplus(v):
    return jnp.maximum(v, 0.0) + jnp.log1p(jnp.exp(-jnp.abs(v)))


def row_at_least():
    rows = lax.broadcasted_iota(jnp.int32, (STRETCH, STRETCH), 0)
    columns = lax.broadcasted_iota(jnp.int32, (STRETCH, STRETCH), 1)
    return rows >= columns


def decays(dt, rate, masks, spread):
    lower = jnp.where(row_at_least(), 1.0, 0.0).astype(BF16)
    cumulative = dot(lower, dt.astype(BF16)) * rate
    last = cumulative[STRETCH - 1 :, :]
    carry = split_dot(jnp.exp(cumulative) * masks[:, 3:4], spread)
    tail = split_dot(jnp.exp(last - cumulative) * masks[:, 4:5], spread)
    keep = split_dot(jnp.broadcast_to(jnp.exp(last) * masks[:1, 5:6], (8, 128)), spread)[:1]
    return cumulative, jnp.transpose(cumulative), carry, tail, keep


def barred(seg_col, seg_row):
    within = row_at_least() & (seg_col == seg_row)
    return jnp.where(within, 0.0, -1e30)


def forward_kernel(
    heads,
    normed,
    returned,
    weights_ref,
    seg_col,
    seg_row,
    masks_ref,
    conv_pack,
    head_pack,
    chan_pack,
    spread_ref,
    pre_out,
    conv_out,
    z_out,
    dt_out,
    y_out,
    mixed_out,
    states_out,
    stats_out,
    extended,
    state,
):
    wide = heads * HEAD
    edge = wide + 2 * STATE
    inner = wide + edge + DT_PAD

    @pl.when(pl.program_id(0) == 0)
    def _():
        state[...] = jnp.zeros_like(state)
        extended[0:8, :] = jnp.zeros((8, edge), F32)

    masks = masks_ref[...]
    spread = spread_ref[...]
    z = dot(normed[...], weights_ref[:, :wide])
    z_out[...] = z
    conv_low = dot(normed[...], weights_ref[:, wide : wide + edge]).astype(BF16)
    conv_out[...] = conv_low
    conv_in = conv_low.astype(F32)
    extended[8 : 8 + STRETCH, :] = conv_in
    pre = conv_pack[4:5, :] + conv_pack[3:4, :] * conv_in
    for by in range(1, KERNEL):
        pre = pre + conv_pack[3 - by : 4 - by, :] * (
            extended[8 - by : 8 - by + STRETCH, :] * masks[:, 3 - by : 4 - by]
        )
    extended[0:8, :] = extended[STRETCH : STRETCH + 8, :]
    pre_out[...] = pre
    act = (pre * sigmoid(pre)).astype(BF16)
    xs = act[:, :wide].astype(F32)
    b_mat = act[:, wide : wide + STATE]
    c_mat = act[:, wide + STATE :]
    dt_pre = dot(normed[...], weights_ref[:, wide + edge : inner]) + head_pack[0:1, :]
    dt_out[...] = dt_pre
    dt = softplus(dt_pre).astype(BF16)
    cumulative, cum_rows, carry, tail, keep = decays(dt, head_pack[1:2, :], masks, spread)
    scaled = xs * dot(dt, spread)
    scaled_low = scaled.astype(BF16)
    bar = barred(seg_col[...], seg_row[...])
    scores = dot(c_mat, b_mat, ((1,), (1,)))
    old = state[...]
    states_out[0] = old
    y_all = dot(c_mat, old.astype(BF16)) * carry + chan_pack[0:1, :] * xs
    state[...] = old * keep + dot(b_mat, (scaled * tail).astype(BF16), ((0,), (0,)))
    first_half = lax.broadcasted_iota(jnp.int32, (STRETCH, 2 * HEAD), 1) < HEAD
    pieces = []
    for pair in range(heads // 2):
        columns = slice(pair * 2 * HEAD, (pair + 1) * 2 * HEAD)
        halves = []
        for h in (2 * pair, 2 * pair + 1):
            weights = scores * jnp.exp(cumulative[:, h : h + 1] - cum_rows[h : h + 1, :] + bar)
            halves.append(dot(weights.astype(BF16), scaled_low[:, columns]))
        pieces.append(jnp.where(first_half, halves[0], halves[1]))
    y_low = (y_all + jnp.concatenate(pieces, axis=1)).astype(BF16)
    y_out[...] = y_low
    gated = y_low.astype(F32) * (z * sigmoid(z))
    d_mixed = dot(returned[...], weights_ref[:, inner:])
    mixed_out[...] = d_mixed
    squares = jnp.sum(gated * gated, axis=1, keepdims=True)
    products = jnp.sum(d_mixed * chan_pack[1:2, :] * gated, axis=1, keepdims=True)
    lane = lax.broadcasted_iota(jnp.int32, (STRETCH, 128), 1)
    both = jnp.where(lane == 0, squares, jnp.where(lane == 1, products, 0.0))
    stats_out[...] = jnp.transpose(both)[0:8, :]


def middle_kernel(
    y_ref, z_ref, d_mixed_ref, stats, chan_pack, mixed_out, d_y_out, d_z_out, d_gain_out
):
    @pl.when(pl.program_id(0) == 0)
    def _():
        d_gain_out[...] = jnp.zeros_like(d_gain_out)

    columns = jnp.transpose(jnp.concatenate([stats[...], jnp.zeros((120, STRETCH), F32)], axis=0))
    rms = lax.rsqrt(columns[:, 0:1] / INNER + NORM_EPS)
    gain = chan_pack[1:2, :]
    y = y_ref[...].astype(F32)
    z = z_ref[...]
    sig = sigmoid(z)
    silu = z * sig
    gated = y * silu
    unit = gated * rms
    d_mixed = d_mixed_ref[...]
    mixed_out[...] = (unit * gain).astype(BF16)
    d_gain_out[0:1, :] += jnp.sum(d_mixed * unit, axis=0, keepdims=True)
    d_gated = d_mixed * gain * rms - unit * (rms * rms / INNER * columns[:, 1:2])
    d_y_out[...] = (d_gated * silu).astype(BF16)
    d_z_out[...] = (d_gated * y * (sig * (1.0 + z * (1.0 - sig)))).astype(BF16)


def backward_kernel(
    heads,
    d_y_ref,
    d_z_ref,
    pre_ref,
    conv_ref,
    dt_ref,
    states,
    seg_col,
    seg_row,
    masks_ref,
    conv_pack,
    head_pack,
    chan_pack,
    spread_ref,
    gather_ref,
    d_proj_out,
    d_conv_out,
    d_head_out,
    extended,
    d_state,
):
    wide = heads * HEAD
    edge = wide + 2 * STATE

    @pl.when(pl.program_id(0) == 0)
    def _():
        d_state[...] = jnp.zeros_like(d_state)
        extended[STRETCH : STRETCH + 8, :] = jnp.zeros((8, edge), F32)
        d_conv_out[...] = jnp.zeros_like(d_conv_out)
        d_head_out[...] = jnp.zeros_like(d_head_out)

    masks = masks_ref[...]
    spread = spread_ref[...]
    gather = gather_ref[...]
    pre = pre_ref[...]
    sig = sigmoid(pre)
    act = (pre * sig).astype(BF16)
    xs = act[:, :wide].astype(F32)
    b_mat = act[:, wide : wide + STATE]
    c_mat = act[:, wide + STATE :]
    dt_pre = dt_ref[...]
    dt = softplus(dt_pre).astype(BF16)
    rate = head_pack[1:2, :]
    cumulative, cum_rows, carry, tail, keep = decays(dt, rate, masks, spread)
    dt_wide = dot(dt, spread)
    scaled = xs * dt_wide
    scaled_low = scaled.astype(BF16)
    bar = barred(seg_col[...], seg_row[...])
    scores = dot(c_mat, b_mat, ((1,), (1,)))
    old = states[0]
    old_low = old.astype(BF16)
    d_new = d_state[...]
    d_new_low = d_new.astype(BF16)
    d_y_low = d_y_ref[...]
    d_y = d_y_low.astype(F32)

    d_carried = d_y * carry
    d_carried_low = d_carried.astype(BF16)
    d_c = dot(d_carried_low, old_low, ((1,), (1,)))
    d_cum = split_dot(d_carried * dot(c_mat, old_low), gather)
    weighed = scaled * tail
    into = dot(b_mat, d_new_low)
    d_b = dot(weighed.astype(BF16), d_new_low, ((1,), (1,)))
    d_scaled = into * tail
    tail_part = split_dot(weighed * into, gather)
    d_cum = d_cum - tail_part
    kept = jnp.sum(d_new * old, axis=0, keepdims=True) * keep
    kept = split_dot(jnp.broadcast_to(kept, (8, wide)), gather)[:1]
    d_last = jnp.sum(tail_part, axis=0, keepdims=True) + kept
    d_state[...] = d_new * keep + dot(c_mat, d_carried_low, ((0,), (0,)))

    lane = lax.broadcasted_iota(jnp.int32, (STRETCH, 128), 1)
    first_half = lane < HEAD
    d_scores = jnp.zeros((STRETCH, STRETCH), F32)
    column_sums = []
    pieces = []
    for pair in range(heads // 2):
        columns = slice(pair * 2 * HEAD, (pair + 1) * 2 * HEAD)
        halves = []
        d_y_pair = d_y_low[:, columns]
        scaled_pair = scaled_low[:, columns]
        zero = jnp.zeros_like(d_y_pair)
        for h in (2 * pair, 2 * pair + 1):
            decay = jnp.exp(cumulative[:, h : h + 1] - cum_rows[h : h + 1, :] + bar)
            weights = scores * decay
            halves.append(dot(weights.astype(BF16), d_y_pair, ((0,), (0,))))
            d_y_head = jnp.where(first_half == (h % 2 == 0), d_y_pair, zero)
            d_weights = dot(d_y_head, scaled_pair, ((1,), (1,)))
            d_scores = d_scores + d_weights * decay
            product = d_weights * weights
            d_cum = d_cum + jnp.where(lane == h, jnp.sum(product, axis=1, keepdims=True), 0.0)
            column_sums.append(jnp.sum(product, axis=0, keepdims=True))
        pieces.append(jnp.where(first_half, halves[0], halves[1]))
    column_sums.append(jnp.zeros((128 - heads, STRETCH), F32))
    d_cum = d_cum - jnp.transpose(jnp.concatenate(column_sums, axis=0))
    row = lax.broadcasted_iota(jnp.int32, (STRETCH, 128), 0)
    d_cum = d_cum + jnp.where(row == STRETCH - 1, d_last, 0.0)
    d_scaled = d_scaled + jnp.concatenate(pieces, axis=1)
    d_scores_low = d_scores.astype(BF16)
    d_c = d_c + dot(d_scores_low, b_mat)
    d_b = d_b + dot(d_scores_low, c_mat, ((0,), (0,)))

    d_xs = d_scaled * dt_wide + chan_pack[0:1, :] * d_y
    rows = lax.broadcasted_iota(jnp.int32, (STRETCH, STRETCH), 0)
    upper = jnp.where(rows <= lax.broadcasted_iota(jnp.int32, (STRETCH, STRETCH), 1), 1.0, 0.0)
    d_dt = split_dot(d_scaled * xs, gather) + rate * tri_dot(upper.astype(BF16), d_cum)
    d_dt_raw = d_dt.astype(BF16).astype(F32) * sigmoid(dt_pre)
    d_head_out[0:1, :] += jnp.sum(d_dt_raw, axis=0, keepdims=True)
    d_head_out[1:2, :] += jnp.sum(d_cum * cumulative, axis=0, keepdims=True)
    d_skip = jnp.sum(d_y * xs, axis=0, keepdims=True)
    d_head_out[2:3, :] += split_dot(jnp.broadcast_to(d_skip, (8, wide)), gather)[:1]

    d_act = jnp.concatenate([d_xs.astype(BF16).astype(F32), d_b, d_c], axis=1)
    d_pre = d_act * (sig * (1.0 + pre * (1.0 - sig)))
    extended[0:STRETCH, :] = d_pre
    conv_in = conv_ref[...].astype(F32)
    d_conv_in = conv_pack[3:4, :] * d_pre
    d_conv_out[3:4, :] += jnp.sum(d_pre * conv_in, axis=0, keepdims=True)
    d_conv_out[4:5, :] += jnp.sum(d_pre, axis=0, keepdims=True)
    for by in range(1, KERNEL):
        moved = extended[by : by + STRETCH, :] * masks[:, 8 + by : 9 + by]
        d_conv_in = d_conv_in + conv_pack[3 - by : 4 - by, :] * moved
        d_conv_out[3 - by : 4 - by, :] += jnp.sum(moved * conv_in, axis=0, keepdims=True)
    extended[STRETCH : STRETCH + 8, :] = extended[0:8, :]
    d_proj_out[:, :wide] = d_z_ref[...]
    d_proj_out[:, wide : wide + edge] = d_conv_in.astype(BF16)
    d_proj_out[:, wide + edge :] = jnp.where(lane < heads, d_dt_raw, 0.0).astype(BF16)


VMEM_BYTES = 56 * 1024 * 1024


def block_masks(segment):
    length = segment.shape[0]
    blocks = segment.reshape(-1, STRETCH)
    prior = jnp.concatenate([segment[:1], blocks[:-1, -1]])[:, None]
    last = blocks[:, -1:]
    columns = [None] * 12
    for by in range(1, KERNEL):
        gap = jnp.full((by,), -1, jnp.int32)
        columns[3 - by] = segment == jnp.concatenate([gap, segment[:-by]])
        columns[8 + by] = segment == jnp.concatenate([segment[by:], gap])
    columns[3] = (blocks == prior).reshape(length)
    columns[4] = (blocks == last).reshape(length)
    columns[5] = jnp.broadcast_to(last == prior, blocks.shape).reshape(length)
    nothing = jnp.zeros((length,), bool)
    packed = jnp.stack([nothing if c is None else c for c in columns], axis=1)
    return jnp.pad(packed.astype(F32), ((0, 0), (0, 116)))


def block(columns, reverse=0):
    if reverse:
        return pl.BlockSpec((STRETCH, columns), lambda i: (reverse - 1 - i, 0))
    return pl.BlockSpec((STRETCH, columns), lambda i: (i, 0))


def whole(*shape):
    return pl.BlockSpec(shape, lambda i: (0,) * len(shape))


def compiler_params():
    return pltpu.CompilerParams(
        vmem_limit_bytes=VMEM_BYTES, dimension_semantics=("arbitrary",)
    )


def run_forward(heads, rows, weights, seg, masks, packs, spread):
    length = rows.shape[0]
    blocks = length // STRETCH
    wide = heads * HEAD
    edge = wide + 2 * STATE
    columns = weights.shape[1]
    flops = 2 * length * D * columns + 2 * length * heads * STRETCH * 128
    return pl.pallas_call(
        partial(forward_kernel, heads),
        grid=(blocks,),
        in_specs=[
            block(D),
            pl.BlockSpec((STRETCH, D), lambda i: (i, 1)),
            whole(D, columns),
            block(1),
            pl.BlockSpec((1, STRETCH), lambda i: (0, i)),
            block(128),
            whole(8, edge),
            whole(8, 128),
            whole(8, wide),
            whole(128, wide),
        ],
        out_specs=[
            block(edge),
            block(edge),
            block(wide),
            block(128),
            block(wide),
            block(wide),
            pl.BlockSpec((1, STATE, wide), lambda i: (i, 0, 0)),
            pl.BlockSpec((8, STRETCH), lambda i: (0, i)),
        ],
        out_shape=[
            jax.ShapeDtypeStruct((length, edge), F32),
            jax.ShapeDtypeStruct((length, edge), BF16),
            jax.ShapeDtypeStruct((length, wide), F32),
            jax.ShapeDtypeStruct((length, 128), F32),
            jax.ShapeDtypeStruct((length, wide), BF16),
            jax.ShapeDtypeStruct((length, wide), F32),
            jax.ShapeDtypeStruct((blocks, STATE, wide), F32),
            jax.ShapeDtypeStruct((8, length), F32),
        ],
        scratch_shapes=[pltpu.VMEM((STRETCH + 8, edge), F32), pltpu.VMEM((STATE, wide), F32)],
        compiler_params=compiler_params(),
        cost_estimate=pl.CostEstimate(
            flops=flops, bytes_accessed=40 * 1024 * 1024, transcendentals=length * heads * STRETCH
        ),
        name="forward_scan",
    )(rows, rows, weights, seg[:, None], seg[None, :], masks, *packs, spread)


def run_middle(heads, y, z, d_mixed, stats, chan_pack):
    length, wide = y.shape
    low = jax.ShapeDtypeStruct((length, wide), BF16)
    return pl.pallas_call(
        middle_kernel,
        grid=(length // STRETCH,),
        in_specs=[
            block(wide),
            block(wide),
            block(wide),
            pl.BlockSpec((8, STRETCH), lambda i: (0, i)),
            whole(8, wide),
        ],
        out_specs=[block(wide), block(wide), block(wide), whole(8, wide)],
        out_shape=[low, low, low, jax.ShapeDtypeStruct((8, wide), F32)],
        compiler_params=compiler_params(),
        cost_estimate=pl.CostEstimate(
            flops=20 * length * wide, bytes_accessed=16 * length * wide, transcendentals=length * wide
        ),
        name="gate_gradients",
    )(y, z, d_mixed, stats, chan_pack)


def run_backward(heads, d_y, d_z, pre, conv, dt_pre, states, seg, masks, packs, spread):
    length = d_y.shape[0]
    blocks = length // STRETCH
    wide = heads * HEAD
    edge = wide + 2 * STATE
    columns = wide + edge + DT_PAD
    flops = 8 * length * heads * STRETCH * 256
    return pl.pallas_call(
        partial(backward_kernel, heads),
        grid=(blocks,),
        in_specs=[
            block(wide, blocks),
            block(wide, blocks),
            block(edge, blocks),
            block(edge, blocks),
            block(128, blocks),
            pl.BlockSpec((1, STATE, wide), lambda i: (blocks - 1 - i, 0, 0)),
            block(1, blocks),
            pl.BlockSpec((1, STRETCH), lambda i: (0, blocks - 1 - i)),
            block(128, blocks),
            whole(8, edge),
            whole(8, 128),
            whole(8, wide),
            whole(128, wide),
            whole(wide, 128),
        ],
        out_specs=[block(columns, blocks), whole(8, edge), whole(8, 128)],
        out_shape=[
            jax.ShapeDtypeStruct((length, columns), BF16),
            jax.ShapeDtypeStruct((8, edge), F32),
            jax.ShapeDtypeStruct((8, 128), F32),
        ],
        scratch_shapes=[pltpu.VMEM((STRETCH + 8, edge), F32), pltpu.VMEM((STATE, wide), F32)],
        compiler_params=compiler_params(),
        cost_estimate=pl.CostEstimate(
            flops=flops, bytes_accessed=40 * 1024 * 1024, transcendentals=length * heads * STRETCH
        ),
        name="backward_scan",
    )(
        d_y, d_z, pre, conv, dt_pre, states, seg[:, None], seg[None, :], masks, *packs, spread, spread.T
    )


class Place:
    def __init__(self, axis, minor):
        self.axis = axis
        self.minor = minor
        self.major = lax.axis_size(axis) // minor
        index = lax.axis_index(axis)
        self.at_major = index // minor
        self.at_minor = index % minor
        self.index = index

    def slot(self, by_major, by_minor):
        return (self.at_major + by_major) % self.major * self.minor + (
            self.at_minor + by_minor
        ) % self.minor

    def others(self):
        along = [self.slot(step, 0) for step in range(1, self.major)]
        return along + [self.slot(0, step) for step in range(1, self.minor)]


def places():
    ring = lax.axis_size("fsdp")
    side = 1
    while 2 * side * 2 * side * 2 <= ring:
        side = 2 * side
    return Place("fsdp", side), Place("seq", 2)


def meet(*all_places):
    barrier = pltpu.get_barrier_semaphore()
    count = 0
    for place in all_places:
        for other in place.others():
            pl.semaphore_signal(
                barrier, inc=1, device_id={place.axis: other}, device_id_type=pl.DeviceIdType.MESH
            )
            count = count + 1
    pl.semaphore_wait(barrier, count)


def send(place, source, target, to, sends, arrivals, at):
    return pltpu.make_async_remote_copy(
        src_ref=source,
        dst_ref=target,
        send_sem=sends.at[at],
        recv_sem=arrivals.at[at],
        device_id={place.axis: to},
        device_id_type=pl.DeviceIdType.MESH,
    )


class Gather:
    def __init__(self, place, own, full, rows, pieces, sems):
        self.place, self.own, self.full = place, own, full
        self.size, self.pieces = rows // pieces, pieces
        self.sends1, self.arrivals1, self.sends2, self.arrivals2, self.here = sems

    @staticmethod
    def scratch(place, pieces):
        first = max(place.major - 1, 1) * pieces
        second = place.major * (place.minor - 1) * pieces
        dma = pltpu.SemaphoreType.DMA
        return [dma((first,)), dma((first,)), dma((second,)), dma((second,)), dma((1,))]

    def rows(self, piece):
        return pl.ds(piece * self.size, self.size)

    def along(self, piece, step):
        place = self.place
        return send(
            place,
            self.own.at[self.rows(piece)],
            self.full.at[place.index, self.rows(piece)],
            place.slot(step, 0),
            self.sends1,
            self.arrivals1,
            piece * (place.major - 1) + step - 1,
        )

    def across(self, piece, step, across):
        place = self.place
        slot = place.slot(-step, 0)
        target = self.full.at[slot, self.rows(piece)]
        source = self.own.at[self.rows(piece)] if step == 0 else target
        at = (piece * place.major + step) * (place.minor - 1) + across - 1
        return send(
            place, source, target, place.slot(0, across), self.sends2, self.arrivals2, at
        )

    def keep(self):
        return pltpu.make_async_copy(self.own, self.full.at[self.place.index], self.here.at[0])

    def begin(self, piece):
        for step in range(1, self.place.major):
            self.along(piece, step).start()
        for across in range(1, self.place.minor):
            self.across(piece, 0, across).start()

    def forward(self, piece):
        for step in range(1, self.place.major):
            self.along(piece, step).wait_recv()
            for across in range(1, self.place.minor):
                self.across(piece, step, across).start()

    def finish(self):
        for piece in range(self.pieces):
            for step in range(1, self.place.major):
                self.along(piece, step).wait_send()
            for step in range(self.place.major):
                for across in range(1, self.place.minor):
                    self.across(piece, step, across).wait()


class Reduce:
    def __init__(self, place, part, total, rows, pieces, scratch):
        self.place, self.part, self.total = place, part, total
        self.size, self.pieces = rows // pieces, pieces
        self.got1, self.mine, self.got2, self.sends1, self.arrivals1, self.sends2, self.arrivals2 = (
            scratch
        )

    @staticmethod
    def scratch(place, rows, columns, pieces):
        dma = pltpu.SemaphoreType.DMA
        first = place.major * (place.minor - 1)
        second = max(place.major - 1, 1)
        return [
            pltpu.VMEM((first, rows, columns), BF16),
            pltpu.VMEM((place.major, rows, columns), BF16),
            pltpu.VMEM((second, rows, columns), BF16),
            dma((first * pieces,)),
            dma((first * pieces,)),
            dma((second * pieces,)),
            dma((second * pieces,)),
        ]

    def items(self):
        place = self.place
        steps = list(range(1, place.major)) + [0]
        return [(piece, step) for piece in range(self.pieces) for step in steps]

    def rows(self, piece):
        return pl.ds(piece * self.size, self.size)

    def across(self, item, across):
        piece, step = item
        place = self.place
        slot = step * (place.minor - 1) + across - 1
        return send(
            place,
            self.part.at[place.slot(step, across), self.rows(piece)],
            self.got1.at[slot, self.rows(piece)],
            place.slot(0, across),
            self.sends1,
            self.arrivals1,
            slot * self.pieces + piece,
        )

    def along(self, item):
        piece, step = item
        place = self.place
        return send(
            place,
            self.mine.at[step, self.rows(piece)],
            self.got2.at[step - 1, self.rows(piece)],
            place.slot(step, 0),
            self.sends2,
            self.arrivals2,
            (step - 1) * self.pieces + piece,
        )

    def begin(self, item):
        for across in range(1, self.place.minor):
            self.across(item, across).start()

    def blocks(self, piece, body):
        def one(at, _):
            body(pl.ds(pl.multiple_of(piece * self.size + at * 16, 16), 16))
            return 0

        lax.fori_loop(0, self.size // 16, one, 0)

    def handle(self, item):
        piece, step = item
        place = self.place
        for across in range(1, place.minor):
            self.across(item, across).wait_recv()
        if step == 0:
            return
        own = place.slot(step, 0)

        def body(rows):
            value = self.part[own, rows].astype(F32)
            for across in range(1, place.minor):
                slot = step * (place.minor - 1) + across - 1
                value = value + self.got1[slot, rows].astype(F32)
            self.mine[step, rows] = value.astype(BF16)

        self.blocks(piece, body)
        self.along(item).start()

    def close(self, piece):
        place = self.place
        for step in range(1, place.major):
            self.along((piece, step)).wait_recv()

        def body(rows):
            value = self.part[place.index, rows].astype(F32)
            for across in range(1, place.minor):
                value = value + self.got1[across - 1, rows].astype(F32)
            for step in range(1, place.major):
                value = value + self.got2[step - 1, rows].astype(F32)
            self.total[rows] = value.astype(self.total.dtype)

        self.blocks(piece, body)

    def finish(self):
        for item in self.items():
            for across in range(1, self.place.minor):
                self.across(item, across).wait_send()
            if item[1]:
                self.along(item).wait_send()


WEIGHT_PIECES = 3
TOKEN_PIECES = 4
HBM = pl.BlockSpec(memory_space=pl.ANY)
VMEM = pl.BlockSpec(memory_space=pltpu.VMEM)


def comm_params(number):
    return pltpu.CompilerParams(
        collective_id=number, has_side_effects=True, vmem_limit_bytes=VMEM_BYTES
    )


def gather_kernel(weights, rows, weights_all, rows_all, *sems):
    ring, seq = places()
    meet(ring, seq)
    first = Gather(ring, weights, weights_all, weights.shape[0], WEIGHT_PIECES, sems[:5])
    second = Gather(seq, rows, rows_all, rows.shape[0], TOKEN_PIECES, sems[5:])
    for piece in range(TOKEN_PIECES):
        if piece < WEIGHT_PIECES:
            first.begin(piece)
        second.begin(piece)
    first.keep().start()
    second.keep().start()
    for piece in range(TOKEN_PIECES):
        second.forward(piece)
        if piece < WEIGHT_PIECES:
            first.forward(piece)
    first.finish()
    second.finish()
    first.keep().wait()
    second.keep().wait()


def run_gather(weights, rows):
    ring, seq = places()
    count, groups = lax.axis_size("fsdp"), lax.axis_size("seq")
    full = [
        jax.ShapeDtypeStruct((count,) + weights.shape, BF16),
        jax.ShapeDtypeStruct((groups,) + rows.shape, BF16),
    ]
    out = pl.pallas_call(
        gather_kernel,
        in_specs=[HBM, HBM],
        out_specs=[HBM, HBM],
        out_shape=full,
        scratch_shapes=Gather.scratch(ring, WEIGHT_PIECES) + Gather.scratch(seq, TOKEN_PIECES),
        compiler_params=comm_params(1),
        name="gather_weights_and_rows",
    )(weights, rows)
    return [x.reshape(x.shape[0] * x.shape[1], x.shape[2]) for x in out]


def reduce_kernel(
    out_part, in_part, branch_part, d_normed_part, out_all, in_all, branch, d_normed, *scratch
):
    ring, seq = places()
    meet(ring, seq)
    out_own, in_own = scratch[:2]
    scratch = scratch[2:]
    rows = out_part.shape[1]
    places_rows = branch_part.shape[1]
    grads = [
        Reduce(ring, out_part, out_own, rows, WEIGHT_PIECES, scratch[:7]),
        Reduce(ring, in_part, in_own, rows, WEIGHT_PIECES, scratch[7:14]),
    ]
    acts = [
        Reduce(seq, branch_part, branch, places_rows, TOKEN_PIECES, scratch[14:21]),
        Reduce(seq, d_normed_part, d_normed, places_rows, TOKEN_PIECES, scratch[21:28]),
    ]
    spread = [
        Gather(seq, out_own, out_all, rows, WEIGHT_PIECES, scratch[28:33]),
        Gather(seq, in_own, in_all, rows, WEIGHT_PIECES, scratch[33:38]),
    ]
    work = [(k, item) for k in (0, 1) for item in grads[k].items()]
    side = [(k, item) for k in (0, 1) for item in acts[k].items()]
    ahead = 4

    def begin(streams, queue, at):
        if at < len(queue):
            streams[queue[at][0]].begin(queue[at][1])

    def close(at):
        k, piece = divmod(at, WEIGHT_PIECES)
        grads[k].close(piece)
        spread[k].begin(piece)

    for at in range(ahead):
        begin(grads, work, at)
        begin(acts, side, at)
    closed = 0
    forwarded = 0
    for at in range(max(len(work), len(side))):
        begin(grads, work, at + ahead)
        begin(acts, side, at + ahead)
        if at < len(work):
            k, item = work[at]
            grads[k].handle(item)
            if item[1] == 0 and closed < k * WEIGHT_PIECES + item[0]:
                close(closed)
                closed = closed + 1
        if at < len(side):
            k, item = side[at]
            acts[k].handle(item)
            if item[1] == 0:
                acts[k].close(item[0])
    while closed < 2 * WEIGHT_PIECES:
        close(closed)
        closed = closed + 1
    for k in (0, 1):
        spread[k].keep().start()
        for piece in range(WEIGHT_PIECES):
            spread[k].forward(piece)
    for k in (0, 1):
        grads[k].finish()
        acts[k].finish()
        spread[k].finish()
        spread[k].keep().wait()


def run_reduce(out_part, in_part, branch, d_normed):
    ring, seq = places()
    count, groups = lax.axis_size("fsdp"), lax.axis_size("seq")

    def split(x, by):
        return x.reshape(by, x.shape[0] // by, x.shape[1])

    grads = [split(out_part, count), split(in_part, count)]
    acts = [split(branch, groups), split(d_normed, groups)]
    scratch = [pltpu.VMEM(x.shape[1:], BF16) for x in grads]
    for x in grads:
        scratch = scratch + Reduce.scratch(ring, x.shape[1], x.shape[2], WEIGHT_PIECES)
    for x in acts:
        scratch = scratch + Reduce.scratch(seq, x.shape[1], x.shape[2], TOKEN_PIECES)
    for x in grads:
        scratch = scratch + Gather.scratch(seq, WEIGHT_PIECES)
    return pl.pallas_call(
        reduce_kernel,
        in_specs=[VMEM] * 4,
        out_specs=[HBM, HBM, VMEM, VMEM],
        out_shape=[jax.ShapeDtypeStruct((groups,) + x.shape[1:], BF16) for x in grads]
        + [jax.ShapeDtypeStruct(x.shape[1:], F32) for x in acts],
        scratch_shapes=scratch,
        compiler_params=comm_params(2),
        name="reduce_gradients",
    )(*grads, *acts)


def exchange(place_axis, level, source, got, sends, arrivals):
    index = lax.axis_index(place_axis)
    other = partner(index, level)
    return pltpu.make_async_remote_copy(
        src_ref=source,
        dst_ref=got,
        send_sem=sends,
        recv_sem=arrivals,
        device_id={place_axis: other},
        device_id_type=pl.DeviceIdType.MESH,
    )


def partner(index, level):
    bit = 2**level
    return index + (1 - 2 * (index // bit % 2)) * bit


def levels_of(axis):
    return lax.axis_size(axis).bit_length() - 1


def meet_partners(*axes):
    barrier = pltpu.get_barrier_semaphore()
    count = 0
    for axis in axes:
        for level in range(levels_of(axis)):
            pl.semaphore_signal(
                barrier,
                inc=1,
                device_id={axis: partner(lax.axis_index(axis), level)},
                device_id_type=pl.DeviceIdType.MESH,
            )
            count = count + 1
    pl.semaphore_wait(barrier, count)


def sum_kernel(axis, part, total, sums, got, sends, arrivals):
    meet_partners(axis)
    levels = levels_of(axis)
    sums[0] = part[...]
    for level in range(levels):
        copy = exchange(
            axis, level, sums.at[level], got.at[level], sends.at[level], arrivals.at[level]
        )
        copy.start()
        copy.wait()
        if level + 1 < levels:
            sums[level + 1] = sums[level] + got[level]
        else:
            total[...] = sums[level] + got[level]


def run_sum(part, axis, number):
    levels = levels_of(axis)
    dma = pltpu.SemaphoreType.DMA
    return pl.pallas_call(
        partial(sum_kernel, axis),
        in_specs=[VMEM],
        out_specs=VMEM,
        out_shape=jax.ShapeDtypeStruct(part.shape, F32),
        scratch_shapes=[
            pltpu.VMEM((levels,) + part.shape, F32),
            pltpu.VMEM((levels,) + part.shape, F32),
            dma((levels,)),
            dma((levels,)),
        ],
        compiler_params=comm_params(number),
        name="sum_over_" + axis,
    )(part)


def small_kernel(part, full, sums, got, sends, arrivals, *sems):
    _, seq = places()
    barrier = pltpu.get_barrier_semaphore()
    count = 0
    for level in range(levels_of("fsdp")):
        pl.semaphore_signal(
            barrier,
            inc=1,
            device_id={"fsdp": partner(lax.axis_index("fsdp"), level)},
            device_id_type=pl.DeviceIdType.MESH,
        )
        count = count + 1
    for other in seq.others():
        pl.semaphore_signal(
            barrier, inc=1, device_id={"seq": other}, device_id_type=pl.DeviceIdType.MESH
        )
        count = count + 1
    pl.semaphore_wait(barrier, count)
    sums[0] = part[...]
    levels = levels_of("fsdp")
    for level in range(levels):
        copy = exchange(
            "fsdp", level, sums.at[level], got.at[level], sends.at[level], arrivals.at[level]
        )
        copy.start()
        copy.wait()
        sums[level + 1] = sums[level] + got[level]
    gather = Gather(seq, sums.at[levels], full, part.shape[0], 1, sems)
    gather.begin(0)
    gather.keep().start()
    gather.forward(0)
    gather.finish()
    gather.keep().wait()


def run_small(part):
    levels = levels_of("fsdp")
    dma = pltpu.SemaphoreType.DMA
    _, seq = places()
    return pl.pallas_call(
        small_kernel,
        in_specs=[VMEM],
        out_specs=VMEM,
        out_shape=jax.ShapeDtypeStruct((lax.axis_size("seq"),) + part.shape, F32),
        scratch_shapes=[
            pltpu.VMEM((levels + 1,) + part.shape, F32),
            pltpu.VMEM((levels,) + part.shape, F32),
            dma((levels,)),
            dma((levels,)),
        ]
        + Gather.scratch(seq, 1),
        compiler_params=comm_params(4),
        name="sum_small_gradients",
    )(part)


def adam_parts(gradient, first_old, second_old):
    first_new = FIRST_DECAY * first_old + (1.0 - FIRST_DECAY) * gradient
    second_new = SECOND_DECAY * second_old + (1.0 - SECOND_DECAY) * gradient * gradient
    direction = (
        first_new
        / (1.0 - FIRST_DECAY**STEP)
        / (jnp.sqrt(second_new / (1.0 - SECOND_DECAY**STEP)) + ADAM_EPSILON)
    )
    return (first_new, second_new, direction)


def shards(
    tokens,
    cotangent,
    segments,
    in_weight,
    out_weight,
    small_params,
    in_first,
    in_second,
    out_first,
    out_second,
    small_first,
    small_second,
):
    in_gain, conv_weight, conv_bias, dt_bias, a_log, skip_gain, out_gain = split_params(
        small_params
    )
    groups = lax.axis_size("seq")
    where_seq = lax.axis_index("seq")
    seq_length = segments.shape[1]
    heads = HEADS // groups
    wide = INNER // groups
    segment_row = segments[0]

    def own(vector, axis=-1):
        size = vector.shape[axis] // groups
        return lax.dynamic_slice_in_dim(vector, where_seq * size, size, axis)

    in_low = in_weight.astype(BF16)
    in_own = jnp.concatenate(
        [
            own(in_low[:, :INNER]),
            own(in_low[:, INNER : 2 * INNER]),
            in_low[:, 2 * INNER : INNER + CONV],
            jnp.pad(own(in_low[:, INNER + CONV :]), ((0, 0), (0, DT_PAD - heads))),
        ],
        axis=1,
    )
    weights_own = jnp.concatenate([in_own, own(out_weight).astype(BF16)], axis=1)

    inputs = tokens[0].astype(F32)
    in_rms = lax.rsqrt(jnp.mean(inputs * inputs, axis=-1, keepdims=True) + NORM_EPS)
    normed_own = (inputs * in_rms * in_gain).astype(BF16)
    weights, rows = run_gather(
        weights_own, jnp.concatenate([normed_own, cotangent[0]], axis=1)
    )
    inner = 2 * wide + 2 * STATE + DT_PAD
    in_cols, out_cols = weights[:, :inner], weights[:, inner:]
    normed, returned = rows[:, :D], rows[:, D:]

    conv_own = jnp.concatenate([own(conv_weight[:, :INNER]), conv_weight[:, INNER:]], axis=1)
    bias_own = jnp.concatenate([own(conv_bias[:INNER]), conv_bias[INNER:]])
    conv_pack = jnp.pad(jnp.concatenate([conv_own, bias_own[None]], axis=0), ((0, 3), (0, 0)))
    head_pack = jnp.pad(
        jnp.stack([own(dt_bias), -jnp.exp(own(a_log))]), ((0, 6), (0, 128 - heads))
    )
    chan_pack = jnp.pad(
        jnp.stack([jnp.repeat(own(skip_gain), HEAD), own(out_gain)]), ((0, 6), (0, 0))
    )
    packs = (conv_pack, head_pack, chan_pack)
    spread_heads = (
        jnp.arange(128)[:, None] == jnp.arange(wide)[None, :] // HEAD
    ).astype(BF16)
    masks = block_masks(segment_row)

    pre, conv_in, gate_z, dt_pre, y, d_mixed, states, stats = run_forward(
        heads, rows, weights, segment_row, masks, packs, spread_heads
    )
    stats = run_sum(stats, "seq", 3)
    mixed, d_y, d_z, d_out_gain = run_middle(heads, y, gate_z, d_mixed, stats, chan_pack)
    d_out_gain = d_out_gain[0]
    contract_rows = (((0,), (0,)), ((), ()))
    contract_columns = (((1,), (1,)), ((), ()))

    out_part = lax.dot_general(returned, mixed, contract_rows, preferred_element_type=F32)
    branch_part = lax.dot_general(mixed, out_cols, contract_columns, preferred_element_type=F32)
    d_projected, d_conv, d_head = run_backward(
        heads, d_y, d_z, pre, conv_in, dt_pre, states, segment_row, masks, packs, spread_heads
    )
    d_conv = d_conv[: KERNEL + 1]
    d_dt_bias, d_a, d_skip = d_head[0, :heads], d_head[1, :heads], d_head[2, :heads]
    in_part = lax.dot_general(normed, d_projected, contract_rows, preferred_element_type=F32)
    d_normed_part = lax.dot_general(
        d_projected, in_cols, contract_columns, preferred_element_type=F32
    )
    out_pieces, in_pieces, branch, d_normed = run_reduce(
        *(x.astype(BF16) for x in (out_part, in_part, branch_part, d_normed_part))
    )
    output = (inputs + branch).astype(BF16)[None]
    slope = d_normed * in_gain[None, :]
    d_inputs = slope * in_rms - inputs * (in_rms**3 / D) * jnp.sum(
        slope * inputs, axis=1, keepdims=True
    )
    input_grad = (cotangent[0].astype(F32) + d_inputs)[None]
    d_in_gain = jnp.sum(d_normed * inputs * in_rms, axis=0)

    edge = 2 * wide + 2 * STATE
    out_pieces = out_pieces.astype(F32)
    in_pieces = in_pieces.astype(F32)

    def spread(pieces, start, size):
        part = pieces[:, :, start : start + size]
        return jnp.transpose(part, (1, 0, 2)).reshape(part.shape[1], groups * size)

    in_grad = jnp.concatenate(
        [
            spread(in_pieces, 0, wide),
            spread(in_pieces, wide, wide),
            jnp.sum(in_pieces[:, :, 2 * wide : edge], axis=0),
            spread(in_pieces, edge, heads),
        ],
        axis=1,
    )
    out_grad = spread(out_pieces, 0, wide)
    in_first_new, in_second_new, in_dir = adam_parts(in_grad, in_first, in_second)
    in_dir = in_dir + WEIGHT_DECAY * in_weight
    out_first_new, out_second_new, out_dir = adam_parts(out_grad, out_first, out_second)
    out_dir = out_dir + WEIGHT_DECAY * out_weight

    partial_sums = jnp.stack(
        [
            jnp.sum(in_weight * in_weight),
            jnp.sum(in_dir * in_dir),
            jnp.sum(out_weight * out_weight),
            jnp.sum(out_dir * out_dir),
        ]
    )
    small_own = [d_conv[:, :wide].reshape(-1), d_dt_bias, d_a, d_skip, d_out_gain]
    small_shared = [d_conv[:, wide:].reshape(-1), d_in_gain]
    packed = jnp.concatenate(small_own + small_shared + [partial_sums])
    packed = jnp.pad(packed, (0, -packed.shape[0] % 1024)).reshape(-1, 128)
    sums = run_small(packed).reshape(groups, -1)
    offset = 0

    def taken(*shape):
        nonlocal offset
        size = 1
        for extent in shape:
            size = size * extent
        piece = sums[:, offset : offset + size].reshape((groups,) + shape)
        offset = offset + size
        return piece

    g_conv = jnp.transpose(taken(KERNEL + 1, wide), (1, 0, 2)).reshape(KERNEL + 1, INNER)
    g_dt_bias, g_a, g_skip = [taken(heads).reshape(-1) for _ in range(3)]
    g_out_gain = taken(wide).reshape(-1)
    g_conv = jnp.concatenate(
        [g_conv, jnp.sum(taken(KERNEL + 1, 2 * STATE), axis=0)], axis=1
    )
    g_in_gain = jnp.sum(taken(D), axis=0)
    totals = taken(4)[0]
    small_grad = jnp.concatenate(
        [g_in_gain, g_conv.reshape(-1), g_dt_bias, g_a, g_skip, g_out_gain]
    )
    norms = jnp.sqrt(totals)
    in_new = in_weight - LEARN_RATE * (norms[0] / norms[1]) * in_dir
    out_new = out_weight - LEARN_RATE * (norms[2] / norms[3]) * out_dir
    small_first_new, small_second_new, small_dir = adam_parts(small_grad, small_first, small_second)
    small_new = small_params - LEARN_RATE * small_dir
    return (
        output,
        input_grad,
        in_grad,
        in_new,
        in_first_new,
        in_second_new,
        out_grad,
        out_new,
        out_first_new,
        out_second_new,
        small_grad,
        small_new,
        small_first_new,
        small_second_new,
        norms,
    )


def solution(mesh):
    matrix = P("fsdp", None)
    rows = P("fsdp", "seq", None)
    return jax.shard_map(
        shards,
        mesh=mesh,
        in_specs=(rows, rows, matrix, matrix, matrix, P(), matrix, matrix, matrix, matrix, P(), P()),
        out_specs=(rows, rows) + (matrix,) * 8 + (P(),) * 5,
        check_vma=False,
    )
```

```python
from functools import partial

import jax
import jax.numpy as jnp
from jax import lax
from jax.experimental import pallas as pl
from jax.experimental.pallas import tpu as pltpu
from jax.sharding import PartitionSpec as P

D = 1536
HEADS = 48
HEAD = 64
STATE = 128
KERNEL = 4
STRETCH = 256
STEP = 5
INNER = 3072
CONV = 3328
PROJ = 6448
DT_PAD = 128

NORM_EPS = 1e-05
FIRST_DECAY = 0.9
SECOND_DECAY = 0.999
ADAM_EPSILON = 1e-06
WEIGHT_DECAY = 0.01
LEARN_RATE = 0.5
F32 = jnp.float32
BF16 = jnp.bfloat16


def split_params(vector):
    offset = 0
    in_gain = vector[offset : offset + D]
    offset = offset + D
    conv_weight = vector[offset : offset + KERNEL * CONV].reshape(KERNEL, CONV)
    offset = offset + KERNEL * CONV
    conv_bias = vector[offset : offset + CONV]
    offset = offset + CONV
    dt_bias = vector[offset : offset + HEADS]
    offset = offset + HEADS
    a_log = vector[offset : offset + HEADS]
    offset = offset + HEADS
    skip_gain = vector[offset : offset + HEADS]
    offset = offset + HEADS
    out_gain = vector[offset : offset + INNER]
    return (in_gain, conv_weight, conv_bias, dt_bias, a_log, skip_gain, out_gain)


def dot(a, b, dims=((1,), (0,))):
    return lax.dot_general(a, b, (dims, ((), ())), preferred_element_type=F32)


def split_dot(value, ones):
    high = value.astype(BF16)
    low = (value - high.astype(F32)).astype(BF16)
    return dot(high, ones) + dot(low, ones)


def tri_dot(ones, value):
    high = value.astype(BF16)
    rest = value - high.astype(F32)
    middle = rest.astype(BF16)
    low = (rest - middle.astype(F32)).astype(BF16)
    return dot(ones, high) + dot(ones, middle) + dot(ones, low)


def sigmoid(v):
    return 1.0 / (1.0 + jnp.exp(-v))


def softplus(v):
    return jnp.maximum(v, 0.0) + jnp.log1p(jnp.exp(-jnp.abs(v)))


def row_at_least():
    rows = lax.broadcasted_iota(jnp.int32, (STRETCH, STRETCH), 0)
    columns = lax.broadcasted_iota(jnp.int32, (STRETCH, STRETCH), 1)
    return rows >= columns


def decays(dt, rate, masks, spread):
    lower = jnp.where(row_at_least(), 1.0, 0.0).astype(BF16)
    cumulative = dot(lower, dt.astype(BF16)) * rate
    last = cumulative[STRETCH - 1 :, :]
    carry = split_dot(jnp.exp(cumulative) * masks[:, 3:4], spread)
    tail = split_dot(jnp.exp(last - cumulative) * masks[:, 4:5], spread)
    keep = split_dot(jnp.broadcast_to(jnp.exp(last) * masks[:1, 5:6], (8, 128)), spread)[:1]
    return cumulative, jnp.transpose(cumulative), carry, tail, keep


def barred(seg_col, seg_row):
    within = row_at_least() & (seg_col == seg_row)
    return jnp.where(within, 0.0, -1e30)


def forward_kernel(
    heads,
    normed,
    returned,
    w_in,
    w_out,
    seg_col,
    seg_row,
    masks_ref,
    conv_pack,
    head_pack,
    chan_pack,
    spread_ref,
    pre_out,
    conv_out,
    z_out,
    dt_out,
    y_out,
    mixed_out,
    states_out,
    stats_out,
    extended,
    state,
):
    wide = heads * HEAD
    edge = wide + 2 * STATE

    @pl.when(pl.program_id(0) == 0)
    def _():
        state[...] = jnp.zeros_like(state)
        extended[0:8, :] = jnp.zeros((8, edge), F32)

    masks = masks_ref[...]
    spread = spread_ref[...]
    z = dot(normed[...], w_in[:, :wide])
    z_out[...] = z
    conv_low = dot(normed[...], w_in[:, wide : wide + edge]).astype(BF16)
    conv_out[...] = conv_low
    conv_in = conv_low.astype(F32)
    extended[8 : 8 + STRETCH, :] = conv_in
    pre = conv_pack[4:5, :] + conv_pack[3:4, :] * conv_in
    for by in range(1, KERNEL):
        pre = pre + conv_pack[3 - by : 4 - by, :] * (
            extended[8 - by : 8 - by + STRETCH, :] * masks[:, 3 - by : 4 - by]
        )
    extended[0:8, :] = extended[STRETCH : STRETCH + 8, :]
    pre_out[...] = pre
    act = (pre * sigmoid(pre)).astype(BF16)
    xs = act[:, :wide].astype(F32)
    b_mat = act[:, wide : wide + STATE]
    c_mat = act[:, wide + STATE :]
    dt_pre = dot(normed[...], w_in[:, wide + edge :]) + head_pack[0:1, :]
    dt_out[...] = dt_pre
    dt = softplus(dt_pre).astype(BF16)
    cumulative, cum_rows, carry, tail, keep = decays(dt, head_pack[1:2, :], masks, spread)
    scaled = xs * dot(dt, spread)
    scaled_low = scaled.astype(BF16)
    bar = barred(seg_col[...], seg_row[...])
    scores = dot(c_mat, b_mat, ((1,), (1,)))
    old = state[...]
    states_out[0] = old
    y_all = dot(c_mat, old.astype(BF16)) * carry + chan_pack[0:1, :] * xs
    state[...] = old * keep + dot(b_mat, (scaled * tail).astype(BF16), ((0,), (0,)))
    first_half = lax.broadcasted_iota(jnp.int32, (STRETCH, 2 * HEAD), 1) < HEAD
    pieces = []
    for pair in range(heads // 2):
        columns = slice(pair * 2 * HEAD, (pair + 1) * 2 * HEAD)
        halves = []
        for h in (2 * pair, 2 * pair + 1):
            weights = scores * jnp.exp(cumulative[:, h : h + 1] - cum_rows[h : h + 1, :] + bar)
            halves.append(dot(weights.astype(BF16), scaled_low[:, columns]))
        pieces.append(jnp.where(first_half, halves[0], halves[1]))
    y_low = (y_all + jnp.concatenate(pieces, axis=1)).astype(BF16)
    y_out[...] = y_low
    gated = y_low.astype(F32) * (z * sigmoid(z))
    d_mixed = dot(returned[...], w_out[...])
    mixed_out[...] = d_mixed
    squares = jnp.sum(gated * gated, axis=1, keepdims=True)
    products = jnp.sum(d_mixed * chan_pack[1:2, :] * gated, axis=1, keepdims=True)
    lane = lax.broadcasted_iota(jnp.int32, (STRETCH, 128), 1)
    both = jnp.where(lane == 0, squares, jnp.where(lane == 1, products, 0.0))
    stats_out[...] = jnp.transpose(both)[0:8, :]


def middle_kernel(
    y_ref, z_ref, d_mixed_ref, stats, chan_pack, mixed_out, d_y_out, d_z_out, d_gain_out
):
    @pl.when(pl.program_id(0) == 0)
    def _():
        d_gain_out[...] = jnp.zeros_like(d_gain_out)

    columns = jnp.transpose(jnp.concatenate([stats[...], jnp.zeros((120, STRETCH), F32)], axis=0))
    rms = lax.rsqrt(columns[:, 0:1] / INNER + NORM_EPS)
    gain = chan_pack[1:2, :]
    y = y_ref[...].astype(F32)
    z = z_ref[...]
    sig = sigmoid(z)
    silu = z * sig
    gated = y * silu
    unit = gated * rms
    d_mixed = d_mixed_ref[...]
    mixed_out[...] = (unit * gain).astype(BF16)
    d_gain_out[0:1, :] += jnp.sum(d_mixed * unit, axis=0, keepdims=True)
    d_gated = d_mixed * gain * rms - unit * (rms * rms / INNER * columns[:, 1:2])
    d_y_out[...] = (d_gated * silu).astype(BF16)
    d_z_out[...] = (d_gated * y * (sig * (1.0 + z * (1.0 - sig)))).astype(BF16)


def backward_block(
    heads,
    d_y_ref,
    pre_ref,
    conv_ref,
    dt_ref,
    states,
    seg_col,
    seg_row,
    masks_ref,
    conv_pack,
    head_pack,
    chan_pack,
    spread_ref,
    gather_ref,
    d_conv_out,
    d_head_out,
    extended,
    d_state,
    d_rest,
):
    wide = heads * HEAD
    edge = wide + 2 * STATE

    @pl.when(pl.program_id(0) == 0)
    def _():
        d_state[...] = jnp.zeros_like(d_state)
        extended[STRETCH : STRETCH + 8, :] = jnp.zeros((8, edge), F32)
        d_conv_out[...] = jnp.zeros_like(d_conv_out)
        d_head_out[...] = jnp.zeros_like(d_head_out)

    masks = masks_ref[...]
    spread = spread_ref[...]
    gather = gather_ref[...]
    pre = pre_ref[...]
    act = (pre * sigmoid(pre)).astype(BF16)
    xs = act[:, :wide].astype(F32)
    b_mat = act[:, wide : wide + STATE]
    c_mat = act[:, wide + STATE :]
    dt_pre = dt_ref[...]
    dt = softplus(dt_pre).astype(BF16)
    rate = head_pack[1:2, :]
    cumulative, cum_rows, carry, tail, keep = decays(dt, rate, masks, spread)
    dt_wide = dot(dt, spread)
    scaled = xs * dt_wide
    scaled_low = scaled.astype(BF16)
    bar = barred(seg_col[...], seg_row[...])
    scores = dot(c_mat, b_mat, ((1,), (1,)))
    old = states[0]
    old_low = old.astype(BF16)
    d_new = d_state[...]
    d_new_low = d_new.astype(BF16)
    d_y_low = d_y_ref[...]
    d_y = d_y_low.astype(F32)

    d_carried = d_y * carry
    d_carried_low = d_carried.astype(BF16)
    d_c = dot(d_carried_low, old_low, ((1,), (1,)))
    d_cum = split_dot(d_carried * dot(c_mat, old_low), gather)
    weighed = scaled * tail
    into = dot(b_mat, d_new_low)
    d_b = dot(weighed.astype(BF16), d_new_low, ((1,), (1,)))
    d_scaled = into * tail
    tail_part = split_dot(weighed * into, gather)
    d_cum = d_cum - tail_part
    kept = jnp.sum(d_new * old, axis=0, keepdims=True) * keep
    kept = split_dot(jnp.broadcast_to(kept, (8, wide)), gather)[:1]
    d_last = jnp.sum(tail_part, axis=0, keepdims=True) + kept
    d_state[...] = d_new * keep + dot(c_mat, d_carried_low, ((0,), (0,)))

    lane = lax.broadcasted_iota(jnp.int32, (STRETCH, 128), 1)
    first_half = lane < HEAD
    d_scores = jnp.zeros((STRETCH, STRETCH), F32)
    column_sums = []
    pieces = []
    for pair in range(heads // 2):
        columns = slice(pair * 2 * HEAD, (pair + 1) * 2 * HEAD)
        halves = []
        d_y_pair = d_y_low[:, columns]
        scaled_pair = scaled_low[:, columns]
        zero = jnp.zeros_like(d_y_pair)
        for h in (2 * pair, 2 * pair + 1):
            decay = jnp.exp(cumulative[:, h : h + 1] - cum_rows[h : h + 1, :] + bar)
            weights = scores * decay
            halves.append(dot(weights.astype(BF16), d_y_pair, ((0,), (0,))))
            d_y_head = jnp.where(first_half == (h % 2 == 0), d_y_pair, zero)
            d_weights = dot(d_y_head, scaled_pair, ((1,), (1,)))
            d_scores = d_scores + d_weights * decay
            product = d_weights * weights
            d_cum = d_cum + jnp.where(lane == h, jnp.sum(product, axis=1, keepdims=True), 0.0)
            column_sums.append(jnp.sum(product, axis=0, keepdims=True))
        pieces.append(jnp.where(first_half, halves[0], halves[1]))
    column_sums.append(jnp.zeros((128 - heads, STRETCH), F32))
    d_cum = d_cum - jnp.transpose(jnp.concatenate(column_sums, axis=0))
    row = lax.broadcasted_iota(jnp.int32, (STRETCH, 128), 0)
    d_cum = d_cum + jnp.where(row == STRETCH - 1, d_last, 0.0)
    d_scaled = d_scaled + jnp.concatenate(pieces, axis=1)
    d_scores_low = d_scores.astype(BF16)
    d_c = d_c + dot(d_scores_low, b_mat)
    d_b = d_b + dot(d_scores_low, c_mat, ((0,), (0,)))

    d_xs = d_scaled * dt_wide + chan_pack[0:1, :] * d_y
    rows = lax.broadcasted_iota(jnp.int32, (STRETCH, STRETCH), 0)
    upper = jnp.where(rows <= lax.broadcasted_iota(jnp.int32, (STRETCH, STRETCH), 1), 1.0, 0.0)
    d_dt = split_dot(d_scaled * xs, gather) + rate * tri_dot(upper.astype(BF16), d_cum)
    d_dt_raw = d_dt.astype(BF16).astype(F32) * sigmoid(dt_pre)
    d_head_out[0:1, :] += jnp.sum(d_dt_raw, axis=0, keepdims=True)
    d_head_out[1:2, :] += jnp.sum(d_cum * cumulative, axis=0, keepdims=True)
    d_skip = jnp.sum(d_y * xs, axis=0, keepdims=True)
    d_head_out[2:3, :] += split_dot(jnp.broadcast_to(d_skip, (8, wide)), gather)[:1]

    extended[0:STRETCH, :wide] = d_xs.astype(BF16).astype(F32)
    extended[0:STRETCH, wide : wide + STATE] = d_b
    extended[0:STRETCH, wide + STATE :] = d_c
    at_row = pl.multiple_of((pl.num_programs(0) - 1 - pl.program_id(0)) * STRETCH, STRETCH)
    here = pl.ds(at_row, STRETCH)
    d_rest[here, edge:] = jnp.where(lane < heads, d_dt_raw, 0.0).astype(BF16)

    def convolve_back(at, _):
        columns = pl.ds(pl.multiple_of(at * 128, 128), 128)
        value = pre_ref[:, columns]
        gate = sigmoid(value)
        d_pre = extended[0:STRETCH, columns] * (gate * (1.0 + value * (1.0 - gate)))
        extended[0:STRETCH, columns] = d_pre
        conv_in = conv_ref[:, columns].astype(F32)
        d_conv_in = conv_pack[3:4, columns] * d_pre
        d_conv_out[3:4, columns] += jnp.sum(d_pre * conv_in, axis=0, keepdims=True)
        d_conv_out[4:5, columns] += jnp.sum(d_pre, axis=0, keepdims=True)
        for by in range(1, KERNEL):
            moved = extended[by : by + STRETCH, columns] * masks_ref[:, 8 + by : 9 + by]
            d_conv_in = d_conv_in + conv_pack[3 - by : 4 - by, columns] * moved
            d_conv_out[3 - by : 4 - by, columns] += jnp.sum(moved * conv_in, axis=0, keepdims=True)
        extended[STRETCH : STRETCH + 8, columns] = extended[0:8, columns]
        d_rest[here, columns] = d_conv_in.astype(BF16)
        return 0

    lax.fori_loop(0, edge // 128, convolve_back, 0)


VMEM_BYTES = 56 * 1024 * 1024


def block_masks(segment):
    length = segment.shape[0]
    blocks = segment.reshape(-1, STRETCH)
    prior = jnp.concatenate([segment[:1], blocks[:-1, -1]])[:, None]
    last = blocks[:, -1:]
    columns = [None] * 12
    for by in range(1, KERNEL):
        gap = jnp.full((by,), -1, jnp.int32)
        columns[3 - by] = segment == jnp.concatenate([gap, segment[:-by]])
        columns[8 + by] = segment == jnp.concatenate([segment[by:], gap])
    columns[3] = (blocks == prior).reshape(length)
    columns[4] = (blocks == last).reshape(length)
    columns[5] = jnp.broadcast_to(last == prior, blocks.shape).reshape(length)
    nothing = jnp.zeros((length,), bool)
    packed = jnp.stack([nothing if c is None else c for c in columns], axis=1)
    return jnp.pad(packed.astype(F32), ((0, 0), (0, 116)))


def block(columns, reverse=0):
    if reverse:
        return pl.BlockSpec((STRETCH, columns), lambda i: (reverse - 1 - i, 0))
    return pl.BlockSpec((STRETCH, columns), lambda i: (i, 0))


def whole(*shape):
    return pl.BlockSpec(shape, lambda i: (0,) * len(shape))


def compiler_params():
    return pltpu.CompilerParams(
        vmem_limit_bytes=VMEM_BYTES, dimension_semantics=("arbitrary",)
    )


def run_forward(heads, rows, w_in, w_out, seg, masks, packs, spread):
    length = rows.shape[0]
    blocks = length // STRETCH
    wide = heads * HEAD
    edge = wide + 2 * STATE
    columns = w_in.shape[1]
    flops = 2 * length * D * (columns + wide) + 2 * length * heads * STRETCH * 128
    return pl.pallas_call(
        partial(forward_kernel, heads),
        grid=(blocks,),
        in_specs=[
            block(D),
            pl.BlockSpec((STRETCH, D), lambda i: (i, 1)),
            whole(D, columns),
            whole(D, wide),
            block(1),
            pl.BlockSpec((1, STRETCH), lambda i: (0, i)),
            block(128),
            whole(8, edge),
            whole(8, 128),
            whole(8, wide),
            whole(128, wide),
        ],
        out_specs=[
            block(edge),
            block(edge),
            block(wide),
            block(128),
            block(wide),
            block(wide),
            pl.BlockSpec((1, STATE, wide), lambda i: (i, 0, 0)),
            pl.BlockSpec((8, STRETCH), lambda i: (0, i)),
        ],
        out_shape=[
            jax.ShapeDtypeStruct((length, edge), F32),
            jax.ShapeDtypeStruct((length, edge), BF16),
            jax.ShapeDtypeStruct((length, wide), F32),
            jax.ShapeDtypeStruct((length, 128), F32),
            jax.ShapeDtypeStruct((length, wide), BF16),
            jax.ShapeDtypeStruct((length, wide), F32),
            jax.ShapeDtypeStruct((blocks, STATE, wide), F32),
            jax.ShapeDtypeStruct((8, length), F32),
        ],
        scratch_shapes=[pltpu.VMEM((STRETCH + 8, edge), F32), pltpu.VMEM((STATE, wide), F32)],
        compiler_params=compiler_params(),
        cost_estimate=pl.CostEstimate(
            flops=flops, bytes_accessed=40 * 1024 * 1024, transcendentals=length * heads * STRETCH
        ),
        name="forward_scan",
    )(rows, rows, w_in, w_out, seg[:, None], seg[None, :], masks, *packs, spread)


def run_middle(heads, y, z, d_mixed, stats, chan_pack):
    length, wide = y.shape
    low = jax.ShapeDtypeStruct((length, wide), BF16)
    return pl.pallas_call(
        middle_kernel,
        grid=(length // STRETCH,),
        in_specs=[
            block(wide),
            block(wide),
            block(wide),
            pl.BlockSpec((8, STRETCH), lambda i: (0, i)),
            whole(8, wide),
        ],
        out_specs=[block(wide), block(wide), block(wide), whole(8, wide)],
        out_shape=[low, low, low, jax.ShapeDtypeStruct((8, wide), F32)],
        compiler_params=compiler_params(),
        cost_estimate=pl.CostEstimate(
            flops=20 * length * wide, bytes_accessed=16 * length * wide, transcendentals=length * wide
        ),
        name="gate_gradients",
    )(y, z, d_mixed, stats, chan_pack)


class Place:
    def __init__(self, axis, minor):
        self.axis = axis
        self.minor = minor
        self.major = lax.axis_size(axis) // minor
        index = lax.axis_index(axis)
        self.at_major = index // minor
        self.at_minor = index % minor
        self.index = index

    def slot(self, by_major, by_minor):
        return (self.at_major + by_major) % self.major * self.minor + (
            self.at_minor + by_minor
        ) % self.minor

    def others(self):
        along = [self.slot(step, 0) for step in range(1, self.major)]
        return along + [self.slot(0, step) for step in range(1, self.minor)]


def places():
    ring = lax.axis_size("fsdp")
    side = 1
    while 2 * side * 2 * side * 2 <= ring:
        side = 2 * side
    return Place("fsdp", side), Place("seq", 2)


def meet(*all_places):
    barrier = pltpu.get_barrier_semaphore()
    count = 0
    for place in all_places:
        for other in place.others():
            pl.semaphore_signal(
                barrier, inc=1, device_id={place.axis: other}, device_id_type=pl.DeviceIdType.MESH
            )
            count = count + 1
    pl.semaphore_wait(barrier, count)


def send(place, source, target, to, sends, arrivals, at):
    return pltpu.make_async_remote_copy(
        src_ref=source,
        dst_ref=target,
        send_sem=sends.at[at],
        recv_sem=arrivals.at[at],
        device_id={place.axis: to},
        device_id_type=pl.DeviceIdType.MESH,
    )


class Gather:
    def __init__(self, place, own, full, rows, pieces, sems):
        self.place, self.own, self.full = place, own, full
        self.size, self.pieces = rows // pieces, pieces
        self.sends1, self.arrivals1, self.sends2, self.arrivals2, self.here = sems

    @staticmethod
    def scratch(place, pieces):
        first = max(place.major - 1, 1) * pieces
        second = place.major * (place.minor - 1) * pieces
        dma = pltpu.SemaphoreType.DMA
        return [dma((first,)), dma((first,)), dma((second,)), dma((second,)), dma((1,))]

    def rows(self, piece):
        return pl.ds(piece * self.size, self.size)

    def along(self, piece, step):
        place = self.place
        return send(
            place,
            self.own.at[self.rows(piece)],
            self.full.at[place.index, self.rows(piece)],
            place.slot(step, 0),
            self.sends1,
            self.arrivals1,
            piece * (place.major - 1) + step - 1,
        )

    def across(self, piece, step, across):
        place = self.place
        slot = place.slot(-step, 0)
        target = self.full.at[slot, self.rows(piece)]
        source = self.own.at[self.rows(piece)] if step == 0 else target
        at = (piece * place.major + step) * (place.minor - 1) + across - 1
        return send(
            place, source, target, place.slot(0, across), self.sends2, self.arrivals2, at
        )

    def keep(self):
        return pltpu.make_async_copy(self.own, self.full.at[self.place.index], self.here.at[0])

    def begin(self, piece):
        for step in range(1, self.place.major):
            self.along(piece, step).start()
        for across in range(1, self.place.minor):
            self.across(piece, 0, across).start()

    def forward(self, piece):
        for step in range(1, self.place.major):
            self.along(piece, step).wait_recv()
            for across in range(1, self.place.minor):
                self.across(piece, step, across).start()

    def finish(self):
        for piece in range(self.pieces):
            for step in range(1, self.place.major):
                self.along(piece, step).wait_send()
            for step in range(self.place.major):
                for across in range(1, self.place.minor):
                    self.across(piece, step, across).wait()


class Reduce:
    def __init__(self, place, part, total, rows, pieces, scratch, loads=None):
        self.place, self.part, self.total, self.loads = place, part, total, loads
        self.size, self.pieces = rows // pieces, pieces
        self.got1, self.mine, self.got2, self.sends1, self.arrivals1, self.sends2, self.arrivals2 = (
            scratch
        )

    @staticmethod
    def scratch(place, rows, columns, pieces):
        dma = pltpu.SemaphoreType.DMA
        first = place.major * (place.minor - 1)
        second = max(place.major - 1, 1)
        return [
            pltpu.VMEM((first, rows, columns), BF16),
            pltpu.VMEM((second, rows, columns), BF16),
            pltpu.VMEM((second, rows, columns), BF16),
            dma((first * pieces,)),
            dma((first * pieces,)),
            dma((second * pieces,)),
            dma((second * pieces,)),
        ]

    def items(self):
        return [(piece, step) for step in self.steps() for piece in range(self.pieces)]

    def steps(self):
        return list(range(1, self.place.major)) + [0]

    def rows(self, piece):
        return pl.ds(piece * self.size, self.size)

    def across(self, item, across):
        piece, step = item
        place = self.place
        slot = step * (place.minor - 1) + across - 1
        return send(
            place,
            self.part.at[place.slot(step, across), self.rows(piece)],
            self.got1.at[slot, self.rows(piece)],
            place.slot(0, across),
            self.sends1,
            self.arrivals1,
            slot * self.pieces + piece,
        )

    def along(self, item):
        piece, step = item
        place = self.place
        return send(
            place,
            self.mine.at[step - 1, self.rows(piece)],
            self.got2.at[step - 1, self.rows(piece)],
            place.slot(step, 0),
            self.sends2,
            self.arrivals2,
            (step - 1) * self.pieces + piece,
        )

    def begin(self, item):
        for across in range(1, self.place.minor):
            self.across(item, across).start()
        if self.loads is not None:
            self.load(item[1]).start()

    def load(self, step):
        target = self.mine.at[step - 1] if step else self.total
        return pltpu.make_async_copy(
            self.part.at[self.place.slot(step, 0)], target, self.loads.at[step]
        )

    def own(self, step, rows):
        if self.loads is None:
            return self.part[self.place.slot(step, 0), rows].astype(F32)
        source = self.mine.at[step - 1] if step else self.total
        return source[rows].astype(F32)

    def blocks(self, piece, body):
        def one(at, _):
            body(pl.ds(pl.multiple_of(piece * self.size + at * 16, 16), 16))
            return 0

        lax.fori_loop(0, self.size // 16, one, 0)

    def handle(self, item):
        piece, step = item
        place = self.place
        for across in range(1, place.minor):
            self.across(item, across).wait_recv()
        if self.loads is not None:
            self.load(step).wait()
        if step == 0:
            return

        def body(rows):
            value = self.own(step, rows)
            for across in range(1, place.minor):
                slot = step * (place.minor - 1) + across - 1
                value = value + self.got1[slot, rows].astype(F32)
            self.mine[step - 1, rows] = value.astype(BF16)

        self.blocks(piece, body)
        self.along(item).start()

    def close(self, piece):
        place = self.place
        for step in range(1, place.major):
            self.along((piece, step)).wait_recv()

        def body(rows):
            value = self.own(0, rows)
            for across in range(1, place.minor):
                value = value + self.got1[across - 1, rows].astype(F32)
            for step in range(1, place.major):
                value = value + self.got2[step - 1, rows].astype(F32)
            self.total[rows] = value.astype(self.total.dtype)

        self.blocks(piece, body)

    def finish(self):
        for item in self.items():
            for across in range(1, self.place.minor):
                self.across(item, across).wait_send()
            if item[1]:
                self.along(item).wait_send()


WEIGHT_PIECES = 3
TOKEN_PIECES = 4
HBM = pl.BlockSpec(memory_space=pl.ANY)
VMEM = pl.BlockSpec(memory_space=pltpu.VMEM)


def comm_params(number):
    return pltpu.CompilerParams(
        collective_id=number, has_side_effects=True, vmem_limit_bytes=VMEM_BYTES
    )


def gather_kernel(w_in, w_out, rows, w_in_all, w_out_all, rows_all, *sems):
    ring, seq = places()
    meet(ring, seq)
    streams = [
        Gather(ring, w_in, w_in_all, w_in.shape[0], WEIGHT_PIECES, sems[:5]),
        Gather(ring, w_out, w_out_all, w_out.shape[0], 1, sems[5:10]),
        Gather(seq, rows, rows_all, rows.shape[0], TOKEN_PIECES, sems[10:]),
    ]
    first, second, third = streams
    for piece in range(TOKEN_PIECES):
        if piece < WEIGHT_PIECES:
            first.begin(piece)
        third.begin(piece)
    second.begin(0)
    for stream in streams:
        stream.keep().start()
    for piece in range(TOKEN_PIECES):
        third.forward(piece)
        if piece < WEIGHT_PIECES:
            first.forward(piece)
    second.forward(0)
    for stream in streams:
        stream.finish()
        stream.keep().wait()


def run_gather(w_in, w_out, rows):
    ring, seq = places()
    count, groups = lax.axis_size("fsdp"), lax.axis_size("seq")
    full = [
        jax.ShapeDtypeStruct((by,) + x.shape, BF16)
        for by, x in ((count, w_in), (count, w_out), (groups, rows))
    ]
    out = pl.pallas_call(
        gather_kernel,
        in_specs=[HBM, HBM, HBM],
        out_specs=[HBM, HBM, HBM],
        out_shape=full,
        scratch_shapes=Gather.scratch(ring, WEIGHT_PIECES)
        + Gather.scratch(ring, 1)
        + Gather.scratch(seq, TOKEN_PIECES),
        compiler_params=comm_params(1),
        name="gather_weights_and_rows",
    )(w_in, w_out, rows)
    return [x.reshape(x.shape[0] * x.shape[1], x.shape[2]) for x in out]


def resident(x):
    return pl.BlockSpec(
        x.shape, lambda i: (0,) * len(x.shape), pipeline_mode=pl.Buffered(buffer_count=1)
    )


def backward_kernel(heads, *refs):
    chunk = refs[:8]
    packs = refs[8:13]
    d_z, weights, normed_t, out_part, z_part, branch_part = refs[13:19]
    out_all, z_all, rest_all, branch, d_normed, d_conv, d_head = refs[19:26]
    extended, d_state, d_rest, rest_part, act_part, out_own, z_own, rest_own = refs[26:34]
    out_loads, z_loads, branch_loads = refs[34:37]
    scratch = refs[37:]
    ring, seq = places()
    rows = out_part.shape[1]
    own_rows = branch_part.shape[1]
    wide = heads * HEAD

    def stream(place, part, total, extent, pieces, at, loads=None):
        return Reduce(place, part, total, extent, pieces, scratch[7 * at : 7 * at + 7], loads)

    def spreading(own, full, pieces, at):
        return Gather(seq, own, full, rows, pieces, scratch[35 + 5 * at : 40 + 5 * at])

    out_sum = stream(ring, out_part, out_own, rows, 1, 0, out_loads)
    z_sum = stream(ring, z_part, z_own, rows, 1, 1, z_loads)
    rest_sum = stream(ring, rest_part, rest_own, rows, WEIGHT_PIECES, 2)
    branch_sum = stream(seq, branch_part, branch, own_rows, 1, 3, branch_loads)
    d_normed_sum = stream(seq, act_part, d_normed, own_rows, 2, 4)
    out_spread = spreading(out_own, out_all, 1, 0)
    z_spread = spreading(z_own, z_all, 1, 1)
    rest_spread = spreading(rest_own, rest_all, WEIGHT_PIECES, 2)
    early = [(s, item) for s in (out_sum, z_sum) for item in s.items()]
    at_step = pl.program_id(0)
    blocks = d_rest.shape[0] // STRETCH

    @pl.when(at_step == 0)
    def _():
        meet(ring, seq)
        for s, item in early:
            s.begin(item)
        for item in branch_sum.items():
            branch_sum.begin(item)

    backward_block(heads, *chunk, *packs, d_conv, d_head, extended, d_state, d_rest)

    for k in range(blocks):

        @pl.when(at_step == k)
        def _():
            s, item = early[k]
            s.handle(item)
            if k == blocks - 1:
                for item in branch_sum.items():
                    branch_sum.handle(item)
                branch_sum.close(0)
                branch_sum.finish()

    @pl.when(at_step == blocks - 1)
    def _():
        def rest_block(slot):
            here = pl.ds(pl.multiple_of(slot * rows, 16), rows)

            def one(at, _):
                columns = pl.ds(pl.multiple_of(at * 384, 128), 384)
                rest_part[slot, :, columns] = dot(
                    normed_t[here, :], d_rest[:, columns]
                ).astype(BF16)
                return 0

            lax.fori_loop(0, d_rest.shape[1] // 384, one, 0)

        def normed_block(slot):
            here = pl.ds(pl.multiple_of(slot * own_rows, own_rows), own_rows)

            def one(at, _):
                columns = pl.ds(pl.multiple_of(at * 512, 128), 512)
                value = dot(d_z[here, :], weights[columns, :wide], ((1,), (1,)))
                value = value + dot(d_rest[here, :], weights[columns, wide:], ((1,), (1,)))
                act_part[slot, :, columns] = value.astype(BF16)
                return 0

            lax.fori_loop(0, D // 512, one, 0)

        for step in rest_sum.steps():
            for across in range(1, ring.minor):
                rest_block(ring.slot(step, across))
            for piece in range(WEIGHT_PIECES):
                rest_sum.begin((piece, step))
        for step in d_normed_sum.steps():
            for across in range(1, seq.minor):
                normed_block(seq.slot(step, across))
            for piece in range(2):
                d_normed_sum.begin((piece, step))
        for step in rest_sum.steps():
            rest_block(ring.slot(step, 0))
        for step in d_normed_sum.steps():
            normed_block(seq.slot(step, 0))
        for s, item in early[blocks:]:
            s.handle(item)
        out_sum.close(0)
        out_spread.begin(0)
        side = d_normed_sum.items()
        for at, item in enumerate(rest_sum.items()):
            rest_sum.handle(item)
            if at < len(side):
                d_normed_sum.handle(side[at])
            if at == WEIGHT_PIECES:
                z_sum.close(0)
                z_spread.begin(0)
                out_spread.forward(0)
        for piece in range(2):
            d_normed_sum.close(piece)
        for piece in range(WEIGHT_PIECES):
            rest_sum.close(piece)
            rest_spread.begin(piece)
        out_spread.keep().start()
        z_spread.keep().start()
        rest_spread.keep().start()
        z_spread.forward(0)
        for piece in range(WEIGHT_PIECES):
            rest_spread.forward(piece)
        for s in (out_sum, z_sum, rest_sum, d_normed_sum):
            s.finish()
        for s in (out_spread, z_spread, rest_spread):
            s.finish()
            s.keep().wait()


def run_backward(
    heads, d_y, pre, conv, dt_pre, states, seg, masks, packs, spread, d_z, weights, normed_t,
    out_part, z_part, branch_part,
):
    length = d_y.shape[0]
    blocks = length // STRETCH
    wide = heads * HEAD
    edge = wide + 2 * STATE
    rest = edge + DT_PAD
    ring, seq = places()
    count, groups = lax.axis_size("fsdp"), lax.axis_size("seq")

    def split(x, by):
        return x.reshape(by, x.shape[0] // by, x.shape[1])

    out_part, z_part = split(out_part, count), split(z_part, count)
    branch_part = split(branch_part, groups)
    rows, own_rows = out_part.shape[1], branch_part.shape[1]
    wholes = [*packs, spread, spread.T, d_z, weights, normed_t]
    scratch = [
        pltpu.VMEM((STRETCH + 8, edge), F32),
        pltpu.VMEM((STATE, wide), F32),
        pltpu.VMEM((length, rest), BF16),
        pltpu.VMEM((count, rows, rest), BF16),
        pltpu.VMEM((groups, own_rows, D), BF16),
        pltpu.VMEM((rows, wide), BF16),
        pltpu.VMEM((rows, wide), BF16),
        pltpu.VMEM((rows, rest), BF16),
        pltpu.SemaphoreType.DMA((ring.major,)),
        pltpu.SemaphoreType.DMA((ring.major,)),
        pltpu.SemaphoreType.DMA((seq.major,)),
    ]
    scratch = scratch + Reduce.scratch(ring, rows, wide, 1) + Reduce.scratch(ring, rows, wide, 1)
    scratch = scratch + Reduce.scratch(ring, rows, rest, WEIGHT_PIECES)
    scratch = scratch + Reduce.scratch(seq, own_rows, D, 1) + Reduce.scratch(seq, own_rows, D, 2)
    for pieces in (1, 1, WEIGHT_PIECES):
        scratch = scratch + Gather.scratch(seq, pieces)
    gathered = [jax.ShapeDtypeStruct((groups, rows, x), BF16) for x in (wide, wide, rest)]
    summed = [
        jax.ShapeDtypeStruct((own_rows, D), BF16),
        jax.ShapeDtypeStruct((own_rows, D), BF16),
        jax.ShapeDtypeStruct((8, edge), F32),
        jax.ShapeDtypeStruct((8, 128), F32),
    ]
    return pl.pallas_call(
        partial(backward_kernel, heads),
        grid=(blocks,),
        in_specs=[
            block(wide, blocks),
            block(edge, blocks),
            block(edge, blocks),
            block(128, blocks),
            pl.BlockSpec((1, STATE, wide), lambda i: (blocks - 1 - i, 0, 0)),
            block(1, blocks),
            pl.BlockSpec((1, STRETCH), lambda i: (0, blocks - 1 - i)),
            block(128, blocks),
        ]
        + [resident(x) for x in wholes]
        + [HBM] * 3,
        out_specs=[HBM, HBM, HBM] + [resident(x) for x in summed],
        out_shape=gathered + summed,
        scratch_shapes=scratch,
        compiler_params=pltpu.CompilerParams(
            collective_id=2,
            has_side_effects=True,
            vmem_limit_bytes=61 * 1024 * 1024,
            dimension_semantics=("arbitrary",),
        ),
        name="backward_and_sums",
    )(d_y, pre, conv, dt_pre, states, seg[:, None], seg[None, :], masks, *wholes, out_part, z_part, branch_part)


def adam_kernel(
    groups,
    z_piece,
    rest_piece,
    tails,
    out_piece,
    choose,
    w_in,
    m_in,
    v_in,
    w_out,
    m_out,
    v_out,
    g_in_new,
    m_in_new,
    v_in_new,
    u_in,
    g_out_new,
    m_out_new,
    v_out_new,
    u_out,
    sums,
):
    j = pl.program_id(0)
    wide = w_in.shape[1]

    @pl.when(j == 0)
    def _():
        sums[...] = jnp.zeros_like(sums)

    def update(gradient, w, m, v, g_new, m_new, v_new, u, at, keep):
        columns = gradient.shape[1]
        first, second, direction = adam_parts(gradient, m[:, :columns], v[:, :columns])
        weight = w[:, :columns]
        direction = direction + WEIGHT_DECAY * weight
        g_new[:, :columns] = gradient
        m_new[:, :columns] = first
        v_new[:, :columns] = second
        u[:, :columns] = direction
        for k, value in ((at, weight * weight), (at + 1, direction * direction)):
            value = jnp.where(keep, value, 0.0) if keep is not None else value
            sums[k : k + 1, :columns] += jnp.sum(value, axis=0, keepdims=True)

    inside = (w_in, m_in, v_in, g_in_new, m_in_new, v_in_new, u_in)

    @pl.when(j < groups)
    def _():
        update(z_piece[0].astype(F32), *inside, 0, None)

    @pl.when((j >= groups) & (j < 2 * groups))
    def _():
        update(rest_piece[0].astype(F32), *inside, 0, None)

    @pl.when(j == 2 * groups)
    def _():
        states = jnp.zeros((w_in.shape[0], 2 * STATE), F32)
        steps = jnp.zeros((w_in.shape[0], DT_PAD), F32)
        for s in range(groups):
            states = states + tails[s, :, : 2 * STATE].astype(F32)
            steps = steps + dot(tails[s, :, 2 * STATE :], choose[s])
        gradient = jnp.concatenate([states, steps], axis=1)
        lane = lax.broadcasted_iota(jnp.int32, gradient.shape, 1)
        update(gradient, *inside, 0, lane < 2 * STATE + HEADS)

    @pl.when(j > 2 * groups)
    def _():
        update(
            out_piece[0].astype(F32),
            w_out, m_out, v_out, g_out_new, m_out_new, v_out_new, u_out, 2, None,
        )


def run_adam(groups, heads, z_all, rest_all, out_all, inside, outside):
    rows = inside[0].shape[0]
    wide = heads * HEAD
    last = 2 * groups
    head = jnp.arange(DT_PAD)
    choose = jnp.stack(
        [
            (head[:, None] + s * heads == head[None, :]) & (head[:, None] < heads)
            for s in range(groups)
        ]
    ).astype(BF16)
    in_spec = pl.BlockSpec((rows, wide), lambda j: (0, jnp.minimum(j, last)))
    out_spec = pl.BlockSpec((rows, wide), lambda j: (0, jnp.maximum(j - last - 1, 0)))
    tail = 2 * STATE + DT_PAD
    return pl.pallas_call(
        partial(adam_kernel, groups),
        grid=(last + 1 + groups,),
        in_specs=[
            pl.BlockSpec((1, rows, wide), lambda j: (jnp.minimum(j, groups - 1), 0, 0)),
            pl.BlockSpec(
                (1, rows, wide), lambda j: (jnp.clip(j - groups, 0, groups - 1), 0, 0)
            ),
            pl.BlockSpec((groups, rows, tail), lambda j: (0, 0, wide // tail)),
            pl.BlockSpec((1, rows, wide), lambda j: (jnp.maximum(j - last - 1, 0), 0, 0)),
            pl.BlockSpec(choose.shape, lambda j: (0, 0, 0)),
        ]
        + [in_spec] * 3
        + [out_spec] * 3,
        out_specs=[in_spec] * 4 + [out_spec] * 4 + [pl.BlockSpec((8, wide), lambda j: (0, 0))],
        out_shape=[jax.ShapeDtypeStruct(inside[0].shape, F32)] * 4
        + [jax.ShapeDtypeStruct(outside[0].shape, F32)] * 4
        + [jax.ShapeDtypeStruct((8, wide), F32)],
        compiler_params=compiler_params(),
        name="adam",
    )(z_all, rest_all, rest_all, out_all, choose, *inside, *outside)


def exchange(place_axis, level, source, got, sends, arrivals):
    index = lax.axis_index(place_axis)
    other = partner(index, level)
    return pltpu.make_async_remote_copy(
        src_ref=source,
        dst_ref=got,
        send_sem=sends,
        recv_sem=arrivals,
        device_id={place_axis: other},
        device_id_type=pl.DeviceIdType.MESH,
    )


def partner(index, level):
    bit = 2**level
    return index + (1 - 2 * (index // bit % 2)) * bit


def levels_of(axis):
    return lax.axis_size(axis).bit_length() - 1


def meet_partners(*axes):
    barrier = pltpu.get_barrier_semaphore()
    count = 0
    for axis in axes:
        for level in range(levels_of(axis)):
            pl.semaphore_signal(
                barrier,
                inc=1,
                device_id={axis: partner(lax.axis_index(axis), level)},
                device_id_type=pl.DeviceIdType.MESH,
            )
            count = count + 1
    pl.semaphore_wait(barrier, count)


def sum_kernel(axis, part, total, sums, got, sends, arrivals):
    meet_partners(axis)
    levels = levels_of(axis)
    sums[0] = part[...]
    for level in range(levels):
        copy = exchange(
            axis, level, sums.at[level], got.at[level], sends.at[level], arrivals.at[level]
        )
        copy.start()
        copy.wait()
        if level + 1 < levels:
            sums[level + 1] = sums[level] + got[level]
        else:
            total[...] = sums[level] + got[level]


def run_sum(part, axis, number):
    levels = levels_of(axis)
    dma = pltpu.SemaphoreType.DMA
    return pl.pallas_call(
        partial(sum_kernel, axis),
        in_specs=[VMEM],
        out_specs=VMEM,
        out_shape=jax.ShapeDtypeStruct(part.shape, F32),
        scratch_shapes=[
            pltpu.VMEM((levels,) + part.shape, F32),
            pltpu.VMEM((levels,) + part.shape, F32),
            dma((levels,)),
            dma((levels,)),
        ],
        compiler_params=comm_params(number),
        name="sum_over_" + axis,
    )(part)


def small_kernel(part, full, sums, got, sends, arrivals, *sems):
    _, seq = places()
    barrier = pltpu.get_barrier_semaphore()
    count = 0
    for level in range(levels_of("fsdp")):
        pl.semaphore_signal(
            barrier,
            inc=1,
            device_id={"fsdp": partner(lax.axis_index("fsdp"), level)},
            device_id_type=pl.DeviceIdType.MESH,
        )
        count = count + 1
    for other in seq.others():
        pl.semaphore_signal(
            barrier, inc=1, device_id={"seq": other}, device_id_type=pl.DeviceIdType.MESH
        )
        count = count + 1
    pl.semaphore_wait(barrier, count)
    sums[0] = part[...]
    levels = levels_of("fsdp")
    for level in range(levels):
        copy = exchange(
            "fsdp", level, sums.at[level], got.at[level], sends.at[level], arrivals.at[level]
        )
        copy.start()
        copy.wait()
        sums[level + 1] = sums[level] + got[level]
    gather = Gather(seq, sums.at[levels], full, part.shape[0], 1, sems)
    gather.begin(0)
    gather.keep().start()
    gather.forward(0)
    gather.finish()
    gather.keep().wait()


def run_small(part):
    levels = levels_of("fsdp")
    dma = pltpu.SemaphoreType.DMA
    _, seq = places()
    return pl.pallas_call(
        small_kernel,
        in_specs=[VMEM],
        out_specs=VMEM,
        out_shape=jax.ShapeDtypeStruct((lax.axis_size("seq"),) + part.shape, F32),
        scratch_shapes=[
            pltpu.VMEM((levels + 1,) + part.shape, F32),
            pltpu.VMEM((levels,) + part.shape, F32),
            dma((levels,)),
            dma((levels,)),
        ]
        + Gather.scratch(seq, 1),
        compiler_params=comm_params(4),
        name="sum_small_gradients",
    )(part)


def adam_parts(gradient, first_old, second_old):
    first_new = FIRST_DECAY * first_old + (1.0 - FIRST_DECAY) * gradient
    second_new = SECOND_DECAY * second_old + (1.0 - SECOND_DECAY) * gradient * gradient
    direction = (
        first_new
        / (1.0 - FIRST_DECAY**STEP)
        / (jnp.sqrt(second_new / (1.0 - SECOND_DECAY**STEP)) + ADAM_EPSILON)
    )
    return (first_new, second_new, direction)


def shards(
    tokens,
    cotangent,
    segments,
    in_weight,
    out_weight,
    small_params,
    in_first,
    in_second,
    out_first,
    out_second,
    small_first,
    small_second,
):
    in_gain, conv_weight, conv_bias, dt_bias, a_log, skip_gain, out_gain = split_params(
        small_params
    )
    groups = lax.axis_size("seq")
    where_seq = lax.axis_index("seq")
    seq_length = segments.shape[1]
    heads = HEADS // groups
    wide = INNER // groups
    segment_row = segments[0]

    def own(vector, axis=-1):
        size = vector.shape[axis] // groups
        return lax.dynamic_slice_in_dim(vector, where_seq * size, size, axis)

    in_low = in_weight.astype(BF16)
    in_own = jnp.concatenate(
        [
            own(in_low[:, :INNER]),
            own(in_low[:, INNER : 2 * INNER]),
            in_low[:, 2 * INNER : INNER + CONV],
            jnp.pad(own(in_low[:, INNER + CONV :]), ((0, 0), (0, DT_PAD - heads))),
        ],
        axis=1,
    )
    out_own = own(out_weight).astype(BF16)

    inputs = tokens[0].astype(F32)
    in_rms = lax.rsqrt(jnp.mean(inputs * inputs, axis=-1, keepdims=True) + NORM_EPS)
    normed_own = (inputs * in_rms * in_gain).astype(BF16)
    w_in, w_out, rows = run_gather(
        in_own, out_own, jnp.concatenate([normed_own, cotangent[0]], axis=1)
    )
    rows_t = rows.T
    normed_t, returned_t = rows_t[:D], rows_t[D:]

    conv_own = jnp.concatenate([own(conv_weight[:, :INNER]), conv_weight[:, INNER:]], axis=1)
    bias_own = jnp.concatenate([own(conv_bias[:INNER]), conv_bias[INNER:]])
    conv_pack = jnp.pad(jnp.concatenate([conv_own, bias_own[None]], axis=0), ((0, 3), (0, 0)))
    head_pack = jnp.pad(
        jnp.stack([own(dt_bias), -jnp.exp(own(a_log))]), ((0, 6), (0, 128 - heads))
    )
    chan_pack = jnp.pad(
        jnp.stack([jnp.repeat(own(skip_gain), HEAD), own(out_gain)]), ((0, 6), (0, 0))
    )
    packs = (conv_pack, head_pack, chan_pack)
    spread_heads = (
        jnp.arange(128)[:, None] == jnp.arange(wide)[None, :] // HEAD
    ).astype(BF16)
    masks = block_masks(segment_row)

    pre, conv_in, gate_z, dt_pre, y, d_mixed, states, stats = run_forward(
        heads, rows, w_in, w_out, segment_row, masks, packs, spread_heads
    )
    stats = run_sum(stats, "seq", 3)
    mixed, d_y, d_z, d_out_gain = run_middle(heads, y, gate_z, d_mixed, stats, chan_pack)
    d_out_gain = d_out_gain[0]
    low = partial(lax.convert_element_type, new_dtype=BF16)
    out_part = low(jnp.dot(returned_t, mixed, preferred_element_type=F32))
    z_part = low(jnp.dot(normed_t, d_z, preferred_element_type=F32))
    branch_part = low(
        lax.dot_general(
            mixed, w_out, (((1,), (1,)), ((), ())), preferred_element_type=F32
        )
    )
    out_all, z_all, rest_all, branch, d_normed, d_conv, d_head = run_backward(
        heads, d_y, pre, conv_in, dt_pre, states, segment_row, masks, packs, spread_heads, d_z,
        w_in, normed_t, out_part, z_part, branch_part,
    )
    d_conv = d_conv[: KERNEL + 1]
    d_dt_bias, d_a, d_skip = d_head[0, :heads], d_head[1, :heads], d_head[2, :heads]
    output = (inputs + branch.astype(F32)).astype(BF16)[None]
    d_normed = d_normed.astype(F32)
    slope = d_normed * in_gain[None, :]
    d_inputs = slope * in_rms - inputs * (in_rms**3 / D) * jnp.sum(
        slope * inputs, axis=1, keepdims=True
    )
    input_grad = (cotangent[0].astype(F32) + d_inputs)[None]
    d_in_gain = jnp.sum(d_normed * inputs * in_rms, axis=0)

    (
        in_grad, in_first_new, in_second_new, in_dir,
        out_grad, out_first_new, out_second_new, out_dir, squares,
    ) = run_adam(
        groups, heads, z_all, rest_all, out_all,
        (in_weight, in_first, in_second), (out_weight, out_first, out_second),
    )
    partial_sums = jnp.sum(squares[:4], axis=1)
    small_own = [d_conv[:, :wide].reshape(-1), d_dt_bias, d_a, d_skip, d_out_gain]
    small_shared = [d_conv[:, wide:].reshape(-1), d_in_gain]
    packed = jnp.concatenate(small_own + small_shared + [partial_sums])
    packed = jnp.pad(packed, (0, -packed.shape[0] % 1024)).reshape(-1, 128)
    sums = run_small(packed).reshape(groups, -1)
    offset = 0

    def taken(*shape):
        nonlocal offset
        size = 1
        for extent in shape:
            size = size * extent
        piece = sums[:, offset : offset + size].reshape((groups,) + shape)
        offset = offset + size
        return piece

    g_conv = jnp.transpose(taken(KERNEL + 1, wide), (1, 0, 2)).reshape(KERNEL + 1, INNER)
    g_dt_bias, g_a, g_skip = [taken(heads).reshape(-1) for _ in range(3)]
    g_out_gain = taken(wide).reshape(-1)
    g_conv = jnp.concatenate(
        [g_conv, jnp.sum(taken(KERNEL + 1, 2 * STATE), axis=0)], axis=1
    )
    g_in_gain = jnp.sum(taken(D), axis=0)
    totals = taken(4)[0]
    small_grad = jnp.concatenate(
        [g_in_gain, g_conv.reshape(-1), g_dt_bias, g_a, g_skip, g_out_gain]
    )
    norms = jnp.sqrt(totals)
    in_new = in_weight - LEARN_RATE * (norms[0] / norms[1]) * in_dir
    out_new = out_weight - LEARN_RATE * (norms[2] / norms[3]) * out_dir
    small_first_new, small_second_new, small_dir = adam_parts(small_grad, small_first, small_second)
    small_new = small_params - LEARN_RATE * small_dir
    return (
        output,
        input_grad,
        in_grad,
        in_new,
        in_first_new,
        in_second_new,
        out_grad,
        out_new,
        out_first_new,
        out_second_new,
        small_grad,
        small_new,
        small_first_new,
        small_second_new,
        norms,
    )


def solution(mesh):
    matrix = P("fsdp", None)
    rows = P("fsdp", "seq", None)
    return jax.shard_map(
        shards,
        mesh=mesh,
        in_specs=(rows, rows, matrix, matrix, matrix, P(), matrix, matrix, matrix, matrix, P(), P()),
        out_specs=(rows, rows) + (matrix,) * 8 + (P(),) * 5,
        check_vma=False,
    )
```

```python
from functools import partial

import jax
import jax.numpy as jnp
from jax import lax
from jax.experimental import pallas as pl
from jax.experimental.pallas import tpu as pltpu
from jax.sharding import PartitionSpec as P

D = 1536
HEADS = 48
HEAD = 64
STATE = 128
KERNEL = 4
STRETCH = 256
STEP = 5
INNER = 3072
CONV = 3328
PROJ = 6448
DT_PAD = 128

NORM_EPS = 1e-05
FIRST_DECAY = 0.9
SECOND_DECAY = 0.999
ADAM_EPSILON = 1e-06
WEIGHT_DECAY = 0.01
LEARN_RATE = 0.5
F32 = jnp.float32
BF16 = jnp.bfloat16


def dot(a, b, dims=((1,), (0,))):
    return lax.dot_general(a, b, (dims, ((), ())), preferred_element_type=F32)


def split_dot(value, ones):
    high = value.astype(BF16)
    low = (value - high.astype(F32)).astype(BF16)
    return dot(high, ones) + dot(low, ones)


def tri_dot(ones, value):
    high = value.astype(BF16)
    rest = value - high.astype(F32)
    middle = rest.astype(BF16)
    low = (rest - middle.astype(F32)).astype(BF16)
    return dot(ones, high) + dot(ones, middle) + dot(ones, low)


def sigmoid(v):
    return 1.0 / (1.0 + jnp.exp(-v))


def softplus(v):
    return jnp.maximum(v, 0.0) + jnp.log1p(jnp.exp(-jnp.abs(v)))


def row_at_least():
    rows = lax.broadcasted_iota(jnp.int32, (STRETCH, STRETCH), 0)
    columns = lax.broadcasted_iota(jnp.int32, (STRETCH, STRETCH), 1)
    return rows >= columns


def decays(dt, rate, masks, spread):
    lower = jnp.where(row_at_least(), 1.0, 0.0).astype(BF16)
    cumulative = dot(lower, dt.astype(BF16)) * rate
    last = cumulative[STRETCH - 1 :, :]
    carry = split_dot(jnp.exp(cumulative) * masks["carry"], spread)
    tail = split_dot(jnp.exp(last - cumulative) * masks["tail"], spread)
    keep = split_dot(jnp.broadcast_to(jnp.exp(last) * masks["keep"], (8, 128)), spread)[:1]
    return cumulative, jnp.transpose(cumulative), carry, tail, keep


EDGE = 8


def block_masks(seg_pad, seg_row, at):
    def rows(by, size=STRETCH):
        return seg_pad[pl.ds(at + EDGE + by, size), :]

    here = rows(0)
    first = jnp.where(at == 0, rows(0, 1), rows(-1, 1))
    last = rows(STRETCH - 1, 1)
    masks = {"carry": here == first, "tail": here == last, "keep": last == first}
    for by in range(1, KERNEL):
        masks[-by] = here == rows(-by)
        masks[by] = here == rows(by)
    masks = {key: jnp.where(value, 1.0, 0.0) for key, value in masks.items()}
    within = row_at_least() & (here == seg_row[:, pl.ds(at, STRETCH)])
    masks["bar"] = jnp.where(within, 0.0, -1e30)
    return masks


def forward_block(heads, at, normed, w_in, masks, packs, spread, outs, z_all, y_all, extended, state):
    conv_pack, head_pack, chan_pack = packs
    pre_out, conv_out, dt_out, states_out = outs
    wide = heads * HEAD
    edge = wide + 2 * STATE
    here = pl.ds(at, STRETCH)
    z_all[here, :] = dot(normed, w_in[:, :wide])
    conv_low = dot(normed, w_in[:, wide : wide + edge]).astype(BF16)
    conv_out[...] = conv_low
    conv_in = conv_low.astype(F32)
    extended[8 : 8 + STRETCH, :] = conv_in
    pre = conv_pack[4:5, :] + conv_pack[3:4, :] * conv_in
    for by in range(1, KERNEL):
        pre = pre + conv_pack[3 - by : 4 - by, :] * (
            extended[8 - by : 8 - by + STRETCH, :] * masks[-by]
        )
    extended[0:8, :] = extended[STRETCH : STRETCH + 8, :]
    pre_out[...] = pre
    act = (pre * sigmoid(pre)).astype(BF16)
    xs = act[:, :wide].astype(F32)
    b_mat = act[:, wide : wide + STATE]
    c_mat = act[:, wide + STATE :]
    dt_pre = dot(normed, w_in[:, wide + edge :]) + head_pack[0:1, :]
    dt_out[...] = dt_pre
    dt = softplus(dt_pre).astype(BF16)
    cumulative, cum_rows, carry, tail, keep = decays(dt, head_pack[1:2, :], masks, spread)
    scaled = xs * dot(dt, spread)
    scaled_low = scaled.astype(BF16)
    scores = dot(c_mat, b_mat, ((1,), (1,)))
    old = state[...]
    states_out[0] = old
    outer = dot(c_mat, old.astype(BF16)) * carry + chan_pack[0:1, :] * xs
    state[...] = old * keep + dot(b_mat, (scaled * tail).astype(BF16), ((0,), (0,)))
    first_half = lax.broadcasted_iota(jnp.int32, (STRETCH, 2 * HEAD), 1) < HEAD
    pieces = []
    for pair in range(heads // 2):
        columns = slice(pair * 2 * HEAD, (pair + 1) * 2 * HEAD)
        halves = []
        for h in (2 * pair, 2 * pair + 1):
            weights = scores * jnp.exp(
                cumulative[:, h : h + 1] - cum_rows[h : h + 1, :] + masks["bar"]
            )
            halves.append(dot(weights.astype(BF16), scaled_low[:, columns]))
        pieces.append(jnp.where(first_half, halves[0], halves[1]))
    y_all[here, :] = (outer + jnp.concatenate(pieces, axis=1)).astype(BF16)


def fill_packs(heads, small, spread, packs, scratch_gain):
    conv_pack, head_pack, chan_pack = packs
    wide = heads * HEAD
    index = lax.axis_index("seq")
    start = pl.multiple_of(index * wide, 128)
    for ref in packs:
        ref[...] = jnp.zeros_like(ref)
    for k in range(KERNEL + 1):
        base = D + k * CONV
        conv_pack[k : k + 1, :wide] = small[:, pl.ds(base + start, wide)]
        conv_pack[k : k + 1, wide:] = small[:, base + INNER : base + CONV]
    base = D + (KERNEL + 1) * CONV
    window = jnp.broadcast_to(small[:, base : base + 256], (8, 256))
    lane = lax.broadcasted_iota(jnp.int32, (8, 256), 1)

    def own(k):
        moved = pltpu.roll(window, 256 - (k * HEADS + index * heads), 1)
        return jnp.where(lane < heads, moved, 0.0)[:, :128]

    head_pack[0:1, :] = own(0)[:1]
    rate = own(1)
    rate = jnp.where(lax.broadcasted_iota(jnp.int32, (8, 128), 1) < heads, -jnp.exp(rate), 0.0)
    head_pack[1:2, :] = rate[:1]
    chan_pack[0:1, :] = tri_spread(own(2), spread)[:1]
    base = base + 3 * HEADS
    shift = base % 128
    gain = jnp.broadcast_to(small[:, base - shift : base - shift + INNER + 128], (8, INNER + 128))
    scratch_gain[...] = pltpu.roll(gain, INNER + 128 - shift, 1)
    chan_pack[1:2, :] = scratch_gain[0:1, pl.ds(start, wide)]


def tri_spread(value, ones):
    high = value.astype(BF16)
    rest = value - high.astype(F32)
    middle = rest.astype(BF16)
    low = (rest - middle.astype(F32)).astype(BF16)
    return dot(high, ones) + dot(middle, ones) + dot(low, ones)


def gate_sums(y, z, d_mixed, gain):
    gated = y.astype(F32) * (z * sigmoid(z))
    squares = jnp.sum(gated * gated, axis=1, keepdims=True)
    products = jnp.sum(d_mixed * gain * gated, axis=1, keepdims=True)
    lane = lax.broadcasted_iota(jnp.int32, (STRETCH, 128), 1)
    both = jnp.where(lane == 0, squares, jnp.where(lane == 1, products, 0.0))
    return jnp.transpose(both)[0:8, :]


def gate_gradients(y_low, z, d_mixed, gain, sums):
    columns = jnp.transpose(jnp.concatenate([sums, jnp.zeros((120, STRETCH), F32)], axis=0))
    rms = lax.rsqrt(columns[:, 0:1] / INNER + NORM_EPS)
    y = y_low.astype(F32)
    sig = sigmoid(z)
    silu = z * sig
    gated = y * silu
    unit = gated * rms
    d_gain = jnp.sum(d_mixed * unit, axis=0, keepdims=True)
    d_gated = d_mixed * gain * rms - unit * (rms * rms / INNER * columns[:, 1:2])
    d_z = d_gated * y * (sig * (1.0 + z * (1.0 - sig)))
    return (unit * gain).astype(BF16), (d_gated * silu).astype(BF16), d_z.astype(BF16), d_gain


def forward_kernel(heads, *refs):
    tokens, cotangent, small, dt_weight, seg_pad, seg_row, spread_ref, in_weight, out_weight = refs[:9]
    outs = refs[9:13]
    d_y, d_z, normed_t, out_part, z_part, branch_part, d_gain = refs[13:20]
    packs = refs[20:23]
    w_in_out = refs[23]
    (
        stage_in, stage_out, own_in, own_out, own_rows, w_in, w_out, rows_all, returned_t,
        z_all, y_all, d_mixed_all, extended, state, scratch_gain, sums, got,
        stage_sems, sum_sends, sum_arrivals,
    ) = refs[24:44]
    sems = refs[44:]
    ring, seq = places()
    wide = heads * HEAD
    edge = wide + 2 * STATE
    step = pl.program_id(0)
    blocks = pl.num_programs(0) - 1
    length = rows_all.shape[0]
    count = length // STRETCH
    first = Gather(ring, own_in, w_in, own_in.shape[0], WEIGHT_PIECES, sems[:5])
    second = Gather(ring, own_out, w_out, own_out.shape[0], 1, sems[5:10])
    third = Gather(seq, own_rows, rows_all, own_rows.shape[0], TOKEN_PIECES, sems[10:15])
    save = pltpu.make_async_copy(w_in, w_in_out, stage_sems.at[5])
    spread = spread_ref[...]
    at = pl.multiple_of(step * STRETCH, STRETCH)

    @pl.when(step == 0)
    def _():
        start = pl.multiple_of(seq.index * wide, 128)
        sources = [
            (in_weight.at[:, pl.ds(start, wide)], stage_in.at[:, :wide]),
            (in_weight.at[:, pl.ds(INNER + start, wide)], stage_in.at[:, wide : 2 * wide]),
            (in_weight.at[:, pl.ds(2 * INNER, 2 * STATE)], stage_in.at[:, 2 * wide :]),
            (out_weight.at[:, pl.ds(start, wide)], stage_out),
        ]
        loads = [
            pltpu.make_async_copy(source, target, stage_sems.at[k])
            for k, (source, target) in enumerate(sources)
        ]
        for load in loads:
            load.start()
        meet(ring, seq)
        inputs = tokens[...].astype(F32)
        rms = lax.rsqrt(jnp.mean(inputs * inputs, axis=-1, keepdims=True) + NORM_EPS)
        own_rows[:, :D] = (inputs * rms * small[:, :D]).astype(BF16)
        own_rows[:, D:] = cotangent[...]
        for load in loads:
            load.wait()
        own_in[:, : wide + edge] = stage_in[...].astype(BF16)
        own_in[:, wide + edge :] = dt_weight[...]
        own_out[...] = stage_out[...].astype(BF16)
        for piece in range(TOKEN_PIECES):
            if piece < WEIGHT_PIECES:
                first.begin(piece)
            third.begin(piece)
        first.keep().start()
        third.keep().start()
        second.keep().start()
        fill_packs(heads, small, spread, packs, scratch_gain)
        state[...] = jnp.zeros_like(state)
        extended[0:8, :] = jnp.zeros((8, edge), F32)
        d_gain[...] = jnp.zeros_like(d_gain)
        for piece in range(TOKEN_PIECES):
            third.forward(piece)
            if piece < WEIGHT_PIECES:
                first.forward(piece)
        second.begin(0)
        third.finish()
        third.keep().wait()

        def turn(k, _):
            here = pl.ds(pl.multiple_of(k * STRETCH, STRETCH), STRETCH)
            normed_t[:, here] = jnp.transpose(rows_all[here, :D])
            returned_t[:, here] = jnp.transpose(rows_all[here, D:])
            return 0

        lax.fori_loop(0, count, turn, 0)
        first.finish()
        first.keep().wait()
        save.start()

    @pl.when(step < blocks)
    def _():
        masks = block_masks(seg_pad, seg_row, at)
        forward_block(
            heads, at, rows_all[pl.ds(at, STRETCH), :D], w_in, masks, packs, spread, outs,
            z_all, y_all, extended, state,
        )

    @pl.when(step == 1)
    def _():
        second.forward(0)

    @pl.when(step == blocks)
    def _():
        second.finish()
        second.keep().wait()
        gain = packs[2][1:2, :]

        def measure(k, _):
            here = pl.ds(pl.multiple_of(k * STRETCH, STRETCH), STRETCH)
            d_mixed = dot(rows_all[here, D:], w_out[...])
            d_mixed_all[here, :] = d_mixed
            sums[0, :, here] = gate_sums(y_all[here, :], z_all[here, :], d_mixed, gain)
            return 0

        lax.fori_loop(0, count, measure, 0)
        for level in range(levels_of("seq")):
            copy = exchange(
                "seq", level, sums.at[level], got.at[level], sum_sends.at[level], sum_arrivals.at[level]
            )
            copy.start()
            copy.wait()
            sums[level + 1] = sums[level] + got[level]
        total = levels_of("seq")

        def differentiate(k, _):
            here = pl.ds(pl.multiple_of(k * STRETCH, STRETCH), STRETCH)
            mixed, d_y_block, d_z_block, d_gain_block = gate_gradients(
                y_all[here, :], z_all[here, :], d_mixed_all[here, :], gain, sums[total, :, here]
            )
            y_all[here, :] = mixed
            d_y[here, :] = d_y_block
            d_z[here, :] = d_z_block
            d_gain[0:1, :] += d_gain_block
            branch_part[here, :] = dot(mixed, w_out[...], ((1,), (1,))).astype(BF16)
            return 0

        lax.fori_loop(0, count, differentiate, 0)

        def contract(k, _):
            here = pl.ds(pl.multiple_of(k * 256, 256), 256)
            out_part[here, :] = dot(returned_t[here, :], y_all[...]).astype(BF16)
            z_part[here, :] = dot(normed_t[here, :], d_z[...]).astype(BF16)
            return 0

        lax.fori_loop(0, D // 256, contract, 0)
        save.wait()


def backward_block(
    heads,
    d_y_ref,
    pre_ref,
    conv_ref,
    dt_ref,
    states,
    seg_pad,
    seg_row,
    conv_pack,
    head_pack,
    chan_pack,
    spread_ref,
    gather_ref,
    d_conv_out,
    d_head_out,
    extended,
    d_state,
    d_rest,
):
    wide = heads * HEAD
    edge = wide + 2 * STATE

    @pl.when(pl.program_id(0) == 0)
    def _():
        d_state[...] = jnp.zeros_like(d_state)
        extended[STRETCH : STRETCH + 8, :] = jnp.zeros((8, edge), F32)
        d_conv_out[...] = jnp.zeros_like(d_conv_out)
        d_head_out[...] = jnp.zeros_like(d_head_out)

    at_row = pl.multiple_of((pl.num_programs(0) - 1 - pl.program_id(0)) * STRETCH, STRETCH)
    masks = block_masks(seg_pad, seg_row, at_row)
    spread = spread_ref[...]
    gather = gather_ref[...]
    pre = pre_ref[...]
    act = (pre * sigmoid(pre)).astype(BF16)
    xs = act[:, :wide].astype(F32)
    b_mat = act[:, wide : wide + STATE]
    c_mat = act[:, wide + STATE :]
    dt_pre = dt_ref[...]
    dt = softplus(dt_pre).astype(BF16)
    rate = head_pack[1:2, :]
    cumulative, cum_rows, carry, tail, keep = decays(dt, rate, masks, spread)
    dt_wide = dot(dt, spread)
    scaled = xs * dt_wide
    scaled_low = scaled.astype(BF16)
    bar = masks["bar"]
    scores = dot(c_mat, b_mat, ((1,), (1,)))
    old = states[0]
    old_low = old.astype(BF16)
    d_new = d_state[...]
    d_new_low = d_new.astype(BF16)
    d_y_low = d_y_ref[...]
    d_y = d_y_low.astype(F32)

    d_carried = d_y * carry
    d_carried_low = d_carried.astype(BF16)
    d_c = dot(d_carried_low, old_low, ((1,), (1,)))
    d_cum = split_dot(d_carried * dot(c_mat, old_low), gather)
    weighed = scaled * tail
    into = dot(b_mat, d_new_low)
    d_b = dot(weighed.astype(BF16), d_new_low, ((1,), (1,)))
    d_scaled = into * tail
    tail_part = split_dot(weighed * into, gather)
    d_cum = d_cum - tail_part
    kept = jnp.sum(d_new * old, axis=0, keepdims=True) * keep
    kept = split_dot(jnp.broadcast_to(kept, (8, wide)), gather)[:1]
    d_last = jnp.sum(tail_part, axis=0, keepdims=True) + kept
    d_state[...] = d_new * keep + dot(c_mat, d_carried_low, ((0,), (0,)))

    lane = lax.broadcasted_iota(jnp.int32, (STRETCH, 128), 1)
    first_half = lane < HEAD
    d_scores = jnp.zeros((STRETCH, STRETCH), F32)
    column_sums = []
    pieces = []
    for pair in range(heads // 2):
        columns = slice(pair * 2 * HEAD, (pair + 1) * 2 * HEAD)
        halves = []
        d_y_pair = d_y_low[:, columns]
        scaled_pair = scaled_low[:, columns]
        zero = jnp.zeros_like(d_y_pair)
        for h in (2 * pair, 2 * pair + 1):
            decay = jnp.exp(cumulative[:, h : h + 1] - cum_rows[h : h + 1, :] + bar)
            weights = scores * decay
            halves.append(dot(weights.astype(BF16), d_y_pair, ((0,), (0,))))
            d_y_head = jnp.where(first_half == (h % 2 == 0), d_y_pair, zero)
            d_weights = dot(d_y_head, scaled_pair, ((1,), (1,)))
            d_scores = d_scores + d_weights * decay
            product = d_weights * weights
            d_cum = d_cum + jnp.where(lane == h, jnp.sum(product, axis=1, keepdims=True), 0.0)
            column_sums.append(jnp.sum(product, axis=0, keepdims=True))
        pieces.append(jnp.where(first_half, halves[0], halves[1]))
    column_sums.append(jnp.zeros((128 - heads, STRETCH), F32))
    d_cum = d_cum - jnp.transpose(jnp.concatenate(column_sums, axis=0))
    row = lax.broadcasted_iota(jnp.int32, (STRETCH, 128), 0)
    d_cum = d_cum + jnp.where(row == STRETCH - 1, d_last, 0.0)
    d_scaled = d_scaled + jnp.concatenate(pieces, axis=1)
    d_scores_low = d_scores.astype(BF16)
    d_c = d_c + dot(d_scores_low, b_mat)
    d_b = d_b + dot(d_scores_low, c_mat, ((0,), (0,)))

    d_xs = d_scaled * dt_wide + chan_pack[0:1, :] * d_y
    rows = lax.broadcasted_iota(jnp.int32, (STRETCH, STRETCH), 0)
    upper = jnp.where(rows <= lax.broadcasted_iota(jnp.int32, (STRETCH, STRETCH), 1), 1.0, 0.0)
    d_dt = split_dot(d_scaled * xs, gather) + rate * tri_dot(upper.astype(BF16), d_cum)
    d_dt_raw = d_dt.astype(BF16).astype(F32) * sigmoid(dt_pre)
    d_head_out[0:1, :] += jnp.sum(d_dt_raw, axis=0, keepdims=True)
    d_head_out[1:2, :] += jnp.sum(d_cum * cumulative, axis=0, keepdims=True)
    d_skip = jnp.sum(d_y * xs, axis=0, keepdims=True)
    d_head_out[2:3, :] += split_dot(jnp.broadcast_to(d_skip, (8, wide)), gather)[:1]

    extended[0:STRETCH, :wide] = d_xs.astype(BF16).astype(F32)
    extended[0:STRETCH, wide : wide + STATE] = d_b
    extended[0:STRETCH, wide + STATE :] = d_c
    here = pl.ds(at_row, STRETCH)
    d_rest[here, edge:] = jnp.where(lane < heads, d_dt_raw, 0.0).astype(BF16)

    def convolve_back(at, _):
        columns = pl.ds(pl.multiple_of(at * 128, 128), 128)
        value = pre_ref[:, columns]
        gate = sigmoid(value)
        d_pre = extended[0:STRETCH, columns] * (gate * (1.0 + value * (1.0 - gate)))
        extended[0:STRETCH, columns] = d_pre
        conv_in = conv_ref[:, columns].astype(F32)
        d_conv_in = conv_pack[3:4, columns] * d_pre
        d_conv_out[3:4, columns] += jnp.sum(d_pre * conv_in, axis=0, keepdims=True)
        d_conv_out[4:5, columns] += jnp.sum(d_pre, axis=0, keepdims=True)
        for by in range(1, KERNEL):
            moved = extended[by : by + STRETCH, columns] * masks[by]
            d_conv_in = d_conv_in + conv_pack[3 - by : 4 - by, columns] * moved
            d_conv_out[3 - by : 4 - by, columns] += jnp.sum(moved * conv_in, axis=0, keepdims=True)
        extended[STRETCH : STRETCH + 8, columns] = extended[0:8, columns]
        d_rest[here, columns] = d_conv_in.astype(BF16)
        return 0

    lax.fori_loop(0, edge // 128, convolve_back, 0)


VMEM_BYTES = 56 * 1024 * 1024


def block(columns, reverse=0):
    if reverse:
        return pl.BlockSpec((STRETCH, columns), lambda i: (reverse - 1 - i, 0))
    return pl.BlockSpec((STRETCH, columns), lambda i: (i, 0))


def whole(*shape):
    return pl.BlockSpec(shape, lambda i: (0,) * len(shape))


def compiler_params():
    return pltpu.CompilerParams(
        vmem_limit_bytes=VMEM_BYTES, dimension_semantics=("arbitrary",)
    )


class Place:
    def __init__(self, axis, minor):
        self.axis = axis
        self.minor = minor
        self.major = lax.axis_size(axis) // minor
        index = lax.axis_index(axis)
        self.at_major = index // minor
        self.at_minor = index % minor
        self.index = index

    def slot(self, by_major, by_minor):
        return (self.at_major + by_major) % self.major * self.minor + (
            self.at_minor + by_minor
        ) % self.minor

    def others(self):
        along = [self.slot(step, 0) for step in range(1, self.major)]
        return along + [self.slot(0, step) for step in range(1, self.minor)]


def places():
    ring = lax.axis_size("fsdp")
    side = 1
    while 2 * side * 2 * side * 2 <= ring:
        side = 2 * side
    return Place("fsdp", side), Place("seq", 2)


def meet(*all_places):
    barrier = pltpu.get_barrier_semaphore()
    count = 0
    for place in all_places:
        for other in place.others():
            pl.semaphore_signal(
                barrier, inc=1, device_id={place.axis: other}, device_id_type=pl.DeviceIdType.MESH
            )
            count = count + 1
    pl.semaphore_wait(barrier, count)


def send(place, source, target, to, sends, arrivals, at):
    return pltpu.make_async_remote_copy(
        src_ref=source,
        dst_ref=target,
        send_sem=sends.at[at],
        recv_sem=arrivals.at[at],
        device_id={place.axis: to},
        device_id_type=pl.DeviceIdType.MESH,
    )


class Gather:
    def __init__(self, place, own, full, rows, pieces, sems):
        self.place, self.own, self.full = place, own, full
        self.size, self.pieces = rows // pieces, pieces
        self.sends1, self.arrivals1, self.sends2, self.arrivals2, self.here = sems

    @staticmethod
    def scratch(place, pieces):
        first = max(place.major - 1, 1) * pieces
        second = place.major * (place.minor - 1) * pieces
        dma = pltpu.SemaphoreType.DMA
        return [dma((first,)), dma((first,)), dma((second,)), dma((second,)), dma((1,))]

    def rows(self, piece):
        return pl.ds(piece * self.size, self.size)

    def target(self, slot, piece):
        if len(self.full.shape) > len(self.own.shape):
            return self.full.at[slot, self.rows(piece)]
        start = slot * (self.size * self.pieces) + piece * self.size
        return self.full.at[pl.ds(pl.multiple_of(start, 16), self.size)]

    def along(self, piece, step):
        place = self.place
        return send(
            place,
            self.own.at[self.rows(piece)],
            self.target(place.index, piece),
            place.slot(step, 0),
            self.sends1,
            self.arrivals1,
            piece * (place.major - 1) + step - 1,
        )

    def across(self, piece, step, across):
        place = self.place
        slot = place.slot(-step, 0)
        target = self.target(slot, piece)
        source = self.own.at[self.rows(piece)] if step == 0 else target
        at = (piece * place.major + step) * (place.minor - 1) + across - 1
        return send(
            place, source, target, place.slot(0, across), self.sends2, self.arrivals2, at
        )

    def keep(self):
        if len(self.full.shape) > len(self.own.shape):
            target = self.full.at[self.place.index]
        else:
            size = self.size * self.pieces
            target = self.full.at[pl.ds(pl.multiple_of(self.place.index * size, 16), size)]
        return pltpu.make_async_copy(self.own, target, self.here.at[0])

    def begin(self, piece):
        for step in range(1, self.place.major):
            self.along(piece, step).start()
        for across in range(1, self.place.minor):
            self.across(piece, 0, across).start()

    def forward(self, piece):
        for step in range(1, self.place.major):
            self.along(piece, step).wait_recv()
            for across in range(1, self.place.minor):
                self.across(piece, step, across).start()

    def finish(self):
        for piece in range(self.pieces):
            for step in range(1, self.place.major):
                self.along(piece, step).wait_send()
            for step in range(self.place.major):
                for across in range(1, self.place.minor):
                    self.across(piece, step, across).wait()


class Reduce:
    def __init__(self, place, part, total, rows, pieces, scratch, loads=None):
        self.place, self.part, self.total, self.loads = place, part, total, loads
        self.size, self.pieces = rows // pieces, pieces
        self.got1, self.mine, self.got2, self.sends1, self.arrivals1, self.sends2, self.arrivals2 = (
            scratch
        )

    @staticmethod
    def scratch(place, rows, columns, pieces):
        dma = pltpu.SemaphoreType.DMA
        first = place.major * (place.minor - 1)
        second = max(place.major - 1, 1)
        return [
            pltpu.VMEM((first, rows, columns), BF16),
            pltpu.VMEM((second, rows, columns), BF16),
            pltpu.VMEM((second, rows, columns), BF16),
            dma((first * pieces,)),
            dma((first * pieces,)),
            dma((second * pieces,)),
            dma((second * pieces,)),
        ]

    def items(self):
        return [(piece, step) for step in self.steps() for piece in range(self.pieces)]

    def steps(self):
        return list(range(1, self.place.major)) + [0]

    def rows(self, piece):
        return pl.ds(piece * self.size, self.size)

    def across(self, item, across):
        piece, step = item
        place = self.place
        slot = step * (place.minor - 1) + across - 1
        return send(
            place,
            self.part.at[place.slot(step, across), self.rows(piece)],
            self.got1.at[slot, self.rows(piece)],
            place.slot(0, across),
            self.sends1,
            self.arrivals1,
            slot * self.pieces + piece,
        )

    def along(self, item):
        piece, step = item
        place = self.place
        return send(
            place,
            self.mine.at[step - 1, self.rows(piece)],
            self.got2.at[step - 1, self.rows(piece)],
            place.slot(step, 0),
            self.sends2,
            self.arrivals2,
            (step - 1) * self.pieces + piece,
        )

    def begin(self, item):
        for across in range(1, self.place.minor):
            self.across(item, across).start()
        if self.loads is not None:
            self.load(item[1]).start()

    def load(self, step):
        target = self.mine.at[step - 1] if step else self.total
        return pltpu.make_async_copy(
            self.part.at[self.place.slot(step, 0)], target, self.loads.at[step]
        )

    def own(self, step, rows):
        if self.loads is None:
            return self.part[self.place.slot(step, 0), rows].astype(F32)
        source = self.mine.at[step - 1] if step else self.total
        return source[rows].astype(F32)

    def blocks(self, piece, body):
        def one(at, _):
            body(pl.ds(pl.multiple_of(piece * self.size + at * 16, 16), 16))
            return 0

        lax.fori_loop(0, self.size // 16, one, 0)

    def handle(self, item):
        piece, step = item
        place = self.place
        for across in range(1, place.minor):
            self.across(item, across).wait_recv()
        if self.loads is not None:
            self.load(step).wait()
        if step == 0:
            return

        def body(rows):
            value = self.own(step, rows)
            for across in range(1, place.minor):
                slot = step * (place.minor - 1) + across - 1
                value = value + self.got1[slot, rows].astype(F32)
            self.mine[step - 1, rows] = value.astype(BF16)

        self.blocks(piece, body)
        self.along(item).start()

    def close(self, piece):
        place = self.place
        for step in range(1, place.major):
            self.along((piece, step)).wait_recv()

        def body(rows):
            value = self.own(0, rows)
            for across in range(1, place.minor):
                value = value + self.got1[across - 1, rows].astype(F32)
            for step in range(1, place.major):
                value = value + self.got2[step - 1, rows].astype(F32)
            self.total[rows] = value.astype(self.total.dtype)

        self.blocks(piece, body)

    def finish(self):
        for item in self.items():
            for across in range(1, self.place.minor):
                self.across(item, across).wait_send()
            if item[1]:
                self.along(item).wait_send()


WEIGHT_PIECES = 3
TOKEN_PIECES = 4
HBM = pl.BlockSpec(memory_space=pl.ANY)
VMEM = pl.BlockSpec(memory_space=pltpu.VMEM)


def comm_params(number):
    return pltpu.CompilerParams(
        collective_id=number, has_side_effects=True, vmem_limit_bytes=VMEM_BYTES
    )


def resident(x):
    return pl.BlockSpec(
        x.shape, lambda i: (0,) * len(x.shape), pipeline_mode=pl.Buffered(buffer_count=1)
    )


def run_forward(heads, tokens, cotangent, small, dt_weight, seg_pad, seg_row, spread, in_weight, out_weight):
    ring, seq = places()
    count, groups = lax.axis_size("fsdp"), lax.axis_size("seq")
    rows, own_rows = in_weight.shape[0], tokens.shape[0]
    length = own_rows * groups
    blocks = length // STRETCH
    wide = heads * HEAD
    edge = wide + 2 * STATE
    inner = wide + edge + DT_PAD
    levels = levels_of("seq")
    shape = jax.ShapeDtypeStruct
    last = blocks - 1

    def chunk(columns):
        return pl.BlockSpec((STRETCH, columns), lambda i: (i - i // blocks, 0))

    wholes = [tokens, cotangent, small, dt_weight, seg_pad, seg_row, spread]
    late = [
        shape((length, wide), BF16),
        shape((length, wide), BF16),
        shape((D, length), BF16),
        shape((D, wide), BF16),
        shape((D, wide), BF16),
        shape((length, D), BF16),
        shape((8, wide), F32),
        shape((8, edge), F32),
        shape((8, 128), F32),
        shape((8, wide), F32),
    ]
    dma = pltpu.SemaphoreType.DMA
    scratch = [
        pltpu.VMEM((rows, wide + edge), F32),
        pltpu.VMEM((rows, wide), F32),
        pltpu.VMEM((rows, inner), BF16),
        pltpu.VMEM((rows, wide), BF16),
        pltpu.VMEM((own_rows, 2 * D), BF16),
        pltpu.VMEM((D, inner), BF16),
        pltpu.VMEM((D, wide), BF16),
        pltpu.VMEM((length, 2 * D), BF16),
        pltpu.VMEM((D, length), BF16),
        pltpu.VMEM((length, wide), F32),
        pltpu.VMEM((length, wide), BF16),
        pltpu.VMEM((length, wide), F32),
        pltpu.VMEM((STRETCH + 8, edge), F32),
        pltpu.VMEM((STATE, wide), F32),
        pltpu.VMEM((8, INNER + 128), F32),
        pltpu.VMEM((levels + 1, 8, length), F32),
        pltpu.VMEM((levels, 8, length), F32),
        dma((6,)),
        dma((levels,)),
        dma((levels,)),
    ]
    scratch = scratch + Gather.scratch(ring, WEIGHT_PIECES) + Gather.scratch(ring, 1)
    scratch = scratch + Gather.scratch(seq, TOKEN_PIECES)
    return pl.pallas_call(
        partial(forward_kernel, heads),
        grid=(blocks + 1,),
        in_specs=[resident(x) for x in wholes] + [HBM, HBM],
        out_specs=[
            chunk(edge),
            chunk(edge),
            chunk(128),
            pl.BlockSpec((1, STATE, wide), lambda i: (i - i // blocks, 0, 0)),
        ]
        + [resident(x) for x in late]
        + [HBM],
        out_shape=[
            shape((length, edge), F32),
            shape((length, edge), BF16),
            shape((length, 128), F32),
            shape((blocks, STATE, wide), F32),
        ]
        + late
        + [shape((D, inner), BF16)],
        scratch_shapes=scratch,
        compiler_params=pltpu.CompilerParams(
            collective_id=1,
            has_side_effects=True,
            vmem_limit_bytes=61 * 1024 * 1024,
            dimension_semantics=("arbitrary",),
        ),
        name="gather_and_forward",
    )(*wholes, in_weight, out_weight)


def backward_kernel(heads, *refs):
    chunk = refs[:5]
    packs = refs[5:12]
    d_z, weights, normed_t, out_part, z_part, branch_part = refs[12:18]
    out_all, z_all, rest_all, branch, d_normed, d_conv, d_head = refs[18:25]
    extended, d_state, d_rest, rest_part, act_part, out_own, z_own, rest_own = refs[25:33]
    out_loads, z_loads, branch_loads = refs[33:36]
    scratch = refs[36:]
    ring, seq = places()
    rows = out_part.shape[1]
    own_rows = branch_part.shape[1]
    wide = heads * HEAD

    def stream(place, part, total, extent, pieces, at, loads=None):
        return Reduce(place, part, total, extent, pieces, scratch[7 * at : 7 * at + 7], loads)

    def spreading(own, full, pieces, at):
        return Gather(seq, own, full, rows, pieces, scratch[35 + 5 * at : 40 + 5 * at])

    out_sum = stream(ring, out_part, out_own, rows, 1, 0, out_loads)
    z_sum = stream(ring, z_part, z_own, rows, 1, 1, z_loads)
    rest_sum = stream(ring, rest_part, rest_own, rows, WEIGHT_PIECES, 2)
    branch_sum = stream(seq, branch_part, branch, own_rows, 1, 3, branch_loads)
    d_normed_sum = stream(seq, act_part, d_normed, own_rows, 2, 4)
    out_spread = spreading(out_own, out_all, 1, 0)
    z_spread = spreading(z_own, z_all, 1, 1)
    rest_spread = spreading(rest_own, rest_all, WEIGHT_PIECES, 2)
    early = [(s, item) for s in (out_sum, z_sum) for item in s.items()]
    at_step = pl.program_id(0)
    blocks = d_rest.shape[0] // STRETCH

    @pl.when(at_step == 0)
    def _():
        meet(ring, seq)
        for s, item in early:
            s.begin(item)
        for item in branch_sum.items():
            branch_sum.begin(item)

    backward_block(heads, *chunk, *packs, d_conv, d_head, extended, d_state, d_rest)

    for k in range(blocks):

        @pl.when(at_step == k)
        def _():
            s, item = early[k]
            s.handle(item)
            if k == blocks - 1:
                for item in branch_sum.items():
                    branch_sum.handle(item)
                branch_sum.close(0)
                branch_sum.finish()

    @pl.when(at_step == blocks - 1)
    def _():
        def rest_block(slot):
            here = pl.ds(pl.multiple_of(slot * rows, 16), rows)

            def one(at, _):
                columns = pl.ds(pl.multiple_of(at * 384, 128), 384)
                rest_part[slot, :, columns] = dot(
                    normed_t[here, :], d_rest[:, columns]
                ).astype(BF16)
                return 0

            lax.fori_loop(0, d_rest.shape[1] // 384, one, 0)

        def normed_block(slot):
            here = pl.ds(pl.multiple_of(slot * own_rows, own_rows), own_rows)

            def one(at, _):
                columns = pl.ds(pl.multiple_of(at * 512, 128), 512)
                value = dot(d_z[here, :], weights[columns, :wide], ((1,), (1,)))
                value = value + dot(d_rest[here, :], weights[columns, wide:], ((1,), (1,)))
                act_part[slot, :, columns] = value.astype(BF16)
                return 0

            lax.fori_loop(0, D // 512, one, 0)

        for step in rest_sum.steps():
            for across in range(1, ring.minor):
                rest_block(ring.slot(step, across))
            for piece in range(WEIGHT_PIECES):
                rest_sum.begin((piece, step))
        for step in d_normed_sum.steps():
            for across in range(1, seq.minor):
                normed_block(seq.slot(step, across))
            for piece in range(2):
                d_normed_sum.begin((piece, step))
        for step in rest_sum.steps():
            rest_block(ring.slot(step, 0))
        for step in d_normed_sum.steps():
            normed_block(seq.slot(step, 0))
        for s, item in early[blocks:]:
            s.handle(item)
        out_sum.close(0)
        out_spread.begin(0)
        side = d_normed_sum.items()
        for at, item in enumerate(rest_sum.items()):
            rest_sum.handle(item)
            if at < len(side):
                d_normed_sum.handle(side[at])
            if at == WEIGHT_PIECES:
                z_sum.close(0)
                z_spread.begin(0)
                out_spread.forward(0)
        for piece in range(2):
            d_normed_sum.close(piece)
        for piece in range(WEIGHT_PIECES):
            rest_sum.close(piece)
            rest_spread.begin(piece)
        out_spread.keep().start()
        z_spread.keep().start()
        rest_spread.keep().start()
        z_spread.forward(0)
        for piece in range(WEIGHT_PIECES):
            rest_spread.forward(piece)
        for s in (out_sum, z_sum, rest_sum, d_normed_sum):
            s.finish()
        for s in (out_spread, z_spread, rest_spread):
            s.finish()
            s.keep().wait()


def run_backward(
    heads, d_y, pre, conv, dt_pre, states, seg_pad, seg_row, packs, spread, d_z, weights, normed_t,
    out_part, z_part, branch_part,
):
    length = d_y.shape[0]
    blocks = length // STRETCH
    wide = heads * HEAD
    edge = wide + 2 * STATE
    rest = edge + DT_PAD
    ring, seq = places()
    count, groups = lax.axis_size("fsdp"), lax.axis_size("seq")

    def split(x, by):
        return x.reshape(by, x.shape[0] // by, x.shape[1])

    out_part, z_part = split(out_part, count), split(z_part, count)
    branch_part = split(branch_part, groups)
    rows, own_rows = out_part.shape[1], branch_part.shape[1]
    wholes = [seg_pad, seg_row, *packs, spread, spread.T, d_z, weights, normed_t]
    scratch = [
        pltpu.VMEM((STRETCH + 8, edge), F32),
        pltpu.VMEM((STATE, wide), F32),
        pltpu.VMEM((length, rest), BF16),
        pltpu.VMEM((count, rows, rest), BF16),
        pltpu.VMEM((groups, own_rows, D), BF16),
        pltpu.VMEM((rows, wide), BF16),
        pltpu.VMEM((rows, wide), BF16),
        pltpu.VMEM((rows, rest), BF16),
        pltpu.SemaphoreType.DMA((ring.major,)),
        pltpu.SemaphoreType.DMA((ring.major,)),
        pltpu.SemaphoreType.DMA((seq.major,)),
    ]
    scratch = scratch + Reduce.scratch(ring, rows, wide, 1) + Reduce.scratch(ring, rows, wide, 1)
    scratch = scratch + Reduce.scratch(ring, rows, rest, WEIGHT_PIECES)
    scratch = scratch + Reduce.scratch(seq, own_rows, D, 1) + Reduce.scratch(seq, own_rows, D, 2)
    for pieces in (1, 1, WEIGHT_PIECES):
        scratch = scratch + Gather.scratch(seq, pieces)
    gathered = [jax.ShapeDtypeStruct((groups, rows, x), BF16) for x in (wide, wide, rest)]
    summed = [
        jax.ShapeDtypeStruct((own_rows, D), BF16),
        jax.ShapeDtypeStruct((own_rows, D), BF16),
        jax.ShapeDtypeStruct((8, edge), F32),
        jax.ShapeDtypeStruct((8, 128), F32),
    ]
    return pl.pallas_call(
        partial(backward_kernel, heads),
        grid=(blocks,),
        in_specs=[
            block(wide, blocks),
            block(edge, blocks),
            block(edge, blocks),
            block(128, blocks),
            pl.BlockSpec((1, STATE, wide), lambda i: (blocks - 1 - i, 0, 0)),
        ]
        + [resident(x) for x in wholes]
        + [HBM] * 3,
        out_specs=[HBM, HBM, HBM] + [resident(x) for x in summed],
        out_shape=gathered + summed,
        scratch_shapes=scratch,
        compiler_params=pltpu.CompilerParams(
            collective_id=2,
            has_side_effects=True,
            vmem_limit_bytes=61 * 1024 * 1024,
            dimension_semantics=("arbitrary",),
        ),
        name="backward_and_sums",
    )(d_y, pre, conv, dt_pre, states, *wholes, out_part, z_part, branch_part)


def adam_kernel(
    groups,
    z_piece,
    rest_piece,
    tails,
    out_piece,
    choose,
    w_in,
    m_in,
    v_in,
    w_out,
    m_out,
    v_out,
    g_in_new,
    m_in_new,
    v_in_new,
    u_in,
    g_out_new,
    m_out_new,
    v_out_new,
    u_out,
    sums,
):
    j = pl.program_id(0)
    wide = w_in.shape[1]

    @pl.when(j == 0)
    def _():
        sums[...] = jnp.zeros_like(sums)

    def update(gradient, w, m, v, g_new, m_new, v_new, u, at, keep):
        columns = gradient.shape[1]
        first, second, direction = adam_parts(gradient, m[:, :columns], v[:, :columns])
        weight = w[:, :columns]
        direction = direction + WEIGHT_DECAY * weight
        g_new[:, :columns] = gradient
        m_new[:, :columns] = first
        v_new[:, :columns] = second
        u[:, :columns] = direction
        for k, value in ((at, weight * weight), (at + 1, direction * direction)):
            value = jnp.where(keep, value, 0.0) if keep is not None else value
            sums[k : k + 1, :columns] += jnp.sum(value, axis=0, keepdims=True)

    inside = (w_in, m_in, v_in, g_in_new, m_in_new, v_in_new, u_in)

    @pl.when(j < groups)
    def _():
        update(z_piece[0].astype(F32), *inside, 0, None)

    @pl.when((j >= groups) & (j < 2 * groups))
    def _():
        update(rest_piece[0].astype(F32), *inside, 0, None)

    @pl.when(j == 2 * groups)
    def _():
        states = jnp.zeros((w_in.shape[0], 2 * STATE), F32)
        steps = jnp.zeros((w_in.shape[0], DT_PAD), F32)
        for s in range(groups):
            states = states + tails[s, :, : 2 * STATE].astype(F32)
            steps = steps + dot(tails[s, :, 2 * STATE :], choose[s])
        gradient = jnp.concatenate([states, steps], axis=1)
        lane = lax.broadcasted_iota(jnp.int32, gradient.shape, 1)
        update(gradient, *inside, 0, lane < 2 * STATE + HEADS)

    @pl.when(j > 2 * groups)
    def _():
        update(
            out_piece[0].astype(F32),
            w_out, m_out, v_out, g_out_new, m_out_new, v_out_new, u_out, 2, None,
        )


def run_adam(groups, heads, z_all, rest_all, out_all, inside, outside):
    rows = inside[0].shape[0]
    wide = heads * HEAD
    last = 2 * groups
    head = jnp.arange(DT_PAD)
    choose = jnp.stack(
        [
            (head[:, None] + s * heads == head[None, :]) & (head[:, None] < heads)
            for s in range(groups)
        ]
    ).astype(BF16)
    in_spec = pl.BlockSpec((rows, wide), lambda j: (0, jnp.minimum(j, last)))
    out_spec = pl.BlockSpec((rows, wide), lambda j: (0, jnp.maximum(j - last - 1, 0)))
    tail = 2 * STATE + DT_PAD
    return pl.pallas_call(
        partial(adam_kernel, groups),
        grid=(last + 1 + groups,),
        in_specs=[
            pl.BlockSpec((1, rows, wide), lambda j: (jnp.minimum(j, groups - 1), 0, 0)),
            pl.BlockSpec(
                (1, rows, wide), lambda j: (jnp.clip(j - groups, 0, groups - 1), 0, 0)
            ),
            pl.BlockSpec((groups, rows, tail), lambda j: (0, 0, wide // tail)),
            pl.BlockSpec((1, rows, wide), lambda j: (jnp.maximum(j - last - 1, 0), 0, 0)),
            pl.BlockSpec(choose.shape, lambda j: (0, 0, 0)),
        ]
        + [in_spec] * 3
        + [out_spec] * 3,
        out_specs=[in_spec] * 4 + [out_spec] * 4 + [pl.BlockSpec((8, wide), lambda j: (0, 0))],
        out_shape=[jax.ShapeDtypeStruct(inside[0].shape, F32)] * 4
        + [jax.ShapeDtypeStruct(outside[0].shape, F32)] * 4
        + [jax.ShapeDtypeStruct((8, wide), F32)],
        compiler_params=compiler_params(),
        name="adam",
    )(z_all, rest_all, rest_all, out_all, choose, *inside, *outside)


def exchange(place_axis, level, source, got, sends, arrivals):
    index = lax.axis_index(place_axis)
    other = partner(index, level)
    return pltpu.make_async_remote_copy(
        src_ref=source,
        dst_ref=got,
        send_sem=sends,
        recv_sem=arrivals,
        device_id={place_axis: other},
        device_id_type=pl.DeviceIdType.MESH,
    )


def partner(index, level):
    bit = 2**level
    return index + (1 - 2 * (index // bit % 2)) * bit


def levels_of(axis):
    return lax.axis_size(axis).bit_length() - 1


def small_kernel(part, full, sums, got, sends, arrivals, *sems):
    _, seq = places()
    barrier = pltpu.get_barrier_semaphore()
    count = 0
    for level in range(levels_of("fsdp")):
        pl.semaphore_signal(
            barrier,
            inc=1,
            device_id={"fsdp": partner(lax.axis_index("fsdp"), level)},
            device_id_type=pl.DeviceIdType.MESH,
        )
        count = count + 1
    for other in seq.others():
        pl.semaphore_signal(
            barrier, inc=1, device_id={"seq": other}, device_id_type=pl.DeviceIdType.MESH
        )
        count = count + 1
    pl.semaphore_wait(barrier, count)
    sums[0] = part[...]
    levels = levels_of("fsdp")
    for level in range(levels):
        copy = exchange(
            "fsdp", level, sums.at[level], got.at[level], sends.at[level], arrivals.at[level]
        )
        copy.start()
        copy.wait()
        sums[level + 1] = sums[level] + got[level]
    gather = Gather(seq, sums.at[levels], full, part.shape[0], 1, sems)
    gather.begin(0)
    gather.keep().start()
    gather.forward(0)
    gather.finish()
    gather.keep().wait()


def run_small(part):
    levels = levels_of("fsdp")
    dma = pltpu.SemaphoreType.DMA
    _, seq = places()
    return pl.pallas_call(
        small_kernel,
        in_specs=[VMEM],
        out_specs=VMEM,
        out_shape=jax.ShapeDtypeStruct((lax.axis_size("seq"),) + part.shape, F32),
        scratch_shapes=[
            pltpu.VMEM((levels + 1,) + part.shape, F32),
            pltpu.VMEM((levels,) + part.shape, F32),
            dma((levels,)),
            dma((levels,)),
        ]
        + Gather.scratch(seq, 1),
        compiler_params=comm_params(4),
        name="sum_small_gradients",
    )(part)


def adam_parts(gradient, first_old, second_old):
    first_new = FIRST_DECAY * first_old + (1.0 - FIRST_DECAY) * gradient
    second_new = SECOND_DECAY * second_old + (1.0 - SECOND_DECAY) * gradient * gradient
    direction = (
        first_new
        / (1.0 - FIRST_DECAY**STEP)
        / (jnp.sqrt(second_new / (1.0 - SECOND_DECAY**STEP)) + ADAM_EPSILON)
    )
    return (first_new, second_new, direction)


def shards(
    tokens,
    cotangent,
    segments,
    in_weight,
    out_weight,
    small_params,
    in_first,
    in_second,
    out_first,
    out_second,
    small_first,
    small_second,
):
    in_gain = small_params[:D]
    groups = lax.axis_size("seq")
    where_seq = lax.axis_index("seq")
    heads = HEADS // groups
    wide = INNER // groups
    segment_row = segments[0]

    def own(vector, axis=-1):
        size = vector.shape[axis] // groups
        return lax.dynamic_slice_in_dim(vector, where_seq * size, size, axis)

    inputs = tokens[0].astype(F32)
    in_rms = lax.rsqrt(jnp.mean(inputs * inputs, axis=-1, keepdims=True) + NORM_EPS)
    dt_weight = jnp.pad(
        own(in_weight[:, INNER + CONV :]), ((0, 0), (0, DT_PAD - heads))
    ).astype(BF16)
    small = jnp.pad(small_params, (0, -small_params.shape[0] % 128))[None, :]
    spread_heads = (
        jnp.arange(128)[:, None] == jnp.arange(wide)[None, :] // HEAD
    ).astype(BF16)
    seg_pad = jnp.pad(segment_row, (EDGE, EDGE), constant_values=-1)[:, None]
    (
        pre, conv_in, dt_pre, states, d_y, d_z, normed_t, out_part, z_part, branch_part, d_out_gain,
        conv_pack, head_pack, chan_pack, w_in,
    ) = run_forward(
        heads, tokens[0], cotangent[0], small, dt_weight, seg_pad, segments, spread_heads,
        in_weight, out_weight,
    )
    d_out_gain = d_out_gain[0]
    packs = (conv_pack, head_pack, chan_pack)
    out_all, z_all, rest_all, branch, d_normed, d_conv, d_head = run_backward(
        heads, d_y, pre, conv_in, dt_pre, states, seg_pad, segments, packs, spread_heads, d_z,
        w_in, normed_t, out_part, z_part, branch_part,
    )
    d_conv = d_conv[: KERNEL + 1]
    d_dt_bias, d_a, d_skip = d_head[0, :heads], d_head[1, :heads], d_head[2, :heads]
    output = (inputs + branch.astype(F32)).astype(BF16)[None]
    d_normed = d_normed.astype(F32)
    slope = d_normed * in_gain[None, :]
    d_inputs = slope * in_rms - inputs * (in_rms**3 / D) * jnp.sum(
        slope * inputs, axis=1, keepdims=True
    )
    input_grad = (cotangent[0].astype(F32) + d_inputs)[None]
    d_in_gain = jnp.sum(d_normed * inputs * in_rms, axis=0)

    (
        in_grad, in_first_new, in_second_new, in_dir,
        out_grad, out_first_new, out_second_new, out_dir, squares,
    ) = run_adam(
        groups, heads, z_all, rest_all, out_all,
        (in_weight, in_first, in_second), (out_weight, out_first, out_second),
    )
    partial_sums = jnp.sum(squares[:4], axis=1)
    small_own = [d_conv[:, :wide].reshape(-1), d_dt_bias, d_a, d_skip, d_out_gain]
    small_shared = [d_conv[:, wide:].reshape(-1), d_in_gain]
    packed = jnp.concatenate(small_own + small_shared + [partial_sums])
    packed = jnp.pad(packed, (0, -packed.shape[0] % 1024)).reshape(-1, 128)
    sums = run_small(packed).reshape(groups, -1)
    offset = 0

    def taken(*shape):
        nonlocal offset
        size = 1
        for extent in shape:
            size = size * extent
        piece = sums[:, offset : offset + size].reshape((groups,) + shape)
        offset = offset + size
        return piece

    g_conv = jnp.transpose(taken(KERNEL + 1, wide), (1, 0, 2)).reshape(KERNEL + 1, INNER)
    g_dt_bias, g_a, g_skip = [taken(heads).reshape(-1) for _ in range(3)]
    g_out_gain = taken(wide).reshape(-1)
    g_conv = jnp.concatenate(
        [g_conv, jnp.sum(taken(KERNEL + 1, 2 * STATE), axis=0)], axis=1
    )
    g_in_gain = jnp.sum(taken(D), axis=0)
    totals = taken(4)[0]
    small_grad = jnp.concatenate(
        [g_in_gain, g_conv.reshape(-1), g_dt_bias, g_a, g_skip, g_out_gain]
    )
    norms = jnp.sqrt(totals)
    in_new = in_weight - LEARN_RATE * (norms[0] / norms[1]) * in_dir
    out_new = out_weight - LEARN_RATE * (norms[2] / norms[3]) * out_dir
    small_first_new, small_second_new, small_dir = adam_parts(small_grad, small_first, small_second)
    small_new = small_params - LEARN_RATE * small_dir
    return (
        output,
        input_grad,
        in_grad,
        in_new,
        in_first_new,
        in_second_new,
        out_grad,
        out_new,
        out_first_new,
        out_second_new,
        small_grad,
        small_new,
        small_first_new,
        small_second_new,
        norms,
    )


def solution(mesh):
    matrix = P("fsdp", None)
    rows = P("fsdp", "seq", None)
    return jax.shard_map(
        shards,
        mesh=mesh,
        in_specs=(rows, rows, matrix, matrix, matrix, P(), matrix, matrix, matrix, matrix, P(), P()),
        out_specs=(rows, rows) + (matrix,) * 8 + (P(),) * 5,
        check_vma=False,
    )
```

```python
from functools import partial

import jax
import jax.numpy as jnp
from jax import lax
from jax.experimental import pallas as pl
from jax.experimental.pallas import tpu as pltpu
from jax.sharding import PartitionSpec as P

D = 1536
HEADS = 48
HEAD = 64
STATE = 128
KERNEL = 4
STRETCH = 256
STEP = 5
INNER = 3072
CONV = 3328
PROJ = 6448
DT_PAD = 128

NORM_EPS = 1e-05
FIRST_DECAY = 0.9
SECOND_DECAY = 0.999
ADAM_EPSILON = 1e-06
WEIGHT_DECAY = 0.01
LEARN_RATE = 0.5
F32 = jnp.float32
BF16 = jnp.bfloat16


def dot(a, b, dims=((1,), (0,))):
    return lax.dot_general(a, b, (dims, ((), ())), preferred_element_type=F32)


def split_dot(value, ones):
    high = value.astype(BF16)
    low = (value - high.astype(F32)).astype(BF16)
    return dot(high, ones) + dot(low, ones)


def tri_dot(ones, value):
    high = value.astype(BF16)
    rest = value - high.astype(F32)
    middle = rest.astype(BF16)
    low = (rest - middle.astype(F32)).astype(BF16)
    return dot(ones, high) + dot(ones, middle) + dot(ones, low)


def sigmoid(v):
    return 1.0 / (1.0 + jnp.exp(-v))


def softplus(v):
    return jnp.maximum(v, 0.0) + jnp.log1p(jnp.exp(-jnp.abs(v)))


def row_at_least():
    rows = lax.broadcasted_iota(jnp.int32, (STRETCH, STRETCH), 0)
    columns = lax.broadcasted_iota(jnp.int32, (STRETCH, STRETCH), 1)
    return rows >= columns


def decays(dt, rate, masks, spread):
    lower = jnp.where(row_at_least(), 1.0, 0.0).astype(BF16)
    cumulative = dot(lower, dt.astype(BF16)) * rate
    last = cumulative[STRETCH - 1 :, :]
    carry = split_dot(jnp.exp(cumulative) * masks["carry"], spread)
    tail = split_dot(jnp.exp(last - cumulative) * masks["tail"], spread)
    keep = split_dot(jnp.broadcast_to(jnp.exp(last) * masks["keep"], (8, 128)), spread)[:1]
    return cumulative, jnp.transpose(cumulative), carry, tail, keep


EDGE = 8


def block_masks(seg_pad, seg_row, at):
    def rows(by, size=STRETCH):
        return seg_pad[pl.ds(at + EDGE + by, size), :]

    here = rows(0)
    first = jnp.where(at == 0, rows(0, 1), rows(-1, 1))
    last = rows(STRETCH - 1, 1)
    masks = {"carry": here == first, "tail": here == last, "keep": last == first}
    for by in range(1, KERNEL):
        masks[-by] = here == rows(-by)
        masks[by] = here == rows(by)
    masks = {key: jnp.where(value, 1.0, 0.0) for key, value in masks.items()}
    within = row_at_least() & (here == seg_row[:, pl.ds(at, STRETCH)])
    masks["bar"] = jnp.where(within, 0.0, -1e30)
    return masks


def forward_block(heads, at, normed, w_in, masks, packs, spread, outs, z_all, y_all, extended, state):
    conv_pack, head_pack, chan_pack = packs
    pre_out, conv_out, dt_out, states_out = outs
    wide = heads * HEAD
    edge = wide + 2 * STATE
    here = pl.ds(at, STRETCH)
    z_all[here, :] = dot(normed, w_in[:, :wide])
    conv_low = dot(normed, w_in[:, wide : wide + edge]).astype(BF16)
    conv_out[...] = conv_low
    conv_in = conv_low.astype(F32)
    extended[8 : 8 + STRETCH, :] = conv_in
    pre = conv_pack[4:5, :] + conv_pack[3:4, :] * conv_in
    for by in range(1, KERNEL):
        pre = pre + conv_pack[3 - by : 4 - by, :] * (
            extended[8 - by : 8 - by + STRETCH, :] * masks[-by]
        )
    extended[0:8, :] = extended[STRETCH : STRETCH + 8, :]
    pre_out[...] = pre
    act = (pre * sigmoid(pre)).astype(BF16)
    xs = act[:, :wide].astype(F32)
    b_mat = act[:, wide : wide + STATE]
    c_mat = act[:, wide + STATE :]
    dt_pre = dot(normed, w_in[:, wide + edge :]) + head_pack[0:1, :]
    dt_out[...] = dt_pre
    dt = softplus(dt_pre).astype(BF16)
    cumulative, cum_rows, carry, tail, keep = decays(dt, head_pack[1:2, :], masks, spread)
    scaled = xs * dot(dt, spread)
    scaled_low = scaled.astype(BF16)
    scores = dot(c_mat, b_mat, ((1,), (1,)))
    old = state[...]
    states_out[0] = old
    outer = dot(c_mat, old.astype(BF16)) * carry + chan_pack[0:1, :] * xs
    state[...] = old * keep + dot(b_mat, (scaled * tail).astype(BF16), ((0,), (0,)))
    first_half = lax.broadcasted_iota(jnp.int32, (STRETCH, 2 * HEAD), 1) < HEAD
    pieces = []
    for pair in range(heads // 2):
        columns = slice(pair * 2 * HEAD, (pair + 1) * 2 * HEAD)
        halves = []
        for h in (2 * pair, 2 * pair + 1):
            weights = scores * jnp.exp(
                cumulative[:, h : h + 1] - cum_rows[h : h + 1, :] + masks["bar"]
            )
            halves.append(dot(weights.astype(BF16), scaled_low[:, columns]))
        pieces.append(jnp.where(first_half, halves[0], halves[1]))
    y_all[here, :] = (outer + jnp.concatenate(pieces, axis=1)).astype(BF16)


def fill_packs(heads, small, spread, packs, scratch_gain):
    conv_pack, head_pack, chan_pack = packs
    wide = heads * HEAD
    index = lax.axis_index("seq")
    start = pl.multiple_of(index * wide, 128)
    for ref in packs:
        ref[...] = jnp.zeros_like(ref)
    for k in range(KERNEL + 1):
        base = D + k * CONV
        conv_pack[k : k + 1, :wide] = small[:, pl.ds(base + start, wide)]
        conv_pack[k : k + 1, wide:] = small[:, base + INNER : base + CONV]
    base = D + (KERNEL + 1) * CONV
    window = jnp.broadcast_to(small[:, base : base + 256], (8, 256))
    lane = lax.broadcasted_iota(jnp.int32, (8, 256), 1)

    def own(k):
        moved = pltpu.roll(window, 256 - (k * HEADS + index * heads), 1)
        return jnp.where(lane < heads, moved, 0.0)[:, :128]

    head_pack[0:1, :] = own(0)[:1]
    rate = own(1)
    rate = jnp.where(lax.broadcasted_iota(jnp.int32, (8, 128), 1) < heads, -jnp.exp(rate), 0.0)
    head_pack[1:2, :] = rate[:1]
    chan_pack[0:1, :] = tri_spread(own(2), spread)[:1]
    base = base + 3 * HEADS
    shift = base % 128
    gain = jnp.broadcast_to(small[:, base - shift : base - shift + INNER + 128], (8, INNER + 128))
    scratch_gain[...] = pltpu.roll(gain, INNER + 128 - shift, 1)
    chan_pack[1:2, :] = scratch_gain[0:1, pl.ds(start, wide)]


def tri_spread(value, ones):
    high = value.astype(BF16)
    rest = value - high.astype(F32)
    middle = rest.astype(BF16)
    low = (rest - middle.astype(F32)).astype(BF16)
    return dot(high, ones) + dot(middle, ones) + dot(low, ones)


def gate_sums(y, z, d_mixed, gain):
    gated = y.astype(F32) * (z * sigmoid(z))
    squares = jnp.sum(gated * gated, axis=1, keepdims=True)
    products = jnp.sum(d_mixed * gain * gated, axis=1, keepdims=True)
    lane = lax.broadcasted_iota(jnp.int32, (STRETCH, 128), 1)
    both = jnp.where(lane == 0, squares, jnp.where(lane == 1, products, 0.0))
    return jnp.transpose(both)[0:8, :]


def gate_gradients(y_low, z, d_mixed, gain, sums):
    columns = jnp.transpose(jnp.concatenate([sums, jnp.zeros((120, STRETCH), F32)], axis=0))
    rms = lax.rsqrt(columns[:, 0:1] / INNER + NORM_EPS)
    y = y_low.astype(F32)
    sig = sigmoid(z)
    silu = z * sig
    gated = y * silu
    unit = gated * rms
    d_gain = jnp.sum(d_mixed * unit, axis=0, keepdims=True)
    d_gated = d_mixed * gain * rms - unit * (rms * rms / INNER * columns[:, 1:2])
    d_z = d_gated * y * (sig * (1.0 + z * (1.0 - sig)))
    return (unit * gain).astype(BF16), (d_gated * silu).astype(BF16), d_z.astype(BF16), d_gain


def forward_kernel(heads, *refs):
    tokens, cotangent, small, dt_weight, seg_pad, seg_row, spread_ref, in_weight, out_weight = refs[:9]
    outs = refs[9:13]
    d_y, d_z, normed_t, out_part, z_part, branch_part, d_gain = refs[13:20]
    packs = refs[20:23]
    w_in_out = refs[23]
    (
        stage_in, stage_out, own_in, own_out, own_rows, w_in, w_out, rows_all, returned_t,
        z_all, y_all, d_mixed_all, extended, state, scratch_gain, sums, got,
        stage_sems, sum_sends, sum_arrivals,
    ) = refs[24:44]
    sems = refs[44:]
    ring, seq = places()
    wide = heads * HEAD
    edge = wide + 2 * STATE
    step = pl.program_id(0)
    blocks = pl.num_programs(0) - 1
    length = rows_all.shape[0]
    count = length // STRETCH
    first = Gather(ring, own_in, w_in, own_in.shape[0], WEIGHT_PIECES, sems[:5])
    second = Gather(ring, own_out, w_out, own_out.shape[0], 1, sems[5:10])
    third = Gather(seq, own_rows, rows_all, own_rows.shape[0], TOKEN_PIECES, sems[10:15])
    save = pltpu.make_async_copy(w_in, w_in_out, stage_sems.at[5])
    spread = spread_ref[...]
    at = pl.multiple_of(step * STRETCH, STRETCH)

    @pl.when(step == 0)
    def _():
        start = pl.multiple_of(seq.index * wide, 128)
        sources = [
            (in_weight.at[:, pl.ds(start, wide)], stage_in.at[:, :wide]),
            (in_weight.at[:, pl.ds(INNER + start, wide)], stage_in.at[:, wide : 2 * wide]),
            (in_weight.at[:, pl.ds(2 * INNER, 2 * STATE)], stage_in.at[:, 2 * wide :]),
            (out_weight.at[:, pl.ds(start, wide)], stage_out),
        ]
        loads = [
            pltpu.make_async_copy(source, target, stage_sems.at[k])
            for k, (source, target) in enumerate(sources)
        ]
        for load in loads:
            load.start()
        meet(ring, seq)
        inputs = tokens[...].astype(F32)
        rms = lax.rsqrt(jnp.mean(inputs * inputs, axis=-1, keepdims=True) + NORM_EPS)
        own_rows[:, :D] = (inputs * rms * small[:, :D]).astype(BF16)
        own_rows[:, D:] = cotangent[...]
        for load in loads:
            load.wait()
        own_in[:, : wide + edge] = stage_in[...].astype(BF16)
        own_in[:, wide + edge :] = dt_weight[...]
        own_out[...] = stage_out[...].astype(BF16)
        for piece in range(TOKEN_PIECES):
            if piece < WEIGHT_PIECES:
                first.begin(piece)
            third.begin(piece)
        first.keep().start()
        third.keep().start()
        second.keep().start()
        fill_packs(heads, small, spread, packs, scratch_gain)
        state[...] = jnp.zeros_like(state)
        extended[0:8, :] = jnp.zeros((8, edge), F32)
        d_gain[...] = jnp.zeros_like(d_gain)
        for piece in range(TOKEN_PIECES):
            third.forward(piece)
            if piece < WEIGHT_PIECES:
                first.forward(piece)
        second.begin(0)
        third.finish()
        third.keep().wait()

        def turn(k, _):
            here = pl.ds(pl.multiple_of(k * STRETCH, STRETCH), STRETCH)
            normed_t[:, here] = jnp.transpose(rows_all[here, :D])
            returned_t[:, here] = jnp.transpose(rows_all[here, D:])
            return 0

        lax.fori_loop(0, count, turn, 0)
        first.finish()
        first.keep().wait()
        save.start()

    @pl.when(step < blocks)
    def _():
        masks = block_masks(seg_pad, seg_row, at)
        forward_block(
            heads, at, rows_all[pl.ds(at, STRETCH), :D], w_in, masks, packs, spread, outs,
            z_all, y_all, extended, state,
        )

    @pl.when(step == 1)
    def _():
        second.forward(0)

    @pl.when(step == blocks)
    def _():
        second.finish()
        second.keep().wait()
        gain = packs[2][1:2, :]

        def measure(k, _):
            here = pl.ds(pl.multiple_of(k * STRETCH, STRETCH), STRETCH)
            d_mixed = dot(rows_all[here, D:], w_out[...])
            d_mixed_all[here, :] = d_mixed
            sums[0, :, here] = gate_sums(y_all[here, :], z_all[here, :], d_mixed, gain)
            return 0

        lax.fori_loop(0, count, measure, 0)
        for level in range(levels_of("seq")):
            copy = exchange(
                "seq", level, sums.at[level], got.at[level], sum_sends.at[level], sum_arrivals.at[level]
            )
            copy.start()
            copy.wait()
            sums[level + 1] = sums[level] + got[level]
        total = levels_of("seq")

        def differentiate(k, _):
            here = pl.ds(pl.multiple_of(k * STRETCH, STRETCH), STRETCH)
            mixed, d_y_block, d_z_block, d_gain_block = gate_gradients(
                y_all[here, :], z_all[here, :], d_mixed_all[here, :], gain, sums[total, :, here]
            )
            y_all[here, :] = mixed
            d_y[here, :] = d_y_block
            d_z[here, :] = d_z_block
            d_gain[0:1, :] += d_gain_block
            branch_part[here, :] = dot(mixed, w_out[...], ((1,), (1,))).astype(BF16)
            return 0

        lax.fori_loop(0, count, differentiate, 0)

        def contract(k, _):
            here = pl.ds(pl.multiple_of(k * 256, 256), 256)
            out_part[here, :] = dot(returned_t[here, :], y_all[...]).astype(BF16)
            z_part[here, :] = dot(normed_t[here, :], d_z[...]).astype(BF16)
            return 0

        lax.fori_loop(0, D // 256, contract, 0)
        save.wait()


def backward_block(
    heads,
    d_y_ref,
    pre_ref,
    conv_ref,
    dt_ref,
    states,
    seg_pad,
    seg_row,
    conv_pack,
    head_pack,
    chan_pack,
    spread_ref,
    gather_ref,
    d_conv_out,
    d_head_out,
    extended,
    d_state,
    d_rest,
):
    wide = heads * HEAD
    edge = wide + 2 * STATE

    @pl.when(pl.program_id(0) == 0)
    def _():
        d_state[...] = jnp.zeros_like(d_state)
        extended[STRETCH : STRETCH + 8, :] = jnp.zeros((8, edge), F32)
        d_conv_out[...] = jnp.zeros_like(d_conv_out)
        d_head_out[...] = jnp.zeros_like(d_head_out)

    at_row = pl.multiple_of((pl.num_programs(0) - 1 - pl.program_id(0)) * STRETCH, STRETCH)
    masks = block_masks(seg_pad, seg_row, at_row)
    spread = spread_ref[...]
    gather = gather_ref[...]
    pre = pre_ref[...]
    act = (pre * sigmoid(pre)).astype(BF16)
    xs = act[:, :wide].astype(F32)
    b_mat = act[:, wide : wide + STATE]
    c_mat = act[:, wide + STATE :]
    dt_pre = dt_ref[...]
    dt = softplus(dt_pre).astype(BF16)
    rate = head_pack[1:2, :]
    cumulative, cum_rows, carry, tail, keep = decays(dt, rate, masks, spread)
    dt_wide = dot(dt, spread)
    scaled = xs * dt_wide
    scaled_low = scaled.astype(BF16)
    bar = masks["bar"]
    scores = dot(c_mat, b_mat, ((1,), (1,)))
    old = states[0]
    old_low = old.astype(BF16)
    d_new = d_state[...]
    d_new_low = d_new.astype(BF16)
    d_y_low = d_y_ref[...]
    d_y = d_y_low.astype(F32)

    d_carried = d_y * carry
    d_carried_low = d_carried.astype(BF16)
    d_c = dot(d_carried_low, old_low, ((1,), (1,)))
    d_cum = split_dot(d_carried * dot(c_mat, old_low), gather)
    weighed = scaled * tail
    into = dot(b_mat, d_new_low)
    d_b = dot(weighed.astype(BF16), d_new_low, ((1,), (1,)))
    d_scaled = into * tail
    tail_part = split_dot(weighed * into, gather)
    d_cum = d_cum - tail_part
    kept = jnp.sum(d_new * old, axis=0, keepdims=True) * keep
    kept = split_dot(jnp.broadcast_to(kept, (8, wide)), gather)[:1]
    d_last = jnp.sum(tail_part, axis=0, keepdims=True) + kept
    d_state[...] = d_new * keep + dot(c_mat, d_carried_low, ((0,), (0,)))

    lane = lax.broadcasted_iota(jnp.int32, (STRETCH, 128), 1)
    first_half = lane < HEAD
    d_scores = jnp.zeros((STRETCH, STRETCH), F32)
    column_sums = []
    pieces = []
    for pair in range(heads // 2):
        columns = slice(pair * 2 * HEAD, (pair + 1) * 2 * HEAD)
        halves = []
        d_y_pair = d_y_low[:, columns]
        scaled_pair = scaled_low[:, columns]
        zero = jnp.zeros_like(d_y_pair)
        for h in (2 * pair, 2 * pair + 1):
            decay = jnp.exp(cumulative[:, h : h + 1] - cum_rows[h : h + 1, :] + bar)
            weights = scores * decay
            halves.append(dot(weights.astype(BF16), d_y_pair, ((0,), (0,))))
            d_y_head = jnp.where(first_half == (h % 2 == 0), d_y_pair, zero)
            d_weights = dot(d_y_head, scaled_pair, ((1,), (1,)))
            d_scores = d_scores + d_weights * decay
            product = d_weights * weights
            d_cum = d_cum + jnp.where(lane == h, jnp.sum(product, axis=1, keepdims=True), 0.0)
            column_sums.append(jnp.sum(product, axis=0, keepdims=True))
        pieces.append(jnp.where(first_half, halves[0], halves[1]))
    column_sums.append(jnp.zeros((128 - heads, STRETCH), F32))
    d_cum = d_cum - jnp.transpose(jnp.concatenate(column_sums, axis=0))
    row = lax.broadcasted_iota(jnp.int32, (STRETCH, 128), 0)
    d_cum = d_cum + jnp.where(row == STRETCH - 1, d_last, 0.0)
    d_scaled = d_scaled + jnp.concatenate(pieces, axis=1)
    d_scores_low = d_scores.astype(BF16)
    d_c = d_c + dot(d_scores_low, b_mat)
    d_b = d_b + dot(d_scores_low, c_mat, ((0,), (0,)))

    d_xs = d_scaled * dt_wide + chan_pack[0:1, :] * d_y
    rows = lax.broadcasted_iota(jnp.int32, (STRETCH, STRETCH), 0)
    upper = jnp.where(rows <= lax.broadcasted_iota(jnp.int32, (STRETCH, STRETCH), 1), 1.0, 0.0)
    d_dt = split_dot(d_scaled * xs, gather) + rate * tri_dot(upper.astype(BF16), d_cum)
    d_dt_raw = d_dt.astype(BF16).astype(F32) * sigmoid(dt_pre)
    d_head_out[0:1, :] += jnp.sum(d_dt_raw, axis=0, keepdims=True)
    d_head_out[1:2, :] += jnp.sum(d_cum * cumulative, axis=0, keepdims=True)
    d_skip = jnp.sum(d_y * xs, axis=0, keepdims=True)
    d_head_out[2:3, :] += split_dot(jnp.broadcast_to(d_skip, (8, wide)), gather)[:1]

    extended[0:STRETCH, :wide] = d_xs.astype(BF16).astype(F32)
    extended[0:STRETCH, wide : wide + STATE] = d_b
    extended[0:STRETCH, wide + STATE :] = d_c
    here = pl.ds(at_row, STRETCH)
    d_rest[here, edge:] = jnp.where(lane < heads, d_dt_raw, 0.0).astype(BF16)

    def convolve_back(at, _):
        columns = pl.ds(pl.multiple_of(at * 128, 128), 128)
        value = pre_ref[:, columns]
        gate = sigmoid(value)
        d_pre = extended[0:STRETCH, columns] * (gate * (1.0 + value * (1.0 - gate)))
        extended[0:STRETCH, columns] = d_pre
        conv_in = conv_ref[:, columns].astype(F32)
        d_conv_in = conv_pack[3:4, columns] * d_pre
        d_conv_out[3:4, columns] += jnp.sum(d_pre * conv_in, axis=0, keepdims=True)
        d_conv_out[4:5, columns] += jnp.sum(d_pre, axis=0, keepdims=True)
        for by in range(1, KERNEL):
            moved = extended[by : by + STRETCH, columns] * masks[by]
            d_conv_in = d_conv_in + conv_pack[3 - by : 4 - by, columns] * moved
            d_conv_out[3 - by : 4 - by, columns] += jnp.sum(moved * conv_in, axis=0, keepdims=True)
        extended[STRETCH : STRETCH + 8, columns] = extended[0:8, columns]
        d_rest[here, columns] = d_conv_in.astype(BF16)
        return 0

    lax.fori_loop(0, edge // 128, convolve_back, 0)


VMEM_BYTES = 56 * 1024 * 1024


def block(columns, reverse=0):
    if reverse:
        return pl.BlockSpec((STRETCH, columns), lambda i: (reverse - 1 - i, 0))
    return pl.BlockSpec((STRETCH, columns), lambda i: (i, 0))


def whole(*shape):
    return pl.BlockSpec(shape, lambda i: (0,) * len(shape))


def compiler_params():
    return pltpu.CompilerParams(
        vmem_limit_bytes=VMEM_BYTES, dimension_semantics=("arbitrary",)
    )


class Place:
    def __init__(self, axis, minor):
        self.axis = axis
        self.minor = minor
        self.major = lax.axis_size(axis) // minor
        index = lax.axis_index(axis)
        self.at_major = index // minor
        self.at_minor = index % minor
        self.index = index

    def slot(self, by_major, by_minor):
        return (self.at_major + by_major) % self.major * self.minor + (
            self.at_minor + by_minor
        ) % self.minor

    def others(self):
        along = [self.slot(step, 0) for step in range(1, self.major)]
        return along + [self.slot(0, step) for step in range(1, self.minor)]


def places():
    ring = lax.axis_size("fsdp")
    side = 1
    while 2 * side * 2 * side * 2 <= ring:
        side = 2 * side
    return Place("fsdp", side), Place("seq", 2)


def meet(*all_places):
    barrier = pltpu.get_barrier_semaphore()
    count = 0
    for place in all_places:
        for other in place.others():
            pl.semaphore_signal(
                barrier, inc=1, device_id={place.axis: other}, device_id_type=pl.DeviceIdType.MESH
            )
            count = count + 1
    pl.semaphore_wait(barrier, count)


def send(place, source, target, to, sends, arrivals, at):
    return pltpu.make_async_remote_copy(
        src_ref=source,
        dst_ref=target,
        send_sem=sends.at[at],
        recv_sem=arrivals.at[at],
        device_id={place.axis: to},
        device_id_type=pl.DeviceIdType.MESH,
    )


class Gather:
    def __init__(self, place, own, full, rows, pieces, sems):
        self.place, self.own, self.full = place, own, full
        self.size, self.pieces = rows // pieces, pieces
        self.sends1, self.arrivals1, self.sends2, self.arrivals2, self.here = sems

    @staticmethod
    def scratch(place, pieces):
        first = max(place.major - 1, 1) * pieces
        second = place.major * (place.minor - 1) * pieces
        dma = pltpu.SemaphoreType.DMA
        return [dma((first,)), dma((first,)), dma((second,)), dma((second,)), dma((1,))]

    def rows(self, piece):
        return pl.ds(piece * self.size, self.size)

    def target(self, slot, piece):
        if len(self.full.shape) > len(self.own.shape):
            return self.full.at[slot, self.rows(piece)]
        start = slot * (self.size * self.pieces) + piece * self.size
        return self.full.at[pl.ds(pl.multiple_of(start, 16), self.size)]

    def along(self, piece, step):
        place = self.place
        return send(
            place,
            self.own.at[self.rows(piece)],
            self.target(place.index, piece),
            place.slot(step, 0),
            self.sends1,
            self.arrivals1,
            piece * (place.major - 1) + step - 1,
        )

    def across(self, piece, step, across):
        place = self.place
        slot = place.slot(-step, 0)
        target = self.target(slot, piece)
        source = self.own.at[self.rows(piece)] if step == 0 else target
        at = (piece * place.major + step) * (place.minor - 1) + across - 1
        return send(
            place, source, target, place.slot(0, across), self.sends2, self.arrivals2, at
        )

    def keep(self):
        if len(self.full.shape) > len(self.own.shape):
            target = self.full.at[self.place.index]
        else:
            size = self.size * self.pieces
            target = self.full.at[pl.ds(pl.multiple_of(self.place.index * size, 16), size)]
        return pltpu.make_async_copy(self.own, target, self.here.at[0])

    def begin(self, piece):
        for step in range(1, self.place.major):
            self.along(piece, step).start()
        for across in range(1, self.place.minor):
            self.across(piece, 0, across).start()

    def forward(self, piece):
        for step in range(1, self.place.major):
            self.along(piece, step).wait_recv()
            for across in range(1, self.place.minor):
                self.across(piece, step, across).start()

    def finish(self):
        for piece in range(self.pieces):
            for step in range(1, self.place.major):
                self.along(piece, step).wait_send()
            for step in range(self.place.major):
                for across in range(1, self.place.minor):
                    self.across(piece, step, across).wait()


class Reduce:
    def __init__(self, place, part, total, rows, pieces, scratch, loads=None):
        self.place, self.part, self.total, self.loads = place, part, total, loads
        self.size, self.pieces = rows // pieces, pieces
        self.got1, self.mine, self.got2, self.sends1, self.arrivals1, self.sends2, self.arrivals2 = (
            scratch
        )

    @staticmethod
    def scratch(place, rows, columns, pieces):
        dma = pltpu.SemaphoreType.DMA
        first = place.major * (place.minor - 1)
        second = max(place.major - 1, 1)
        return [
            pltpu.VMEM((first, rows, columns), BF16),
            pltpu.VMEM((second, rows, columns), BF16),
            pltpu.VMEM((second, rows, columns), BF16),
            dma((first * pieces,)),
            dma((first * pieces,)),
            dma((second * pieces,)),
            dma((second * pieces,)),
        ]

    def items(self):
        return [(piece, step) for step in self.steps() for piece in range(self.pieces)]

    def steps(self):
        return list(range(1, self.place.major)) + [0]

    def rows(self, piece):
        return pl.ds(piece * self.size, self.size)

    def across(self, item, across):
        piece, step = item
        place = self.place
        slot = step * (place.minor - 1) + across - 1
        return send(
            place,
            self.part.at[place.slot(step, across), self.rows(piece)],
            self.got1.at[slot, self.rows(piece)],
            place.slot(0, across),
            self.sends1,
            self.arrivals1,
            slot * self.pieces + piece,
        )

    def along(self, item):
        piece, step = item
        place = self.place
        return send(
            place,
            self.mine.at[step - 1, self.rows(piece)],
            self.got2.at[step - 1, self.rows(piece)],
            place.slot(step, 0),
            self.sends2,
            self.arrivals2,
            (step - 1) * self.pieces + piece,
        )

    def begin(self, item):
        for across in range(1, self.place.minor):
            self.across(item, across).start()
        if self.loads is not None:
            self.load(item[1]).start()

    def load(self, step):
        target = self.mine.at[step - 1] if step else self.total
        return pltpu.make_async_copy(
            self.part.at[self.place.slot(step, 0)], target, self.loads.at[step]
        )

    def own(self, step, rows):
        if self.loads is None:
            return self.part[self.place.slot(step, 0), rows].astype(F32)
        source = self.mine.at[step - 1] if step else self.total
        return source[rows].astype(F32)

    def blocks(self, piece, body):
        def one(at, _):
            body(pl.ds(pl.multiple_of(piece * self.size + at * 16, 16), 16))
            return 0

        lax.fori_loop(0, self.size // 16, one, 0)

    def handle(self, item):
        piece, step = item
        place = self.place
        for across in range(1, place.minor):
            self.across(item, across).wait_recv()
        if self.loads is not None:
            self.load(step).wait()
        if step == 0:
            return

        def body(rows):
            value = self.own(step, rows)
            for across in range(1, place.minor):
                slot = step * (place.minor - 1) + across - 1
                value = value + self.got1[slot, rows].astype(F32)
            self.mine[step - 1, rows] = value.astype(BF16)

        self.blocks(piece, body)
        self.along(item).start()

    def close(self, piece):
        place = self.place
        for step in range(1, place.major):
            self.along((piece, step)).wait_recv()

        def body(rows):
            value = self.own(0, rows)
            for across in range(1, place.minor):
                value = value + self.got1[across - 1, rows].astype(F32)
            for step in range(1, place.major):
                value = value + self.got2[step - 1, rows].astype(F32)
            self.total[rows] = value.astype(self.total.dtype)

        self.blocks(piece, body)

    def finish(self):
        for item in self.items():
            for across in range(1, self.place.minor):
                self.across(item, across).wait_send()
            if item[1]:
                self.along(item).wait_send()


WEIGHT_PIECES = 3
TOKEN_PIECES = 4
HBM = pl.BlockSpec(memory_space=pl.ANY)
VMEM = pl.BlockSpec(memory_space=pltpu.VMEM)


def comm_params(number):
    return pltpu.CompilerParams(
        collective_id=number, has_side_effects=True, vmem_limit_bytes=VMEM_BYTES
    )


def resident(x):
    return pl.BlockSpec(
        x.shape, lambda i: (0,) * len(x.shape), pipeline_mode=pl.Buffered(buffer_count=1)
    )


def run_forward(heads, tokens, cotangent, small, dt_weight, seg_pad, seg_row, spread, in_weight, out_weight):
    ring, seq = places()
    count, groups = lax.axis_size("fsdp"), lax.axis_size("seq")
    rows, own_rows = in_weight.shape[0], tokens.shape[0]
    length = own_rows * groups
    blocks = length // STRETCH
    wide = heads * HEAD
    edge = wide + 2 * STATE
    inner = wide + edge + DT_PAD
    levels = levels_of("seq")
    shape = jax.ShapeDtypeStruct
    last = blocks - 1

    def chunk(columns):
        return pl.BlockSpec((STRETCH, columns), lambda i: (i - i // blocks, 0))

    wholes = [tokens, cotangent, small, dt_weight, seg_pad, seg_row, spread]
    late = [
        shape((length, wide), BF16),
        shape((length, wide), BF16),
        shape((D, length), BF16),
        shape((D, wide), BF16),
        shape((D, wide), BF16),
        shape((length, D), BF16),
        shape((8, wide), F32),
        shape((8, edge), F32),
        shape((8, 128), F32),
        shape((8, wide), F32),
    ]
    dma = pltpu.SemaphoreType.DMA
    scratch = [
        pltpu.VMEM((rows, wide + edge), F32),
        pltpu.VMEM((rows, wide), F32),
        pltpu.VMEM((rows, inner), BF16),
        pltpu.VMEM((rows, wide), BF16),
        pltpu.VMEM((own_rows, 2 * D), BF16),
        pltpu.VMEM((D, inner), BF16),
        pltpu.VMEM((D, wide), BF16),
        pltpu.VMEM((length, 2 * D), BF16),
        pltpu.VMEM((D, length), BF16),
        pltpu.VMEM((length, wide), F32),
        pltpu.VMEM((length, wide), BF16),
        pltpu.VMEM((length, wide), F32),
        pltpu.VMEM((STRETCH + 8, edge), F32),
        pltpu.VMEM((STATE, wide), F32),
        pltpu.VMEM((8, INNER + 128), F32),
        pltpu.VMEM((levels + 1, 8, length), F32),
        pltpu.VMEM((levels, 8, length), F32),
        dma((6,)),
        dma((levels,)),
        dma((levels,)),
    ]
    scratch = scratch + Gather.scratch(ring, WEIGHT_PIECES) + Gather.scratch(ring, 1)
    scratch = scratch + Gather.scratch(seq, TOKEN_PIECES)
    return pl.pallas_call(
        partial(forward_kernel, heads),
        grid=(blocks + 1,),
        in_specs=[resident(x) for x in wholes] + [HBM, HBM],
        out_specs=[
            chunk(edge),
            chunk(edge),
            chunk(128),
            pl.BlockSpec((1, STATE, wide), lambda i: (i - i // blocks, 0, 0)),
        ]
        + [resident(x) for x in late]
        + [HBM],
        out_shape=[
            shape((length, edge), F32),
            shape((length, edge), BF16),
            shape((length, 128), F32),
            shape((blocks, STATE, wide), F32),
        ]
        + late
        + [shape((D, inner), BF16)],
        scratch_shapes=scratch,
        compiler_params=pltpu.CompilerParams(
            collective_id=1,
            has_side_effects=True,
            vmem_limit_bytes=61 * 1024 * 1024,
            dimension_semantics=("arbitrary",),
        ),
        name="gather_and_forward",
    )(*wholes, in_weight, out_weight)


def backward_kernel(heads, *refs):
    chunk = refs[:5]
    packs = refs[5:12]
    d_z, weights, normed_t, out_part, z_part, branch_part = refs[12:18]
    out_all, z_all, rest_all, branch, d_normed, d_conv, d_head = refs[18:25]
    extended, d_state, d_rest, rest_part, act_part, out_own, z_own, rest_own = refs[25:33]
    out_loads, z_loads, branch_loads = refs[33:36]
    scratch = refs[36:]
    ring, seq = places()
    rows = out_part.shape[1]
    own_rows = branch_part.shape[1]
    wide = heads * HEAD

    def stream(place, part, total, extent, pieces, at, loads=None):
        return Reduce(place, part, total, extent, pieces, scratch[7 * at : 7 * at + 7], loads)

    def spreading(own, full, pieces, at):
        return Gather(seq, own, full, rows, pieces, scratch[35 + 5 * at : 40 + 5 * at])

    out_sum = stream(ring, out_part, out_own, rows, 1, 0, out_loads)
    z_sum = stream(ring, z_part, z_own, rows, 1, 1, z_loads)
    rest_sum = stream(ring, rest_part, rest_own, rows, WEIGHT_PIECES, 2)
    branch_sum = stream(seq, branch_part, branch, own_rows, 1, 3, branch_loads)
    d_normed_sum = stream(seq, act_part, d_normed, own_rows, 2, 4)
    out_spread = spreading(out_own, out_all, 1, 0)
    z_spread = spreading(z_own, z_all, 1, 1)
    rest_spread = spreading(rest_own, rest_all, WEIGHT_PIECES, 2)
    early = [(s, item) for s in (out_sum, z_sum) for item in s.items()]
    at_step = pl.program_id(0)
    blocks = d_rest.shape[0] // STRETCH

    @pl.when(at_step == 0)
    def _():
        meet(ring, seq)
        for s, item in early:
            s.begin(item)
        for item in branch_sum.items():
            branch_sum.begin(item)

    backward_block(heads, *chunk, *packs, d_conv, d_head, extended, d_state, d_rest)

    for k in range(blocks):

        @pl.when(at_step == k)
        def _():
            s, item = early[k]
            s.handle(item)
            if k == blocks - 1:
                for item in branch_sum.items():
                    branch_sum.handle(item)
                branch_sum.close(0)
                branch_sum.finish()

    @pl.when(at_step == blocks - 1)
    def _():
        def rest_block(slot):
            here = pl.ds(pl.multiple_of(slot * rows, 16), rows)

            def one(at, _):
                columns = pl.ds(pl.multiple_of(at * 384, 128), 384)
                rest_part[slot, :, columns] = dot(
                    normed_t[here, :], d_rest[:, columns]
                ).astype(BF16)
                return 0

            lax.fori_loop(0, d_rest.shape[1] // 384, one, 0)

        def normed_block(slot):
            here = pl.ds(pl.multiple_of(slot * own_rows, own_rows), own_rows)

            def one(at, _):
                columns = pl.ds(pl.multiple_of(at * 512, 128), 512)
                value = dot(d_z[here, :], weights[columns, :wide], ((1,), (1,)))
                value = value + dot(d_rest[here, :], weights[columns, wide:], ((1,), (1,)))
                act_part[slot, :, columns] = value.astype(BF16)
                return 0

            lax.fori_loop(0, D // 512, one, 0)

        for step in rest_sum.steps():
            for across in range(1, ring.minor):
                rest_block(ring.slot(step, across))
            for piece in range(WEIGHT_PIECES):
                rest_sum.begin((piece, step))
        for step in d_normed_sum.steps():
            for across in range(1, seq.minor):
                normed_block(seq.slot(step, across))
            for piece in range(2):
                d_normed_sum.begin((piece, step))
        for step in rest_sum.steps():
            rest_block(ring.slot(step, 0))
        for step in d_normed_sum.steps():
            normed_block(seq.slot(step, 0))
        for s, item in early[blocks:]:
            s.handle(item)
        out_sum.close(0)
        out_spread.begin(0)
        side = d_normed_sum.items()
        for at, item in enumerate(rest_sum.items()):
            rest_sum.handle(item)
            if at < len(side):
                d_normed_sum.handle(side[at])
            if at == WEIGHT_PIECES:
                z_sum.close(0)
                z_spread.begin(0)
                out_spread.forward(0)
        for piece in range(2):
            d_normed_sum.close(piece)
        for piece in range(WEIGHT_PIECES):
            rest_sum.close(piece)
            rest_spread.begin(piece)
        out_spread.keep().start()
        z_spread.keep().start()
        rest_spread.keep().start()
        z_spread.forward(0)
        for piece in range(WEIGHT_PIECES):
            rest_spread.forward(piece)
        for s in (out_sum, z_sum, rest_sum, d_normed_sum):
            s.finish()
        for s in (out_spread, z_spread, rest_spread):
            s.finish()
            s.keep().wait()


def run_backward(
    heads, d_y, pre, conv, dt_pre, states, seg_pad, seg_row, packs, spread, d_z, weights, normed_t,
    out_part, z_part, branch_part,
):
    length = d_y.shape[0]
    blocks = length // STRETCH
    wide = heads * HEAD
    edge = wide + 2 * STATE
    rest = edge + DT_PAD
    ring, seq = places()
    count, groups = lax.axis_size("fsdp"), lax.axis_size("seq")

    def split(x, by):
        return x.reshape(by, x.shape[0] // by, x.shape[1])

    out_part, z_part = split(out_part, count), split(z_part, count)
    branch_part = split(branch_part, groups)
    rows, own_rows = out_part.shape[1], branch_part.shape[1]
    wholes = [seg_pad, seg_row, *packs, spread, spread.T, d_z, weights, normed_t]
    scratch = [
        pltpu.VMEM((STRETCH + 8, edge), F32),
        pltpu.VMEM((STATE, wide), F32),
        pltpu.VMEM((length, rest), BF16),
        pltpu.VMEM((count, rows, rest), BF16),
        pltpu.VMEM((groups, own_rows, D), BF16),
        pltpu.VMEM((rows, wide), BF16),
        pltpu.VMEM((rows, wide), BF16),
        pltpu.VMEM((rows, rest), BF16),
        pltpu.SemaphoreType.DMA((ring.major,)),
        pltpu.SemaphoreType.DMA((ring.major,)),
        pltpu.SemaphoreType.DMA((seq.major,)),
    ]
    scratch = scratch + Reduce.scratch(ring, rows, wide, 1) + Reduce.scratch(ring, rows, wide, 1)
    scratch = scratch + Reduce.scratch(ring, rows, rest, WEIGHT_PIECES)
    scratch = scratch + Reduce.scratch(seq, own_rows, D, 1) + Reduce.scratch(seq, own_rows, D, 2)
    for pieces in (1, 1, WEIGHT_PIECES):
        scratch = scratch + Gather.scratch(seq, pieces)
    gathered = [jax.ShapeDtypeStruct((groups, rows, x), BF16) for x in (wide, wide, rest)]
    summed = [
        jax.ShapeDtypeStruct((own_rows, D), BF16),
        jax.ShapeDtypeStruct((own_rows, D), BF16),
        jax.ShapeDtypeStruct((8, edge), F32),
        jax.ShapeDtypeStruct((8, 128), F32),
    ]
    return pl.pallas_call(
        partial(backward_kernel, heads),
        grid=(blocks,),
        in_specs=[
            block(wide, blocks),
            block(edge, blocks),
            block(edge, blocks),
            block(128, blocks),
            pl.BlockSpec((1, STATE, wide), lambda i: (blocks - 1 - i, 0, 0)),
        ]
        + [resident(x) for x in wholes]
        + [HBM] * 3,
        out_specs=[HBM, HBM, HBM] + [resident(x) for x in summed],
        out_shape=gathered + summed,
        scratch_shapes=scratch,
        compiler_params=pltpu.CompilerParams(
            collective_id=2,
            has_side_effects=True,
            vmem_limit_bytes=61 * 1024 * 1024,
            dimension_semantics=("arbitrary",),
        ),
        name="backward_and_sums",
    )(d_y, pre, conv, dt_pre, states, *wholes, out_part, z_part, branch_part)


def exchange(place_axis, level, source, got, sends, arrivals):
    index = lax.axis_index(place_axis)
    other = partner(index, level)
    return pltpu.make_async_remote_copy(
        src_ref=source,
        dst_ref=got,
        send_sem=sends,
        recv_sem=arrivals,
        device_id={place_axis: other},
        device_id_type=pl.DeviceIdType.MESH,
    )


def partner(index, level):
    bit = 2**level
    return index + (1 - 2 * (index // bit % 2)) * bit


def levels_of(axis):
    return lax.axis_size(axis).bit_length() - 1


class Push:
    def __init__(self, axis, own, slots, sends, arrivals):
        self.axis, self.own, self.slots = axis, own, slots
        self.sends, self.arrivals = sends, arrivals
        self.count = lax.axis_size(axis)

    def copy(self, step):
        index = lax.axis_index(self.axis)
        return pltpu.make_async_remote_copy(
            src_ref=self.own,
            dst_ref=self.slots.at[index],
            send_sem=self.sends.at[step - 1],
            recv_sem=self.arrivals.at[step - 1],
            device_id={self.axis: (index + step) % self.count},
            device_id_type=pl.DeviceIdType.MESH,
        )

    def begin(self):
        for step in range(1, self.count):
            self.copy(step).start()

    def finish(self):
        for step in range(1, self.count):
            self.copy(step).wait()


def update_kernel(groups, heads, *refs):
    z_piece, rest_piece, tails, out_piece = refs[:4]
    choose, d_conv, d_head, d_out_gain, d_in_gain, small_w, small_m, small_v = refs[4:12]
    w_in, m_in, v_in, w_out, m_out, v_out = refs[12:18]
    g_in_new, m_in_new, v_in_new, g_out_new, m_out_new, v_out_new, in_new, out_new = refs[18:26]
    small_g_out, small_w_out, small_m_out, small_v_out, norms_out = refs[26:31]
    (
        kept_w, kept_u, sums, own_sums, slots, small_sums, small_got, small_all, small_grad, push_sends,
        push_arrivals, level_sends, level_arrivals,
    ) = refs[31:44]
    sems = refs[44:]
    ring, seq = places()
    j = pl.program_id(0)
    steps = pl.num_programs(0) // 2
    wide = heads * HEAD
    edge = wide + 2 * STATE
    levels = levels_of("fsdp")
    push = Push("fsdp", own_sums, slots, push_sends, push_arrivals)
    gather = Gather(seq, small_sums.at[levels], small_all, 8, 1, sems)

    def swap(level):
        return exchange(
            "fsdp",
            level,
            small_sums.at[level],
            small_got.at[level],
            level_sends.at[level],
            level_arrivals.at[level],
        )

    @pl.when(j == 0)
    def _():
        sums[...] = jnp.zeros_like(sums)
        small_sums[0] = jnp.zeros(small_sums.shape[1:], F32)
        small_sums[0, 0 : KERNEL + 1, :edge] = d_conv[0 : KERNEL + 1, :]
        small_sums[0, 5:6, :] = d_in_gain[...]
        small_sums[0, 6:7, :wide] = d_out_gain[0:1, :]
        for k in range(3):
            small_sums[0, 7:8, 128 * k : 128 * (k + 1)] = d_head[k : k + 1, :]
        barrier = pltpu.get_barrier_semaphore()
        count = 0
        others = [("fsdp", (ring.index + k) % push.count) for k in range(1, push.count)]
        others = others + [("seq", other) for other in seq.others()]
        for axis, other in others:
            pl.semaphore_signal(
                barrier, inc=1, device_id={axis: other}, device_id_type=pl.DeviceIdType.MESH
            )
            count = count + 1
        pl.semaphore_wait(barrier, count)
        swap(0).start()

    for level in range(levels):

        @pl.when(j == 2 * level + 2)
        def _():
            swap(level).wait()
            small_sums[level + 1] = small_sums[level] + small_got[level]
            if level + 1 < levels:
                swap(level + 1).start()
            else:
                gather.begin(0)
                gather.keep().start()

    @pl.when(j == 2 * levels + 2)
    def _():
        gather.forward(0)

    def update(gradient, w, m, v, g_new, m_new, v_new, at, keep):
        columns = gradient.shape[1]
        first, second, direction = adam_parts(gradient, m[:, :columns], v[:, :columns])
        weight = w[:, :columns]
        direction = direction + WEIGHT_DECAY * weight
        g_new[:, :columns] = gradient
        m_new[:, :columns] = first
        v_new[:, :columns] = second
        kept_w[j, :, :columns] = weight
        kept_u[j, :, :columns] = direction
        for k, value in ((at, weight * weight), (at + 1, direction * direction)):
            value = jnp.where(keep, value, 0.0) if keep is not None else value
            sums[k : k + 1, :columns] += jnp.sum(value, axis=0, keepdims=True)

    inside = (w_in, m_in, v_in, g_in_new, m_in_new, v_in_new)

    @pl.when(j < groups)
    def _():
        update(z_piece[0].astype(F32), *inside, 0, None)

    @pl.when((j >= groups) & (j < 2 * groups))
    def _():
        update(rest_piece[0].astype(F32), *inside, 0, None)

    @pl.when(j == 2 * groups)
    def _():
        states = jnp.zeros((w_in.shape[0], 2 * STATE), F32)
        lags = jnp.zeros((w_in.shape[0], DT_PAD), F32)
        for s in range(groups):
            states = states + tails[s, :, : 2 * STATE].astype(F32)
            lags = lags + dot(tails[s, :, 2 * STATE :], choose[s])
        gradient = jnp.concatenate([states, lags], axis=1)
        lane = lax.broadcasted_iota(jnp.int32, gradient.shape, 1)
        update(gradient, *inside, 0, lane < 2 * STATE + HEADS)

    @pl.when((j > 2 * groups) & (j < steps))
    def _():
        outside = (w_out, m_out, v_out, g_out_new, m_out_new, v_out_new)
        update(out_piece[0].astype(F32), *outside, 2, None)

    @pl.when(j == steps)
    def _():
        total = jnp.sum(sums[...], axis=1, keepdims=True)
        own_sums[...] = jnp.broadcast_to(total, (8, 128))
        slots[ring.index] = own_sums[...]
        push.begin()
        gather.finish()
        gather.keep().wait()
        everyone = [small_all[s] for s in range(groups)]
        shared = everyone[0]
        for other in everyone[1:]:
            shared = shared + other
        small_grad[:, :D] = shared[5:6, :]
        for k in range(KERNEL + 1):
            base = D + k * CONV
            for s in range(groups):
                small_grad[:, base + s * wide : base + (s + 1) * wide] = everyone[s][k : k + 1, :wide]
            small_grad[:, base + INNER : base + CONV] = shared[k : k + 1, wide:edge]
        size = 3 * HEADS + INNER
        size = size + -size % 128
        lane = lax.broadcasted_iota(jnp.int32, (8, size), 1)
        rest = jnp.zeros((8, size), F32)
        gap = jnp.zeros((8, size - 128), F32)
        for s in range(groups):
            for k in range(3):
                part = jnp.broadcast_to(everyone[s][7:8, 128 * k : 128 * (k + 1)], (8, 128))
                part = jnp.concatenate([part, gap], axis=1)
                part = jnp.where(lane < heads, part, 0.0)
                move = k * HEADS + s * heads
                rest = rest + (pltpu.roll(part, move, 1) if move else part)
        gains = [jnp.broadcast_to(one[6:7, :wide], (8, wide)) for one in everyone]
        gains = gains + [jnp.zeros((8, size - INNER), F32)]
        rest = rest + pltpu.roll(jnp.concatenate(gains, axis=1), 3 * HEADS, 1)
        base = D + (KERNEL + 1) * CONV
        small_grad[:, base : base + size] = rest[0:1, :]
        gradient = small_grad[...]
        first, second, direction = adam_parts(gradient, small_m[...], small_v[...])
        extent = small_g_out.shape[1]
        small_g_out[...] = gradient[:, :extent]
        small_m_out[...] = first[:, :extent]
        small_v_out[...] = second[:, :extent]
        small_w_out[...] = (small_w[...] - LEARN_RATE * direction)[:, :extent]
        push.finish()
        total = slots[0]
        for k in range(1, push.count):
            total = total + slots[k]
        sums[:, :128] = jnp.sqrt(total)
        norms_out[...] = sums[:, :128]

    def apply(at, new):
        rate = LEARN_RATE * (sums[at : at + 1, :1] / sums[at + 1 : at + 2, :1])
        new[...] = kept_w[j - steps] - rate * kept_u[j - steps]

    @pl.when((j >= steps) & (j <= steps + 2 * groups))
    def _():
        apply(0, in_new)

    @pl.when(j > steps + 2 * groups)
    def _():
        apply(2, out_new)


def run_update(groups, heads, z_all, rest_all, out_all, smalls, inside, outside):
    d_conv, d_head, d_out_gain, d_in_gain, small_w, small_m, small_v = smalls
    rows = inside[0].shape[0]
    wide = heads * HEAD
    count = lax.axis_size("fsdp")
    levels = levels_of("fsdp")
    _, seq = places()
    half = 3 * groups + 1
    steps = 2 * half
    head = jnp.arange(DT_PAD)
    choose = jnp.stack(
        [
            (head[:, None] + s * heads == head[None, :]) & (head[:, None] < heads)
            for s in range(groups)
        ]
    ).astype(BF16)
    tail = 2 * STATE + DT_PAD

    def ramp(j, start, extent):
        after = (j + steps - start) // steps
        over = (j + steps - (start + extent)) // steps
        return after * (j - start) - over * (j - start - extent + 1)

    def matrix(start, extent):
        return pl.BlockSpec((rows, wide), lambda j: (0, ramp(j, start, extent)))

    def piece(start):
        return pl.BlockSpec((1, rows, wide), lambda j: (ramp(j, start, groups), 0, 0))

    last = 2 * groups
    wholes = [choose, d_conv, d_head, d_out_gain, d_in_gain, small_w, small_m, small_v]
    shape = jax.ShapeDtypeStruct
    extent = D + (KERNEL + 1) * CONV + 3 * HEADS + INNER
    small_out = [shape((1, extent), F32)] * 4 + [shape((8, 128), F32)]
    dma = pltpu.SemaphoreType.DMA
    in_like, out_like = shape(inside[0].shape, F32), shape(outside[0].shape, F32)
    return pl.pallas_call(
        partial(update_kernel, groups, heads),
        grid=(steps,),
        in_specs=[
            piece(0),
            piece(groups),
            pl.BlockSpec((groups, rows, tail), lambda j: (0, 0, wide // tail)),
            piece(last + 1),
        ]
        + [resident(x) for x in wholes]
        + [matrix(0, last + 1)] * 3
        + [matrix(last + 1, groups)] * 3,
        out_specs=[matrix(0, last + 1)] * 3
        + [matrix(last + 1, groups)] * 3
        + [matrix(half, last + 1), matrix(half + last + 1, groups)]
        + [resident(x) for x in small_out],
        out_shape=[in_like] * 3 + [out_like] * 3 + [in_like, out_like] + small_out,
        scratch_shapes=[
            pltpu.VMEM((half, rows, wide), F32),
            pltpu.VMEM((half, rows, wide), F32),
            pltpu.VMEM((8, wide), F32),
            pltpu.VMEM((8, 128), F32),
            pltpu.VMEM((count, 8, 128), F32),
            pltpu.VMEM((levels + 1, 8, D), F32),
            pltpu.VMEM((levels, 8, D), F32),
            pltpu.VMEM((groups, 8, D), F32),
            pltpu.VMEM(small_w.shape, F32),
            dma((count - 1,)),
            dma((count - 1,)),
            dma((levels,)),
            dma((levels,)),
        ]
        + Gather.scratch(seq, 1),
        compiler_params=pltpu.CompilerParams(
            collective_id=4,
            has_side_effects=True,
            vmem_limit_bytes=VMEM_BYTES,
            dimension_semantics=("arbitrary",),
        ),
        name="update",
    )(z_all, rest_all, rest_all, out_all, *wholes, *inside, *outside)


def adam_parts(gradient, first_old, second_old):
    first_new = FIRST_DECAY * first_old + (1.0 - FIRST_DECAY) * gradient
    second_new = SECOND_DECAY * second_old + (1.0 - SECOND_DECAY) * (gradient * gradient)
    first_scale = 1.0 / (1.0 - FIRST_DECAY**STEP)
    second_scale = 1.0 / (1.0 - SECOND_DECAY**STEP)
    direction = (first_new * first_scale) / (jnp.sqrt(second_new * second_scale) + ADAM_EPSILON)
    return (first_new, second_new, direction)


def wide_row(vector):
    return jnp.pad(vector, (0, -vector.shape[0] % 128))[None, :]


def shards(
    tokens,
    cotangent,
    segments,
    in_weight,
    out_weight,
    small_params,
    in_first,
    in_second,
    out_first,
    out_second,
    small_first,
    small_second,
):
    in_gain = small_params[:D]
    groups = lax.axis_size("seq")
    where_seq = lax.axis_index("seq")
    heads = HEADS // groups
    wide = INNER // groups
    segment_row = segments[0]

    def own(vector, axis=-1):
        size = vector.shape[axis] // groups
        return lax.dynamic_slice_in_dim(vector, where_seq * size, size, axis)

    inputs = tokens[0].astype(F32)
    in_rms = lax.rsqrt(jnp.mean(inputs * inputs, axis=-1, keepdims=True) + NORM_EPS)
    dt_weight = jnp.pad(
        own(in_weight[:, INNER + CONV :]), ((0, 0), (0, DT_PAD - heads))
    ).astype(BF16)
    small = wide_row(small_params)
    spread_heads = (
        jnp.arange(128)[:, None] == jnp.arange(wide)[None, :] // HEAD
    ).astype(BF16)
    seg_pad = jnp.pad(segment_row, (EDGE, EDGE), constant_values=-1)[:, None]
    (
        pre, conv_in, dt_pre, states, d_y, d_z, normed_t, out_part, z_part, branch_part, d_out_gain,
        conv_pack, head_pack, chan_pack, w_in,
    ) = run_forward(
        heads, tokens[0], cotangent[0], small, dt_weight, seg_pad, segments, spread_heads,
        in_weight, out_weight,
    )
    packs = (conv_pack, head_pack, chan_pack)
    out_all, z_all, rest_all, branch, d_normed, d_conv, d_head = run_backward(
        heads, d_y, pre, conv_in, dt_pre, states, seg_pad, segments, packs, spread_heads, d_z,
        w_in, normed_t, out_part, z_part, branch_part,
    )
    output = (inputs + branch.astype(F32)).astype(BF16)[None]
    d_normed = d_normed.astype(F32)
    slope = d_normed * in_gain[None, :]
    d_inputs = slope * in_rms - inputs * (in_rms**3 / D) * jnp.sum(
        slope * inputs, axis=1, keepdims=True
    )
    input_grad = (cotangent[0].astype(F32) + d_inputs)[None]
    d_in_gain = jnp.sum(d_normed * inputs * in_rms, axis=0, keepdims=True)

    (
        in_grad, in_first_new, in_second_new, out_grad, out_first_new, out_second_new, in_new, out_new,
        small_grad, small_new, small_first_new, small_second_new, norms,
    ) = run_update(
        groups, heads, z_all, rest_all, out_all,
        (d_conv, d_head, d_out_gain, d_in_gain, small, wide_row(small_first), wide_row(small_second)),
        (in_weight, in_first, in_second), (out_weight, out_first, out_second),
    )
    small_grad, small_new, small_first_new, small_second_new = [
        x[0] for x in (small_grad, small_new, small_first_new, small_second_new)
    ]
    norms = norms[:4, 0]
    return (
        output,
        input_grad,
        in_grad,
        in_new,
        in_first_new,
        in_second_new,
        out_grad,
        out_new,
        out_first_new,
        out_second_new,
        small_grad,
        small_new,
        small_first_new,
        small_second_new,
        norms,
    )


def solution(mesh):
    matrix = P("fsdp", None)
    rows = P("fsdp", "seq", None)
    return jax.shard_map(
        shards,
        mesh=mesh,
        in_specs=(rows, rows, matrix, matrix, matrix, P(), matrix, matrix, matrix, matrix, P(), P()),
        out_specs=(rows, rows) + (matrix,) * 8 + (P(),) * 5,
        check_vma=False,
    )
```

```python
from functools import partial

import jax
import jax.numpy as jnp
from jax import lax
from jax.experimental import pallas as pl
from jax.experimental.pallas import tpu as pltpu
from jax.sharding import PartitionSpec as P

D = 1536
HEADS = 48
HEAD = 64
STATE = 128
KERNEL = 4
STRETCH = 256
STEP = 5
INNER = 3072
CONV = 3328
PROJ = 6448
DT_PAD = 128
SHARED = 2 * STATE + DT_PAD

NORM_EPS = 1e-05
FIRST_DECAY = 0.9
SECOND_DECAY = 0.999
ADAM_EPSILON = 1e-06
WEIGHT_DECAY = 0.01
LEARN_RATE = 0.5
F32 = jnp.float32
BF16 = jnp.bfloat16


def dot(a, b, dims=((1,), (0,))):
    return lax.dot_general(a, b, (dims, ((), ())), preferred_element_type=F32)


def split_dot(value, ones):
    high = value.astype(BF16)
    low = (value - high.astype(F32)).astype(BF16)
    return dot(high, ones) + dot(low, ones)


def tri_dot(ones, value):
    high = value.astype(BF16)
    rest = value - high.astype(F32)
    middle = rest.astype(BF16)
    low = (rest - middle.astype(F32)).astype(BF16)
    return dot(ones, high) + dot(ones, middle) + dot(ones, low)


def sigmoid(v):
    return 1.0 / (1.0 + jnp.exp(-v))


def softplus(v):
    return jnp.maximum(v, 0.0) + jnp.log1p(jnp.exp(-jnp.abs(v)))


def row_at_least():
    rows = lax.broadcasted_iota(jnp.int32, (STRETCH, STRETCH), 0)
    columns = lax.broadcasted_iota(jnp.int32, (STRETCH, STRETCH), 1)
    return rows >= columns


class Decays:
    def __init__(self, dt, rate, masks, spread):
        self.dt, self.spread = dt, spread
        lower = jnp.where(row_at_least(), 1.0, 0.0).astype(BF16)
        self.columns = dot(lower, dt) * rate
        self.rows = jnp.transpose(self.columns)
        last = self.columns[STRETCH - 1 :, :]
        self.into = jnp.exp(self.columns) * masks["carry"]
        self.out = jnp.exp(last - self.columns) * masks["tail"]
        self.through = jnp.broadcast_to(jnp.exp(last) * masks["keep"], (8, 128))
        self.bar = masks["bar"]

    def of(self, columns):
        ones = self.spread[:, columns]
        return (
            dot(self.dt, ones),
            split_dot(self.into, ones),
            split_dot(self.out, ones),
            split_dot(self.through, ones)[:1],
        )

    def between(self, head):
        return jnp.exp(self.columns[:, head : head + 1] - self.rows[head : head + 1, :] + self.bar)


EDGE = 8


def block_masks(seg_pad, seg_row, at):
    def rows(by, size=STRETCH):
        return seg_pad[pl.ds(at + EDGE + by, size), :]

    here = rows(0)
    first = jnp.where(at == 0, rows(0, 1), rows(-1, 1))
    last = rows(STRETCH - 1, 1)
    masks = {"carry": here == first, "tail": here == last, "keep": last == first}
    for by in range(1, KERNEL):
        masks[-by] = here == rows(-by)
        masks[by] = here == rows(by)
    masks = {key: jnp.where(value, 1.0, 0.0) for key, value in masks.items()}
    within = row_at_least() & (here == seg_row[:, pl.ds(at, STRETCH)])
    masks["bar"] = jnp.where(within, 0.0, -1e30)
    return masks


def forward_block(
    heads, at, normed, w_x, shared_columns, masks, packs, spread, outs, y_all, extended, state
):
    conv_pack, head_pack, chan_pack = packs
    pre_out, conv_out, dt_out, states_out = outs
    wide = heads * HEAD
    here = pl.ds(at, STRETCH)
    conv_low = jnp.concatenate([dot(normed, w_x[...]), dot(normed, shared_columns(0, 2 * STATE))], axis=1)
    conv_low = conv_low.astype(BF16)
    conv_out[...] = conv_low
    conv_in = conv_low.astype(F32)
    extended[8 : 8 + STRETCH, :] = conv_in
    pre = conv_pack[4:5, :] + conv_pack[3:4, :] * conv_in
    for by in range(1, KERNEL):
        pre = pre + conv_pack[3 - by : 4 - by, :] * (
            extended[8 - by : 8 - by + STRETCH, :] * masks[-by]
        )
    extended[0:8, :] = extended[STRETCH : STRETCH + 8, :]
    pre_out[...] = pre
    act = (pre * sigmoid(pre)).astype(BF16)
    b_mat = act[:, wide : wide + STATE]
    c_mat = act[:, wide + STATE :]
    lane = lax.broadcasted_iota(jnp.int32, (STRETCH, DT_PAD), 1)
    dt_pre = pltpu.roll(
        dot(normed, shared_columns(2 * STATE, DT_PAD)), DT_PAD - lax.axis_index("seq") * heads, 1
    )
    dt_pre = jnp.where(lane < heads, dt_pre, 0.0) + head_pack[0:1, :]
    dt_out[...] = dt_pre
    dt = softplus(dt_pre).astype(BF16)
    decay = Decays(dt, head_pack[1:2, :], masks, spread)
    scores = dot(c_mat, b_mat, ((1,), (1,)))
    first_half = lax.broadcasted_iota(jnp.int32, (STRETCH, 2 * HEAD), 1) < HEAD
    for pair in range(heads // 2):
        columns = slice(pair * 2 * HEAD, (pair + 1) * 2 * HEAD)
        steps, carry, tail, keep = decay.of(columns)
        xs = act[:, columns].astype(F32)
        scaled = xs * steps
        scaled_low = scaled.astype(BF16)
        old = state[:, columns]
        states_out[0, :, columns] = old
        y = dot(c_mat, old.astype(BF16)) * carry + chan_pack[0:1, columns] * xs
        state[:, columns] = old * keep + dot(b_mat, (scaled * tail).astype(BF16), ((0,), (0,)))
        halves = [
            dot((scores * decay.between(h)).astype(BF16), scaled_low)
            for h in (2 * pair, 2 * pair + 1)
        ]
        y_all[here, columns] = (y + jnp.where(first_half, halves[0], halves[1])).astype(BF16)


def fill_packs(heads, small, spread, packs, scratch_gain):
    conv_pack, head_pack, chan_pack = packs
    wide = heads * HEAD
    index = lax.axis_index("seq")
    start = pl.multiple_of(index * wide, 128)
    for ref in packs:
        ref[...] = jnp.zeros_like(ref)
    for k in range(KERNEL + 1):
        base = D + k * CONV
        conv_pack[k : k + 1, :wide] = small[:, pl.ds(base + start, wide)]
        conv_pack[k : k + 1, wide:] = small[:, base + INNER : base + CONV]
    base = D + (KERNEL + 1) * CONV
    window = jnp.broadcast_to(small[:, base : base + 256], (8, 256))
    lane = lax.broadcasted_iota(jnp.int32, (8, 256), 1)

    def own(k):
        moved = pltpu.roll(window, 256 - (k * HEADS + index * heads), 1)
        return jnp.where(lane < heads, moved, 0.0)[:, :128]

    head_pack[0:1, :] = own(0)[:1]
    rate = own(1)
    rate = jnp.where(lax.broadcasted_iota(jnp.int32, (8, 128), 1) < heads, -jnp.exp(rate), 0.0)
    head_pack[1:2, :] = rate[:1]
    chan_pack[0:1, :] = tri_spread(own(2), spread)[:1]
    base = base + 3 * HEADS
    shift = base % 128
    gain = jnp.broadcast_to(small[:, base - shift : base - shift + INNER + 128], (8, INNER + 128))
    scratch_gain[...] = pltpu.roll(gain, INNER + 128 - shift, 1)
    chan_pack[1:2, :] = scratch_gain[0:1, pl.ds(start, wide)]


def tri_spread(value, ones):
    high = value.astype(BF16)
    rest = value - high.astype(F32)
    middle = rest.astype(BF16)
    low = (rest - middle.astype(F32)).astype(BF16)
    return dot(high, ones) + dot(middle, ones) + dot(low, ones)


def gate_sums(y, z, d_mixed, gain):
    gated = y.astype(F32) * (z * sigmoid(z))
    squares = jnp.sum(gated * gated, axis=1, keepdims=True)
    products = jnp.sum(d_mixed * gain * gated, axis=1, keepdims=True)
    lane = lax.broadcasted_iota(jnp.int32, (STRETCH, 128), 1)
    both = jnp.where(lane == 0, squares, jnp.where(lane == 1, products, 0.0))
    return jnp.transpose(both)[0:8, :]


def gate_gradients(y_low, z, d_mixed, gain, sums):
    columns = jnp.transpose(jnp.concatenate([sums, jnp.zeros((120, STRETCH), F32)], axis=0))
    rms = lax.rsqrt(columns[:, 0:1] / INNER + NORM_EPS)
    y = y_low.astype(F32)
    sig = sigmoid(z)
    silu = z * sig
    gated = y * silu
    unit = gated * rms
    d_gain = jnp.sum(d_mixed * unit, axis=0, keepdims=True)
    d_gated = d_mixed * gain * rms - unit * (rms * rms / INNER * columns[:, 1:2])
    d_z = d_gated * y * (sig * (1.0 + z * (1.0 - sig)))
    return (unit * gain).astype(BF16), (d_gated * silu).astype(BF16), d_z.astype(BF16), d_gain


def halved(rows, groups):
    return rows % (16 * groups) == 0


def forward_kernel(heads, *refs):
    tokens, cotangent, small, dt_weight, seg_pad, seg_row, spread_ref, in_weight, out_weight = refs[:9]
    outs = refs[9:13]
    d_y, d_z, normed_t, out_part, z_part, d_gain = refs[13:19]
    packs = refs[19:22]
    w_x_out, w_z_out, w_s_out, branch_part = refs[22:26]
    (
        stage_s, own_x, own_z, own_o, own_s, own_rows, w_x, w_z, w_o, w_s,
        shared_own, branch_stage, rows_all, returned_t, z_all, y_all, d_mixed_all, extended, state,
        scratch_gain, sums, got, stage_sems, sum_sends, sum_arrivals,
    ) = refs[26:51]
    sems = refs[51:]
    ring, seq = places()
    wide = heads * HEAD
    edge = wide + 2 * STATE
    step = pl.program_id(0)
    blocks = pl.num_programs(0) - 1
    length = rows_all.shape[0]
    count = length // STRETCH
    rows = own_x.shape[0]
    split = halved(rows, seq.major * seq.minor)
    stage_x, stage_z, stage_o = [d_mixed_all.at[pl.ds(k * rows, rows)] for k in range(3)]

    def shared_columns(start, size):
        if split:
            return w_s[:, :, :, start : start + size].reshape(D, size)
        return w_s[:, start : start + size]

    get_x = Gather(ring, own_x, w_x, rows, WEIGHT_PIECES, sems[:5])
    get_z = Gather(ring, own_z, w_z, rows, 1, sems[5:10])
    get_o = Gather(ring, own_o, w_o, rows, 1, sems[10:15])
    get_rows = Gather(seq, own_rows, rows_all, own_rows.shape[0], TOKEN_PIECES, sems[15:20])
    if split:
        get_s = Gather(ring, own_s, shared_own, own_s.shape[0], 1, sems[20:25])
        pass_s = Gather(
            seq, shared_own, w_s, shared_own.shape[0], 1, sems[25:30],
            lambda slot, piece: w_s.at[:, slot],
        )
    else:
        get_s = Gather(ring, own_s, w_s, rows, 1, sems[20:25])
    saves = [
        pltpu.make_async_copy(source, target, stage_sems.at[4 + k])
        for k, (source, target) in enumerate(((w_x, w_x_out), (w_z, w_z_out), (w_s, w_s_out)))
    ]
    spread = spread_ref[...]
    at = pl.multiple_of(step * STRETCH, STRETCH)

    @pl.when(step == 0)
    def _():
        start = pl.multiple_of(seq.index * wide, 128)
        own_shared = own_s.shape[0]
        first_row = pl.multiple_of(seq.index * own_shared, 16) if split else 0
        sources = [
            (in_weight.at[pl.ds(first_row, own_shared), pl.ds(2 * INNER, 2 * STATE)], stage_s),
            (in_weight.at[:, pl.ds(INNER + start, wide)], stage_x),
            (in_weight.at[:, pl.ds(start, wide)], stage_z),
            (out_weight.at[:, pl.ds(start, wide)], stage_o),
        ]
        loads = [
            pltpu.make_async_copy(source, target, stage_sems.at[k])
            for k, (source, target) in enumerate(sources)
        ]
        for load in loads:
            load.start()
        meet(ring, seq)
        loads[0].wait()
        own_s[:, : 2 * STATE] = stage_s[...].astype(BF16)
        own_s[:, 2 * STATE :] = dt_weight[pl.ds(first_row, own_shared), :]
        get_s.begin(0)
        get_s.keep().start()
        loads[1].wait()
        own_x[...] = stage_x[...].astype(BF16)
        for piece in range(WEIGHT_PIECES):
            get_x.begin(piece)
        get_x.keep().start()
        inputs = tokens[...].astype(F32)
        rms = lax.rsqrt(jnp.mean(inputs * inputs, axis=-1, keepdims=True) + NORM_EPS)
        own_rows[:, :D] = (inputs * rms * small[:, :D]).astype(BF16)
        own_rows[:, D:] = cotangent[...]
        for piece in range(TOKEN_PIECES):
            get_rows.begin(piece)
        get_rows.keep().start()
        loads[2].wait()
        loads[3].wait()
        own_z[...] = stage_z[...].astype(BF16)
        own_o[...] = stage_o[...].astype(BF16)
        get_z.keep().start()
        get_o.keep().start()
        fill_packs(heads, small, spread, packs, scratch_gain)
        state[...] = jnp.zeros_like(state)
        extended[0:8, :] = jnp.zeros((8, edge), F32)
        d_gain[...] = jnp.zeros_like(d_gain)
        get_s.forward(0)
        get_rows.forward(0)
        get_x.forward(0)
        get_s.finish()
        get_s.keep().wait()
        if split:
            pass_s.begin(0)
            pass_s.keep().start()
        get_rows.forward(1)
        get_x.forward(1)
        get_z.begin(0)
        get_rows.forward(2)
        get_x.forward(2)
        get_o.begin(0)
        for piece in range(3, TOKEN_PIECES):
            get_rows.forward(piece)
        if split:
            pass_s.forward(0)
        get_rows.finish()
        get_rows.keep().wait()

        def turn(k, _):
            here = pl.ds(pl.multiple_of(k * STRETCH, STRETCH), STRETCH)
            normed_t[:, here] = jnp.transpose(rows_all[here, :D])
            returned_t[:, here] = jnp.transpose(rows_all[here, D:])
            return 0

        lax.fori_loop(0, count, turn, 0)
        if split:
            pass_s.finish()
            pass_s.keep().wait()
        get_x.finish()
        get_x.keep().wait()
        saves[0].start()
        saves[2].start()

    @pl.when(step < blocks)
    def _():
        masks = block_masks(seg_pad, seg_row, at)
        forward_block(
            heads, at, rows_all[pl.ds(at, STRETCH), :D], w_x, shared_columns, masks, packs, spread, outs,
            y_all, extended, state,
        )

    forwards = [(stream, k) for stream in (get_z, get_o) for k in range(1, ring.major)]
    ahead = min(count, len(forwards))
    for k in range(ahead):

        @pl.when(step == k)
        def _():
            stream, by = forwards[k]
            stream.forward_step(0, by)

    @pl.when(step == blocks)
    def _():
        for stream, by in forwards[ahead:]:
            stream.forward_step(0, by)
        get_z.finish()
        get_z.keep().wait()
        saves[1].start()

        def gate(k, _):
            here = pl.ds(pl.multiple_of(k * STRETCH, STRETCH), STRETCH)
            z_all[here, :] = dot(rows_all[here, :D], w_z[...])
            return 0

        lax.fori_loop(0, count, gate, 0)
        get_o.finish()
        get_o.keep().wait()
        gain = packs[2][1:2, :]

        def measure(k, _):
            here = pl.ds(pl.multiple_of(k * STRETCH, STRETCH), STRETCH)
            d_mixed = dot(rows_all[here, D:], w_o[...])
            d_mixed_all[here, :] = d_mixed
            sums[0, :, here] = gate_sums(y_all[here, :], z_all[here, :], d_mixed, gain)
            return 0

        lax.fori_loop(0, count, measure, 0)
        for level in range(levels_of("seq")):
            copy = exchange(
                "seq", level, sums.at[level], got.at[level], sum_sends.at[level], sum_arrivals.at[level]
            )
            copy.start()
            copy.wait()
            sums[level + 1] = sums[level] + got[level]
        total = levels_of("seq")

        def differentiate(k, _):
            here = pl.ds(pl.multiple_of(k * STRETCH, STRETCH), STRETCH)
            mixed, d_y_block, d_z_block, d_gain_block = gate_gradients(
                y_all[here, :], z_all[here, :], d_mixed_all[here, :], gain, sums[total, :, here]
            )
            y_all[here, :] = mixed
            d_y[here, :] = d_y_block
            d_z[here, :] = d_z_block
            d_gain[0:1, :] += d_gain_block
            branch_stage[...] = dot(mixed, w_o[...], ((1,), (1,))).astype(BF16)
            out = pltpu.make_async_copy(branch_stage, branch_part.at[here], stage_sems.at[7])
            out.start()
            out.wait()
            return 0

        lax.fori_loop(0, count, differentiate, 0)

        def contract(k, _):
            here = pl.ds(pl.multiple_of(k * 256, 256), 256)
            out_part[here, :] = dot(returned_t[here, :], y_all[...]).astype(BF16)
            z_part[here, :] = dot(normed_t[here, :], d_z[...]).astype(BF16)
            return 0

        lax.fori_loop(0, D // 256, contract, 0)
        for save in saves:
            save.wait()


def backward_block(
    heads,
    d_y_ref,
    pre_ref,
    conv_ref,
    dt_ref,
    states,
    seg_pad,
    seg_row,
    conv_pack,
    head_pack,
    chan_pack,
    spread_ref,
    gather_ref,
    d_conv_out,
    d_head_out,
    extended,
    d_state,
    d_rest,
):
    wide = heads * HEAD
    edge = wide + 2 * STATE

    @pl.when(pl.program_id(0) == 0)
    def _():
        d_state[...] = jnp.zeros_like(d_state)
        extended[STRETCH : STRETCH + 8, :] = jnp.zeros((8, edge), F32)
        d_conv_out[...] = jnp.zeros_like(d_conv_out)
        d_head_out[...] = jnp.zeros_like(d_head_out)

    at_row = pl.multiple_of((pl.num_programs(0) - 1 - pl.program_id(0)) * STRETCH, STRETCH)
    masks = block_masks(seg_pad, seg_row, at_row)
    spread = spread_ref[...]
    gather = gather_ref[...]
    pre = pre_ref[...]
    act = (pre * sigmoid(pre)).astype(BF16)
    b_mat = act[:, wide : wide + STATE]
    c_mat = act[:, wide + STATE :]
    dt_pre = dt_ref[...]
    dt = softplus(dt_pre).astype(BF16)
    rate = head_pack[1:2, :]
    decay = Decays(dt, rate, masks, spread)
    scores = dot(c_mat, b_mat, ((1,), (1,)))
    lane = lax.broadcasted_iota(jnp.int32, (STRETCH, 128), 1)
    first_half = lane < HEAD
    d_b = jnp.zeros((STRETCH, STATE), F32)
    d_c = jnp.zeros((STRETCH, STATE), F32)
    d_scores = jnp.zeros((STRETCH, STRETCH), F32)
    d_cum = jnp.zeros((STRETCH, 128), F32)
    d_dt = jnp.zeros((STRETCH, 128), F32)
    d_last = jnp.zeros((1, 128), F32)
    column_sums = []
    for pair in range(heads // 2):
        columns = slice(pair * 2 * HEAD, (pair + 1) * 2 * HEAD)
        ones = gather[columns, :]
        steps, carry, tail, keep = decay.of(columns)
        xs = act[:, columns].astype(F32)
        scaled = xs * steps
        scaled_low = scaled.astype(BF16)
        old = states[0, :, columns]
        old_low = old.astype(BF16)
        d_new = d_state[:, columns]
        d_new_low = d_new.astype(BF16)
        d_y_low = d_y_ref[:, columns]
        d_y = d_y_low.astype(F32)
        d_carried = d_y * carry
        d_carried_low = d_carried.astype(BF16)
        d_c = d_c + dot(d_carried_low, old_low, ((1,), (1,)))
        d_cum = d_cum + split_dot(d_carried * dot(c_mat, old_low), ones)
        weighed = scaled * tail
        into = dot(b_mat, d_new_low)
        d_b = d_b + dot(weighed.astype(BF16), d_new_low, ((1,), (1,)))
        tail_part = split_dot(weighed * into, ones)
        d_cum = d_cum - tail_part
        kept = jnp.sum(d_new * old, axis=0, keepdims=True) * keep
        kept = split_dot(jnp.broadcast_to(kept, (8, 128)), ones)[:1]
        d_last = d_last + jnp.sum(tail_part, axis=0, keepdims=True) + kept
        d_state[:, columns] = d_new * keep + dot(c_mat, d_carried_low, ((0,), (0,)))
        halves = []
        for h in (2 * pair, 2 * pair + 1):
            between = decay.between(h)
            weights = scores * between
            halves.append(dot(weights.astype(BF16), d_y_low, ((0,), (0,))))
            d_y_head = jnp.where(first_half == (h % 2 == 0), d_y_low, jnp.zeros_like(d_y_low))
            d_weights = dot(d_y_head, scaled_low, ((1,), (1,)))
            d_scores = d_scores + d_weights * between
            product = d_weights * weights
            d_cum = d_cum + jnp.where(lane == h, jnp.sum(product, axis=1, keepdims=True), 0.0)
            column_sums.append(jnp.sum(product, axis=0, keepdims=True))
        d_scaled = into * tail + jnp.where(first_half, halves[0], halves[1])
        d_xs = d_scaled * steps + chan_pack[0:1, columns] * d_y
        extended[0:STRETCH, columns] = d_xs.astype(BF16).astype(F32)
        d_dt = d_dt + split_dot(d_scaled * xs, ones)
        d_skip = jnp.sum(d_y * xs, axis=0, keepdims=True)
        d_head_out[2:3, :] += split_dot(jnp.broadcast_to(d_skip, (8, 128)), ones)[:1]
    column_sums.append(jnp.zeros((128 - heads, STRETCH), F32))
    d_cum = d_cum - jnp.transpose(jnp.concatenate(column_sums, axis=0))
    row = lax.broadcasted_iota(jnp.int32, (STRETCH, 128), 0)
    d_cum = d_cum + jnp.where(row == STRETCH - 1, d_last, 0.0)
    d_scores_low = d_scores.astype(BF16)
    d_c = d_c + dot(d_scores_low, b_mat)
    d_b = d_b + dot(d_scores_low, c_mat, ((0,), (0,)))

    rows = lax.broadcasted_iota(jnp.int32, (STRETCH, STRETCH), 0)
    upper = jnp.where(rows <= lax.broadcasted_iota(jnp.int32, (STRETCH, STRETCH), 1), 1.0, 0.0)
    d_dt = d_dt + rate * tri_dot(upper.astype(BF16), d_cum)
    d_dt_raw = d_dt.astype(BF16).astype(F32) * sigmoid(dt_pre)
    d_head_out[0:1, :] += jnp.sum(d_dt_raw, axis=0, keepdims=True)
    d_head_out[1:2, :] += jnp.sum(d_cum * decay.columns, axis=0, keepdims=True)

    extended[0:STRETCH, wide : wide + STATE] = d_b
    extended[0:STRETCH, wide + STATE :] = d_c
    here = pl.ds(at_row, STRETCH)
    moved = pltpu.roll(jnp.where(lane < heads, d_dt_raw, 0.0), lax.axis_index("seq") * heads, 1)
    d_rest[here, edge:] = moved.astype(BF16)

    def convolve_back(at, _):
        columns = pl.ds(pl.multiple_of(at * 128, 128), 128)
        value = pre_ref[:, columns]
        gate = sigmoid(value)
        d_pre = extended[0:STRETCH, columns] * (gate * (1.0 + value * (1.0 - gate)))
        extended[0:STRETCH, columns] = d_pre
        conv_in = conv_ref[:, columns].astype(F32)
        d_conv_in = conv_pack[3:4, columns] * d_pre
        d_conv_out[3:4, columns] += jnp.sum(d_pre * conv_in, axis=0, keepdims=True)
        d_conv_out[4:5, columns] += jnp.sum(d_pre, axis=0, keepdims=True)
        for by in range(1, KERNEL):
            moved = extended[by : by + STRETCH, columns] * masks[by]
            d_conv_in = d_conv_in + conv_pack[3 - by : 4 - by, columns] * moved
            d_conv_out[3 - by : 4 - by, columns] += jnp.sum(moved * conv_in, axis=0, keepdims=True)
        extended[STRETCH : STRETCH + 8, columns] = extended[0:8, columns]
        d_rest[here, columns] = d_conv_in.astype(BF16)
        return 0

    lax.fori_loop(0, edge // 128, convolve_back, 0)


VMEM_BYTES = 56 * 1024 * 1024


def block(columns, reverse=0):
    if reverse:
        return pl.BlockSpec((STRETCH, columns), lambda i: (reverse - 1 - i, 0))
    return pl.BlockSpec((STRETCH, columns), lambda i: (i, 0))


def whole(*shape):
    return pl.BlockSpec(shape, lambda i: (0,) * len(shape))


def compiler_params():
    return pltpu.CompilerParams(
        vmem_limit_bytes=VMEM_BYTES, dimension_semantics=("arbitrary",)
    )


class Place:
    def __init__(self, axis, minor):
        self.axis = axis
        self.minor = minor
        self.major = lax.axis_size(axis) // minor
        index = lax.axis_index(axis)
        self.at_major = index // minor
        self.at_minor = index % minor
        self.index = index

    def slot(self, by_major, by_minor):
        return (self.at_major + by_major) % self.major * self.minor + (
            self.at_minor + by_minor
        ) % self.minor

    def others(self):
        along = [self.slot(step, 0) for step in range(1, self.major)]
        return along + [self.slot(0, step) for step in range(1, self.minor)]


def places():
    ring = lax.axis_size("fsdp")
    side = 1
    while 2 * side * 2 * side * 2 <= ring:
        side = 2 * side
    return Place("fsdp", side), Place("seq", 2)


def meet(*all_places):
    barrier = pltpu.get_barrier_semaphore()
    count = 0
    for place in all_places:
        for other in place.others():
            pl.semaphore_signal(
                barrier, inc=1, device_id={place.axis: other}, device_id_type=pl.DeviceIdType.MESH
            )
            count = count + 1
    pl.semaphore_wait(barrier, count)


def send(place, source, target, to, sends, arrivals, at):
    return pltpu.make_async_remote_copy(
        src_ref=source,
        dst_ref=target,
        send_sem=sends.at[at],
        recv_sem=arrivals.at[at],
        device_id={place.axis: to},
        device_id_type=pl.DeviceIdType.MESH,
    )


class Gather:
    def __init__(self, place, own, full, rows, pieces, sems, target=None):
        self.place, self.own, self.full, self.landing = place, own, full, target
        self.size, self.pieces = rows // pieces, pieces
        self.sends1, self.arrivals1, self.sends2, self.arrivals2, self.here = sems

    @staticmethod
    def scratch(place, pieces):
        first = max(place.major - 1, 1) * pieces
        second = place.major * (place.minor - 1) * pieces
        dma = pltpu.SemaphoreType.DMA
        return [dma((first,)), dma((first,)), dma((second,)), dma((second,)), dma((1,))]

    def rows(self, piece):
        return pl.ds(piece * self.size, self.size)

    def target(self, slot, piece):
        if self.landing is not None:
            return self.landing(slot, piece)
        if len(self.full.shape) > len(self.own.shape):
            return self.full.at[slot, self.rows(piece)]
        start = slot * (self.size * self.pieces) + piece * self.size
        return self.full.at[pl.ds(pl.multiple_of(start, 16), self.size)]

    def along(self, piece, step):
        place = self.place
        return send(
            place,
            self.own.at[self.rows(piece)],
            self.target(place.index, piece),
            place.slot(step, 0),
            self.sends1,
            self.arrivals1,
            piece * (place.major - 1) + step - 1,
        )

    def across(self, piece, step, across):
        place = self.place
        slot = place.slot(-step, 0)
        target = self.target(slot, piece)
        source = self.own.at[self.rows(piece)] if step == 0 else target
        at = (piece * place.major + step) * (place.minor - 1) + across - 1
        return send(
            place, source, target, place.slot(0, across), self.sends2, self.arrivals2, at
        )

    def keep(self):
        if self.landing is not None:
            target = self.landing(self.place.index, 0)
        elif len(self.full.shape) > len(self.own.shape):
            target = self.full.at[self.place.index]
        else:
            size = self.size * self.pieces
            target = self.full.at[pl.ds(pl.multiple_of(self.place.index * size, 16), size)]
        return pltpu.make_async_copy(self.own, target, self.here.at[0])

    def begin(self, piece):
        for step in range(1, self.place.major):
            self.along(piece, step).start()
        for across in range(1, self.place.minor):
            self.across(piece, 0, across).start()

    def forward(self, piece):
        for step in range(1, self.place.major):
            self.forward_step(piece, step)

    def forward_step(self, piece, step):
        self.along(piece, step).wait_recv()
        for across in range(1, self.place.minor):
            self.across(piece, step, across).start()

    def finish(self):
        for piece in range(self.pieces):
            for step in range(1, self.place.major):
                self.along(piece, step).wait_send()
            for step in range(self.place.major):
                for across in range(1, self.place.minor):
                    self.across(piece, step, across).wait()


class Reduce:
    def __init__(self, place, part, total, rows, pieces, scratch, loads=None):
        self.place, self.part, self.total, self.loads = place, part, total, loads
        self.size, self.pieces = rows // pieces, pieces
        self.got1, self.mine, self.got2, self.sends1, self.arrivals1, self.sends2, self.arrivals2 = (
            scratch
        )

    @staticmethod
    def scratch(place, rows, columns, pieces):
        dma = pltpu.SemaphoreType.DMA
        first = place.major * (place.minor - 1)
        second = max(place.major - 1, 1)
        return [
            pltpu.VMEM((first, rows, columns), BF16),
            pltpu.VMEM((second, rows, columns), BF16),
            pltpu.VMEM((second, rows, columns), BF16),
            dma((first * pieces,)),
            dma((first * pieces,)),
            dma((second * pieces,)),
            dma((second * pieces,)),
        ]

    def items(self):
        return [(piece, step) for step in self.steps() for piece in range(self.pieces)]

    def steps(self):
        return list(range(1, self.place.major)) + [0]

    def rows(self, piece):
        return pl.ds(piece * self.size, self.size)

    def part_rows(self, slot, rows_start, size):
        if len(self.part.shape) == 3:
            return slot, pl.ds(rows_start, size)
        start = slot * (self.size * self.pieces) + rows_start
        return (pl.ds(pl.multiple_of(start, 16), size),)

    def across(self, item, across):
        piece, step = item
        place = self.place
        slot = step * (place.minor - 1) + across - 1
        index = self.part_rows(place.slot(step, across), piece * self.size, self.size)
        return send(
            place,
            self.part.at[index],
            self.got1.at[slot, self.rows(piece)],
            place.slot(0, across),
            self.sends1,
            self.arrivals1,
            slot * self.pieces + piece,
        )

    def along(self, item):
        piece, step = item
        place = self.place
        return send(
            place,
            self.mine.at[step - 1, self.rows(piece)],
            self.got2.at[step - 1, self.rows(piece)],
            place.slot(step, 0),
            self.sends2,
            self.arrivals2,
            (step - 1) * self.pieces + piece,
        )

    def begin(self, item):
        for across in range(1, self.place.minor):
            self.across(item, across).start()
        if self.loads is not None:
            self.load(item[1]).start()

    def load(self, step):
        target = self.mine.at[step - 1] if step else self.total
        return pltpu.make_async_copy(
            self.part.at[self.place.slot(step, 0)], target, self.loads.at[step]
        )

    def own(self, step, rows):
        if self.loads is None:
            return self.part[self.part_rows(self.place.slot(step, 0), rows, 16)].astype(F32)
        source = self.mine.at[step - 1] if step else self.total
        return source[pl.ds(rows, 16)].astype(F32)

    def blocks(self, piece, body):
        def one(at, _):
            body(pl.multiple_of(piece * self.size + at * 16, 16))
            return 0

        lax.fori_loop(0, self.size // 16, one, 0)

    def handle(self, item):
        piece, step = item
        place = self.place
        for across in range(1, place.minor):
            self.across(item, across).wait_recv()
        if self.loads is not None:
            self.load(step).wait()
        if step == 0:
            return

        def body(start):
            value = self.own(step, start)
            rows = pl.ds(start, 16)
            for across in range(1, place.minor):
                slot = step * (place.minor - 1) + across - 1
                value = value + self.got1[slot, rows].astype(F32)
            self.mine[step - 1, rows] = value.astype(BF16)

        self.blocks(piece, body)
        self.along(item).start()

    def close(self, piece):
        place = self.place
        for step in range(1, place.major):
            self.along((piece, step)).wait_recv()

        def body(start):
            value = self.own(0, start)
            rows = pl.ds(start, 16)
            for across in range(1, place.minor):
                value = value + self.got1[across - 1, rows].astype(F32)
            for step in range(1, place.major):
                value = value + self.got2[step - 1, rows].astype(F32)
            self.total[rows] = value.astype(self.total.dtype)

        self.blocks(piece, body)

    def finish(self):
        for item in self.items():
            for across in range(1, self.place.minor):
                self.across(item, across).wait_send()
            if item[1]:
                self.along(item).wait_send()


WEIGHT_PIECES = 3
TOKEN_PIECES = 4
HBM = pl.BlockSpec(memory_space=pl.ANY)
VMEM = pl.BlockSpec(memory_space=pltpu.VMEM)


def comm_params(number):
    return pltpu.CompilerParams(
        collective_id=number, has_side_effects=True, vmem_limit_bytes=VMEM_BYTES
    )


def resident(x):
    return pl.BlockSpec(
        x.shape, lambda i: (0,) * len(x.shape), pipeline_mode=pl.Buffered(buffer_count=1)
    )


def run_forward(heads, tokens, cotangent, small, dt_weight, seg_pad, seg_row, spread, in_weight, out_weight):
    ring, seq = places()
    count, groups = lax.axis_size("fsdp"), lax.axis_size("seq")
    rows, own_rows = in_weight.shape[0], tokens.shape[0]
    length = own_rows * groups
    blocks = length // STRETCH
    wide = heads * HEAD
    edge = wide + 2 * STATE
    levels = levels_of("seq")
    shape = jax.ShapeDtypeStruct
    split = halved(rows, groups)
    own_shared = rows // groups if split else rows
    shared_shape = (count, groups, own_shared, SHARED) if split else (D, SHARED)

    def chunk(columns):
        return pl.BlockSpec((STRETCH, columns), lambda i: (i - i // blocks, 0))

    wholes = [tokens, cotangent, small, dt_weight, seg_pad, seg_row, spread]
    late = [
        shape((length, wide), BF16),
        shape((length, wide), BF16),
        shape((D, length), BF16),
        shape((D, wide), BF16),
        shape((D, wide), BF16),
        shape((8, wide), F32),
        shape((8, edge), F32),
        shape((8, 128), F32),
        shape((8, wide), F32),
    ]
    dma = pltpu.SemaphoreType.DMA
    scratch = [
        pltpu.VMEM((own_shared, 2 * STATE), F32),
        pltpu.VMEM((rows, wide), BF16),
        pltpu.VMEM((rows, wide), BF16),
        pltpu.VMEM((rows, wide), BF16),
        pltpu.VMEM((own_shared, SHARED), BF16),
        pltpu.VMEM((own_rows, 2 * D), BF16),
        pltpu.VMEM((D, wide), BF16),
        pltpu.VMEM((D, wide), BF16),
        pltpu.VMEM((D, wide), BF16),
        pltpu.VMEM(shared_shape, BF16),
        pltpu.VMEM((count, own_shared, SHARED) if split else (16, 128), BF16),
        pltpu.VMEM((STRETCH, D), BF16),
        pltpu.VMEM((length, 2 * D), BF16),
        pltpu.VMEM((D, length), BF16),
        pltpu.VMEM((length, wide), F32),
        pltpu.VMEM((length, wide), BF16),
        pltpu.VMEM((length, wide), F32),
        pltpu.VMEM((STRETCH + 8, edge), F32),
        pltpu.VMEM((STATE, wide), F32),
        pltpu.VMEM((8, INNER + 128), F32),
        pltpu.VMEM((levels + 1, 8, length), F32),
        pltpu.VMEM((levels, 8, length), F32),
        dma((8,)),
        dma((levels,)),
        dma((levels,)),
    ]
    scratch = scratch + Gather.scratch(ring, WEIGHT_PIECES) + Gather.scratch(ring, 1)
    scratch = scratch + Gather.scratch(ring, 1) + Gather.scratch(seq, TOKEN_PIECES)
    scratch = scratch + Gather.scratch(ring, 1) + Gather.scratch(seq, 1)
    return pl.pallas_call(
        partial(forward_kernel, heads),
        grid=(blocks + 1,),
        in_specs=[resident(x) for x in wholes] + [HBM, HBM],
        out_specs=[
            chunk(edge),
            chunk(edge),
            chunk(128),
            pl.BlockSpec((1, STATE, wide), lambda i: (i - i // blocks, 0, 0)),
        ]
        + [resident(x) for x in late]
        + [HBM] * 4,
        out_shape=[
            shape((length, edge), F32),
            shape((length, edge), BF16),
            shape((length, 128), F32),
            shape((blocks, STATE, wide), F32),
        ]
        + late
        + [shape((D, wide), BF16), shape((D, wide), BF16), shape(shared_shape, BF16)]
        + [shape((length, D), BF16)],
        scratch_shapes=scratch,
        compiler_params=pltpu.CompilerParams(
            collective_id=1,
            has_side_effects=True,
            vmem_limit_bytes=61 * 1024 * 1024,
            dimension_semantics=("arbitrary",),
        ),
        name="gather_and_forward",
    )(*wholes, in_weight, out_weight)


def backward_kernel(heads, *refs):
    chunk = refs[:5]
    packs = refs[5:12]
    d_z, w_z, w_x, w_s, normed_t, tokens, small, d_gain = refs[12:20]
    out_part, z_part, branch_part = refs[20:23]
    out_all, z_all, x_all, s_all, small_all, branch, d_normed, d_conv, d_head = refs[23:32]
    extended, d_state, d_rest, x_part, s_part, act_part, out_own, z_own, x_own, s_own, s_mid = refs[32:43]
    small_sums, small_got, small_sends, small_arrivals, out_loads, z_loads, branch_loads = refs[43:50]
    scratch = refs[50:]
    ring, seq = places()
    rows = x_own.shape[0]
    own_rows = act_part.shape[1]
    wide = heads * HEAD
    edge = wide + 2 * STATE
    groups = seq.major * seq.minor
    own_shared = s_own.shape[0]
    split = halved(rows, groups)
    levels = levels_of("fsdp")

    def stream(place, part, total, extent, pieces, at, loads=None):
        return Reduce(place, part, total, extent, pieces, scratch[7 * at : 7 * at + 7], loads)

    def spreading(own, full, pieces, at):
        return Gather(seq, own, full, own.shape[0], pieces, scratch[49 + 5 * at : 54 + 5 * at])

    out_sum = stream(ring, out_part, out_own, rows, 1, 0, out_loads)
    z_sum = stream(ring, z_part, z_own, rows, 1, 1, z_loads)
    x_sum = stream(ring, x_part, x_own, rows, WEIGHT_PIECES, 2)
    branch_sum = stream(seq, branch_part, branch, own_rows, 1, 3, branch_loads)
    d_normed_sum = stream(seq, act_part, d_normed, own_rows, 2, 4)
    if split:
        mid_sum = stream(seq, s_part, s_mid, s_mid.shape[0], 1, 5)
        s_sum = stream(ring, s_mid, s_own, own_shared, 1, 6)
    else:
        s_sum = stream(ring, s_part, s_own, rows, 1, 6)
    out_spread = spreading(out_own, out_all, 1, 0)
    z_spread = spreading(z_own, z_all, 1, 1)
    x_spread = spreading(x_own, x_all, WEIGHT_PIECES, 2)
    s_spread = spreading(s_own, s_all, 1, 3)
    small_spread = spreading(small_sums.at[levels], small_all, 1, 4)
    early = [(s, item) for s in (out_sum, z_sum) for item in s.items()]
    at_step = pl.program_id(0)
    blocks = d_rest.shape[0] // STRETCH

    def swap(level):
        return exchange(
            "fsdp",
            level,
            small_sums.at[level],
            small_got.at[level],
            small_sends.at[level],
            small_arrivals.at[level],
        )

    @pl.when(at_step == 0)
    def _():
        meet(ring, seq)
        for s, item in early:
            s.begin(item)
        for item in branch_sum.items():
            branch_sum.begin(item)

    backward_block(heads, *chunk, *packs, d_conv, d_head, extended, d_state, d_rest)

    for k in range(blocks):

        @pl.when(at_step == k)
        def _():
            s, item = early[k]
            s.handle(item)
            if k == blocks - 1:
                for item in branch_sum.items():
                    branch_sum.handle(item)
                branch_sum.close(0)
                branch_sum.finish()

    @pl.when(at_step == blocks - 1)
    def _():
        def x_block(slot):
            here = pl.ds(pl.multiple_of(slot * rows, 16), rows)

            def one(at, _):
                columns = pl.ds(pl.multiple_of(at * 384, 128), 384)
                x_part[slot, :, columns] = dot(normed_t[here, :], d_rest[:, columns]).astype(BF16)
                return 0

            lax.fori_loop(0, wide // 384, one, 0)

        def s_block(slot, _):
            here = pl.ds(pl.multiple_of(slot * rows, 16), rows)
            value = dot(normed_t[here, :], d_rest[:, wide:]).astype(BF16)
            if split:
                target = pl.ds(pl.multiple_of(slot * own_shared, 16), own_shared)
                for s in range(groups):
                    s_part[s, target, :] = value[s * own_shared : (s + 1) * own_shared]
            else:
                s_part[slot] = value
            return 0

        def normed_block(slot):
            here = pl.ds(pl.multiple_of(slot * own_rows, own_rows), own_rows)

            def one(at, _):
                columns = pl.ds(pl.multiple_of(at * 512, 128), 512)
                value = dot(d_z[here, :], w_z[columns, :], ((1,), (1,)))
                value = value + dot(d_rest[here, :wide], w_x[columns, :], ((1,), (1,)))
                value = value + dot(d_rest[here, wide:], w_s[columns, :], ((1,), (1,)))
                act_part[slot, :, columns] = value.astype(BF16)
                return 0

            lax.fori_loop(0, D // 512, one, 0)

        lax.fori_loop(0, ring.major * ring.minor, s_block, 0)
        if split:
            for item in mid_sum.items():
                mid_sum.begin(item)
        else:
            for item in s_sum.items():
                s_sum.begin(item)
        for step in x_sum.steps():
            for across in range(1, ring.minor):
                x_block(ring.slot(step, across))
            for piece in range(WEIGHT_PIECES):
                x_sum.begin((piece, step))
        if split:
            for item in mid_sum.items():
                mid_sum.handle(item)
        for step in d_normed_sum.steps():
            for across in range(1, seq.minor):
                normed_block(seq.slot(step, across))
            for piece in range(2):
                d_normed_sum.begin((piece, step))
        if split:
            mid_sum.close(0)
            for item in s_sum.items():
                s_sum.begin(item)
        for step in x_sum.steps():
            x_block(ring.slot(step, 0))
        for s, item in early[blocks:]:
            s.handle(item)
        for step in d_normed_sum.steps():
            normed_block(seq.slot(step, 0))
        out_sum.close(0)
        out_spread.begin(0)
        side = d_normed_sum.items() + [None] * (2 + levels)
        work = [(x_sum, item) for item in x_sum.items()] + [(s_sum, item) for item in s_sum.items()]

        def sideways(at):
            first = len(d_normed_sum.items())
            if at < first:
                d_normed_sum.handle(side[at])
                return
            if at == first:
                for piece in range(2):
                    d_normed_sum.close(piece)
                inputs = tokens[...].astype(F32)
                rms = lax.rsqrt(jnp.mean(inputs * inputs, axis=-1, keepdims=True) + NORM_EPS)
                small_sums[0] = jnp.zeros(small_sums.shape[1:], F32)
                small_sums[0, 0 : KERNEL + 1, :edge] = d_conv[0 : KERNEL + 1, :]
                small_sums[0, 5:6, :] = jnp.sum(
                    d_normed[...].astype(F32) * (inputs * rms), axis=0, keepdims=True
                )
                small_sums[0, 6:7, :wide] = d_gain[0:1, :]
                for k in range(3):
                    small_sums[0, 7:8, 128 * k : 128 * (k + 1)] = d_head[k : k + 1, :]
                swap(0).start()
                return
            level = at - first - 1
            if level < levels:
                swap(level).wait()
                small_sums[level + 1] = small_sums[level] + small_got[level]
                if level + 1 < levels:
                    swap(level + 1).start()
                else:
                    small_spread.begin(0)
                    small_spread.keep().start()

        done = 0
        for at, (s, item) in enumerate(work):
            s.handle(item)
            sideways(at)
            done = at + 1
            if at == WEIGHT_PIECES:
                z_sum.close(0)
                z_spread.begin(0)
                out_spread.forward(0)
        for at in range(done, len(side)):
            sideways(at)
        for piece in range(WEIGHT_PIECES):
            x_sum.close(piece)
            x_spread.begin(piece)
        s_sum.close(0)
        s_spread.begin(0)
        spreads = (out_spread, z_spread, x_spread, s_spread)
        for s in spreads:
            s.keep().start()
        z_spread.forward(0)
        small_spread.forward(0)
        for piece in range(WEIGHT_PIECES):
            x_spread.forward(piece)
        s_spread.forward(0)
        for s in (out_sum, z_sum, x_sum, s_sum, d_normed_sum):
            s.finish()
        if split:
            mid_sum.finish()
        for s in spreads + (small_spread,):
            s.finish()
            s.keep().wait()


def run_backward(
    heads, d_y, pre, conv, dt_pre, states, seg_pad, seg_row, packs, spread, d_z, weights, normed_t,
    tokens, small, d_gain, out_part, z_part, branch_part,
):
    length = d_y.shape[0]
    blocks = length // STRETCH
    wide = heads * HEAD
    edge = wide + 2 * STATE
    ring, seq = places()
    count, groups = lax.axis_size("fsdp"), lax.axis_size("seq")
    levels = levels_of("fsdp")

    def parted(x, by):
        return x.reshape(by, x.shape[0] // by, x.shape[1])

    out_part, z_part = parted(out_part, count), parted(z_part, count)
    branch_part = parted(branch_part, groups)
    rows, own_rows = out_part.shape[1], branch_part.shape[1]
    split = halved(rows, groups)
    own_shared = rows // groups if split else rows
    mid_rows = own_shared * count if split else 16
    wholes = [
        seg_pad, seg_row, *packs, spread, spread.T, d_z, *weights, normed_t, tokens, small, d_gain
    ]
    dma = pltpu.SemaphoreType.DMA
    scratch = [
        pltpu.VMEM((STRETCH + 8, edge), F32),
        pltpu.VMEM((STATE, wide), F32),
        pltpu.VMEM((length, wide + SHARED), BF16),
        pltpu.VMEM((count, rows, wide), BF16),
        pltpu.VMEM((groups, mid_rows, SHARED) if split else (count, rows, SHARED), BF16),
        pltpu.VMEM((groups, own_rows, D), BF16),
        pltpu.VMEM((rows, wide), BF16),
        pltpu.VMEM((rows, wide), BF16),
        pltpu.VMEM((rows, wide), BF16),
        pltpu.VMEM((own_shared, SHARED), BF16),
        pltpu.VMEM((mid_rows, SHARED), BF16),
        pltpu.VMEM((levels + 1, 8, D), F32),
        pltpu.VMEM((levels, 8, D), F32),
        dma((levels,)),
        dma((levels,)),
        dma((ring.major,)),
        dma((ring.major,)),
        dma((seq.major,)),
    ]
    scratch = scratch + Reduce.scratch(ring, rows, wide, 1) + Reduce.scratch(ring, rows, wide, 1)
    scratch = scratch + Reduce.scratch(ring, rows, wide, WEIGHT_PIECES)
    scratch = scratch + Reduce.scratch(seq, own_rows, D, 1) + Reduce.scratch(seq, own_rows, D, 2)
    scratch = scratch + Reduce.scratch(seq, mid_rows, SHARED, 1)
    scratch = scratch + Reduce.scratch(ring, own_shared, SHARED, 1)
    for pieces in (1, 1, WEIGHT_PIECES, 1, 1):
        scratch = scratch + Gather.scratch(seq, pieces)
    shape = jax.ShapeDtypeStruct
    gathered = [
        shape((groups, rows, wide), BF16),
        shape((groups, rows, wide), BF16),
        shape((groups, rows, wide), BF16),
        shape((groups, own_shared, SHARED), BF16),
        shape((groups, 8, D), F32),
    ]
    summed = [
        shape((own_rows, D), BF16),
        shape((own_rows, D), BF16),
        shape((8, edge), F32),
        shape((8, 128), F32),
    ]
    return pl.pallas_call(
        partial(backward_kernel, heads),
        grid=(blocks,),
        in_specs=[
            block(wide, blocks),
            block(edge, blocks),
            block(edge, blocks),
            block(128, blocks),
            pl.BlockSpec((1, STATE, wide), lambda i: (blocks - 1 - i, 0, 0)),
        ]
        + [resident(x) for x in wholes]
        + [HBM] * 3,
        out_specs=[HBM] * 5 + [resident(x) for x in summed],
        out_shape=gathered + summed,
        scratch_shapes=scratch,
        compiler_params=pltpu.CompilerParams(
            collective_id=2,
            has_side_effects=True,
            vmem_limit_bytes=61 * 1024 * 1024,
            dimension_semantics=("arbitrary",),
        ),
        name="backward_and_sums",
    )(d_y, pre, conv, dt_pre, states, *wholes, out_part, z_part, branch_part)


def exchange(place_axis, level, source, got, sends, arrivals):
    index = lax.axis_index(place_axis)
    other = partner(index, level)
    return pltpu.make_async_remote_copy(
        src_ref=source,
        dst_ref=got,
        send_sem=sends,
        recv_sem=arrivals,
        device_id={place_axis: other},
        device_id_type=pl.DeviceIdType.MESH,
    )


def partner(index, level):
    bit = 2**level
    return index + (1 - 2 * (index // bit % 2)) * bit


def levels_of(axis):
    return lax.axis_size(axis).bit_length() - 1


class Push:
    def __init__(self, axis, own, slots, sends, arrivals):
        self.axis, self.own, self.slots = axis, own, slots
        self.sends, self.arrivals = sends, arrivals
        self.count = lax.axis_size(axis)

    def copy(self, step):
        index = lax.axis_index(self.axis)
        return pltpu.make_async_remote_copy(
            src_ref=self.own,
            dst_ref=self.slots.at[index],
            send_sem=self.sends.at[step - 1],
            recv_sem=self.arrivals.at[step - 1],
            device_id={self.axis: (index + step) % self.count},
            device_id_type=pl.DeviceIdType.MESH,
        )

    def begin(self):
        for step in range(1, self.count):
            self.copy(step).start()

    def finish(self):
        for step in range(1, self.count):
            self.copy(step).wait()


def norm_kernel(sums, norms_out, own, slots, sends, arrivals):
    push = Push("fsdp", own, slots, sends, arrivals)
    index = lax.axis_index("fsdp")
    barrier = pltpu.get_barrier_semaphore()
    for step in range(1, push.count):
        other = (index + step) % push.count
        pl.semaphore_signal(
            barrier, inc=1, device_id={"fsdp": other}, device_id_type=pl.DeviceIdType.MESH
        )
    own[...] = jnp.broadcast_to(jnp.sum(sums[...], axis=1, keepdims=True), (8, 128))
    slots[index] = own[...]
    pl.semaphore_wait(barrier, push.count - 1)
    push.begin()
    push.finish()
    total = slots[0]
    for k in range(1, push.count):
        total = total + slots[k]
    norms_out[...] = jnp.sqrt(total)


def run_norms(sums):
    count = lax.axis_size("fsdp")
    dma = pltpu.SemaphoreType.DMA
    return pl.pallas_call(
        norm_kernel,
        in_specs=[VMEM],
        out_specs=VMEM,
        out_shape=jax.ShapeDtypeStruct((8, 128), F32),
        scratch_shapes=[
            pltpu.VMEM((8, 128), F32),
            pltpu.VMEM((count, 8, 128), F32),
            dma((count - 1,)),
            dma((count - 1,)),
        ],
        compiler_params=comm_params(3),
        name="norms",
    )(sums)


def small_update(groups, heads, small_all, small_w, small_m, small_v, outs, small_grad):
    wide = heads * HEAD
    edge = wide + 2 * STATE
    everyone = [small_all[s] for s in range(groups)]
    shared = everyone[0]
    for other in everyone[1:]:
        shared = shared + other
    small_grad[:, :D] = shared[5:6, :]
    for k in range(KERNEL + 1):
        base = D + k * CONV
        for s in range(groups):
            small_grad[:, base + s * wide : base + (s + 1) * wide] = everyone[s][k : k + 1, :wide]
        small_grad[:, base + INNER : base + CONV] = shared[k : k + 1, wide:edge]
    size = 3 * HEADS + INNER
    size = size + -size % 128
    lane = lax.broadcasted_iota(jnp.int32, (8, size), 1)
    rest = jnp.zeros((8, size), F32)
    gap = jnp.zeros((8, size - 128), F32)
    for s in range(groups):
        for k in range(3):
            part = jnp.broadcast_to(everyone[s][7:8, 128 * k : 128 * (k + 1)], (8, 128))
            part = jnp.concatenate([part, gap], axis=1)
            part = jnp.where(lane < heads, part, 0.0)
            move = k * HEADS + s * heads
            rest = rest + (pltpu.roll(part, move, 1) if move else part)
    gains = [jnp.broadcast_to(one[6:7, :wide], (8, wide)) for one in everyone]
    gains = gains + [jnp.zeros((8, size - INNER), F32)]
    rest = rest + pltpu.roll(jnp.concatenate(gains, axis=1), 3 * HEADS, 1)
    base = D + (KERNEL + 1) * CONV
    small_grad[:, base : base + size] = rest[0:1, :]
    gradient = small_grad[...]
    first, second, direction = adam_parts(gradient, small_m[...], small_v[...])
    values = (gradient, small_w[...] - LEARN_RATE * direction, first, second)
    for ref, value in zip(outs, values, strict=True):
        ref[...] = value[:, : ref.shape[1]]


def moments_kernel(groups, heads, *refs):
    z_piece, x_piece, tails, out_piece = refs[:4]
    small_all, small_w, small_m, small_v = refs[4:8]
    w_in, m_in, v_in, w_out, m_out, v_out = refs[8:14]
    g_in_new, m_in_new, v_in_new, u_in, g_out_new, m_out_new, v_out_new, u_out = refs[14:22]
    sums = refs[22]
    small_outs = refs[23:27]
    small_grad = refs[27]
    j = pl.program_id(0)

    @pl.when(j == 0)
    def _():
        sums[...] = jnp.zeros_like(sums)
        small_update(groups, heads, small_all, small_w, small_m, small_v, small_outs, small_grad)

    def update(gradient, w, m, v, g_new, m_new, v_new, u, at, keep):
        columns = gradient.shape[1]
        first, second, direction = adam_parts(gradient, m[:, :columns], v[:, :columns])
        weight = w[:, :columns]
        direction = direction + WEIGHT_DECAY * weight
        g_new[:, :columns] = gradient
        m_new[:, :columns] = first
        v_new[:, :columns] = second
        u[:, :columns] = direction
        for k, value in ((at, weight * weight), (at + 1, direction * direction)):
            value = jnp.where(keep, value, 0.0) if keep is not None else value
            sums[k : k + 1, :columns] += jnp.sum(value, axis=0, keepdims=True)

    inside = (w_in, m_in, v_in, g_in_new, m_in_new, v_in_new, u_in)

    @pl.when(j < groups)
    def _():
        update(z_piece[0].astype(F32), *inside, 0, None)

    @pl.when((j >= groups) & (j < 2 * groups))
    def _():
        update(x_piece[0].astype(F32), *inside, 0, None)

    @pl.when(j == 2 * groups)
    def _():
        rows = w_in.shape[0]
        if tails.shape[1] < rows:
            gradient = tails[...].astype(F32).reshape(rows, SHARED)
        else:
            gradient = tails[0].astype(F32)
            for s in range(1, groups):
                gradient = gradient + tails[s].astype(F32)
        lane = lax.broadcasted_iota(jnp.int32, gradient.shape, 1)
        update(gradient, *inside, 0, lane < 2 * STATE + HEADS)

    @pl.when(j > 2 * groups)
    def _():
        outside = (w_out, m_out, v_out, g_out_new, m_out_new, v_out_new, u_out)
        update(out_piece[0].astype(F32), *outside, 2, None)


def matrix_specs(groups, rows, wide):
    last = 2 * groups
    inside = pl.BlockSpec((rows, wide), lambda j: (0, jnp.minimum(j, last)))
    outside = pl.BlockSpec((rows, wide), lambda j: (0, jnp.maximum(j - last - 1, 0)))
    return inside, outside


def run_moments(groups, heads, z_all, x_all, s_all, out_all, smalls, inside, outside):
    rows = inside[0].shape[0]
    wide = heads * HEAD
    last = 2 * groups
    in_spec, out_spec = matrix_specs(groups, rows, wide)

    def piece(start):
        return pl.BlockSpec(
            (1, rows, wide), lambda j: (jnp.clip(j - start, 0, groups - 1), 0, 0)
        )

    shape = jax.ShapeDtypeStruct
    extent = D + (KERNEL + 1) * CONV + 3 * HEADS + INNER
    small_out = [shape((1, extent), F32)] * 4
    in_like, out_like = shape(inside[0].shape, F32), shape(outside[0].shape, F32)
    return pl.pallas_call(
        partial(moments_kernel, groups, heads),
        grid=(last + 1 + groups,),
        in_specs=[
            piece(0),
            piece(groups),
            resident(s_all),
            piece(last + 1),
        ]
        + [resident(x) for x in smalls]
        + [in_spec] * 3
        + [out_spec] * 3,
        out_specs=[in_spec] * 4
        + [out_spec] * 4
        + [pl.BlockSpec((8, wide), lambda j: (0, 0))]
        + [resident(x) for x in small_out],
        out_shape=[in_like] * 4 + [out_like] * 4 + [shape((8, wide), F32)] + small_out,
        scratch_shapes=[pltpu.VMEM(smalls[1].shape, F32)],
        compiler_params=compiler_params(),
        name="moments",
    )(z_all, x_all, s_all, out_all, *smalls, *inside, *outside)


def weights_kernel(groups, norms, w_in, u_in, w_out, u_out, in_new, out_new):
    j = pl.program_id(0)

    def apply(at, w, u, new):
        rate = LEARN_RATE * (norms[at : at + 1, :1] / norms[at + 1 : at + 2, :1])
        new[...] = w[...] - rate * u[...]

    @pl.when(j <= 2 * groups)
    def _():
        apply(0, w_in, u_in, in_new)

    @pl.when(j > 2 * groups)
    def _():
        apply(2, w_out, u_out, out_new)


def run_weights(groups, heads, norms, w_in, u_in, w_out, u_out):
    in_spec, out_spec = matrix_specs(groups, w_in.shape[0], heads * HEAD)
    return pl.pallas_call(
        partial(weights_kernel, groups),
        grid=(3 * groups + 1,),
        in_specs=[resident(norms), in_spec, in_spec, out_spec, out_spec],
        out_specs=[in_spec, out_spec],
        out_shape=[
            jax.ShapeDtypeStruct(w_in.shape, F32),
            jax.ShapeDtypeStruct(w_out.shape, F32),
        ],
        compiler_params=compiler_params(),
        name="weights",
    )(norms, w_in, u_in, w_out, u_out)


def adam_parts(gradient, first_old, second_old):
    first_new = FIRST_DECAY * first_old + (1.0 - FIRST_DECAY) * gradient
    second_new = SECOND_DECAY * second_old + (1.0 - SECOND_DECAY) * (gradient * gradient)
    first_scale = 1.0 / (1.0 - FIRST_DECAY**STEP)
    second_scale = 1.0 / (1.0 - SECOND_DECAY**STEP)
    direction = (first_new * first_scale) / (jnp.sqrt(second_new * second_scale) + ADAM_EPSILON)
    return (first_new, second_new, direction)


def wide_row(vector):
    return jnp.pad(vector, (0, -vector.shape[0] % 128))[None, :]


def shards(
    tokens,
    cotangent,
    segments,
    in_weight,
    out_weight,
    small_params,
    in_first,
    in_second,
    out_first,
    out_second,
    small_first,
    small_second,
):
    in_gain = small_params[:D]
    groups = lax.axis_size("seq")
    where_seq = lax.axis_index("seq")
    heads = HEADS // groups
    wide = INNER // groups
    segment_row = segments[0]

    def own(vector, axis=-1):
        size = vector.shape[axis] // groups
        return lax.dynamic_slice_in_dim(vector, where_seq * size, size, axis)

    inputs = tokens[0].astype(F32)
    in_rms = lax.rsqrt(jnp.mean(inputs * inputs, axis=-1, keepdims=True) + NORM_EPS)
    dt_weight = jnp.pad(
        in_weight[:, INNER + CONV :].astype(BF16), ((0, 0), (0, DT_PAD - HEADS))
    )
    small = wide_row(small_params)
    spread_heads = (
        jnp.arange(128)[:, None] == jnp.arange(wide)[None, :] // HEAD
    ).astype(BF16)
    seg_pad = jnp.pad(segment_row, (EDGE, EDGE), constant_values=-1)[:, None]
    (
        pre, conv_in, dt_pre, states, d_y, d_z, normed_t, out_part, z_part, d_out_gain,
        conv_pack, head_pack, chan_pack, w_x, w_z, w_s, branch_part,
    ) = run_forward(
        heads, tokens[0], cotangent[0], small, dt_weight, seg_pad, segments, spread_heads,
        in_weight, out_weight,
    )
    packs = (conv_pack, head_pack, chan_pack)
    out_all, z_all, x_all, s_all, small_all, branch, d_normed, _, _ = run_backward(
        heads, d_y, pre, conv_in, dt_pre, states, seg_pad, segments, packs, spread_heads, d_z,
        (w_z, w_x, w_s.reshape(D, SHARED)), normed_t, tokens[0], small, d_out_gain, out_part, z_part, branch_part,
    )
    output = (inputs + branch.astype(F32)).astype(BF16)[None]
    d_normed = d_normed.astype(F32)
    slope = d_normed * in_gain[None, :]
    d_inputs = slope * in_rms - inputs * (in_rms**3 / D) * jnp.sum(
        slope * inputs, axis=1, keepdims=True
    )
    input_grad = (cotangent[0].astype(F32) + d_inputs)[None]

    (
        in_grad, in_first_new, in_second_new, in_dir, out_grad, out_first_new, out_second_new, out_dir,
        squares, small_grad, small_new, small_first_new, small_second_new,
    ) = run_moments(
        groups, heads, z_all, x_all, s_all, out_all,
        (small_all, small, wide_row(small_first), wide_row(small_second)),
        (in_weight, in_first, in_second), (out_weight, out_first, out_second),
    )
    norms = run_norms(squares)
    in_new, out_new = run_weights(
        groups, heads, norms, in_weight, in_dir, out_weight, out_dir
    )
    small_grad, small_new, small_first_new, small_second_new = [
        x[0] for x in (small_grad, small_new, small_first_new, small_second_new)
    ]
    norms = norms[:4, 0]
    return (
        output,
        input_grad,
        in_grad,
        in_new,
        in_first_new,
        in_second_new,
        out_grad,
        out_new,
        out_first_new,
        out_second_new,
        small_grad,
        small_new,
        small_first_new,
        small_second_new,
        norms,
    )


def solution(mesh):
    matrix = P("fsdp", None)
    rows = P("fsdp", "seq", None)
    return jax.shard_map(
        shards,
        mesh=mesh,
        in_specs=(rows, rows, matrix, matrix, matrix, P(), matrix, matrix, matrix, matrix, P(), P()),
        out_specs=(rows, rows) + (matrix,) * 8 + (P(),) * 5,
        check_vma=False,
    )
```

```python
from functools import partial

import jax
import jax.numpy as jnp
from jax import lax
from jax.experimental import pallas as pl
from jax.experimental.pallas import tpu as pltpu
from jax.sharding import PartitionSpec as P

D = 1536
HEADS = 48
HEAD = 64
STATE = 128
KERNEL = 4
STRETCH = 256
STEP = 5
INNER = 3072
CONV = 3328
PROJ = 6448
DT_PAD = 128
SHARED = 2 * STATE + DT_PAD

NORM_EPS = 1e-05
FIRST_DECAY = 0.9
SECOND_DECAY = 0.999
ADAM_EPSILON = 1e-06
WEIGHT_DECAY = 0.01
LEARN_RATE = 0.5
F32 = jnp.float32
BF16 = jnp.bfloat16


def dot(a, b, dims=((1,), (0,))):
    return lax.dot_general(a, b, (dims, ((), ())), preferred_element_type=F32)


def split_dot(value, ones):
    high = value.astype(BF16)
    low = (value - high.astype(F32)).astype(BF16)
    return dot(high, ones) + dot(low, ones)


def tri_dot(ones, value):
    high = value.astype(BF16)
    rest = value - high.astype(F32)
    middle = rest.astype(BF16)
    low = (rest - middle.astype(F32)).astype(BF16)
    return dot(ones, high) + dot(ones, middle) + dot(ones, low)


def sigmoid(v):
    return 1.0 / (1.0 + jnp.exp(-v))


def softplus(v):
    return jnp.maximum(v, 0.0) + jnp.log1p(jnp.exp(-jnp.abs(v)))


def row_at_least():
    rows = lax.broadcasted_iota(jnp.int32, (STRETCH, STRETCH), 0)
    columns = lax.broadcasted_iota(jnp.int32, (STRETCH, STRETCH), 1)
    return rows >= columns


class Decays:
    def __init__(self, dt, rate, masks, spread):
        self.dt, self.spread = dt, spread
        lower = jnp.where(row_at_least(), 1.0, 0.0).astype(BF16)
        self.columns = dot(lower, dt) * rate
        self.rows = jnp.transpose(self.columns)
        last = self.columns[STRETCH - 1 :, :]
        self.into = jnp.exp(self.columns) * masks["carry"]
        self.out = jnp.exp(last - self.columns) * masks["tail"]
        self.through = jnp.broadcast_to(jnp.exp(last) * masks["keep"], (8, 128))
        self.bar = masks["bar"]

    def of(self, columns):
        ones = self.spread[:, columns]
        return (
            dot(self.dt, ones),
            split_dot(self.into, ones),
            split_dot(self.out, ones),
            split_dot(self.through, ones)[:1],
        )

    def between(self, head):
        return jnp.exp(self.columns[:, head : head + 1] - self.rows[head : head + 1, :] + self.bar)


EDGE = 8


def block_masks(seg_pad, seg_row, at):
    def rows(by, size=STRETCH):
        return seg_pad[pl.ds(at + EDGE + by, size), :]

    here = rows(0)
    first = jnp.where(at == 0, rows(0, 1), rows(-1, 1))
    last = rows(STRETCH - 1, 1)
    masks = {"carry": here == first, "tail": here == last, "keep": last == first}
    for by in range(1, KERNEL):
        masks[-by] = here == rows(-by)
        masks[by] = here == rows(by)
    masks = {key: jnp.where(value, 1.0, 0.0) for key, value in masks.items()}
    within = row_at_least() & (here == seg_row[:, pl.ds(at, STRETCH)])
    masks["bar"] = jnp.where(within, 0.0, -1e30)
    return masks


def forward_block(
    heads, at, normed, w_x, shared_columns, masks, packs, spread, outs, y_all, extended, state
):
    conv_pack, head_pack, chan_pack = packs
    pre_out, conv_out, dt_out, states_out = outs
    wide = heads * HEAD
    here = pl.ds(at, STRETCH)
    conv_low = jnp.concatenate([dot(normed, w_x[...]), dot(normed, shared_columns(0, 2 * STATE))], axis=1)
    conv_low = conv_low.astype(BF16)
    conv_out[...] = conv_low
    conv_in = conv_low.astype(F32)
    extended[8 : 8 + STRETCH, :] = conv_in
    pre = conv_pack[4:5, :] + conv_pack[3:4, :] * conv_in
    for by in range(1, KERNEL):
        pre = pre + conv_pack[3 - by : 4 - by, :] * (
            extended[8 - by : 8 - by + STRETCH, :] * masks[-by]
        )
    extended[0:8, :] = extended[STRETCH : STRETCH + 8, :]
    pre_out[...] = pre
    act = (pre * sigmoid(pre)).astype(BF16)
    b_mat = act[:, wide : wide + STATE]
    c_mat = act[:, wide + STATE :]
    lane = lax.broadcasted_iota(jnp.int32, (STRETCH, DT_PAD), 1)
    dt_pre = pltpu.roll(
        dot(normed, shared_columns(2 * STATE, DT_PAD)), DT_PAD - lax.axis_index("seq") * heads, 1
    )
    dt_pre = jnp.where(lane < heads, dt_pre, 0.0) + head_pack[0:1, :]
    dt_out[...] = dt_pre
    dt = softplus(dt_pre).astype(BF16)
    decay = Decays(dt, head_pack[1:2, :], masks, spread)
    scores = dot(c_mat, b_mat, ((1,), (1,)))
    first_half = lax.broadcasted_iota(jnp.int32, (STRETCH, 2 * HEAD), 1) < HEAD
    for pair in range(heads // 2):
        columns = slice(pair * 2 * HEAD, (pair + 1) * 2 * HEAD)
        steps, carry, tail, keep = decay.of(columns)
        xs = act[:, columns].astype(F32)
        scaled = xs * steps
        scaled_low = scaled.astype(BF16)
        old = state[:, columns]
        states_out[0, :, columns] = old
        y = dot(c_mat, old.astype(BF16)) * carry + chan_pack[0:1, columns] * xs
        state[:, columns] = old * keep + dot(b_mat, (scaled * tail).astype(BF16), ((0,), (0,)))
        halves = [
            dot((scores * decay.between(h)).astype(BF16), scaled_low)
            for h in (2 * pair, 2 * pair + 1)
        ]
        y_all[here, columns] = (y + jnp.where(first_half, halves[0], halves[1])).astype(BF16)


def fill_packs(heads, small, spread, packs, scratch_gain):
    conv_pack, head_pack, chan_pack = packs
    wide = heads * HEAD
    index = lax.axis_index("seq")
    start = pl.multiple_of(index * wide, 128)
    for ref in packs:
        ref[...] = jnp.zeros_like(ref)
    for k in range(KERNEL + 1):
        base = D + k * CONV
        conv_pack[k : k + 1, :wide] = small[:, pl.ds(base + start, wide)]
        conv_pack[k : k + 1, wide:] = small[:, base + INNER : base + CONV]
    base = D + (KERNEL + 1) * CONV
    window = jnp.broadcast_to(small[:, base : base + 256], (8, 256))
    lane = lax.broadcasted_iota(jnp.int32, (8, 256), 1)

    def own(k):
        moved = pltpu.roll(window, 256 - (k * HEADS + index * heads), 1)
        return jnp.where(lane < heads, moved, 0.0)[:, :128]

    head_pack[0:1, :] = own(0)[:1]
    rate = own(1)
    rate = jnp.where(lax.broadcasted_iota(jnp.int32, (8, 128), 1) < heads, -jnp.exp(rate), 0.0)
    head_pack[1:2, :] = rate[:1]
    chan_pack[0:1, :] = tri_spread(own(2), spread)[:1]
    base = base + 3 * HEADS
    shift = base % 128
    gain = jnp.broadcast_to(small[:, base - shift : base - shift + INNER + 128], (8, INNER + 128))
    scratch_gain[...] = pltpu.roll(gain, INNER + 128 - shift, 1)
    chan_pack[1:2, :] = scratch_gain[0:1, pl.ds(start, wide)]


def tri_spread(value, ones):
    high = value.astype(BF16)
    rest = value - high.astype(F32)
    middle = rest.astype(BF16)
    low = (rest - middle.astype(F32)).astype(BF16)
    return dot(high, ones) + dot(middle, ones) + dot(low, ones)


def as_row(column):
    lane = lax.broadcasted_iota(jnp.int32, (STRETCH, 128), 1)
    return jnp.transpose(jnp.where(lane == 0, column, 0.0))[0:8, :]


def as_column(rows):
    return jnp.transpose(jnp.concatenate([rows, jnp.zeros((120, STRETCH), F32)], axis=0))[:, 0:1]


def inverse_rms(squares):
    return lax.rsqrt(as_column(squares) / INNER + NORM_EPS)


def gate_gradients(y_low, z, d_mixed, gain, squares, products):
    rms = inverse_rms(squares)
    y = y_low.astype(F32)
    sig = sigmoid(z)
    silu = z * sig
    gated = y * silu
    unit = gated * rms
    d_gain = jnp.sum(d_mixed * unit, axis=0, keepdims=True)
    d_gated = d_mixed * gain * rms - unit * (rms * rms / INNER * as_column(products))
    d_z = d_gated * y * (sig * (1.0 + z * (1.0 - sig)))
    return (d_gated * silu).astype(BF16), d_z.astype(BF16), d_gain


def halved(rows, groups):
    return rows % (16 * groups) == 0


def forward_kernel(heads, *refs):
    tokens, cotangent, small, dt_weight, seg_pad, seg_row, spread_ref, in_weight, out_weight = refs[:9]
    outs = refs[9:13]
    d_y, d_z, normed_t, out_part, z_part, d_gain = refs[13:19]
    packs = refs[19:22]
    w_x_out, w_z_out, w_s_out, branch_part = refs[22:26]
    (
        stage_s, own_x, own_z, own_o, own_s, own_rows, w_x, w_z, w_o, w_s,
        shared_own, branch_stage, rows_all, returned_t, z_all, y_all, d_mixed_all, extended, state,
        scratch_gain, mixed_all, sums, got, stage_sems, sum_sends, sum_arrivals,
    ) = refs[26:52]
    sems = refs[52:]
    ring, seq = places()
    wide = heads * HEAD
    edge = wide + 2 * STATE
    step = pl.program_id(0)
    blocks = pl.num_programs(0) - 1
    length = rows_all.shape[0]
    count = length // STRETCH
    rows = own_x.shape[0]
    split = halved(rows, seq.major * seq.minor)
    stage_x, stage_z, stage_o = [d_mixed_all.at[pl.ds(k * rows, rows)] for k in range(3)]

    def shared_columns(start, size):
        if split:
            return w_s[:, :, :, start : start + size].reshape(D, size)
        return w_s[:, start : start + size]

    get_x = Gather(ring, own_x, w_x, rows, WEIGHT_PIECES, sems[:5])
    get_z = Gather(ring, own_z, w_z, rows, 1, sems[5:10])
    get_o = Gather(ring, own_o, w_o, rows, 1, sems[10:15])
    get_rows = Gather(seq, own_rows, rows_all, own_rows.shape[0], TOKEN_PIECES, sems[15:20])
    if split:
        get_s = Gather(ring, own_s, shared_own, own_s.shape[0], 1, sems[20:25])
        pass_s = Gather(
            seq, shared_own, w_s, shared_own.shape[0], 1, sems[25:30],
            lambda slot, piece: w_s.at[:, slot],
        )
    else:
        get_s = Gather(ring, own_s, w_s, rows, 1, sems[20:25])
    saves = [
        pltpu.make_async_copy(source, target, stage_sems.at[4 + k])
        for k, (source, target) in enumerate(((w_x, w_x_out), (w_z, w_z_out), (w_s, w_s_out)))
    ]
    spread = spread_ref[...]
    at = pl.multiple_of(step * STRETCH, STRETCH)

    @pl.when(step == 0)
    def _():
        start = pl.multiple_of(seq.index * wide, 128)
        own_shared = own_s.shape[0]
        first_row = pl.multiple_of(seq.index * own_shared, 16) if split else 0
        sources = [
            (in_weight.at[pl.ds(first_row, own_shared), pl.ds(2 * INNER, 2 * STATE)], stage_s),
            (in_weight.at[:, pl.ds(INNER + start, wide)], stage_x),
            (in_weight.at[:, pl.ds(start, wide)], stage_z),
            (out_weight.at[:, pl.ds(start, wide)], stage_o),
        ]
        loads = [
            pltpu.make_async_copy(source, target, stage_sems.at[k])
            for k, (source, target) in enumerate(sources)
        ]
        for load in loads:
            load.start()
        meet(ring, seq)
        loads[0].wait()
        own_s[:, : 2 * STATE] = stage_s[...].astype(BF16)
        own_s[:, 2 * STATE :] = dt_weight[pl.ds(first_row, own_shared), :]
        get_s.begin(0)
        get_s.keep().start()
        loads[1].wait()
        own_x[...] = stage_x[...].astype(BF16)
        for piece in range(WEIGHT_PIECES):
            get_x.begin(piece)
        get_x.keep().start()
        inputs = tokens[...].astype(F32)
        rms = lax.rsqrt(jnp.mean(inputs * inputs, axis=-1, keepdims=True) + NORM_EPS)
        own_rows[:, :D] = (inputs * rms * small[:, :D]).astype(BF16)
        own_rows[:, D:] = cotangent[...]
        for piece in range(TOKEN_PIECES):
            get_rows.begin(piece)
        get_rows.keep().start()
        loads[2].wait()
        loads[3].wait()
        own_z[...] = stage_z[...].astype(BF16)
        own_o[...] = stage_o[...].astype(BF16)
        get_z.keep().start()
        get_o.keep().start()
        fill_packs(heads, small, spread, packs, scratch_gain)
        state[...] = jnp.zeros_like(state)
        extended[0:8, :] = jnp.zeros((8, edge), F32)
        d_gain[...] = jnp.zeros_like(d_gain)
        get_s.forward(0)
        get_rows.forward(0)
        get_x.forward(0)
        get_s.finish()
        get_s.keep().wait()
        if split:
            pass_s.begin(0)
            pass_s.keep().start()
        get_rows.forward(1)
        get_x.forward(1)
        get_z.begin(0)
        get_rows.forward(2)
        get_x.forward(2)
        get_o.begin(0)
        for piece in range(3, TOKEN_PIECES):
            get_rows.forward(piece)
        if split:
            pass_s.forward(0)
        get_rows.finish()
        get_rows.keep().wait()

        def turn(k, _):
            here = pl.ds(pl.multiple_of(k * STRETCH, STRETCH), STRETCH)
            normed_t[:, here] = jnp.transpose(rows_all[here, :D])
            returned_t[:, here] = jnp.transpose(rows_all[here, D:])
            return 0

        lax.fori_loop(0, count, turn, 0)
        if split:
            pass_s.finish()
            pass_s.keep().wait()
        get_x.finish()
        get_x.keep().wait()
        saves[0].start()
        saves[2].start()

    @pl.when(step < blocks)
    def _():
        masks = block_masks(seg_pad, seg_row, at)
        forward_block(
            heads, at, rows_all[pl.ds(at, STRETCH), :D], w_x, shared_columns, masks, packs, spread, outs,
            y_all, extended, state,
        )

    forwards = [(stream, k) for stream in (get_z, get_o) for k in range(1, ring.major)]
    ahead = min(count, len(forwards))
    for k in range(ahead):

        @pl.when(step == k)
        def _():
            stream, by = forwards[k]
            stream.forward_step(0, by)

    @pl.when(step == blocks)
    def _():
        later = list(forwards[ahead:])
        while later and later[0][0] is get_z:
            stream, by = later.pop(0)
            stream.forward_step(0, by)
        get_z.finish()
        get_z.keep().wait()
        saves[1].start()
        levels = levels_of("seq")
        gain = packs[2][1:2, :]

        def chunk_rows(k):
            return pl.ds(pl.multiple_of(k * STRETCH, STRETCH), STRETCH)

        def gated_at(here):
            z = z_all[here, :]
            return y_all[here, :].astype(F32) * (z * sigmoid(z))

        def summed(which):
            base = which * (levels + 1)
            for level in range(levels):
                at = which * levels + level
                copy = exchange(
                    "seq", level, sums.at[base + level], got.at[at], sum_sends.at[at], sum_arrivals.at[at]
                )
                copy.start()
                copy.wait()
                sums[base + level + 1] = sums[base + level] + got[at]
            return base + levels

        def gate(k, _):
            here = chunk_rows(k)
            z_all[here, :] = dot(rows_all[here, :D], w_z[...])
            gated = gated_at(here)
            sums[0, :, here] = as_row(jnp.sum(gated * gated, axis=1, keepdims=True))
            return 0

        lax.fori_loop(0, count, gate, 0)
        if later:
            stream, by = later.pop(0)
            stream.forward_step(0, by)
        squares = summed(0)

        def mix(k, _):
            here = chunk_rows(k)
            mixed_all[here, :] = (
                gated_at(here) * inverse_rms(sums[squares, :, here]) * gain
            ).astype(BF16)
            return 0

        lax.fori_loop(0, count, mix, 0)
        for stream, by in later:
            stream.forward_step(0, by)

        def contract_out(k, _):
            here = pl.ds(pl.multiple_of(k * 256, 256), 256)
            out_part[here, :] = dot(returned_t[here, :], mixed_all[...]).astype(BF16)
            return 0

        lax.fori_loop(0, D // 256, contract_out, 0)
        get_o.finish()
        get_o.keep().wait()

        def measure(k, _):
            here = chunk_rows(k)
            d_mixed = dot(rows_all[here, D:], w_o[...])
            d_mixed_all[here, :] = d_mixed
            product = jnp.sum(d_mixed * gain * gated_at(here), axis=1, keepdims=True)
            sums[levels + 1, :, here] = as_row(product)
            return 0

        lax.fori_loop(0, count, measure, 0)
        products = summed(1)

        def differentiate(k, _):
            here = chunk_rows(k)
            d_y_block, d_z_block, d_gain_block = gate_gradients(
                y_all[here, :], z_all[here, :], d_mixed_all[here, :], gain,
                sums[squares, :, here], sums[products, :, here],
            )
            d_y[here, :] = d_y_block
            d_z[here, :] = d_z_block
            d_gain[0:1, :] += d_gain_block
            branch_stage[...] = dot(mixed_all[here, :], w_o[...], ((1,), (1,))).astype(BF16)
            out = pltpu.make_async_copy(branch_stage, branch_part.at[here], stage_sems.at[7])
            out.start()
            out.wait()
            return 0

        lax.fori_loop(0, count, differentiate, 0)

        def contract_z(k, _):
            here = pl.ds(pl.multiple_of(k * 256, 256), 256)
            z_part[here, :] = dot(normed_t[here, :], d_z[...]).astype(BF16)
            return 0

        lax.fori_loop(0, D // 256, contract_z, 0)
        for save in saves:
            save.wait()


def backward_block(
    heads,
    d_y_ref,
    pre_ref,
    conv_ref,
    dt_ref,
    states,
    seg_pad,
    seg_row,
    conv_pack,
    head_pack,
    chan_pack,
    spread_ref,
    gather_ref,
    d_conv_out,
    d_head_out,
    extended,
    d_state,
    d_rest,
):
    wide = heads * HEAD
    edge = wide + 2 * STATE

    @pl.when(pl.program_id(0) == 0)
    def _():
        d_state[...] = jnp.zeros_like(d_state)
        extended[STRETCH : STRETCH + 8, :] = jnp.zeros((8, edge), F32)
        d_conv_out[...] = jnp.zeros_like(d_conv_out)
        d_head_out[...] = jnp.zeros_like(d_head_out)

    at_row = pl.multiple_of((pl.num_programs(0) - 1 - pl.program_id(0)) * STRETCH, STRETCH)
    masks = block_masks(seg_pad, seg_row, at_row)
    spread = spread_ref[...]
    gather = gather_ref[...]
    pre = pre_ref[...]
    act = (pre * sigmoid(pre)).astype(BF16)
    b_mat = act[:, wide : wide + STATE]
    c_mat = act[:, wide + STATE :]
    dt_pre = dt_ref[...]
    dt = softplus(dt_pre).astype(BF16)
    rate = head_pack[1:2, :]
    decay = Decays(dt, rate, masks, spread)
    scores = dot(c_mat, b_mat, ((1,), (1,)))
    lane = lax.broadcasted_iota(jnp.int32, (STRETCH, 128), 1)
    first_half = lane < HEAD
    d_b = jnp.zeros((STRETCH, STATE), F32)
    d_c = jnp.zeros((STRETCH, STATE), F32)
    d_scores = jnp.zeros((STRETCH, STRETCH), F32)
    d_cum = jnp.zeros((STRETCH, 128), F32)
    d_dt = jnp.zeros((STRETCH, 128), F32)
    d_last = jnp.zeros((1, 128), F32)
    column_sums = []
    for pair in range(heads // 2):
        columns = slice(pair * 2 * HEAD, (pair + 1) * 2 * HEAD)
        ones = gather[columns, :]
        steps, carry, tail, keep = decay.of(columns)
        xs = act[:, columns].astype(F32)
        scaled = xs * steps
        scaled_low = scaled.astype(BF16)
        old = states[0, :, columns]
        old_low = old.astype(BF16)
        d_new = d_state[:, columns]
        d_new_low = d_new.astype(BF16)
        d_y_low = d_y_ref[:, columns]
        d_y = d_y_low.astype(F32)
        d_carried = d_y * carry
        d_carried_low = d_carried.astype(BF16)
        d_c = d_c + dot(d_carried_low, old_low, ((1,), (1,)))
        d_cum = d_cum + split_dot(d_carried * dot(c_mat, old_low), ones)
        weighed = scaled * tail
        into = dot(b_mat, d_new_low)
        d_b = d_b + dot(weighed.astype(BF16), d_new_low, ((1,), (1,)))
        tail_part = split_dot(weighed * into, ones)
        d_cum = d_cum - tail_part
        kept = jnp.sum(d_new * old, axis=0, keepdims=True) * keep
        kept = split_dot(jnp.broadcast_to(kept, (8, 128)), ones)[:1]
        d_last = d_last + jnp.sum(tail_part, axis=0, keepdims=True) + kept
        d_state[:, columns] = d_new * keep + dot(c_mat, d_carried_low, ((0,), (0,)))
        halves = []
        for h in (2 * pair, 2 * pair + 1):
            between = decay.between(h)
            weights = scores * between
            halves.append(dot(weights.astype(BF16), d_y_low, ((0,), (0,))))
            d_y_head = jnp.where(first_half == (h % 2 == 0), d_y_low, jnp.zeros_like(d_y_low))
            d_weights = dot(d_y_head, scaled_low, ((1,), (1,)))
            d_scores = d_scores + d_weights * between
            product = d_weights * weights
            d_cum = d_cum + jnp.where(lane == h, jnp.sum(product, axis=1, keepdims=True), 0.0)
            column_sums.append(jnp.sum(product, axis=0, keepdims=True))
        d_scaled = into * tail + jnp.where(first_half, halves[0], halves[1])
        d_xs = d_scaled * steps + chan_pack[0:1, columns] * d_y
        extended[0:STRETCH, columns] = d_xs.astype(BF16).astype(F32)
        d_dt = d_dt + split_dot(d_scaled * xs, ones)
        d_skip = jnp.sum(d_y * xs, axis=0, keepdims=True)
        d_head_out[2:3, :] += split_dot(jnp.broadcast_to(d_skip, (8, 128)), ones)[:1]
    column_sums.append(jnp.zeros((128 - heads, STRETCH), F32))
    d_cum = d_cum - jnp.transpose(jnp.concatenate(column_sums, axis=0))
    row = lax.broadcasted_iota(jnp.int32, (STRETCH, 128), 0)
    d_cum = d_cum + jnp.where(row == STRETCH - 1, d_last, 0.0)
    d_scores_low = d_scores.astype(BF16)
    d_c = d_c + dot(d_scores_low, b_mat)
    d_b = d_b + dot(d_scores_low, c_mat, ((0,), (0,)))

    rows = lax.broadcasted_iota(jnp.int32, (STRETCH, STRETCH), 0)
    upper = jnp.where(rows <= lax.broadcasted_iota(jnp.int32, (STRETCH, STRETCH), 1), 1.0, 0.0)
    d_dt = d_dt + rate * tri_dot(upper.astype(BF16), d_cum)
    d_dt_raw = d_dt.astype(BF16).astype(F32) * sigmoid(dt_pre)
    d_head_out[0:1, :] += jnp.sum(d_dt_raw, axis=0, keepdims=True)
    d_head_out[1:2, :] += jnp.sum(d_cum * decay.columns, axis=0, keepdims=True)

    extended[0:STRETCH, wide : wide + STATE] = d_b
    extended[0:STRETCH, wide + STATE :] = d_c
    here = pl.ds(at_row, STRETCH)
    moved = pltpu.roll(jnp.where(lane < heads, d_dt_raw, 0.0), lax.axis_index("seq") * heads, 1)
    d_rest[here, edge:] = moved.astype(BF16)

    def convolve_back(at, _):
        columns = pl.ds(pl.multiple_of(at * 128, 128), 128)
        value = pre_ref[:, columns]
        gate = sigmoid(value)
        d_pre = extended[0:STRETCH, columns] * (gate * (1.0 + value * (1.0 - gate)))
        extended[0:STRETCH, columns] = d_pre
        conv_in = conv_ref[:, columns].astype(F32)
        d_conv_in = conv_pack[3:4, columns] * d_pre
        d_conv_out[3:4, columns] += jnp.sum(d_pre * conv_in, axis=0, keepdims=True)
        d_conv_out[4:5, columns] += jnp.sum(d_pre, axis=0, keepdims=True)
        for by in range(1, KERNEL):
            moved = extended[by : by + STRETCH, columns] * masks[by]
            d_conv_in = d_conv_in + conv_pack[3 - by : 4 - by, columns] * moved
            d_conv_out[3 - by : 4 - by, columns] += jnp.sum(moved * conv_in, axis=0, keepdims=True)
        extended[STRETCH : STRETCH + 8, columns] = extended[0:8, columns]
        d_rest[here, columns] = d_conv_in.astype(BF16)
        return 0

    lax.fori_loop(0, edge // 128, convolve_back, 0)


VMEM_BYTES = 56 * 1024 * 1024


def block(columns, reverse=0):
    if reverse:
        return pl.BlockSpec((STRETCH, columns), lambda i: (reverse - 1 - i, 0))
    return pl.BlockSpec((STRETCH, columns), lambda i: (i, 0))


def whole(*shape):
    return pl.BlockSpec(shape, lambda i: (0,) * len(shape))


def compiler_params():
    return pltpu.CompilerParams(
        vmem_limit_bytes=VMEM_BYTES, dimension_semantics=("arbitrary",)
    )


class Place:
    def __init__(self, axis, minor):
        self.axis = axis
        self.minor = minor
        self.major = lax.axis_size(axis) // minor
        index = lax.axis_index(axis)
        self.at_major = index // minor
        self.at_minor = index % minor
        self.index = index

    def slot(self, by_major, by_minor):
        return (self.at_major + by_major) % self.major * self.minor + (
            self.at_minor + by_minor
        ) % self.minor

    def others(self):
        along = [self.slot(step, 0) for step in range(1, self.major)]
        return along + [self.slot(0, step) for step in range(1, self.minor)]


def places():
    ring = lax.axis_size("fsdp")
    side = 1
    while 2 * side * 2 * side * 2 <= ring:
        side = 2 * side
    return Place("fsdp", side), Place("seq", 2)


def meet(*all_places):
    barrier = pltpu.get_barrier_semaphore()
    count = 0
    for place in all_places:
        for other in place.others():
            pl.semaphore_signal(
                barrier, inc=1, device_id={place.axis: other}, device_id_type=pl.DeviceIdType.MESH
            )
            count = count + 1
    pl.semaphore_wait(barrier, count)


def send(place, source, target, to, sends, arrivals, at):
    return pltpu.make_async_remote_copy(
        src_ref=source,
        dst_ref=target,
        send_sem=sends.at[at],
        recv_sem=arrivals.at[at],
        device_id={place.axis: to},
        device_id_type=pl.DeviceIdType.MESH,
    )


class Gather:
    def __init__(self, place, own, full, rows, pieces, sems, target=None):
        self.place, self.own, self.full, self.landing = place, own, full, target
        self.size, self.pieces = rows // pieces, pieces
        self.sends1, self.arrivals1, self.sends2, self.arrivals2, self.here = sems

    @staticmethod
    def scratch(place, pieces):
        first = max(place.major - 1, 1) * pieces
        second = place.major * (place.minor - 1) * pieces
        dma = pltpu.SemaphoreType.DMA
        return [dma((first,)), dma((first,)), dma((second,)), dma((second,)), dma((1,))]

    def rows(self, piece):
        return pl.ds(piece * self.size, self.size)

    def target(self, slot, piece):
        if self.landing is not None:
            return self.landing(slot, piece)
        if len(self.full.shape) > len(self.own.shape):
            return self.full.at[slot, self.rows(piece)]
        start = slot * (self.size * self.pieces) + piece * self.size
        return self.full.at[pl.ds(pl.multiple_of(start, 16), self.size)]

    def along(self, piece, step):
        place = self.place
        return send(
            place,
            self.own.at[self.rows(piece)],
            self.target(place.index, piece),
            place.slot(step, 0),
            self.sends1,
            self.arrivals1,
            piece * (place.major - 1) + step - 1,
        )

    def across(self, piece, step, across):
        place = self.place
        slot = place.slot(-step, 0)
        target = self.target(slot, piece)
        source = self.own.at[self.rows(piece)] if step == 0 else target
        at = (piece * place.major + step) * (place.minor - 1) + across - 1
        return send(
            place, source, target, place.slot(0, across), self.sends2, self.arrivals2, at
        )

    def keep(self):
        if self.landing is not None:
            target = self.landing(self.place.index, 0)
        elif len(self.full.shape) > len(self.own.shape):
            target = self.full.at[self.place.index]
        else:
            size = self.size * self.pieces
            target = self.full.at[pl.ds(pl.multiple_of(self.place.index * size, 16), size)]
        return pltpu.make_async_copy(self.own, target, self.here.at[0])

    def begin(self, piece):
        for step in range(1, self.place.major):
            self.along(piece, step).start()
        for across in range(1, self.place.minor):
            self.across(piece, 0, across).start()

    def forward(self, piece):
        for step in range(1, self.place.major):
            self.forward_step(piece, step)

    def forward_step(self, piece, step):
        self.along(piece, step).wait_recv()
        for across in range(1, self.place.minor):
            self.across(piece, step, across).start()

    def finish(self):
        for piece in range(self.pieces):
            for step in range(1, self.place.major):
                self.along(piece, step).wait_send()
            for step in range(self.place.major):
                for across in range(1, self.place.minor):
                    self.across(piece, step, across).wait()


class Reduce:
    def __init__(self, place, part, total, rows, pieces, scratch, loads=None):
        self.place, self.part, self.total, self.loads = place, part, total, loads
        self.size, self.pieces = rows // pieces, pieces
        self.got1, self.mine, self.got2, self.sends1, self.arrivals1, self.sends2, self.arrivals2 = (
            scratch
        )

    @staticmethod
    def scratch(place, rows, columns, pieces):
        dma = pltpu.SemaphoreType.DMA
        first = place.major * (place.minor - 1)
        second = max(place.major - 1, 1)
        return [
            pltpu.VMEM((first, rows, columns), BF16),
            pltpu.VMEM((second, rows, columns), BF16),
            pltpu.VMEM((second, rows, columns), BF16),
            dma((first * pieces,)),
            dma((first * pieces,)),
            dma((second * pieces,)),
            dma((second * pieces,)),
        ]

    def items(self):
        return [(piece, step) for step in self.steps() for piece in range(self.pieces)]

    def steps(self):
        return list(range(1, self.place.major)) + [0]

    def rows(self, piece):
        return pl.ds(piece * self.size, self.size)

    def part_rows(self, slot, rows_start, size):
        if len(self.part.shape) == 3:
            return slot, pl.ds(rows_start, size)
        start = slot * (self.size * self.pieces) + rows_start
        return (pl.ds(pl.multiple_of(start, 16), size),)

    def across(self, item, across):
        piece, step = item
        place = self.place
        slot = step * (place.minor - 1) + across - 1
        index = self.part_rows(place.slot(step, across), piece * self.size, self.size)
        return send(
            place,
            self.part.at[index],
            self.got1.at[slot, self.rows(piece)],
            place.slot(0, across),
            self.sends1,
            self.arrivals1,
            slot * self.pieces + piece,
        )

    def along(self, item):
        piece, step = item
        place = self.place
        return send(
            place,
            self.mine.at[step - 1, self.rows(piece)],
            self.got2.at[step - 1, self.rows(piece)],
            place.slot(step, 0),
            self.sends2,
            self.arrivals2,
            (step - 1) * self.pieces + piece,
        )

    def begin(self, item):
        for across in range(1, self.place.minor):
            self.across(item, across).start()
        if self.loads is not None:
            self.load(item[1]).start()

    def load(self, step):
        target = self.mine.at[step - 1] if step else self.total
        return pltpu.make_async_copy(
            self.part.at[self.place.slot(step, 0)], target, self.loads.at[step]
        )

    def own(self, step, rows):
        if self.loads is None:
            return self.part[self.part_rows(self.place.slot(step, 0), rows, 16)].astype(F32)
        source = self.mine.at[step - 1] if step else self.total
        return source[pl.ds(rows, 16)].astype(F32)

    def blocks(self, piece, body):
        def one(at, _):
            body(pl.multiple_of(piece * self.size + at * 16, 16))
            return 0

        lax.fori_loop(0, self.size // 16, one, 0)

    def handle(self, item):
        piece, step = item
        place = self.place
        for across in range(1, place.minor):
            self.across(item, across).wait_recv()
        if self.loads is not None:
            self.load(step).wait()
        if step == 0:
            return

        def body(start):
            value = self.own(step, start)
            rows = pl.ds(start, 16)
            for across in range(1, place.minor):
                slot = step * (place.minor - 1) + across - 1
                value = value + self.got1[slot, rows].astype(F32)
            self.mine[step - 1, rows] = value.astype(BF16)

        self.blocks(piece, body)
        self.along(item).start()

    def close(self, piece):
        place = self.place
        for step in range(1, place.major):
            self.along((piece, step)).wait_recv()

        def body(start):
            value = self.own(0, start)
            rows = pl.ds(start, 16)
            for across in range(1, place.minor):
                value = value + self.got1[across - 1, rows].astype(F32)
            for step in range(1, place.major):
                value = value + self.got2[step - 1, rows].astype(F32)
            self.total[rows] = value.astype(self.total.dtype)

        self.blocks(piece, body)

    def finish(self):
        for item in self.items():
            for across in range(1, self.place.minor):
                self.across(item, across).wait_send()
            if item[1]:
                self.along(item).wait_send()


WEIGHT_PIECES = 3
TOKEN_PIECES = 4
HBM = pl.BlockSpec(memory_space=pl.ANY)
VMEM = pl.BlockSpec(memory_space=pltpu.VMEM)


def comm_params(number):
    return pltpu.CompilerParams(
        collective_id=number, has_side_effects=True, vmem_limit_bytes=VMEM_BYTES
    )


def resident(x):
    return pl.BlockSpec(
        x.shape, lambda i: (0,) * len(x.shape), pipeline_mode=pl.Buffered(buffer_count=1)
    )


def run_forward(heads, tokens, cotangent, small, dt_weight, seg_pad, seg_row, spread, in_weight, out_weight):
    ring, seq = places()
    count, groups = lax.axis_size("fsdp"), lax.axis_size("seq")
    rows, own_rows = in_weight.shape[0], tokens.shape[0]
    length = own_rows * groups
    blocks = length // STRETCH
    wide = heads * HEAD
    edge = wide + 2 * STATE
    levels = levels_of("seq")
    shape = jax.ShapeDtypeStruct
    split = halved(rows, groups)
    own_shared = rows // groups if split else rows
    shared_shape = (count, groups, own_shared, SHARED) if split else (D, SHARED)

    def chunk(columns):
        return pl.BlockSpec((STRETCH, columns), lambda i: (i - i // blocks, 0))

    wholes = [tokens, cotangent, small, dt_weight, seg_pad, seg_row, spread]
    late = [
        shape((length, wide), BF16),
        shape((length, wide), BF16),
        shape((D, length), BF16),
        shape((D, wide), BF16),
        shape((D, wide), BF16),
        shape((8, wide), F32),
        shape((8, edge), F32),
        shape((8, 128), F32),
        shape((8, wide), F32),
    ]
    dma = pltpu.SemaphoreType.DMA
    scratch = [
        pltpu.VMEM((own_shared, 2 * STATE), F32),
        pltpu.VMEM((rows, wide), BF16),
        pltpu.VMEM((rows, wide), BF16),
        pltpu.VMEM((rows, wide), BF16),
        pltpu.VMEM((own_shared, SHARED), BF16),
        pltpu.VMEM((own_rows, 2 * D), BF16),
        pltpu.VMEM((D, wide), BF16),
        pltpu.VMEM((D, wide), BF16),
        pltpu.VMEM((D, wide), BF16),
        pltpu.VMEM(shared_shape, BF16),
        pltpu.VMEM((count, own_shared, SHARED) if split else (16, 128), BF16),
        pltpu.VMEM((STRETCH, D), BF16),
        pltpu.VMEM((length, 2 * D), BF16),
        pltpu.VMEM((D, length), BF16),
        pltpu.VMEM((length, wide), F32),
        pltpu.VMEM((length, wide), BF16),
        pltpu.VMEM((length, wide), F32),
        pltpu.VMEM((STRETCH + 8, edge), F32),
        pltpu.VMEM((STATE, wide), F32),
        pltpu.VMEM((8, INNER + 128), F32),
        pltpu.VMEM((length, wide), BF16),
        pltpu.VMEM((2 * (levels + 1), 8, length), F32),
        pltpu.VMEM((2 * levels, 8, length), F32),
        dma((8,)),
        dma((2 * levels,)),
        dma((2 * levels,)),
    ]
    scratch = scratch + Gather.scratch(ring, WEIGHT_PIECES) + Gather.scratch(ring, 1)
    scratch = scratch + Gather.scratch(ring, 1) + Gather.scratch(seq, TOKEN_PIECES)
    scratch = scratch + Gather.scratch(ring, 1) + Gather.scratch(seq, 1)
    return pl.pallas_call(
        partial(forward_kernel, heads),
        grid=(blocks + 1,),
        in_specs=[resident(x) for x in wholes] + [HBM, HBM],
        out_specs=[
            chunk(edge),
            chunk(edge),
            chunk(128),
            pl.BlockSpec((1, STATE, wide), lambda i: (i - i // blocks, 0, 0)),
        ]
        + [resident(x) for x in late]
        + [HBM] * 4,
        out_shape=[
            shape((length, edge), F32),
            shape((length, edge), BF16),
            shape((length, 128), F32),
            shape((blocks, STATE, wide), F32),
        ]
        + late
        + [shape((D, wide), BF16), shape((D, wide), BF16), shape(shared_shape, BF16)]
        + [shape((length, D), BF16)],
        scratch_shapes=scratch,
        compiler_params=pltpu.CompilerParams(
            collective_id=1,
            has_side_effects=True,
            vmem_limit_bytes=61 * 1024 * 1024,
            dimension_semantics=("arbitrary",),
        ),
        name="gather_and_forward",
    )(*wholes, in_weight, out_weight)


def backward_kernel(heads, *refs):
    chunk = refs[:5]
    packs = refs[5:12]
    d_z, w_z, w_x, w_s, normed_t, tokens, small, d_gain = refs[12:20]
    out_part, z_part, branch_part = refs[20:23]
    out_all, z_all, x_all, s_all, small_all, branch, d_normed, d_conv, d_head = refs[23:32]
    extended, d_state, d_rest, x_part, s_part, act_part, out_own, z_own, x_own, s_own, s_mid = refs[32:43]
    small_sums, small_got, small_sends, small_arrivals, out_loads, z_loads, branch_loads = refs[43:50]
    scratch = refs[50:]
    ring, seq = places()
    rows = x_own.shape[0]
    own_rows = act_part.shape[1]
    wide = heads * HEAD
    edge = wide + 2 * STATE
    groups = seq.major * seq.minor
    own_shared = s_own.shape[0]
    split = halved(rows, groups)
    levels = levels_of("fsdp")

    def stream(place, part, total, extent, pieces, at, loads=None):
        return Reduce(place, part, total, extent, pieces, scratch[7 * at : 7 * at + 7], loads)

    def spreading(own, full, pieces, at):
        return Gather(seq, own, full, own.shape[0], pieces, scratch[49 + 5 * at : 54 + 5 * at])

    out_sum = stream(ring, out_part, out_own, rows, 1, 0, out_loads)
    z_sum = stream(ring, z_part, z_own, rows, 1, 1, z_loads)
    x_sum = stream(ring, x_part, x_own, rows, WEIGHT_PIECES, 2)
    branch_sum = stream(seq, branch_part, branch, own_rows, 1, 3, branch_loads)
    d_normed_sum = stream(seq, act_part, d_normed, own_rows, 2, 4)
    if split:
        mid_sum = stream(seq, s_part, s_mid, s_mid.shape[0], 1, 5)
        s_sum = stream(ring, s_mid, s_own, own_shared, 1, 6)
    else:
        s_sum = stream(ring, s_part, s_own, rows, 1, 6)
    out_spread = spreading(out_own, out_all, 1, 0)
    z_spread = spreading(z_own, z_all, 1, 1)
    x_spread = spreading(x_own, x_all, WEIGHT_PIECES, 2)
    s_spread = spreading(s_own, s_all, 1, 3)
    small_spread = spreading(small_sums.at[levels], small_all, 1, 4)
    early = [(s, item) for s in (out_sum, z_sum) for item in s.items()]
    at_step = pl.program_id(0)
    blocks = d_rest.shape[0] // STRETCH

    def swap(level):
        return exchange(
            "fsdp",
            level,
            small_sums.at[level],
            small_got.at[level],
            small_sends.at[level],
            small_arrivals.at[level],
        )

    @pl.when(at_step == 0)
    def _():
        meet(ring, seq)
        for s, item in early:
            s.begin(item)
        for item in branch_sum.items():
            branch_sum.begin(item)

    backward_block(heads, *chunk, *packs, d_conv, d_head, extended, d_state, d_rest)

    for k in range(blocks):

        @pl.when(at_step == k)
        def _():
            s, item = early[k]
            s.handle(item)
            if k == blocks - 1:
                for item in branch_sum.items():
                    branch_sum.handle(item)
                branch_sum.close(0)
                branch_sum.finish()

    @pl.when(at_step == blocks - 1)
    def _():
        def x_block(slot):
            here = pl.ds(pl.multiple_of(slot * rows, 16), rows)

            def one(at, _):
                columns = pl.ds(pl.multiple_of(at * 384, 128), 384)
                x_part[slot, :, columns] = dot(normed_t[here, :], d_rest[:, columns]).astype(BF16)
                return 0

            lax.fori_loop(0, wide // 384, one, 0)

        def s_block(slot, _):
            here = pl.ds(pl.multiple_of(slot * rows, 16), rows)
            value = dot(normed_t[here, :], d_rest[:, wide:]).astype(BF16)
            if split:
                target = pl.ds(pl.multiple_of(slot * own_shared, 16), own_shared)
                for s in range(groups):
                    s_part[s, target, :] = value[s * own_shared : (s + 1) * own_shared]
            else:
                s_part[slot] = value
            return 0

        def normed_block(slot):
            here = pl.ds(pl.multiple_of(slot * own_rows, own_rows), own_rows)

            def one(at, _):
                columns = pl.ds(pl.multiple_of(at * 512, 128), 512)
                value = dot(d_z[here, :], w_z[columns, :], ((1,), (1,)))
                value = value + dot(d_rest[here, :wide], w_x[columns, :], ((1,), (1,)))
                value = value + dot(d_rest[here, wide:], w_s[columns, :], ((1,), (1,)))
                act_part[slot, :, columns] = value.astype(BF16)
                return 0

            lax.fori_loop(0, D // 512, one, 0)

        waiting = early[blocks:]

        def handle_early(amount=1):
            for _ in range(min(amount, len(waiting))):
                s, item = waiting.pop(0)
                s.handle(item)

        lax.fori_loop(0, ring.major * ring.minor, s_block, 0)
        if split:
            for item in mid_sum.items():
                mid_sum.begin(item)
        else:
            for item in s_sum.items():
                s_sum.begin(item)
        handle_early()
        for step in x_sum.steps():
            for across in range(1, ring.minor):
                x_block(ring.slot(step, across))
            for piece in range(WEIGHT_PIECES):
                x_sum.begin((piece, step))
        if split:
            for item in mid_sum.items():
                mid_sum.handle(item)
        handle_early()
        for step in d_normed_sum.steps():
            for across in range(1, seq.minor):
                normed_block(seq.slot(step, across))
            for piece in range(2):
                d_normed_sum.begin((piece, step))
        if split:
            mid_sum.close(0)
            for item in s_sum.items():
                s_sum.begin(item)
        handle_early()
        for step in x_sum.steps():
            x_block(ring.slot(step, 0))
        for step in d_normed_sum.steps():
            normed_block(seq.slot(step, 0))
        handle_early(len(waiting))
        out_sum.close(0)
        out_spread.begin(0)
        side = d_normed_sum.items() + [None] * (2 + levels)
        work = [(x_sum, item) for item in x_sum.items()] + [(s_sum, item) for item in s_sum.items()]

        def sideways(at):
            first = len(d_normed_sum.items())
            if at < first:
                d_normed_sum.handle(side[at])
                return
            if at == first:
                for piece in range(2):
                    d_normed_sum.close(piece)
                inputs = tokens[...].astype(F32)
                rms = lax.rsqrt(jnp.mean(inputs * inputs, axis=-1, keepdims=True) + NORM_EPS)
                small_sums[0] = jnp.zeros(small_sums.shape[1:], F32)
                small_sums[0, 0 : KERNEL + 1, :edge] = d_conv[0 : KERNEL + 1, :]
                small_sums[0, 5:6, :] = jnp.sum(
                    d_normed[...].astype(F32) * (inputs * rms), axis=0, keepdims=True
                )
                small_sums[0, 6:7, :wide] = d_gain[0:1, :]
                for k in range(3):
                    small_sums[0, 7:8, 128 * k : 128 * (k + 1)] = d_head[k : k + 1, :]
                swap(0).start()
                return
            level = at - first - 1
            if level < levels:
                swap(level).wait()
                small_sums[level + 1] = small_sums[level] + small_got[level]
                if level + 1 < levels:
                    swap(level + 1).start()
                else:
                    small_spread.begin(0)
                    small_spread.keep().start()

        done = 0
        for at, (s, item) in enumerate(work):
            s.handle(item)
            sideways(at)
            done = at + 1
            if at == WEIGHT_PIECES:
                z_sum.close(0)
                z_spread.begin(0)
                out_spread.forward(0)
        for at in range(done, len(side)):
            sideways(at)
        for piece in range(WEIGHT_PIECES):
            x_sum.close(piece)
            x_spread.begin(piece)
        s_sum.close(0)
        s_spread.begin(0)
        spreads = (out_spread, z_spread, x_spread, s_spread)
        for s in spreads:
            s.keep().start()
        z_spread.forward(0)
        small_spread.forward(0)
        for piece in range(WEIGHT_PIECES):
            x_spread.forward(piece)
        s_spread.forward(0)
        for s in (out_sum, z_sum, x_sum, s_sum, d_normed_sum):
            s.finish()
        if split:
            mid_sum.finish()
        for s in spreads + (small_spread,):
            s.finish()
            s.keep().wait()


def run_backward(
    heads, d_y, pre, conv, dt_pre, states, seg_pad, seg_row, packs, spread, d_z, weights, normed_t,
    tokens, small, d_gain, out_part, z_part, branch_part,
):
    length = d_y.shape[0]
    blocks = length // STRETCH
    wide = heads * HEAD
    edge = wide + 2 * STATE
    ring, seq = places()
    count, groups = lax.axis_size("fsdp"), lax.axis_size("seq")
    levels = levels_of("fsdp")

    def parted(x, by):
        return x.reshape(by, x.shape[0] // by, x.shape[1])

    out_part, z_part = parted(out_part, count), parted(z_part, count)
    branch_part = parted(branch_part, groups)
    rows, own_rows = out_part.shape[1], branch_part.shape[1]
    split = halved(rows, groups)
    own_shared = rows // groups if split else rows
    mid_rows = own_shared * count if split else 16
    wholes = [
        seg_pad, seg_row, *packs, spread, spread.T, d_z, *weights, normed_t, tokens, small, d_gain
    ]
    dma = pltpu.SemaphoreType.DMA
    scratch = [
        pltpu.VMEM((STRETCH + 8, edge), F32),
        pltpu.VMEM((STATE, wide), F32),
        pltpu.VMEM((length, wide + SHARED), BF16),
        pltpu.VMEM((count, rows, wide), BF16),
        pltpu.VMEM((groups, mid_rows, SHARED) if split else (count, rows, SHARED), BF16),
        pltpu.VMEM((groups, own_rows, D), BF16),
        pltpu.VMEM((rows, wide), BF16),
        pltpu.VMEM((rows, wide), BF16),
        pltpu.VMEM((rows, wide), BF16),
        pltpu.VMEM((own_shared, SHARED), BF16),
        pltpu.VMEM((mid_rows, SHARED), BF16),
        pltpu.VMEM((levels + 1, 8, D), F32),
        pltpu.VMEM((levels, 8, D), F32),
        dma((levels,)),
        dma((levels,)),
        dma((ring.major,)),
        dma((ring.major,)),
        dma((seq.major,)),
    ]
    scratch = scratch + Reduce.scratch(ring, rows, wide, 1) + Reduce.scratch(ring, rows, wide, 1)
    scratch = scratch + Reduce.scratch(ring, rows, wide, WEIGHT_PIECES)
    scratch = scratch + Reduce.scratch(seq, own_rows, D, 1) + Reduce.scratch(seq, own_rows, D, 2)
    scratch = scratch + Reduce.scratch(seq, mid_rows, SHARED, 1)
    scratch = scratch + Reduce.scratch(ring, own_shared, SHARED, 1)
    for pieces in (1, 1, WEIGHT_PIECES, 1, 1):
        scratch = scratch + Gather.scratch(seq, pieces)
    shape = jax.ShapeDtypeStruct
    gathered = [
        shape((groups, rows, wide), BF16),
        shape((groups, rows, wide), BF16),
        shape((groups, rows, wide), BF16),
        shape((groups, own_shared, SHARED), BF16),
        shape((groups, 8, D), F32),
    ]
    summed = [
        shape((own_rows, D), BF16),
        shape((own_rows, D), BF16),
        shape((8, edge), F32),
        shape((8, 128), F32),
    ]
    return pl.pallas_call(
        partial(backward_kernel, heads),
        grid=(blocks,),
        in_specs=[
            block(wide, blocks),
            block(edge, blocks),
            block(edge, blocks),
            block(128, blocks),
            pl.BlockSpec((1, STATE, wide), lambda i: (blocks - 1 - i, 0, 0)),
        ]
        + [resident(x) for x in wholes]
        + [HBM] * 3,
        out_specs=[HBM] * 5 + [resident(x) for x in summed],
        out_shape=gathered + summed,
        scratch_shapes=scratch,
        compiler_params=pltpu.CompilerParams(
            collective_id=2,
            has_side_effects=True,
            vmem_limit_bytes=61 * 1024 * 1024,
            dimension_semantics=("arbitrary",),
        ),
        name="backward_and_sums",
    )(d_y, pre, conv, dt_pre, states, *wholes, out_part, z_part, branch_part)


def exchange(place_axis, level, source, got, sends, arrivals):
    index = lax.axis_index(place_axis)
    other = partner(index, level)
    return pltpu.make_async_remote_copy(
        src_ref=source,
        dst_ref=got,
        send_sem=sends,
        recv_sem=arrivals,
        device_id={place_axis: other},
        device_id_type=pl.DeviceIdType.MESH,
    )


def partner(index, level):
    bit = 2**level
    return index + (1 - 2 * (index // bit % 2)) * bit


def levels_of(axis):
    return lax.axis_size(axis).bit_length() - 1


class Push:
    def __init__(self, axis, own, slots, sends, arrivals):
        self.axis, self.own, self.slots = axis, own, slots
        self.sends, self.arrivals = sends, arrivals
        self.count = lax.axis_size(axis)

    def copy(self, step):
        index = lax.axis_index(self.axis)
        return pltpu.make_async_remote_copy(
            src_ref=self.own,
            dst_ref=self.slots.at[index],
            send_sem=self.sends.at[step - 1],
            recv_sem=self.arrivals.at[step - 1],
            device_id={self.axis: (index + step) % self.count},
            device_id_type=pl.DeviceIdType.MESH,
        )

    def begin(self):
        for step in range(1, self.count):
            self.copy(step).start()

    def finish(self):
        for step in range(1, self.count):
            self.copy(step).wait()


def norm_kernel(sums, norms_out, own, slots, sends, arrivals):
    push = Push("fsdp", own, slots, sends, arrivals)
    index = lax.axis_index("fsdp")
    barrier = pltpu.get_barrier_semaphore()
    for step in range(1, push.count):
        other = (index + step) % push.count
        pl.semaphore_signal(
            barrier, inc=1, device_id={"fsdp": other}, device_id_type=pl.DeviceIdType.MESH
        )
    own[...] = jnp.broadcast_to(jnp.sum(sums[...], axis=1, keepdims=True), (8, 128))
    slots[index] = own[...]
    pl.semaphore_wait(barrier, push.count - 1)
    push.begin()
    push.finish()
    total = slots[0]
    for k in range(1, push.count):
        total = total + slots[k]
    norms_out[...] = jnp.sqrt(total)


def run_norms(sums):
    count = lax.axis_size("fsdp")
    dma = pltpu.SemaphoreType.DMA
    return pl.pallas_call(
        norm_kernel,
        in_specs=[VMEM],
        out_specs=VMEM,
        out_shape=jax.ShapeDtypeStruct((8, 128), F32),
        scratch_shapes=[
            pltpu.VMEM((8, 128), F32),
            pltpu.VMEM((count, 8, 128), F32),
            dma((count - 1,)),
            dma((count - 1,)),
        ],
        compiler_params=comm_params(3),
        name="norms",
    )(sums)


def small_update(groups, heads, small_all, small_w, small_m, small_v, outs, small_grad):
    wide = heads * HEAD
    edge = wide + 2 * STATE
    everyone = [small_all[s] for s in range(groups)]
    shared = everyone[0]
    for other in everyone[1:]:
        shared = shared + other
    small_grad[:, :D] = shared[5:6, :]
    for k in range(KERNEL + 1):
        base = D + k * CONV
        for s in range(groups):
            small_grad[:, base + s * wide : base + (s + 1) * wide] = everyone[s][k : k + 1, :wide]
        small_grad[:, base + INNER : base + CONV] = shared[k : k + 1, wide:edge]
    size = 3 * HEADS + INNER
    size = size + -size % 128
    lane = lax.broadcasted_iota(jnp.int32, (8, size), 1)
    rest = jnp.zeros((8, size), F32)
    gap = jnp.zeros((8, size - 128), F32)
    for s in range(groups):
        for k in range(3):
            part = jnp.broadcast_to(everyone[s][7:8, 128 * k : 128 * (k + 1)], (8, 128))
            part = jnp.concatenate([part, gap], axis=1)
            part = jnp.where(lane < heads, part, 0.0)
            move = k * HEADS + s * heads
            rest = rest + (pltpu.roll(part, move, 1) if move else part)
    gains = [jnp.broadcast_to(one[6:7, :wide], (8, wide)) for one in everyone]
    gains = gains + [jnp.zeros((8, size - INNER), F32)]
    rest = rest + pltpu.roll(jnp.concatenate(gains, axis=1), 3 * HEADS, 1)
    base = D + (KERNEL + 1) * CONV
    small_grad[:, base : base + size] = rest[0:1, :]
    gradient = small_grad[...]
    first, second, direction = adam_parts(gradient, small_m[...], small_v[...])
    values = (gradient, small_w[...] - LEARN_RATE * direction, first, second)
    for ref, value in zip(outs, values, strict=True):
        ref[...] = value[:, : ref.shape[1]]


def moments_kernel(groups, heads, *refs):
    z_piece, x_piece, tails, out_piece = refs[:4]
    small_all, small_w, small_m, small_v = refs[4:8]
    w_in, m_in, v_in, w_out, m_out, v_out = refs[8:14]
    g_in_new, m_in_new, v_in_new, u_in, g_out_new, m_out_new, v_out_new, u_out = refs[14:22]
    sums = refs[22]
    small_outs = refs[23:27]
    small_grad = refs[27]
    wide = heads * HEAD

    @pl.when(pl.program_id(0) == 0)
    def _():
        sums[...] = jnp.zeros_like(sums)
        small_update(groups, heads, small_all, small_w, small_m, small_v, small_outs, small_grad)

    def update(gradient, start, w, m, v, g_new, m_new, v_new, u, at):
        size = min(gradient.shape[1], w.shape[1] - start)
        here = slice(start, start + size)
        gradient = gradient[:, :size]
        first, second, direction = adam_parts(gradient, m[:, here], v[:, here])
        weight = w[:, here]
        direction = direction + WEIGHT_DECAY * weight
        g_new[:, here] = gradient
        m_new[:, here] = first
        v_new[:, here] = second
        u[:, here] = direction
        sums[at : at + 1, :size] += jnp.sum(weight * weight, axis=0, keepdims=True)
        sums[at + 1 : at + 2, :size] += jnp.sum(direction * direction, axis=0, keepdims=True)

    inside = (w_in, m_in, v_in, g_in_new, m_in_new, v_in_new, u_in)
    outside = (w_out, m_out, v_out, g_out_new, m_out_new, v_out_new, u_out)
    for s in range(groups):
        update(z_piece[s].astype(F32), s * wide, *inside, 0)
        update(x_piece[s].astype(F32), INNER + s * wide, *inside, 0)
        update(out_piece[s].astype(F32), s * wide, *outside, 2)
    gradient = tails[0].astype(F32)
    for s in range(1, tails.shape[0]):
        gradient = gradient + tails[s].astype(F32)
    update(gradient, 2 * INNER, *inside, 0)


ROWS = 16


def by_rows(columns):
    return pl.BlockSpec((ROWS, columns), lambda i: (i, 0))


def run_moments(groups, heads, z_all, x_all, s_all, out_all, smalls, inside, outside):
    rows = inside[0].shape[0]
    wide = heads * HEAD
    piece = pl.BlockSpec((groups, ROWS, wide), lambda i: (0, i, 0))
    if s_all.shape[1] < rows:
        parts = s_all.shape[1] // ROWS
        tails = pl.BlockSpec((1, ROWS, SHARED), lambda i: (i // parts, i % parts, 0))
    else:
        tails = pl.BlockSpec((groups, ROWS, SHARED), lambda i: (0, i, 0))
    shape = jax.ShapeDtypeStruct
    extent = D + (KERNEL + 1) * CONV + 3 * HEADS + INNER
    small_out = [shape((1, extent), F32)] * 4
    in_like, out_like = shape(inside[0].shape, F32), shape(outside[0].shape, F32)
    in_spec, out_spec = by_rows(PROJ), by_rows(INNER)
    return pl.pallas_call(
        partial(moments_kernel, groups, heads),
        grid=(rows // ROWS,),
        in_specs=[piece, piece, tails, piece]
        + [resident(x) for x in smalls]
        + [in_spec] * 3
        + [out_spec] * 3,
        out_specs=[in_spec] * 4
        + [out_spec] * 4
        + [pl.BlockSpec((8, wide), lambda i: (0, 0))]
        + [resident(x) for x in small_out],
        out_shape=[in_like] * 4 + [out_like] * 4 + [shape((8, wide), F32)] + small_out,
        scratch_shapes=[pltpu.VMEM(smalls[1].shape, F32)],
        compiler_params=compiler_params(),
        name="moments",
    )(z_all, x_all, s_all, out_all, *smalls, *inside, *outside)


def weights_kernel(norms, w_in, u_in, w_out, u_out, in_new, out_new):
    for at, w, u, new in ((0, w_in, u_in, in_new), (2, w_out, u_out, out_new)):
        rate = LEARN_RATE * (norms[at : at + 1, :1] / norms[at + 1 : at + 2, :1])
        new[...] = w[...] - rate * u[...]


def run_weights(norms, w_in, u_in, w_out, u_out):
    in_spec, out_spec = by_rows(PROJ), by_rows(INNER)
    return pl.pallas_call(
        weights_kernel,
        grid=(w_in.shape[0] // ROWS,),
        in_specs=[resident(norms), in_spec, in_spec, out_spec, out_spec],
        out_specs=[in_spec, out_spec],
        out_shape=[
            jax.ShapeDtypeStruct(w_in.shape, F32),
            jax.ShapeDtypeStruct(w_out.shape, F32),
        ],
        compiler_params=compiler_params(),
        name="weights",
    )(norms, w_in, u_in, w_out, u_out)


def adam_parts(gradient, first_old, second_old):
    first_new = FIRST_DECAY * first_old + (1.0 - FIRST_DECAY) * gradient
    second_new = SECOND_DECAY * second_old + (1.0 - SECOND_DECAY) * (gradient * gradient)
    first_scale = 1.0 / (1.0 - FIRST_DECAY**STEP)
    second_scale = 1.0 / (1.0 - SECOND_DECAY**STEP)
    direction = (first_new * first_scale) / (jnp.sqrt(second_new * second_scale) + ADAM_EPSILON)
    return (first_new, second_new, direction)


def wide_row(vector):
    return jnp.pad(vector, (0, -vector.shape[0] % 128))[None, :]


def shards(
    tokens,
    cotangent,
    segments,
    in_weight,
    out_weight,
    small_params,
    in_first,
    in_second,
    out_first,
    out_second,
    small_first,
    small_second,
):
    in_gain = small_params[:D]
    groups = lax.axis_size("seq")
    where_seq = lax.axis_index("seq")
    heads = HEADS // groups
    wide = INNER // groups
    segment_row = segments[0]

    def own(vector, axis=-1):
        size = vector.shape[axis] // groups
        return lax.dynamic_slice_in_dim(vector, where_seq * size, size, axis)

    inputs = tokens[0].astype(F32)
    in_rms = lax.rsqrt(jnp.mean(inputs * inputs, axis=-1, keepdims=True) + NORM_EPS)
    dt_weight = jnp.pad(
        in_weight[:, INNER + CONV :].astype(BF16), ((0, 0), (0, DT_PAD - HEADS))
    )
    small = wide_row(small_params)
    spread_heads = (
        jnp.arange(128)[:, None] == jnp.arange(wide)[None, :] // HEAD
    ).astype(BF16)
    seg_pad = jnp.pad(segment_row, (EDGE, EDGE), constant_values=-1)[:, None]
    (
        pre, conv_in, dt_pre, states, d_y, d_z, normed_t, out_part, z_part, d_out_gain,
        conv_pack, head_pack, chan_pack, w_x, w_z, w_s, branch_part,
    ) = run_forward(
        heads, tokens[0], cotangent[0], small, dt_weight, seg_pad, segments, spread_heads,
        in_weight, out_weight,
    )
    packs = (conv_pack, head_pack, chan_pack)
    out_all, z_all, x_all, s_all, small_all, branch, d_normed, _, _ = run_backward(
        heads, d_y, pre, conv_in, dt_pre, states, seg_pad, segments, packs, spread_heads, d_z,
        (w_z, w_x, w_s.reshape(D, SHARED)), normed_t, tokens[0], small, d_out_gain, out_part, z_part, branch_part,
    )
    output = (inputs + branch.astype(F32)).astype(BF16)[None]
    d_normed = d_normed.astype(F32)
    slope = d_normed * in_gain[None, :]
    d_inputs = slope * in_rms - inputs * (in_rms**3 / D) * jnp.sum(
        slope * inputs, axis=1, keepdims=True
    )
    input_grad = (cotangent[0].astype(F32) + d_inputs)[None]

    (
        in_grad, in_first_new, in_second_new, in_dir, out_grad, out_first_new, out_second_new, out_dir,
        squares, small_grad, small_new, small_first_new, small_second_new,
    ) = run_moments(
        groups, heads, z_all, x_all, s_all, out_all,
        (small_all, small, wide_row(small_first), wide_row(small_second)),
        (in_weight, in_first, in_second), (out_weight, out_first, out_second),
    )
    norms = run_norms(squares)
    in_new, out_new = run_weights(norms, in_weight, in_dir, out_weight, out_dir)
    small_grad, small_new, small_first_new, small_second_new = [
        x[0] for x in (small_grad, small_new, small_first_new, small_second_new)
    ]
    norms = norms[:4, 0]
    return (
        output,
        input_grad,
        in_grad,
        in_new,
        in_first_new,
        in_second_new,
        out_grad,
        out_new,
        out_first_new,
        out_second_new,
        small_grad,
        small_new,
        small_first_new,
        small_second_new,
        norms,
    )


def solution(mesh):
    matrix = P("fsdp", None)
    rows = P("fsdp", "seq", None)
    return jax.shard_map(
        shards,
        mesh=mesh,
        in_specs=(rows, rows, matrix, matrix, matrix, P(), matrix, matrix, matrix, matrix, P(), P()),
        out_specs=(rows, rows) + (matrix,) * 8 + (P(),) * 5,
        check_vma=False,
    )
```

```python
from functools import partial

import jax
import jax.numpy as jnp
from jax import lax
from jax.experimental import pallas as pl
from jax.experimental.pallas import tpu as pltpu
from jax.sharding import PartitionSpec as P

D = 1536
HEADS = 48
HEAD = 64
STATE = 128
KERNEL = 4
STRETCH = 256
STEP = 5
INNER = 3072
CONV = 3328
PROJ = 6448
DT_PAD = 128
SHARED = 2 * STATE + DT_PAD

NORM_EPS = 1e-05
FIRST_DECAY = 0.9
SECOND_DECAY = 0.999
ADAM_EPSILON = 1e-06
WEIGHT_DECAY = 0.01
LEARN_RATE = 0.5
F32 = jnp.float32
BF16 = jnp.bfloat16


def dot(a, b, dims=((1,), (0,))):
    return lax.dot_general(a, b, (dims, ((), ())), preferred_element_type=F32)


def split_dot(value, ones):
    high = value.astype(BF16)
    low = (value - high.astype(F32)).astype(BF16)
    return dot(high, ones) + dot(low, ones)


def tri_dot(ones, value):
    high = value.astype(BF16)
    rest = value - high.astype(F32)
    middle = rest.astype(BF16)
    low = (rest - middle.astype(F32)).astype(BF16)
    return dot(ones, high) + dot(ones, middle) + dot(ones, low)


def sigmoid(v):
    return 1.0 / (1.0 + jnp.exp(-v))


def softplus(v):
    return jnp.maximum(v, 0.0) + jnp.log1p(jnp.exp(-jnp.abs(v)))


def row_at_least():
    rows = lax.broadcasted_iota(jnp.int32, (STRETCH, STRETCH), 0)
    columns = lax.broadcasted_iota(jnp.int32, (STRETCH, STRETCH), 1)
    return rows >= columns


class Decays:
    def __init__(self, dt, rate, masks, spread):
        self.dt, self.spread = dt, spread
        lower = jnp.where(row_at_least(), 1.0, 0.0).astype(BF16)
        self.columns = dot(lower, dt) * rate
        self.rows = jnp.transpose(self.columns)
        last = self.columns[STRETCH - 1 :, :]
        self.into = jnp.exp(self.columns) * masks["carry"]
        self.out = jnp.exp(last - self.columns) * masks["tail"]
        self.through = jnp.broadcast_to(jnp.exp(last) * masks["keep"], (8, 128))
        self.bar = masks["bar"]

    def of(self, columns):
        ones = self.spread[:, columns]
        return (
            dot(self.dt, ones),
            split_dot(self.into, ones),
            split_dot(self.out, ones),
            split_dot(self.through, ones)[:1],
        )

    def between(self, head):
        return jnp.exp(self.columns[:, head : head + 1] - self.rows[head : head + 1, :] + self.bar)


EDGE = 8


def block_masks(seg_pad, seg_row, at):
    def rows(by, size=STRETCH):
        return seg_pad[pl.ds(at + EDGE + by, size), :]

    here = rows(0)
    first = jnp.where(at == 0, rows(0, 1), rows(-1, 1))
    last = rows(STRETCH - 1, 1)
    masks = {"carry": here == first, "tail": here == last, "keep": last == first}
    for by in range(1, KERNEL):
        masks[-by] = here == rows(-by)
        masks[by] = here == rows(by)
    masks = {key: jnp.where(value, 1.0, 0.0) for key, value in masks.items()}
    within = row_at_least() & (here == seg_row[:, pl.ds(at, STRETCH)])
    masks["bar"] = jnp.where(within, 0.0, -1e30)
    return masks


def forward_block(
    heads, at, normed, w_x, shared_columns, masks, packs, spread, outs, y_all, extended, state
):
    conv_pack, head_pack, chan_pack = packs
    pre_out, conv_out, dt_out, states_out = outs
    wide = heads * HEAD
    here = pl.ds(at, STRETCH)
    conv_low = jnp.concatenate([dot(normed, w_x[...]), dot(normed, shared_columns(0, 2 * STATE))], axis=1)
    conv_low = conv_low.astype(BF16)
    conv_out[...] = conv_low
    conv_in = conv_low.astype(F32)
    extended[8 : 8 + STRETCH, :] = conv_in
    pre = conv_pack[4:5, :] + conv_pack[3:4, :] * conv_in
    for by in range(1, KERNEL):
        pre = pre + conv_pack[3 - by : 4 - by, :] * (
            extended[8 - by : 8 - by + STRETCH, :] * masks[-by]
        )
    extended[0:8, :] = extended[STRETCH : STRETCH + 8, :]
    pre_out[...] = pre
    act = (pre * sigmoid(pre)).astype(BF16)
    b_mat = act[:, wide : wide + STATE]
    c_mat = act[:, wide + STATE :]
    lane = lax.broadcasted_iota(jnp.int32, (STRETCH, DT_PAD), 1)
    dt_pre = pltpu.roll(
        dot(normed, shared_columns(2 * STATE, DT_PAD)), DT_PAD - lax.axis_index("seq") * heads, 1
    )
    dt_pre = jnp.where(lane < heads, dt_pre, 0.0) + head_pack[0:1, :]
    dt_out[...] = dt_pre
    dt = softplus(dt_pre).astype(BF16)
    decay = Decays(dt, head_pack[1:2, :], masks, spread)
    scores = dot(c_mat, b_mat, ((1,), (1,)))
    first_half = lax.broadcasted_iota(jnp.int32, (STRETCH, 2 * HEAD), 1) < HEAD
    for pair in range(heads // 2):
        columns = slice(pair * 2 * HEAD, (pair + 1) * 2 * HEAD)
        steps, carry, tail, keep = decay.of(columns)
        xs = act[:, columns].astype(F32)
        scaled = xs * steps
        scaled_low = scaled.astype(BF16)
        old = state[:, columns]
        states_out[0, :, columns] = old
        y = dot(c_mat, old.astype(BF16)) * carry + chan_pack[0:1, columns] * xs
        state[:, columns] = old * keep + dot(b_mat, (scaled * tail).astype(BF16), ((0,), (0,)))
        halves = [
            dot((scores * decay.between(h)).astype(BF16), scaled_low)
            for h in (2 * pair, 2 * pair + 1)
        ]
        y_all[here, columns] = (y + jnp.where(first_half, halves[0], halves[1])).astype(BF16)


def fill_packs(heads, small, spread, packs, scratch_gain):
    conv_pack, head_pack, chan_pack = packs
    wide = heads * HEAD
    index = lax.axis_index("seq")
    start = pl.multiple_of(index * wide, 128)
    for ref in packs:
        ref[...] = jnp.zeros_like(ref)
    for k in range(KERNEL + 1):
        base = D + k * CONV
        conv_pack[k : k + 1, :wide] = small[:, pl.ds(base + start, wide)]
        conv_pack[k : k + 1, wide:] = small[:, base + INNER : base + CONV]
    base = D + (KERNEL + 1) * CONV
    window = jnp.broadcast_to(small[:, base : base + 256], (8, 256))
    lane = lax.broadcasted_iota(jnp.int32, (8, 256), 1)

    def own(k):
        moved = pltpu.roll(window, 256 - (k * HEADS + index * heads), 1)
        return jnp.where(lane < heads, moved, 0.0)[:, :128]

    head_pack[0:1, :] = own(0)[:1]
    rate = own(1)
    rate = jnp.where(lax.broadcasted_iota(jnp.int32, (8, 128), 1) < heads, -jnp.exp(rate), 0.0)
    head_pack[1:2, :] = rate[:1]
    chan_pack[0:1, :] = tri_spread(own(2), spread)[:1]
    base = base + 3 * HEADS
    shift = base % 128
    gain = jnp.broadcast_to(small[:, base - shift : base - shift + INNER + 128], (8, INNER + 128))
    scratch_gain[...] = pltpu.roll(gain, INNER + 128 - shift, 1)
    chan_pack[1:2, :] = scratch_gain[0:1, pl.ds(start, wide)]


def tri_spread(value, ones):
    high = value.astype(BF16)
    rest = value - high.astype(F32)
    middle = rest.astype(BF16)
    low = (rest - middle.astype(F32)).astype(BF16)
    return dot(high, ones) + dot(middle, ones) + dot(low, ones)


def as_row(column):
    lane = lax.broadcasted_iota(jnp.int32, (STRETCH, 128), 1)
    return jnp.transpose(jnp.where(lane == 0, column, 0.0))[0:8, :]


def as_column(rows):
    return jnp.transpose(jnp.concatenate([rows, jnp.zeros((120, STRETCH), F32)], axis=0))[:, 0:1]


def inverse_rms(squares):
    return lax.rsqrt(as_column(squares) / INNER + NORM_EPS)


def gate_gradients(y_low, z, d_mixed, gain, squares, products):
    rms = inverse_rms(squares)
    y = y_low.astype(F32)
    sig = sigmoid(z)
    silu = z * sig
    gated = y * silu
    unit = gated * rms
    d_gain = jnp.sum(d_mixed * unit, axis=0, keepdims=True)
    d_gated = d_mixed * gain * rms - unit * (rms * rms / INNER * as_column(products))
    d_z = d_gated * y * (sig * (1.0 + z * (1.0 - sig)))
    return (d_gated * silu).astype(BF16), d_z.astype(BF16), d_gain


def halved(rows, groups):
    return rows % (16 * groups) == 0


def forward_kernel(heads, *refs):
    tokens, cotangent, small, dt_weight, seg_pad, seg_row, spread_ref, in_weight, out_weight = refs[:9]
    outs = refs[9:13]
    d_y, d_z, normed_t, out_part, z_part, d_gain = refs[13:19]
    packs = refs[19:22]
    w_x_out, w_z_out, w_s_out, branch_part = refs[22:26]
    (
        stage_s, own_x, own_z, own_o, own_s, own_rows, w_x, w_z, w_o, w_s,
        shared_own, branch_stage, rows_all, returned_t, z_all, y_all, d_mixed_all, extended, state,
        scratch_gain, mixed_all, sums, got, stage_sems, sum_sends, sum_arrivals,
    ) = refs[26:52]
    sems = refs[52:]
    ring, seq = places()
    wide = heads * HEAD
    edge = wide + 2 * STATE
    step = pl.program_id(0)
    blocks = pl.num_programs(0) - 1
    length = rows_all.shape[0]
    count = length // STRETCH
    rows = own_x.shape[0]
    split = halved(rows, seq.major * seq.minor)
    stage_x, stage_z, stage_o = [d_mixed_all.at[pl.ds(k * rows, rows)] for k in range(3)]

    def shared_columns(start, size):
        if split:
            return w_s[:, :, :, start : start + size].reshape(D, size)
        return w_s[:, start : start + size]

    get_x = Gather(ring, own_x, w_x, rows, WEIGHT_PIECES, sems[:5])
    get_z = Gather(ring, own_z, w_z, rows, 1, sems[5:10])
    get_o = Gather(ring, own_o, w_o, rows, 1, sems[10:15])
    get_rows = Gather(seq, own_rows, rows_all, own_rows.shape[0], TOKEN_PIECES, sems[15:20])
    if split:
        get_s = Gather(ring, own_s, shared_own, own_s.shape[0], 1, sems[20:25])
        pass_s = Gather(
            seq, shared_own, w_s, shared_own.shape[0], 1, sems[25:30],
            lambda slot, piece: w_s.at[:, slot],
        )
    else:
        get_s = Gather(ring, own_s, w_s, rows, 1, sems[20:25])
    saves = [
        pltpu.make_async_copy(source, target, stage_sems.at[4 + k])
        for k, (source, target) in enumerate(((w_x, w_x_out), (w_z, w_z_out), (w_s, w_s_out)))
    ]
    spread = spread_ref[...]
    at = pl.multiple_of(step * STRETCH, STRETCH)

    @pl.when(step == 0)
    def _():
        start = pl.multiple_of(seq.index * wide, 128)
        own_shared = own_s.shape[0]
        first_row = pl.multiple_of(seq.index * own_shared, 16) if split else 0
        sources = [
            (in_weight.at[pl.ds(first_row, own_shared), pl.ds(2 * INNER, 2 * STATE)], stage_s),
            (in_weight.at[:, pl.ds(INNER + start, wide)], stage_x),
            (in_weight.at[:, pl.ds(start, wide)], stage_z),
            (out_weight.at[:, pl.ds(start, wide)], stage_o),
        ]
        loads = [
            pltpu.make_async_copy(source, target, stage_sems.at[k])
            for k, (source, target) in enumerate(sources)
        ]
        for load in loads:
            load.start()
        meet(ring, seq)
        loads[0].wait()
        own_s[:, : 2 * STATE] = stage_s[...].astype(BF16)
        own_s[:, 2 * STATE :] = dt_weight[pl.ds(first_row, own_shared), :]
        get_s.begin(0)
        get_s.keep().start()
        loads[1].wait()
        own_x[...] = stage_x[...].astype(BF16)
        for piece in range(WEIGHT_PIECES):
            get_x.begin(piece)
        get_x.keep().start()
        inputs = tokens[...].astype(F32)
        rms = lax.rsqrt(jnp.mean(inputs * inputs, axis=-1, keepdims=True) + NORM_EPS)
        own_rows[:, :D] = (inputs * rms * small[:, :D]).astype(BF16)
        own_rows[:, D:] = cotangent[...]
        for piece in range(TOKEN_PIECES):
            get_rows.begin(piece)
        get_rows.keep().start()
        loads[2].wait()
        loads[3].wait()
        own_z[...] = stage_z[...].astype(BF16)
        own_o[...] = stage_o[...].astype(BF16)
        get_z.keep().start()
        get_o.keep().start()
        fill_packs(heads, small, spread, packs, scratch_gain)
        state[...] = jnp.zeros_like(state)
        extended[0:8, :] = jnp.zeros((8, edge), F32)
        d_gain[...] = jnp.zeros_like(d_gain)
        get_s.forward(0)
        get_rows.forward(0)
        get_x.forward(0)
        get_s.finish()
        get_s.keep().wait()
        if split:
            pass_s.begin(0)
            pass_s.keep().start()
        get_rows.forward(1)
        get_x.forward(1)
        get_z.begin(0)
        get_rows.forward(2)
        get_x.forward(2)
        get_o.begin(0)
        for piece in range(3, TOKEN_PIECES):
            get_rows.forward(piece)
        if split:
            pass_s.forward(0)
        get_rows.finish()
        get_rows.keep().wait()

        def turn(k, _):
            here = pl.ds(pl.multiple_of(k * STRETCH, STRETCH), STRETCH)
            normed_t[:, here] = jnp.transpose(rows_all[here, :D])
            returned_t[:, here] = jnp.transpose(rows_all[here, D:])
            return 0

        lax.fori_loop(0, count, turn, 0)
        if split:
            pass_s.finish()
            pass_s.keep().wait()
        get_x.finish()
        get_x.keep().wait()
        saves[0].start()
        saves[2].start()

    @pl.when(step < blocks)
    def _():
        masks = block_masks(seg_pad, seg_row, at)
        forward_block(
            heads, at, rows_all[pl.ds(at, STRETCH), :D], w_x, shared_columns, masks, packs, spread, outs,
            y_all, extended, state,
        )

    forwards = [(stream, k) for stream in (get_z, get_o) for k in range(1, ring.major)]
    ahead = min(count, len(forwards))
    for k in range(ahead):

        @pl.when(step == k)
        def _():
            stream, by = forwards[k]
            stream.forward_step(0, by)

    @pl.when(step == blocks)
    def _():
        later = list(forwards[ahead:])
        while later and later[0][0] is get_z:
            stream, by = later.pop(0)
            stream.forward_step(0, by)
        get_z.finish()
        get_z.keep().wait()
        saves[1].start()
        levels = levels_of("seq")
        gain = packs[2][1:2, :]

        def chunk_rows(k):
            return pl.ds(pl.multiple_of(k * STRETCH, STRETCH), STRETCH)

        def gated_at(here):
            z = z_all[here, :]
            return y_all[here, :].astype(F32) * (z * sigmoid(z))

        def summed(which):
            base = which * (levels + 1)
            for level in range(levels):
                at = which * levels + level
                copy = exchange(
                    "seq", level, sums.at[base + level], got.at[at], sum_sends.at[at], sum_arrivals.at[at]
                )
                copy.start()
                copy.wait()
                sums[base + level + 1] = sums[base + level] + got[at]
            return base + levels

        def gate(k, _):
            here = chunk_rows(k)
            z_all[here, :] = dot(rows_all[here, :D], w_z[...])
            gated = gated_at(here)
            sums[0, :, here] = as_row(jnp.sum(gated * gated, axis=1, keepdims=True))
            return 0

        lax.fori_loop(0, count, gate, 0)
        if later:
            stream, by = later.pop(0)
            stream.forward_step(0, by)
        squares = summed(0)

        def mix(k, _):
            here = chunk_rows(k)
            mixed_all[here, :] = (
                gated_at(here) * inverse_rms(sums[squares, :, here]) * gain
            ).astype(BF16)
            return 0

        lax.fori_loop(0, count, mix, 0)
        for stream, by in later:
            stream.forward_step(0, by)

        def contract_out(k, _):
            here = pl.ds(pl.multiple_of(k * 256, 256), 256)
            out_part[here, :] = dot(returned_t[here, :], mixed_all[...]).astype(BF16)
            return 0

        lax.fori_loop(0, D // 256, contract_out, 0)
        get_o.finish()
        get_o.keep().wait()

        def measure(k, _):
            here = chunk_rows(k)
            d_mixed = dot(rows_all[here, D:], w_o[...])
            d_mixed_all[here, :] = d_mixed
            product = jnp.sum(d_mixed * gain * gated_at(here), axis=1, keepdims=True)
            sums[levels + 1, :, here] = as_row(product)
            return 0

        lax.fori_loop(0, count, measure, 0)
        products = summed(1)

        def differentiate(k, _):
            here = chunk_rows(k)
            d_y_block, d_z_block, d_gain_block = gate_gradients(
                y_all[here, :], z_all[here, :], d_mixed_all[here, :], gain,
                sums[squares, :, here], sums[products, :, here],
            )
            d_y[here, :] = d_y_block
            d_z[here, :] = d_z_block
            d_gain[0:1, :] += d_gain_block
            branch_stage[...] = dot(mixed_all[here, :], w_o[...], ((1,), (1,))).astype(BF16)
            out = pltpu.make_async_copy(branch_stage, branch_part.at[here], stage_sems.at[7])
            out.start()
            out.wait()
            return 0

        lax.fori_loop(0, count, differentiate, 0)

        def contract_z(k, _):
            here = pl.ds(pl.multiple_of(k * 256, 256), 256)
            z_part[here, :] = dot(normed_t[here, :], d_z[...]).astype(BF16)
            return 0

        lax.fori_loop(0, D // 256, contract_z, 0)
        for save in saves:
            save.wait()


def backward_block(
    heads,
    d_y_ref,
    pre_ref,
    conv_ref,
    dt_ref,
    states,
    seg_pad,
    seg_row,
    conv_pack,
    head_pack,
    chan_pack,
    spread_ref,
    gather_ref,
    d_conv_out,
    d_head_out,
    extended,
    d_state,
    d_rest,
):
    wide = heads * HEAD
    edge = wide + 2 * STATE

    @pl.when(pl.program_id(0) == 0)
    def _():
        d_state[...] = jnp.zeros_like(d_state)
        extended[STRETCH : STRETCH + 8, :] = jnp.zeros((8, edge), F32)
        d_conv_out[...] = jnp.zeros_like(d_conv_out)
        d_head_out[...] = jnp.zeros_like(d_head_out)

    at_row = pl.multiple_of((pl.num_programs(0) - 1 - pl.program_id(0)) * STRETCH, STRETCH)
    masks = block_masks(seg_pad, seg_row, at_row)
    spread = spread_ref[...]
    gather = gather_ref[...]
    pre = pre_ref[...]
    act = (pre * sigmoid(pre)).astype(BF16)
    b_mat = act[:, wide : wide + STATE]
    c_mat = act[:, wide + STATE :]
    dt_pre = dt_ref[...]
    dt = softplus(dt_pre).astype(BF16)
    rate = head_pack[1:2, :]
    decay = Decays(dt, rate, masks, spread)
    scores = dot(c_mat, b_mat, ((1,), (1,)))
    lane = lax.broadcasted_iota(jnp.int32, (STRETCH, 128), 1)
    first_half = lane < HEAD
    d_b = jnp.zeros((STRETCH, STATE), F32)
    d_c = jnp.zeros((STRETCH, STATE), F32)
    d_scores = jnp.zeros((STRETCH, STRETCH), F32)
    d_cum = jnp.zeros((STRETCH, 128), F32)
    d_dt = jnp.zeros((STRETCH, 128), F32)
    d_last = jnp.zeros((1, 128), F32)
    column_sums = []
    for pair in range(heads // 2):
        columns = slice(pair * 2 * HEAD, (pair + 1) * 2 * HEAD)
        ones = gather[columns, :]
        steps, carry, tail, keep = decay.of(columns)
        xs = act[:, columns].astype(F32)
        scaled = xs * steps
        scaled_low = scaled.astype(BF16)
        old = states[0, :, columns]
        old_low = old.astype(BF16)
        d_new = d_state[:, columns]
        d_new_low = d_new.astype(BF16)
        d_y_low = d_y_ref[:, columns]
        d_y = d_y_low.astype(F32)
        d_carried = d_y * carry
        d_carried_low = d_carried.astype(BF16)
        d_c = d_c + dot(d_carried_low, old_low, ((1,), (1,)))
        d_cum = d_cum + split_dot(d_carried * dot(c_mat, old_low), ones)
        weighed = scaled * tail
        into = dot(b_mat, d_new_low)
        d_b = d_b + dot(weighed.astype(BF16), d_new_low, ((1,), (1,)))
        tail_part = split_dot(weighed * into, ones)
        d_cum = d_cum - tail_part
        kept = jnp.sum(d_new * old, axis=0, keepdims=True) * keep
        kept = split_dot(jnp.broadcast_to(kept, (8, 128)), ones)[:1]
        d_last = d_last + jnp.sum(tail_part, axis=0, keepdims=True) + kept
        d_state[:, columns] = d_new * keep + dot(c_mat, d_carried_low, ((0,), (0,)))
        halves = []
        for h in (2 * pair, 2 * pair + 1):
            between = decay.between(h)
            weights = scores * between
            halves.append(dot(weights.astype(BF16), d_y_low, ((0,), (0,))))
            d_y_head = jnp.where(first_half == (h % 2 == 0), d_y_low, jnp.zeros_like(d_y_low))
            d_weights = dot(d_y_head, scaled_low, ((1,), (1,)))
            d_scores = d_scores + d_weights * between
            product = d_weights * weights
            d_cum = d_cum + jnp.where(lane == h, jnp.sum(product, axis=1, keepdims=True), 0.0)
            column_sums.append(jnp.sum(product, axis=0, keepdims=True))
        d_scaled = into * tail + jnp.where(first_half, halves[0], halves[1])
        d_xs = d_scaled * steps + chan_pack[0:1, columns] * d_y
        extended[0:STRETCH, columns] = d_xs.astype(BF16).astype(F32)
        d_dt = d_dt + split_dot(d_scaled * xs, ones)
        d_skip = jnp.sum(d_y * xs, axis=0, keepdims=True)
        d_head_out[2:3, :] += split_dot(jnp.broadcast_to(d_skip, (8, 128)), ones)[:1]
    column_sums.append(jnp.zeros((128 - heads, STRETCH), F32))
    d_cum = d_cum - jnp.transpose(jnp.concatenate(column_sums, axis=0))
    row = lax.broadcasted_iota(jnp.int32, (STRETCH, 128), 0)
    d_cum = d_cum + jnp.where(row == STRETCH - 1, d_last, 0.0)
    d_scores_low = d_scores.astype(BF16)
    d_c = d_c + dot(d_scores_low, b_mat)
    d_b = d_b + dot(d_scores_low, c_mat, ((0,), (0,)))

    rows = lax.broadcasted_iota(jnp.int32, (STRETCH, STRETCH), 0)
    upper = jnp.where(rows <= lax.broadcasted_iota(jnp.int32, (STRETCH, STRETCH), 1), 1.0, 0.0)
    d_dt = d_dt + rate * tri_dot(upper.astype(BF16), d_cum)
    d_dt_raw = d_dt.astype(BF16).astype(F32) * sigmoid(dt_pre)
    d_head_out[0:1, :] += jnp.sum(d_dt_raw, axis=0, keepdims=True)
    d_head_out[1:2, :] += jnp.sum(d_cum * decay.columns, axis=0, keepdims=True)

    extended[0:STRETCH, wide : wide + STATE] = d_b
    extended[0:STRETCH, wide + STATE :] = d_c
    here = pl.ds(at_row, STRETCH)
    moved = pltpu.roll(jnp.where(lane < heads, d_dt_raw, 0.0), lax.axis_index("seq") * heads, 1)
    d_rest[here, edge:] = moved.astype(BF16)

    def convolve_back(at, _):
        columns = pl.ds(pl.multiple_of(at * 128, 128), 128)
        value = pre_ref[:, columns]
        gate = sigmoid(value)
        d_pre = extended[0:STRETCH, columns] * (gate * (1.0 + value * (1.0 - gate)))
        extended[0:STRETCH, columns] = d_pre
        conv_in = conv_ref[:, columns].astype(F32)
        d_conv_in = conv_pack[3:4, columns] * d_pre
        d_conv_out[3:4, columns] += jnp.sum(d_pre * conv_in, axis=0, keepdims=True)
        d_conv_out[4:5, columns] += jnp.sum(d_pre, axis=0, keepdims=True)
        for by in range(1, KERNEL):
            moved = extended[by : by + STRETCH, columns] * masks[by]
            d_conv_in = d_conv_in + conv_pack[3 - by : 4 - by, columns] * moved
            d_conv_out[3 - by : 4 - by, columns] += jnp.sum(moved * conv_in, axis=0, keepdims=True)
        extended[STRETCH : STRETCH + 8, columns] = extended[0:8, columns]
        d_rest[here, columns] = d_conv_in.astype(BF16)
        return 0

    lax.fori_loop(0, edge // 128, convolve_back, 0)


VMEM_BYTES = 56 * 1024 * 1024


def block(columns, reverse=0):
    if reverse:
        return pl.BlockSpec((STRETCH, columns), lambda i: (reverse - 1 - i, 0))
    return pl.BlockSpec((STRETCH, columns), lambda i: (i, 0))


def whole(*shape):
    return pl.BlockSpec(shape, lambda i: (0,) * len(shape))


def compiler_params():
    return pltpu.CompilerParams(
        vmem_limit_bytes=VMEM_BYTES, dimension_semantics=("arbitrary",)
    )


class Place:
    def __init__(self, axis, minor):
        self.axis = axis
        self.minor = minor
        self.major = lax.axis_size(axis) // minor
        index = lax.axis_index(axis)
        self.at_major = index // minor
        self.at_minor = index % minor
        self.index = index

    def slot(self, by_major, by_minor):
        return (self.at_major + by_major) % self.major * self.minor + (
            self.at_minor + by_minor
        ) % self.minor

    def others(self):
        along = [self.slot(step, 0) for step in range(1, self.major)]
        return along + [self.slot(0, step) for step in range(1, self.minor)]


def places():
    ring = lax.axis_size("fsdp")
    side = 1
    while 2 * side * 2 * side * 2 <= ring:
        side = 2 * side
    return Place("fsdp", side), Place("seq", 2)


def meet(*all_places):
    barrier = pltpu.get_barrier_semaphore()
    count = 0
    for place in all_places:
        for other in place.others():
            pl.semaphore_signal(
                barrier, inc=1, device_id={place.axis: other}, device_id_type=pl.DeviceIdType.MESH
            )
            count = count + 1
    pl.semaphore_wait(barrier, count)


def send(place, source, target, to, sends, arrivals, at):
    return pltpu.make_async_remote_copy(
        src_ref=source,
        dst_ref=target,
        send_sem=sends.at[at],
        recv_sem=arrivals.at[at],
        device_id={place.axis: to},
        device_id_type=pl.DeviceIdType.MESH,
    )


class Gather:
    def __init__(self, place, own, full, rows, pieces, sems, target=None):
        self.place, self.own, self.full, self.landing = place, own, full, target
        self.size, self.pieces = rows // pieces, pieces
        self.sends1, self.arrivals1, self.sends2, self.arrivals2, self.here = sems

    @staticmethod
    def scratch(place, pieces):
        first = max(place.major - 1, 1) * pieces
        second = place.major * (place.minor - 1) * pieces
        dma = pltpu.SemaphoreType.DMA
        return [dma((first,)), dma((first,)), dma((second,)), dma((second,)), dma((1,))]

    def rows(self, piece):
        return pl.ds(piece * self.size, self.size)

    def target(self, slot, piece):
        if self.landing is not None:
            return self.landing(slot, piece)
        if len(self.full.shape) > len(self.own.shape):
            return self.full.at[slot, self.rows(piece)]
        start = slot * (self.size * self.pieces) + piece * self.size
        return self.full.at[pl.ds(pl.multiple_of(start, 16), self.size)]

    def along(self, piece, step):
        place = self.place
        return send(
            place,
            self.own.at[self.rows(piece)],
            self.target(place.index, piece),
            place.slot(step, 0),
            self.sends1,
            self.arrivals1,
            piece * (place.major - 1) + step - 1,
        )

    def across(self, piece, step, across):
        place = self.place
        slot = place.slot(-step, 0)
        target = self.target(slot, piece)
        source = self.own.at[self.rows(piece)] if step == 0 else target
        at = (piece * place.major + step) * (place.minor - 1) + across - 1
        return send(
            place, source, target, place.slot(0, across), self.sends2, self.arrivals2, at
        )

    def keep(self):
        if self.landing is not None:
            target = self.landing(self.place.index, 0)
        elif len(self.full.shape) > len(self.own.shape):
            target = self.full.at[self.place.index]
        else:
            size = self.size * self.pieces
            target = self.full.at[pl.ds(pl.multiple_of(self.place.index * size, 16), size)]
        return pltpu.make_async_copy(self.own, target, self.here.at[0])

    def begin(self, piece):
        for step in range(1, self.place.major):
            self.along(piece, step).start()
        for across in range(1, self.place.minor):
            self.across(piece, 0, across).start()

    def forward(self, piece):
        for step in range(1, self.place.major):
            self.forward_step(piece, step)

    def forward_step(self, piece, step):
        self.along(piece, step).wait_recv()
        for across in range(1, self.place.minor):
            self.across(piece, step, across).start()

    def finish(self):
        for piece in range(self.pieces):
            for step in range(1, self.place.major):
                self.along(piece, step).wait_send()
            for step in range(self.place.major):
                for across in range(1, self.place.minor):
                    self.across(piece, step, across).wait()


class Reduce:
    def __init__(self, place, part, total, rows, pieces, scratch, loads=None):
        self.place, self.part, self.total, self.loads = place, part, total, loads
        self.size, self.pieces = rows // pieces, pieces
        self.got1, self.mine, self.got2, self.sends1, self.arrivals1, self.sends2, self.arrivals2 = (
            scratch
        )

    @staticmethod
    def scratch(place, rows, columns, pieces):
        dma = pltpu.SemaphoreType.DMA
        first = place.major * (place.minor - 1)
        second = max(place.major - 1, 1)
        return [
            pltpu.VMEM((first, rows, columns), BF16),
            pltpu.VMEM((second, rows, columns), BF16),
            pltpu.VMEM((second, rows, columns), BF16),
            dma((first * pieces,)),
            dma((first * pieces,)),
            dma((second * pieces,)),
            dma((second * pieces,)),
        ]

    def items(self):
        return [(piece, step) for step in self.steps() for piece in range(self.pieces)]

    def piece_items(self):
        return [(piece, step) for piece in range(self.pieces) for step in self.steps()]

    def steps(self):
        return list(range(1, self.place.major)) + [0]

    def rows(self, piece):
        return pl.ds(piece * self.size, self.size)

    def part_rows(self, slot, rows_start, size):
        if len(self.part.shape) == 3:
            return slot, pl.ds(rows_start, size)
        start = slot * (self.size * self.pieces) + rows_start
        return (pl.ds(pl.multiple_of(start, 16), size),)

    def across(self, item, across):
        piece, step = item
        place = self.place
        slot = step * (place.minor - 1) + across - 1
        index = self.part_rows(place.slot(step, across), piece * self.size, self.size)
        return send(
            place,
            self.part.at[index],
            self.got1.at[slot, self.rows(piece)],
            place.slot(0, across),
            self.sends1,
            self.arrivals1,
            slot * self.pieces + piece,
        )

    def along(self, item):
        piece, step = item
        place = self.place
        return send(
            place,
            self.mine.at[step - 1, self.rows(piece)],
            self.got2.at[step - 1, self.rows(piece)],
            place.slot(step, 0),
            self.sends2,
            self.arrivals2,
            (step - 1) * self.pieces + piece,
        )

    def begin(self, item):
        for across in range(1, self.place.minor):
            self.across(item, across).start()
        if self.loads is not None:
            self.load(item[1]).start()

    def load(self, step):
        target = self.mine.at[step - 1] if step else self.total
        return pltpu.make_async_copy(
            self.part.at[self.place.slot(step, 0)], target, self.loads.at[step]
        )

    def own(self, step, rows):
        if self.loads is None:
            return self.part[self.part_rows(self.place.slot(step, 0), rows, 16)].astype(F32)
        source = self.mine.at[step - 1] if step else self.total
        return source[pl.ds(rows, 16)].astype(F32)

    def blocks(self, piece, body):
        def one(at, _):
            body(pl.multiple_of(piece * self.size + at * 16, 16))
            return 0

        lax.fori_loop(0, self.size // 16, one, 0)

    def handle(self, item):
        piece, step = item
        place = self.place
        for across in range(1, place.minor):
            self.across(item, across).wait_recv()
        if self.loads is not None:
            self.load(step).wait()
        if step == 0:
            return

        def body(start):
            value = self.own(step, start)
            rows = pl.ds(start, 16)
            for across in range(1, place.minor):
                slot = step * (place.minor - 1) + across - 1
                value = value + self.got1[slot, rows].astype(F32)
            self.mine[step - 1, rows] = value.astype(BF16)

        self.blocks(piece, body)
        self.along(item).start()

    def close(self, piece):
        place = self.place
        for step in range(1, place.major):
            self.along((piece, step)).wait_recv()

        def body(start):
            value = self.own(0, start)
            rows = pl.ds(start, 16)
            for across in range(1, place.minor):
                value = value + self.got1[across - 1, rows].astype(F32)
            for step in range(1, place.major):
                value = value + self.got2[step - 1, rows].astype(F32)
            self.total[rows] = value.astype(self.total.dtype)

        self.blocks(piece, body)

    def finish(self):
        for item in self.items():
            for across in range(1, self.place.minor):
                self.across(item, across).wait_send()
            if item[1]:
                self.along(item).wait_send()


WEIGHT_PIECES = 3
TOKEN_PIECES = 4
HBM = pl.BlockSpec(memory_space=pl.ANY)
VMEM = pl.BlockSpec(memory_space=pltpu.VMEM)


def comm_params(number):
    return pltpu.CompilerParams(
        collective_id=number, has_side_effects=True, vmem_limit_bytes=VMEM_BYTES
    )


def resident(x):
    return pl.BlockSpec(
        x.shape, lambda i: (0,) * len(x.shape), pipeline_mode=pl.Buffered(buffer_count=1)
    )


def run_forward(heads, tokens, cotangent, small, dt_weight, seg_pad, seg_row, spread, in_weight, out_weight):
    ring, seq = places()
    count, groups = lax.axis_size("fsdp"), lax.axis_size("seq")
    rows, own_rows = in_weight.shape[0], tokens.shape[0]
    length = own_rows * groups
    blocks = length // STRETCH
    wide = heads * HEAD
    edge = wide + 2 * STATE
    levels = levels_of("seq")
    shape = jax.ShapeDtypeStruct
    split = halved(rows, groups)
    own_shared = rows // groups if split else rows
    shared_shape = (count, groups, own_shared, SHARED) if split else (D, SHARED)

    def chunk(columns):
        return pl.BlockSpec((STRETCH, columns), lambda i: (i - i // blocks, 0))

    wholes = [tokens, cotangent, small, dt_weight, seg_pad, seg_row, spread]
    late = [
        shape((length, wide), BF16),
        shape((length, wide), BF16),
        shape((D, length), BF16),
        shape((D, wide), BF16),
        shape((D, wide), BF16),
        shape((8, wide), F32),
        shape((8, edge), F32),
        shape((8, 128), F32),
        shape((8, wide), F32),
    ]
    dma = pltpu.SemaphoreType.DMA
    scratch = [
        pltpu.VMEM((own_shared, 2 * STATE), F32),
        pltpu.VMEM((rows, wide), BF16),
        pltpu.VMEM((rows, wide), BF16),
        pltpu.VMEM((rows, wide), BF16),
        pltpu.VMEM((own_shared, SHARED), BF16),
        pltpu.VMEM((own_rows, 2 * D), BF16),
        pltpu.VMEM((D, wide), BF16),
        pltpu.VMEM((D, wide), BF16),
        pltpu.VMEM((D, wide), BF16),
        pltpu.VMEM(shared_shape, BF16),
        pltpu.VMEM((count, own_shared, SHARED) if split else (16, 128), BF16),
        pltpu.VMEM((STRETCH, D), BF16),
        pltpu.VMEM((length, 2 * D), BF16),
        pltpu.VMEM((D, length), BF16),
        pltpu.VMEM((length, wide), F32),
        pltpu.VMEM((length, wide), BF16),
        pltpu.VMEM((length, wide), F32),
        pltpu.VMEM((STRETCH + 8, edge), F32),
        pltpu.VMEM((STATE, wide), F32),
        pltpu.VMEM((8, INNER + 128), F32),
        pltpu.VMEM((length, wide), BF16),
        pltpu.VMEM((2 * (levels + 1), 8, length), F32),
        pltpu.VMEM((2 * levels, 8, length), F32),
        dma((8,)),
        dma((2 * levels,)),
        dma((2 * levels,)),
    ]
    scratch = scratch + Gather.scratch(ring, WEIGHT_PIECES) + Gather.scratch(ring, 1)
    scratch = scratch + Gather.scratch(ring, 1) + Gather.scratch(seq, TOKEN_PIECES)
    scratch = scratch + Gather.scratch(ring, 1) + Gather.scratch(seq, 1)
    return pl.pallas_call(
        partial(forward_kernel, heads),
        grid=(blocks + 1,),
        in_specs=[resident(x) for x in wholes] + [HBM, HBM],
        out_specs=[
            chunk(edge),
            chunk(edge),
            chunk(128),
            pl.BlockSpec((1, STATE, wide), lambda i: (i - i // blocks, 0, 0)),
        ]
        + [resident(x) for x in late]
        + [HBM] * 4,
        out_shape=[
            shape((length, edge), F32),
            shape((length, edge), BF16),
            shape((length, 128), F32),
            shape((blocks, STATE, wide), F32),
        ]
        + late
        + [shape((D, wide), BF16), shape((D, wide), BF16), shape(shared_shape, BF16)]
        + [shape((length, D), BF16)],
        scratch_shapes=scratch,
        compiler_params=pltpu.CompilerParams(
            collective_id=1,
            has_side_effects=True,
            vmem_limit_bytes=61 * 1024 * 1024,
            dimension_semantics=("arbitrary",),
        ),
        name="gather_and_forward",
    )(*wholes, in_weight, out_weight)


def backward_kernel(heads, *refs):
    chunk = refs[:5]
    packs = refs[5:12]
    d_z, w_z, w_x, w_s, normed_t, tokens, small, d_gain = refs[12:20]
    out_part, z_part, branch_part = refs[20:23]
    out_all, z_all, x_all, s_all, small_all, branch, d_normed, d_conv, d_head = refs[23:32]
    extended, d_state, d_rest, x_part, s_part, act_part, out_own, z_own, x_own, s_own, s_mid = refs[32:43]
    small_sums, small_got, small_sends, small_arrivals, out_loads, z_loads, branch_loads = refs[43:50]
    scratch = refs[50:]
    ring, seq = places()
    rows = x_own.shape[0]
    own_rows = act_part.shape[1]
    wide = heads * HEAD
    edge = wide + 2 * STATE
    groups = seq.major * seq.minor
    own_shared = s_own.shape[0]
    split = halved(rows, groups)
    levels = levels_of("fsdp")

    def stream(place, part, total, extent, pieces, at, loads=None):
        return Reduce(place, part, total, extent, pieces, scratch[7 * at : 7 * at + 7], loads)

    def spreading(own, full, pieces, at):
        return Gather(seq, own, full, own.shape[0], pieces, scratch[49 + 5 * at : 54 + 5 * at])

    out_sum = stream(ring, out_part, out_own, rows, 1, 0, out_loads)
    z_sum = stream(ring, z_part, z_own, rows, 1, 1, z_loads)
    x_sum = stream(ring, x_part, x_own, rows, WEIGHT_PIECES, 2)
    branch_sum = stream(seq, branch_part, branch, own_rows, 1, 3, branch_loads)
    d_normed_sum = stream(seq, act_part, d_normed, own_rows, 2, 4)
    if split:
        mid_sum = stream(seq, s_part, s_mid, s_mid.shape[0], 1, 5)
        s_sum = stream(ring, s_mid, s_own, own_shared, 1, 6)
    else:
        s_sum = stream(ring, s_part, s_own, rows, 1, 6)
    out_spread = spreading(out_own, out_all, 1, 0)
    z_spread = spreading(z_own, z_all, 1, 1)
    x_spread = spreading(x_own, x_all, WEIGHT_PIECES, 2)
    s_spread = spreading(s_own, s_all, 1, 3)
    small_spread = spreading(small_sums.at[levels], small_all, 1, 4)
    early = [(s, item) for s in (out_sum, z_sum) for item in s.items()]
    at_step = pl.program_id(0)
    blocks = d_rest.shape[0] // STRETCH

    def swap(level):
        return exchange(
            "fsdp",
            level,
            small_sums.at[level],
            small_got.at[level],
            small_sends.at[level],
            small_arrivals.at[level],
        )

    @pl.when(at_step == 0)
    def _():
        meet(ring, seq)
        for s, item in early:
            s.begin(item)
        for item in branch_sum.items():
            branch_sum.begin(item)

    backward_block(heads, *chunk, *packs, d_conv, d_head, extended, d_state, d_rest)

    for k in range(blocks):

        @pl.when(at_step == k)
        def _():
            s, item = early[k]
            s.handle(item)
            if k == blocks - 1:
                for item in branch_sum.items():
                    branch_sum.handle(item)
                branch_sum.close(0)
                branch_sum.finish()

    @pl.when(at_step == blocks - 1)
    def _():
        def x_block(slot):
            here = pl.ds(pl.multiple_of(slot * rows, 16), rows)

            def one(at, _):
                columns = pl.ds(pl.multiple_of(at * 384, 128), 384)
                x_part[slot, :, columns] = dot(normed_t[here, :], d_rest[:, columns]).astype(BF16)
                return 0

            lax.fori_loop(0, wide // 384, one, 0)

        def s_block(slot, _):
            here = pl.ds(pl.multiple_of(slot * rows, 16), rows)
            value = dot(normed_t[here, :], d_rest[:, wide:]).astype(BF16)
            if split:
                target = pl.ds(pl.multiple_of(slot * own_shared, 16), own_shared)
                for s in range(groups):
                    s_part[s, target, :] = value[s * own_shared : (s + 1) * own_shared]
            else:
                s_part[slot] = value
            return 0

        def normed_block(slot):
            here = pl.ds(pl.multiple_of(slot * own_rows, own_rows), own_rows)

            def one(at, _):
                columns = pl.ds(pl.multiple_of(at * 512, 128), 512)
                value = dot(d_z[here, :], w_z[columns, :], ((1,), (1,)))
                value = value + dot(d_rest[here, :wide], w_x[columns, :], ((1,), (1,)))
                value = value + dot(d_rest[here, wide:], w_s[columns, :], ((1,), (1,)))
                act_part[slot, :, columns] = value.astype(BF16)
                return 0

            lax.fori_loop(0, D // 512, one, 0)

        waiting = early[blocks:]

        def handle_early(amount=1):
            for _ in range(min(amount, len(waiting))):
                s, item = waiting.pop(0)
                s.handle(item)

        lax.fori_loop(0, ring.major * ring.minor, s_block, 0)
        if split:
            for item in mid_sum.items():
                mid_sum.begin(item)
        else:
            for item in s_sum.items():
                s_sum.begin(item)
        handle_early()
        for step in x_sum.steps():
            for across in range(1, ring.minor):
                x_block(ring.slot(step, across))
        for item in x_sum.piece_items():
            x_sum.begin(item)
        if split:
            for item in mid_sum.items():
                mid_sum.handle(item)
        handle_early()
        for step in d_normed_sum.steps():
            for across in range(1, seq.minor):
                normed_block(seq.slot(step, across))
            for piece in range(2):
                d_normed_sum.begin((piece, step))
        if split:
            mid_sum.close(0)
            for item in s_sum.items():
                s_sum.begin(item)
        handle_early()
        for step in x_sum.steps():
            x_block(ring.slot(step, 0))
        for step in d_normed_sum.steps():
            normed_block(seq.slot(step, 0))
        handle_early(len(waiting))
        out_sum.close(0)
        out_spread.begin(0)
        side = d_normed_sum.items() + [None] * (2 + levels)
        work = [(x_sum, item) for item in x_sum.piece_items()] + [(s_sum, item) for item in s_sum.items()]

        def sideways(at):
            first = len(d_normed_sum.items())
            if at < first:
                d_normed_sum.handle(side[at])
                return
            if at == first:
                for piece in range(2):
                    d_normed_sum.close(piece)
                inputs = tokens[...].astype(F32)
                rms = lax.rsqrt(jnp.mean(inputs * inputs, axis=-1, keepdims=True) + NORM_EPS)
                small_sums[0] = jnp.zeros(small_sums.shape[1:], F32)
                small_sums[0, 0 : KERNEL + 1, :edge] = d_conv[0 : KERNEL + 1, :]
                small_sums[0, 5:6, :] = jnp.sum(
                    d_normed[...].astype(F32) * (inputs * rms), axis=0, keepdims=True
                )
                small_sums[0, 6:7, :wide] = d_gain[0:1, :]
                for k in range(3):
                    small_sums[0, 7:8, 128 * k : 128 * (k + 1)] = d_head[k : k + 1, :]
                swap(0).start()
                return
            level = at - first - 1
            if level < levels:
                swap(level).wait()
                small_sums[level + 1] = small_sums[level] + small_got[level]
                if level + 1 < levels:
                    swap(level + 1).start()
                else:
                    small_spread.begin(0)
                    small_spread.keep().start()

        done = 0
        for at, (s, item) in enumerate(work):
            s.handle(item)
            sideways(at)
            done = at + 1
            if at == WEIGHT_PIECES:
                z_sum.close(0)
                z_spread.begin(0)
                out_spread.forward(0)
            if s is x_sum and item[0] and item[1] == 2:
                x_sum.close(item[0] - 1)
                x_spread.begin(item[0] - 1)
        x_sum.close(WEIGHT_PIECES - 1)
        x_spread.begin(WEIGHT_PIECES - 1)
        for at in range(done, len(side)):
            sideways(at)
        s_sum.close(0)
        s_spread.begin(0)
        spreads = (out_spread, z_spread, x_spread, s_spread)
        for s in spreads:
            s.keep().start()
        z_spread.forward(0)
        small_spread.forward(0)
        for piece in range(WEIGHT_PIECES):
            x_spread.forward(piece)
        s_spread.forward(0)
        for s in (out_sum, z_sum, x_sum, s_sum, d_normed_sum):
            s.finish()
        if split:
            mid_sum.finish()
        for s in spreads + (small_spread,):
            s.finish()
            s.keep().wait()


def run_backward(
    heads, d_y, pre, conv, dt_pre, states, seg_pad, seg_row, packs, spread, d_z, weights, normed_t,
    tokens, small, d_gain, out_part, z_part, branch_part,
):
    length = d_y.shape[0]
    blocks = length // STRETCH
    wide = heads * HEAD
    edge = wide + 2 * STATE
    ring, seq = places()
    count, groups = lax.axis_size("fsdp"), lax.axis_size("seq")
    levels = levels_of("fsdp")

    def parted(x, by):
        return x.reshape(by, x.shape[0] // by, x.shape[1])

    out_part, z_part = parted(out_part, count), parted(z_part, count)
    branch_part = parted(branch_part, groups)
    rows, own_rows = out_part.shape[1], branch_part.shape[1]
    split = halved(rows, groups)
    own_shared = rows // groups if split else rows
    mid_rows = own_shared * count if split else 16
    wholes = [
        seg_pad, seg_row, *packs, spread, spread.T, d_z, *weights, normed_t, tokens, small, d_gain
    ]
    dma = pltpu.SemaphoreType.DMA
    scratch = [
        pltpu.VMEM((STRETCH + 8, edge), F32),
        pltpu.VMEM((STATE, wide), F32),
        pltpu.VMEM((length, wide + SHARED), BF16),
        pltpu.VMEM((count, rows, wide), BF16),
        pltpu.VMEM((groups, mid_rows, SHARED) if split else (count, rows, SHARED), BF16),
        pltpu.VMEM((groups, own_rows, D), BF16),
        pltpu.VMEM((rows, wide), BF16),
        pltpu.VMEM((rows, wide), BF16),
        pltpu.VMEM((rows, wide), BF16),
        pltpu.VMEM((own_shared, SHARED), BF16),
        pltpu.VMEM((mid_rows, SHARED), BF16),
        pltpu.VMEM((levels + 1, 8, D), F32),
        pltpu.VMEM((levels, 8, D), F32),
        dma((levels,)),
        dma((levels,)),
        dma((ring.major,)),
        dma((ring.major,)),
        dma((seq.major,)),
    ]
    scratch = scratch + Reduce.scratch(ring, rows, wide, 1) + Reduce.scratch(ring, rows, wide, 1)
    scratch = scratch + Reduce.scratch(ring, rows, wide, WEIGHT_PIECES)
    scratch = scratch + Reduce.scratch(seq, own_rows, D, 1) + Reduce.scratch(seq, own_rows, D, 2)
    scratch = scratch + Reduce.scratch(seq, mid_rows, SHARED, 1)
    scratch = scratch + Reduce.scratch(ring, own_shared, SHARED, 1)
    for pieces in (1, 1, WEIGHT_PIECES, 1, 1):
        scratch = scratch + Gather.scratch(seq, pieces)
    shape = jax.ShapeDtypeStruct
    gathered = [
        shape((groups, rows, wide), BF16),
        shape((groups, rows, wide), BF16),
        shape((groups, rows, wide), BF16),
        shape((groups, own_shared, SHARED), BF16),
        shape((groups, 8, D), F32),
    ]
    summed = [
        shape((own_rows, D), BF16),
        shape((own_rows, D), BF16),
        shape((8, edge), F32),
        shape((8, 128), F32),
    ]
    return pl.pallas_call(
        partial(backward_kernel, heads),
        grid=(blocks,),
        in_specs=[
            block(wide, blocks),
            block(edge, blocks),
            block(edge, blocks),
            block(128, blocks),
            pl.BlockSpec((1, STATE, wide), lambda i: (blocks - 1 - i, 0, 0)),
        ]
        + [resident(x) for x in wholes]
        + [HBM] * 3,
        out_specs=[HBM] * 5 + [resident(x) for x in summed],
        out_shape=gathered + summed,
        scratch_shapes=scratch,
        compiler_params=pltpu.CompilerParams(
            collective_id=2,
            has_side_effects=True,
            vmem_limit_bytes=61 * 1024 * 1024,
            dimension_semantics=("arbitrary",),
        ),
        name="backward_and_sums",
    )(d_y, pre, conv, dt_pre, states, *wholes, out_part, z_part, branch_part)


def exchange(place_axis, level, source, got, sends, arrivals):
    index = lax.axis_index(place_axis)
    other = partner(index, level)
    return pltpu.make_async_remote_copy(
        src_ref=source,
        dst_ref=got,
        send_sem=sends,
        recv_sem=arrivals,
        device_id={place_axis: other},
        device_id_type=pl.DeviceIdType.MESH,
    )


def partner(index, level):
    bit = 2**level
    return index + (1 - 2 * (index // bit % 2)) * bit


def levels_of(axis):
    return lax.axis_size(axis).bit_length() - 1


class Push:
    def __init__(self, axis, own, slots, sends, arrivals):
        self.axis, self.own, self.slots = axis, own, slots
        self.sends, self.arrivals = sends, arrivals
        self.count = lax.axis_size(axis)

    def copy(self, step):
        index = lax.axis_index(self.axis)
        return pltpu.make_async_remote_copy(
            src_ref=self.own,
            dst_ref=self.slots.at[index],
            send_sem=self.sends.at[step - 1],
            recv_sem=self.arrivals.at[step - 1],
            device_id={self.axis: (index + step) % self.count},
            device_id_type=pl.DeviceIdType.MESH,
        )

    def begin(self):
        for step in range(1, self.count):
            self.copy(step).start()

    def finish(self):
        for step in range(1, self.count):
            self.copy(step).wait()


def norm_kernel(sums, norms_out, own, slots, sends, arrivals):
    push = Push("fsdp", own, slots, sends, arrivals)
    index = lax.axis_index("fsdp")
    barrier = pltpu.get_barrier_semaphore()
    for step in range(1, push.count):
        other = (index + step) % push.count
        pl.semaphore_signal(
            barrier, inc=1, device_id={"fsdp": other}, device_id_type=pl.DeviceIdType.MESH
        )
    own[...] = jnp.broadcast_to(jnp.sum(sums[...], axis=1, keepdims=True), (8, 128))
    slots[index] = own[...]
    pl.semaphore_wait(barrier, push.count - 1)
    push.begin()
    push.finish()
    total = slots[0]
    for k in range(1, push.count):
        total = total + slots[k]
    norms_out[...] = jnp.sqrt(total)


def run_norms(sums):
    count = lax.axis_size("fsdp")
    dma = pltpu.SemaphoreType.DMA
    return pl.pallas_call(
        norm_kernel,
        in_specs=[VMEM],
        out_specs=VMEM,
        out_shape=jax.ShapeDtypeStruct((8, 128), F32),
        scratch_shapes=[
            pltpu.VMEM((8, 128), F32),
            pltpu.VMEM((count, 8, 128), F32),
            dma((count - 1,)),
            dma((count - 1,)),
        ],
        compiler_params=comm_params(3),
        name="norms",
    )(sums)


def small_update(groups, heads, small_all, small_w, small_m, small_v, outs, small_grad):
    wide = heads * HEAD
    edge = wide + 2 * STATE
    everyone = [small_all[s] for s in range(groups)]
    shared = everyone[0]
    for other in everyone[1:]:
        shared = shared + other
    small_grad[:, :D] = shared[5:6, :]
    for k in range(KERNEL + 1):
        base = D + k * CONV
        for s in range(groups):
            small_grad[:, base + s * wide : base + (s + 1) * wide] = everyone[s][k : k + 1, :wide]
        small_grad[:, base + INNER : base + CONV] = shared[k : k + 1, wide:edge]
    size = 3 * HEADS + INNER
    size = size + -size % 128
    lane = lax.broadcasted_iota(jnp.int32, (8, size), 1)
    rest = jnp.zeros((8, size), F32)
    gap = jnp.zeros((8, size - 128), F32)
    for s in range(groups):
        for k in range(3):
            part = jnp.broadcast_to(everyone[s][7:8, 128 * k : 128 * (k + 1)], (8, 128))
            part = jnp.concatenate([part, gap], axis=1)
            part = jnp.where(lane < heads, part, 0.0)
            move = k * HEADS + s * heads
            rest = rest + (pltpu.roll(part, move, 1) if move else part)
    gains = [jnp.broadcast_to(one[6:7, :wide], (8, wide)) for one in everyone]
    gains = gains + [jnp.zeros((8, size - INNER), F32)]
    rest = rest + pltpu.roll(jnp.concatenate(gains, axis=1), 3 * HEADS, 1)
    base = D + (KERNEL + 1) * CONV
    small_grad[:, base : base + size] = rest[0:1, :]
    gradient = small_grad[...]
    first, second, direction = adam_parts(gradient, small_m[...], small_v[...])
    values = (gradient, small_w[...] - LEARN_RATE * direction, first, second)
    for ref, value in zip(outs, values, strict=True):
        ref[...] = value[:, : ref.shape[1]]


def moments_kernel(groups, heads, *refs):
    z_piece, x_piece, tails, out_piece = refs[:4]
    small_all, small_w, small_m, small_v = refs[4:8]
    w_in, m_in, v_in, w_out, m_out, v_out = refs[8:14]
    g_in_new, m_in_new, v_in_new, u_in, g_out_new, m_out_new, v_out_new, u_out = refs[14:22]
    sums = refs[22]
    small_outs = refs[23:27]
    u_tail, small_grad = refs[27:29]
    wide = heads * HEAD

    @pl.when(pl.program_id(0) == 0)
    def _():
        sums[...] = jnp.zeros_like(sums)
        small_update(groups, heads, small_all, small_w, small_m, small_v, small_outs, small_grad)

    def update(gradient, start, w, m, v, g_new, m_new, v_new, u, at):
        size = min(gradient.shape[1], w.shape[1] - start)
        here = slice(start, start + size)
        gradient = gradient[:, :size]
        first, second, direction = adam_parts(gradient, m[:, here], v[:, here])
        weight = w[:, here]
        direction = direction + WEIGHT_DECAY * weight
        g_new[:, here] = gradient
        m_new[:, here] = first
        v_new[:, here] = second
        if u is None:
            u_tail[:, :size] = direction
        else:
            u[:, here] = direction.astype(BF16)
        sums[at : at + 1, :size] += jnp.sum(weight * weight, axis=0, keepdims=True)
        sums[at + 1 : at + 2, :size] += jnp.sum(direction * direction, axis=0, keepdims=True)

    inside = (w_in, m_in, v_in, g_in_new, m_in_new, v_in_new, u_in)
    outside = (w_out, m_out, v_out, g_out_new, m_out_new, v_out_new, u_out)
    for s in range(groups):
        update(z_piece[s].astype(F32), s * wide, *inside, 0)
        update(x_piece[s].astype(F32), INNER + s * wide, *inside, 0)
        update(out_piece[s].astype(F32), s * wide, *outside, 2)
    gradient = tails[0].astype(F32)
    for s in range(1, tails.shape[0]):
        gradient = gradient + tails[s].astype(F32)
    update(gradient, 2 * INNER, *inside[:-1], None, 0)


ROWS = 16


def by_rows(columns):
    return pl.BlockSpec((ROWS, columns), lambda i: (i, 0))


def run_moments(groups, heads, z_all, x_all, s_all, out_all, smalls, inside, outside):
    rows = inside[0].shape[0]
    wide = heads * HEAD
    piece = pl.BlockSpec((groups, ROWS, wide), lambda i: (0, i, 0))
    if s_all.shape[1] < rows:
        parts = s_all.shape[1] // ROWS
        tails = pl.BlockSpec((1, ROWS, SHARED), lambda i: (i // parts, i % parts, 0))
    else:
        tails = pl.BlockSpec((groups, ROWS, SHARED), lambda i: (0, i, 0))
    shape = jax.ShapeDtypeStruct
    extent = D + (KERNEL + 1) * CONV + 3 * HEADS + INNER
    small_out = [shape((1, extent), F32)] * 4
    in_like, out_like = shape(inside[0].shape, F32), shape(outside[0].shape, F32)
    in_spec, out_spec = by_rows(PROJ), by_rows(INNER)
    return pl.pallas_call(
        partial(moments_kernel, groups, heads),
        grid=(rows // ROWS,),
        in_specs=[piece, piece, tails, piece]
        + [resident(x) for x in smalls]
        + [in_spec] * 3
        + [out_spec] * 3,
        out_specs=[in_spec] * 3
        + [by_rows(2 * INNER)]
        + [out_spec] * 4
        + [pl.BlockSpec((8, wide), lambda i: (0, 0))]
        + [resident(x) for x in small_out]
        + [by_rows(SHARED)],
        out_shape=[in_like] * 3
        + [shape((rows, 2 * INNER), BF16)]
        + [out_like] * 3
        + [shape(out_like.shape, BF16), shape((8, wide), F32)]
        + small_out
        + [shape((rows, SHARED), F32)],
        scratch_shapes=[pltpu.VMEM(smalls[1].shape, F32)],
        compiler_params=compiler_params(),
        name="moments",
    )(z_all, x_all, s_all, out_all, *smalls, *inside, *outside)


def weights_kernel(norms, w_in, u_in, u_tail, w_out, u_out, in_new, out_new):
    in_rate, out_rate = [
        LEARN_RATE * (norms[at : at + 1, :1] / norms[at + 1 : at + 2, :1]) for at in (0, 2)
    ]
    edge = u_in.shape[1]
    rest = w_in.shape[1] - edge
    in_new[:, :edge] = w_in[:, :edge] - in_rate * u_in[...].astype(F32)
    in_new[:, edge:] = w_in[:, edge:] - in_rate * u_tail[:, :rest]
    out_new[...] = w_out[...] - out_rate * u_out[...].astype(F32)


def run_weights(norms, w_in, u_in, u_tail, w_out, u_out):
    in_spec, out_spec = by_rows(PROJ), by_rows(INNER)
    return pl.pallas_call(
        weights_kernel,
        grid=(w_in.shape[0] // ROWS,),
        in_specs=[
            resident(norms), in_spec, by_rows(2 * INNER), by_rows(SHARED), out_spec, out_spec
        ],
        out_specs=[in_spec, out_spec],
        out_shape=[
            jax.ShapeDtypeStruct(w_in.shape, F32),
            jax.ShapeDtypeStruct(w_out.shape, F32),
        ],
        compiler_params=compiler_params(),
        name="weights",
    )(norms, w_in, u_in, u_tail, w_out, u_out)


def adam_parts(gradient, first_old, second_old):
    first_new = FIRST_DECAY * first_old + (1.0 - FIRST_DECAY) * gradient
    second_new = SECOND_DECAY * second_old + (1.0 - SECOND_DECAY) * (gradient * gradient)
    first_scale = 1.0 / (1.0 - FIRST_DECAY**STEP)
    second_scale = 1.0 / (1.0 - SECOND_DECAY**STEP)
    direction = (first_new * first_scale) / (jnp.sqrt(second_new * second_scale) + ADAM_EPSILON)
    return (first_new, second_new, direction)


def wide_row(vector):
    return jnp.pad(vector, (0, -vector.shape[0] % 128))[None, :]


def shards(
    tokens,
    cotangent,
    segments,
    in_weight,
    out_weight,
    small_params,
    in_first,
    in_second,
    out_first,
    out_second,
    small_first,
    small_second,
):
    in_gain = small_params[:D]
    groups = lax.axis_size("seq")
    where_seq = lax.axis_index("seq")
    heads = HEADS // groups
    wide = INNER // groups
    segment_row = segments[0]

    def own(vector, axis=-1):
        size = vector.shape[axis] // groups
        return lax.dynamic_slice_in_dim(vector, where_seq * size, size, axis)

    inputs = tokens[0].astype(F32)
    in_rms = lax.rsqrt(jnp.mean(inputs * inputs, axis=-1, keepdims=True) + NORM_EPS)
    dt_weight = jnp.pad(
        in_weight[:, INNER + CONV :].astype(BF16), ((0, 0), (0, DT_PAD - HEADS))
    )
    small = wide_row(small_params)
    spread_heads = (
        jnp.arange(128)[:, None] == jnp.arange(wide)[None, :] // HEAD
    ).astype(BF16)
    seg_pad = jnp.pad(segment_row, (EDGE, EDGE), constant_values=-1)[:, None]
    (
        pre, conv_in, dt_pre, states, d_y, d_z, normed_t, out_part, z_part, d_out_gain,
        conv_pack, head_pack, chan_pack, w_x, w_z, w_s, branch_part,
    ) = run_forward(
        heads, tokens[0], cotangent[0], small, dt_weight, seg_pad, segments, spread_heads,
        in_weight, out_weight,
    )
    packs = (conv_pack, head_pack, chan_pack)
    out_all, z_all, x_all, s_all, small_all, branch, d_normed, _, _ = run_backward(
        heads, d_y, pre, conv_in, dt_pre, states, seg_pad, segments, packs, spread_heads, d_z,
        (w_z, w_x, w_s.reshape(D, SHARED)), normed_t, tokens[0], small, d_out_gain, out_part, z_part, branch_part,
    )
    output = (inputs + branch.astype(F32)).astype(BF16)[None]
    d_normed = d_normed.astype(F32)
    slope = d_normed * in_gain[None, :]
    d_inputs = slope * in_rms - inputs * (in_rms**3 / D) * jnp.sum(
        slope * inputs, axis=1, keepdims=True
    )
    input_grad = (cotangent[0].astype(F32) + d_inputs)[None]

    (
        in_grad, in_first_new, in_second_new, in_dir, out_grad, out_first_new, out_second_new, out_dir,
        squares, small_grad, small_new, small_first_new, small_second_new, in_tail,
    ) = run_moments(
        groups, heads, z_all, x_all, s_all, out_all,
        (small_all, small, wide_row(small_first), wide_row(small_second)),
        (in_weight, in_first, in_second), (out_weight, out_first, out_second),
    )
    norms = run_norms(squares)
    in_new, out_new = run_weights(norms, in_weight, in_dir, in_tail, out_weight, out_dir)
    small_grad, small_new, small_first_new, small_second_new = [
        x[0] for x in (small_grad, small_new, small_first_new, small_second_new)
    ]
    norms = norms[:4, 0]
    return (
        output,
        input_grad,
        in_grad,
        in_new,
        in_first_new,
        in_second_new,
        out_grad,
        out_new,
        out_first_new,
        out_second_new,
        small_grad,
        small_new,
        small_first_new,
        small_second_new,
        norms,
    )


def solution(mesh):
    matrix = P("fsdp", None)
    rows = P("fsdp", "seq", None)
    return jax.shard_map(
        shards,
        mesh=mesh,
        in_specs=(rows, rows, matrix, matrix, matrix, P(), matrix, matrix, matrix, matrix, P(), P()),
        out_specs=(rows, rows) + (matrix,) * 8 + (P(),) * 5,
        check_vma=False,
    )
```

```python
from functools import partial

import jax
import jax.numpy as jnp
from jax import lax
from jax.experimental import pallas as pl
from jax.experimental.pallas import tpu as pltpu
from jax.sharding import PartitionSpec as P

D = 1536
HEADS = 48
HEAD = 64
STATE = 128
KERNEL = 4
STRETCH = 256
STEP = 5
INNER = 3072
CONV = 3328
PROJ = 6448
DT_PAD = 128
SHARED = 2 * STATE + DT_PAD

NORM_EPS = 1e-05
FIRST_DECAY = 0.9
SECOND_DECAY = 0.999
ADAM_EPSILON = 1e-06
WEIGHT_DECAY = 0.01
LEARN_RATE = 0.5
F32 = jnp.float32
BF16 = jnp.bfloat16


def dot(a, b, dims=((1,), (0,))):
    return lax.dot_general(a, b, (dims, ((), ())), preferred_element_type=F32)


def split_dot(value, ones):
    high = value.astype(BF16)
    low = (value - high.astype(F32)).astype(BF16)
    return dot(high, ones) + dot(low, ones)


def tri_dot(ones, value):
    high = value.astype(BF16)
    rest = value - high.astype(F32)
    middle = rest.astype(BF16)
    low = (rest - middle.astype(F32)).astype(BF16)
    return dot(ones, high) + dot(ones, middle) + dot(ones, low)


def sigmoid(v):
    return 1.0 / (1.0 + jnp.exp(-v))


def softplus(v):
    return jnp.maximum(v, 0.0) + jnp.log1p(jnp.exp(-jnp.abs(v)))


def row_at_least():
    rows = lax.broadcasted_iota(jnp.int32, (STRETCH, STRETCH), 0)
    columns = lax.broadcasted_iota(jnp.int32, (STRETCH, STRETCH), 1)
    return rows >= columns


class Decays:
    def __init__(self, dt, rate, masks, spread):
        self.dt, self.spread = dt, spread
        lower = jnp.where(row_at_least(), 1.0, 0.0).astype(BF16)
        self.columns = dot(lower, dt) * rate
        self.rows = jnp.transpose(self.columns)
        last = self.columns[STRETCH - 1 :, :]
        self.into = jnp.exp(self.columns) * masks["carry"]
        self.out = jnp.exp(last - self.columns) * masks["tail"]
        self.through = jnp.broadcast_to(jnp.exp(last) * masks["keep"], (8, 128))
        self.bar = masks["bar"]

    def of(self, columns):
        ones = self.spread[:, columns]
        return (
            dot(self.dt, ones),
            split_dot(self.into, ones),
            split_dot(self.out, ones),
            split_dot(self.through, ones)[:1],
        )

    def between(self, head):
        return jnp.exp(self.columns[:, head : head + 1] - self.rows[head : head + 1, :] + self.bar)


EDGE = 8


def block_masks(seg_pad, seg_row, at):
    def rows(by, size=STRETCH):
        return seg_pad[pl.ds(at + EDGE + by, size), :]

    here = rows(0)
    first = jnp.where(at == 0, rows(0, 1), rows(-1, 1))
    last = rows(STRETCH - 1, 1)
    masks = {"carry": here == first, "tail": here == last, "keep": last == first}
    for by in range(1, KERNEL):
        masks[-by] = here == rows(-by)
        masks[by] = here == rows(by)
    masks = {key: jnp.where(value, 1.0, 0.0) for key, value in masks.items()}
    within = row_at_least() & (here == seg_row[:, pl.ds(at, STRETCH)])
    masks["bar"] = jnp.where(within, 0.0, -1e30)
    return masks


def forward_block(
    heads, at, normed, w_x, shared_columns, masks, packs, spread, outs, y_all, extended, state
):
    conv_pack, head_pack, chan_pack = packs
    pre_out, conv_out, dt_out, states_out = outs
    wide = heads * HEAD
    here = pl.ds(at, STRETCH)
    conv_low = jnp.concatenate([dot(normed, w_x[...]), dot(normed, shared_columns(0, 2 * STATE))], axis=1)
    conv_low = conv_low.astype(BF16)
    conv_out[...] = conv_low
    conv_in = conv_low.astype(F32)
    extended[8 : 8 + STRETCH, :] = conv_in
    pre = conv_pack[4:5, :] + conv_pack[3:4, :] * conv_in
    for by in range(1, KERNEL):
        pre = pre + conv_pack[3 - by : 4 - by, :] * (
            extended[8 - by : 8 - by + STRETCH, :] * masks[-by]
        )
    extended[0:8, :] = extended[STRETCH : STRETCH + 8, :]
    pre_out[...] = pre
    act = (pre * sigmoid(pre)).astype(BF16)
    b_mat = act[:, wide : wide + STATE]
    c_mat = act[:, wide + STATE :]
    lane = lax.broadcasted_iota(jnp.int32, (STRETCH, DT_PAD), 1)
    dt_pre = pltpu.roll(
        dot(normed, shared_columns(2 * STATE, DT_PAD)), DT_PAD - lax.axis_index("seq") * heads, 1
    )
    dt_pre = jnp.where(lane < heads, dt_pre, 0.0) + head_pack[0:1, :]
    dt_out[...] = dt_pre
    dt = softplus(dt_pre).astype(BF16)
    decay = Decays(dt, head_pack[1:2, :], masks, spread)
    scores = dot(c_mat, b_mat, ((1,), (1,)))
    first_half = lax.broadcasted_iota(jnp.int32, (STRETCH, 2 * HEAD), 1) < HEAD
    for pair in range(heads // 2):
        columns = slice(pair * 2 * HEAD, (pair + 1) * 2 * HEAD)
        steps, carry, tail, keep = decay.of(columns)
        xs = act[:, columns].astype(F32)
        scaled = xs * steps
        scaled_low = scaled.astype(BF16)
        old = state[:, columns]
        states_out[0, :, columns] = old
        y = dot(c_mat, old.astype(BF16)) * carry + chan_pack[0:1, columns] * xs
        state[:, columns] = old * keep + dot(b_mat, (scaled * tail).astype(BF16), ((0,), (0,)))
        halves = [
            dot((scores * decay.between(h)).astype(BF16), scaled_low)
            for h in (2 * pair, 2 * pair + 1)
        ]
        y_all[here, columns] = (y + jnp.where(first_half, halves[0], halves[1])).astype(BF16)


def fill_packs(heads, small, spread, packs, scratch_gain):
    conv_pack, head_pack, chan_pack = packs
    wide = heads * HEAD
    index = lax.axis_index("seq")
    start = pl.multiple_of(index * wide, 128)
    for ref in packs:
        ref[...] = jnp.zeros_like(ref)
    for k in range(KERNEL + 1):
        base = D + k * CONV
        conv_pack[k : k + 1, :wide] = small[:, pl.ds(base + start, wide)]
        conv_pack[k : k + 1, wide:] = small[:, base + INNER : base + CONV]
    base = D + (KERNEL + 1) * CONV
    window = jnp.broadcast_to(small[:, base : base + 256], (8, 256))
    lane = lax.broadcasted_iota(jnp.int32, (8, 256), 1)

    def own(k):
        moved = pltpu.roll(window, 256 - (k * HEADS + index * heads), 1)
        return jnp.where(lane < heads, moved, 0.0)[:, :128]

    head_pack[0:1, :] = own(0)[:1]
    rate = own(1)
    rate = jnp.where(lax.broadcasted_iota(jnp.int32, (8, 128), 1) < heads, -jnp.exp(rate), 0.0)
    head_pack[1:2, :] = rate[:1]
    chan_pack[0:1, :] = tri_spread(own(2), spread)[:1]
    base = base + 3 * HEADS
    shift = base % 128
    gain = jnp.broadcast_to(small[:, base - shift : base - shift + INNER + 128], (8, INNER + 128))
    scratch_gain[...] = pltpu.roll(gain, INNER + 128 - shift, 1)
    chan_pack[1:2, :] = scratch_gain[0:1, pl.ds(start, wide)]


def tri_spread(value, ones):
    high = value.astype(BF16)
    rest = value - high.astype(F32)
    middle = rest.astype(BF16)
    low = (rest - middle.astype(F32)).astype(BF16)
    return dot(high, ones) + dot(middle, ones) + dot(low, ones)


def as_row(column):
    lane = lax.broadcasted_iota(jnp.int32, (STRETCH, 128), 1)
    return jnp.transpose(jnp.where(lane == 0, column, 0.0))[0:8, :]


def as_column(rows):
    return jnp.transpose(jnp.concatenate([rows, jnp.zeros((120, STRETCH), F32)], axis=0))[:, 0:1]


def inverse_rms(squares):
    return lax.rsqrt(as_column(squares) / INNER + NORM_EPS)


def gate_gradients(y_low, z, d_mixed, gain, squares, products):
    rms = inverse_rms(squares)
    y = y_low.astype(F32)
    sig = sigmoid(z)
    silu = z * sig
    gated = y * silu
    unit = gated * rms
    d_gain = jnp.sum(d_mixed * unit, axis=0, keepdims=True)
    d_gated = d_mixed * gain * rms - unit * (rms * rms / INNER * as_column(products))
    d_z = d_gated * y * (sig * (1.0 + z * (1.0 - sig)))
    return (d_gated * silu).astype(BF16), d_z.astype(BF16), d_gain


def halved(rows, groups):
    return rows % (16 * groups) == 0


def forward_kernel(heads, *refs):
    tokens, cotangent, small, dt_weight, seg_pad, seg_row, spread_ref, in_weight, out_weight = refs[:9]
    outs = refs[9:13]
    z_part, d_gain = refs[13:15]
    packs = refs[15:18]
    w_x_out, w_z_out, w_s_out, branch_part, d_y_out, d_z_out, normed_t_out, out_part_out = refs[18:26]
    (
        stage_s, own_x, own_z, own_o, own_s, own_rows, w_x, w_z, w_o, w_s,
        shared_own, branch_stage, rows_all, returned_t, z_all, y_all, d_mixed_all, extended, state,
        scratch_gain, mixed_all, d_y, d_z, normed_t, out_part, sums, got, stage_sems, sum_sends, sum_arrivals,
    ) = refs[26:56]
    sems = refs[56:]
    ring, seq = places()
    wide = heads * HEAD
    edge = wide + 2 * STATE
    step = pl.program_id(0)
    blocks = pl.num_programs(0) - 1
    length = rows_all.shape[0]
    count = length // STRETCH
    rows = own_x.shape[0]
    split = halved(rows, seq.major * seq.minor)
    stage_x, stage_z, stage_o = [d_mixed_all.at[pl.ds(k * rows, rows)] for k in range(3)]

    def shared_columns(start, size):
        if split:
            return w_s[:, :, :, start : start + size].reshape(D, size)
        return w_s[:, start : start + size]

    get_x = Gather(ring, own_x, w_x, rows, WEIGHT_PIECES, sems[:5])
    get_z = Gather(ring, own_z, w_z, rows, 1, sems[5:10])
    get_o = Gather(ring, own_o, w_o, rows, 1, sems[10:15])
    get_rows = Gather(seq, own_rows, rows_all, own_rows.shape[0], TOKEN_PIECES, sems[15:20])
    if split:
        get_s = Gather(ring, own_s, shared_own, own_s.shape[0], 1, sems[20:25])
        pass_s = Gather(
            seq, shared_own, w_s, shared_own.shape[0], 1, sems[25:30],
            lambda slot, piece: w_s.at[:, slot],
        )
    else:
        get_s = Gather(ring, own_s, w_s, rows, 1, sems[20:25])
    saves = [
        pltpu.make_async_copy(source, target, stage_sems.at[4 + k])
        for k, (source, target) in enumerate(
            (
                (w_x, w_x_out),
                (w_z, w_z_out),
                (w_s, w_s_out),
                (normed_t, normed_t_out),
                (out_part, out_part_out),
                (d_y, d_y_out),
                (d_z, d_z_out),
            )
        )
    ]
    spread = spread_ref[...]
    at = pl.multiple_of(step * STRETCH, STRETCH)

    @pl.when(step == 0)
    def _():
        start = pl.multiple_of(seq.index * wide, 128)
        own_shared = own_s.shape[0]
        first_row = pl.multiple_of(seq.index * own_shared, 16) if split else 0
        sources = [
            (in_weight.at[pl.ds(first_row, own_shared), pl.ds(2 * INNER, 2 * STATE)], stage_s),
            (in_weight.at[:, pl.ds(INNER + start, wide)], stage_x),
            (in_weight.at[:, pl.ds(start, wide)], stage_z),
            (out_weight.at[:, pl.ds(start, wide)], stage_o),
        ]
        loads = [
            pltpu.make_async_copy(source, target, stage_sems.at[k])
            for k, (source, target) in enumerate(sources)
        ]
        for load in loads:
            load.start()
        meet(ring, seq)
        loads[0].wait()
        own_s[:, : 2 * STATE] = stage_s[...].astype(BF16)
        own_s[:, 2 * STATE :] = dt_weight[pl.ds(first_row, own_shared), :]
        get_s.begin(0)
        get_s.keep().start()
        loads[1].wait()
        own_x[...] = stage_x[...].astype(BF16)
        for piece in range(WEIGHT_PIECES):
            get_x.begin(piece)
        get_x.keep().start()
        inputs = tokens[...].astype(F32)
        rms = lax.rsqrt(jnp.mean(inputs * inputs, axis=-1, keepdims=True) + NORM_EPS)
        own_rows[:, :D] = (inputs * rms * small[:, :D]).astype(BF16)
        own_rows[:, D:] = cotangent[...]
        for piece in range(TOKEN_PIECES):
            get_rows.begin(piece)
        get_rows.keep().start()
        loads[2].wait()
        loads[3].wait()
        own_z[...] = stage_z[...].astype(BF16)
        own_o[...] = stage_o[...].astype(BF16)
        get_z.keep().start()
        get_o.keep().start()
        fill_packs(heads, small, spread, packs, scratch_gain)
        state[...] = jnp.zeros_like(state)
        extended[0:8, :] = jnp.zeros((8, edge), F32)
        d_gain[...] = jnp.zeros_like(d_gain)
        get_s.forward(0)
        get_rows.forward(0)
        get_x.forward(0)
        get_s.finish()
        get_s.keep().wait()
        if split:
            pass_s.begin(0)
            pass_s.keep().start()
        get_rows.forward(1)
        get_x.forward(1)
        get_z.begin(0)
        get_rows.forward(2)
        get_x.forward(2)
        get_o.begin(0)
        for piece in range(3, TOKEN_PIECES):
            get_rows.forward(piece)
        if split:
            pass_s.forward(0)
        get_rows.finish()
        get_rows.keep().wait()

        def turn(k, _):
            here = pl.ds(pl.multiple_of(k * STRETCH, STRETCH), STRETCH)
            normed_t[:, here] = jnp.transpose(rows_all[here, :D])
            returned_t[:, here] = jnp.transpose(rows_all[here, D:])
            return 0

        lax.fori_loop(0, count, turn, 0)
        if split:
            pass_s.finish()
            pass_s.keep().wait()
        get_x.finish()
        get_x.keep().wait()
        saves[0].start()
        saves[2].start()
        saves[3].start()

    @pl.when(step < blocks)
    def _():
        masks = block_masks(seg_pad, seg_row, at)
        forward_block(
            heads, at, rows_all[pl.ds(at, STRETCH), :D], w_x, shared_columns, masks, packs, spread, outs,
            y_all, extended, state,
        )

    forwards = [(stream, k) for stream in (get_z, get_o) for k in range(1, ring.major)]
    ahead = min(count, len(forwards))
    for k in range(ahead):

        @pl.when(step == k)
        def _():
            stream, by = forwards[k]
            stream.forward_step(0, by)

    @pl.when(step == blocks)
    def _():
        later = list(forwards[ahead:])
        while later and later[0][0] is get_z:
            stream, by = later.pop(0)
            stream.forward_step(0, by)
        get_z.finish()
        get_z.keep().wait()
        saves[1].start()
        levels = levels_of("seq")
        gain = packs[2][1:2, :]

        def chunk_rows(k):
            return pl.ds(pl.multiple_of(k * STRETCH, STRETCH), STRETCH)

        def gated_at(here):
            z = z_all[here, :]
            return y_all[here, :].astype(F32) * (z * sigmoid(z))

        def summed(which):
            base = which * (levels + 1)
            for level in range(levels):
                at = which * levels + level
                copy = exchange(
                    "seq", level, sums.at[base + level], got.at[at], sum_sends.at[at], sum_arrivals.at[at]
                )
                copy.start()
                copy.wait()
                sums[base + level + 1] = sums[base + level] + got[at]
            return base + levels

        def gate(k, _):
            here = chunk_rows(k)
            z_all[here, :] = dot(rows_all[here, :D], w_z[...])
            gated = gated_at(here)
            sums[0, :, here] = as_row(jnp.sum(gated * gated, axis=1, keepdims=True))
            return 0

        lax.fori_loop(0, count, gate, 0)
        if later:
            stream, by = later.pop(0)
            stream.forward_step(0, by)
        squares = summed(0)

        def mix(k, _):
            here = chunk_rows(k)
            mixed_all[here, :] = (
                gated_at(here) * inverse_rms(sums[squares, :, here]) * gain
            ).astype(BF16)
            return 0

        lax.fori_loop(0, count, mix, 0)
        for stream, by in later:
            stream.forward_step(0, by)

        def contract_out(k, _):
            here = pl.ds(pl.multiple_of(k * 256, 256), 256)
            out_part[here, :] = dot(returned_t[here, :], mixed_all[...]).astype(BF16)
            return 0

        lax.fori_loop(0, D // 256, contract_out, 0)
        saves[4].start()
        get_o.finish()
        get_o.keep().wait()

        def measure(k, _):
            here = chunk_rows(k)
            d_mixed = dot(rows_all[here, D:], w_o[...])
            d_mixed_all[here, :] = d_mixed
            product = jnp.sum(d_mixed * gain * gated_at(here), axis=1, keepdims=True)
            sums[levels + 1, :, here] = as_row(product)
            return 0

        lax.fori_loop(0, count, measure, 0)
        products = summed(1)

        def differentiate(k, _):
            here = chunk_rows(k)
            d_y_block, d_z_block, d_gain_block = gate_gradients(
                y_all[here, :], z_all[here, :], d_mixed_all[here, :], gain,
                sums[squares, :, here], sums[products, :, here],
            )
            d_y[here, :] = d_y_block
            d_z[here, :] = d_z_block
            d_gain[0:1, :] += d_gain_block
            branch_stage[...] = dot(mixed_all[here, :], w_o[...], ((1,), (1,))).astype(BF16)
            out = pltpu.make_async_copy(branch_stage, branch_part.at[here], stage_sems.at[11])
            out.start()
            out.wait()
            return 0

        lax.fori_loop(0, count, differentiate, 0)
        saves[5].start()
        saves[6].start()

        def contract_z(k, _):
            here = pl.ds(pl.multiple_of(k * 256, 256), 256)
            z_part[here, :] = dot(normed_t[here, :], d_z[...]).astype(BF16)
            return 0

        lax.fori_loop(0, D // 256, contract_z, 0)
        for save in saves:
            save.wait()


def backward_block(
    heads,
    d_y_ref,
    pre_ref,
    conv_ref,
    dt_ref,
    states,
    seg_pad,
    seg_row,
    conv_pack,
    head_pack,
    chan_pack,
    spread_ref,
    gather_ref,
    d_conv_out,
    d_head_out,
    extended,
    d_state,
    d_rest,
):
    wide = heads * HEAD
    edge = wide + 2 * STATE

    @pl.when(pl.program_id(0) == 0)
    def _():
        d_state[...] = jnp.zeros_like(d_state)
        extended[STRETCH : STRETCH + 8, :] = jnp.zeros((8, edge), F32)
        d_conv_out[...] = jnp.zeros_like(d_conv_out)
        d_head_out[...] = jnp.zeros_like(d_head_out)

    at_row = pl.multiple_of((pl.num_programs(0) - 1 - pl.program_id(0)) * STRETCH, STRETCH)
    masks = block_masks(seg_pad, seg_row, at_row)
    spread = spread_ref[...]
    gather = gather_ref[...]
    pre = pre_ref[...]
    act = (pre * sigmoid(pre)).astype(BF16)
    b_mat = act[:, wide : wide + STATE]
    c_mat = act[:, wide + STATE :]
    dt_pre = dt_ref[...]
    dt = softplus(dt_pre).astype(BF16)
    rate = head_pack[1:2, :]
    decay = Decays(dt, rate, masks, spread)
    scores = dot(c_mat, b_mat, ((1,), (1,)))
    lane = lax.broadcasted_iota(jnp.int32, (STRETCH, 128), 1)
    first_half = lane < HEAD
    d_b = jnp.zeros((STRETCH, STATE), F32)
    d_c = jnp.zeros((STRETCH, STATE), F32)
    d_scores = jnp.zeros((STRETCH, STRETCH), F32)
    d_cum = jnp.zeros((STRETCH, 128), F32)
    d_dt = jnp.zeros((STRETCH, 128), F32)
    d_last = jnp.zeros((1, 128), F32)
    column_sums = []
    for pair in range(heads // 2):
        columns = slice(pair * 2 * HEAD, (pair + 1) * 2 * HEAD)
        ones = gather[columns, :]
        steps, carry, tail, keep = decay.of(columns)
        xs = act[:, columns].astype(F32)
        scaled = xs * steps
        scaled_low = scaled.astype(BF16)
        old = states[0, :, columns]
        old_low = old.astype(BF16)
        d_new = d_state[:, columns]
        d_new_low = d_new.astype(BF16)
        d_y_low = d_y_ref[:, columns]
        d_y = d_y_low.astype(F32)
        d_carried = d_y * carry
        d_carried_low = d_carried.astype(BF16)
        d_c = d_c + dot(d_carried_low, old_low, ((1,), (1,)))
        d_cum = d_cum + split_dot(d_carried * dot(c_mat, old_low), ones)
        weighed = scaled * tail
        into = dot(b_mat, d_new_low)
        d_b = d_b + dot(weighed.astype(BF16), d_new_low, ((1,), (1,)))
        tail_part = split_dot(weighed * into, ones)
        d_cum = d_cum - tail_part
        kept = jnp.sum(d_new * old, axis=0, keepdims=True) * keep
        kept = split_dot(jnp.broadcast_to(kept, (8, 128)), ones)[:1]
        d_last = d_last + jnp.sum(tail_part, axis=0, keepdims=True) + kept
        d_state[:, columns] = d_new * keep + dot(c_mat, d_carried_low, ((0,), (0,)))
        halves = []
        for h in (2 * pair, 2 * pair + 1):
            between = decay.between(h)
            weights = scores * between
            halves.append(dot(weights.astype(BF16), d_y_low, ((0,), (0,))))
            d_y_head = jnp.where(first_half == (h % 2 == 0), d_y_low, jnp.zeros_like(d_y_low))
            d_weights = dot(d_y_head, scaled_low, ((1,), (1,)))
            d_scores = d_scores + d_weights * between
            product = d_weights * weights
            d_cum = d_cum + jnp.where(lane == h, jnp.sum(product, axis=1, keepdims=True), 0.0)
            column_sums.append(jnp.sum(product, axis=0, keepdims=True))
        d_scaled = into * tail + jnp.where(first_half, halves[0], halves[1])
        d_xs = d_scaled * steps + chan_pack[0:1, columns] * d_y
        extended[0:STRETCH, columns] = d_xs.astype(BF16).astype(F32)
        d_dt = d_dt + split_dot(d_scaled * xs, ones)
        d_skip = jnp.sum(d_y * xs, axis=0, keepdims=True)
        d_head_out[2:3, :] += split_dot(jnp.broadcast_to(d_skip, (8, 128)), ones)[:1]
    column_sums.append(jnp.zeros((128 - heads, STRETCH), F32))
    d_cum = d_cum - jnp.transpose(jnp.concatenate(column_sums, axis=0))
    row = lax.broadcasted_iota(jnp.int32, (STRETCH, 128), 0)
    d_cum = d_cum + jnp.where(row == STRETCH - 1, d_last, 0.0)
    d_scores_low = d_scores.astype(BF16)
    d_c = d_c + dot(d_scores_low, b_mat)
    d_b = d_b + dot(d_scores_low, c_mat, ((0,), (0,)))

    rows = lax.broadcasted_iota(jnp.int32, (STRETCH, STRETCH), 0)
    upper = jnp.where(rows <= lax.broadcasted_iota(jnp.int32, (STRETCH, STRETCH), 1), 1.0, 0.0)
    d_dt = d_dt + rate * tri_dot(upper.astype(BF16), d_cum)
    d_dt_raw = d_dt.astype(BF16).astype(F32) * sigmoid(dt_pre)
    d_head_out[0:1, :] += jnp.sum(d_dt_raw, axis=0, keepdims=True)
    d_head_out[1:2, :] += jnp.sum(d_cum * decay.columns, axis=0, keepdims=True)

    extended[0:STRETCH, wide : wide + STATE] = d_b
    extended[0:STRETCH, wide + STATE :] = d_c
    here = pl.ds(at_row, STRETCH)
    moved = pltpu.roll(jnp.where(lane < heads, d_dt_raw, 0.0), lax.axis_index("seq") * heads, 1)
    d_rest[here, edge:] = moved.astype(BF16)

    def convolve_back(at, _):
        columns = pl.ds(pl.multiple_of(at * 128, 128), 128)
        value = pre_ref[:, columns]
        gate = sigmoid(value)
        d_pre = extended[0:STRETCH, columns] * (gate * (1.0 + value * (1.0 - gate)))
        extended[0:STRETCH, columns] = d_pre
        conv_in = conv_ref[:, columns].astype(F32)
        d_conv_in = conv_pack[3:4, columns] * d_pre
        d_conv_out[3:4, columns] += jnp.sum(d_pre * conv_in, axis=0, keepdims=True)
        d_conv_out[4:5, columns] += jnp.sum(d_pre, axis=0, keepdims=True)
        for by in range(1, KERNEL):
            moved = extended[by : by + STRETCH, columns] * masks[by]
            d_conv_in = d_conv_in + conv_pack[3 - by : 4 - by, columns] * moved
            d_conv_out[3 - by : 4 - by, columns] += jnp.sum(moved * conv_in, axis=0, keepdims=True)
        extended[STRETCH : STRETCH + 8, columns] = extended[0:8, columns]
        d_rest[here, columns] = d_conv_in.astype(BF16)
        return 0

    lax.fori_loop(0, edge // 128, convolve_back, 0)


VMEM_BYTES = 56 * 1024 * 1024


def block(columns, reverse=0):
    if reverse:
        return pl.BlockSpec((STRETCH, columns), lambda i: (reverse - 1 - i, 0))
    return pl.BlockSpec((STRETCH, columns), lambda i: (i, 0))


def whole(*shape):
    return pl.BlockSpec(shape, lambda i: (0,) * len(shape))


def compiler_params():
    return pltpu.CompilerParams(
        vmem_limit_bytes=VMEM_BYTES, dimension_semantics=("arbitrary",)
    )


class Place:
    def __init__(self, axis, minor):
        self.axis = axis
        self.minor = minor
        self.major = lax.axis_size(axis) // minor
        index = lax.axis_index(axis)
        self.at_major = index // minor
        self.at_minor = index % minor
        self.index = index

    def slot(self, by_major, by_minor):
        return (self.at_major + by_major) % self.major * self.minor + (
            self.at_minor + by_minor
        ) % self.minor

    def others(self):
        along = [self.slot(step, 0) for step in range(1, self.major)]
        return along + [self.slot(0, step) for step in range(1, self.minor)]


def places():
    ring = lax.axis_size("fsdp")
    side = 1
    while 2 * side * 2 * side * 2 <= ring:
        side = 2 * side
    return Place("fsdp", side), Place("seq", 2)


def meet(*all_places):
    barrier = pltpu.get_barrier_semaphore()
    count = 0
    for place in all_places:
        for other in place.others():
            pl.semaphore_signal(
                barrier, inc=1, device_id={place.axis: other}, device_id_type=pl.DeviceIdType.MESH
            )
            count = count + 1
    pl.semaphore_wait(barrier, count)


def send(place, source, target, to, sends, arrivals, at):
    return pltpu.make_async_remote_copy(
        src_ref=source,
        dst_ref=target,
        send_sem=sends.at[at],
        recv_sem=arrivals.at[at],
        device_id={place.axis: to},
        device_id_type=pl.DeviceIdType.MESH,
    )


class Gather:
    def __init__(self, place, own, full, rows, pieces, sems, target=None):
        self.place, self.own, self.full, self.landing = place, own, full, target
        self.size, self.pieces = rows // pieces, pieces
        self.sends1, self.arrivals1, self.sends2, self.arrivals2, self.here = sems

    @staticmethod
    def scratch(place, pieces):
        first = max(place.major - 1, 1) * pieces
        second = place.major * (place.minor - 1) * pieces
        dma = pltpu.SemaphoreType.DMA
        return [dma((first,)), dma((first,)), dma((second,)), dma((second,)), dma((1,))]

    def rows(self, piece):
        return pl.ds(piece * self.size, self.size)

    def target(self, slot, piece):
        if self.landing is not None:
            return self.landing(slot, piece)
        if len(self.full.shape) > len(self.own.shape):
            return self.full.at[slot, self.rows(piece)]
        start = slot * (self.size * self.pieces) + piece * self.size
        return self.full.at[pl.ds(pl.multiple_of(start, 16), self.size)]

    def along(self, piece, step):
        place = self.place
        return send(
            place,
            self.own.at[self.rows(piece)],
            self.target(place.index, piece),
            place.slot(step, 0),
            self.sends1,
            self.arrivals1,
            piece * (place.major - 1) + step - 1,
        )

    def across(self, piece, step, across):
        place = self.place
        slot = place.slot(-step, 0)
        target = self.target(slot, piece)
        source = self.own.at[self.rows(piece)] if step == 0 else target
        at = (piece * place.major + step) * (place.minor - 1) + across - 1
        return send(
            place, source, target, place.slot(0, across), self.sends2, self.arrivals2, at
        )

    def keep(self):
        if self.landing is not None:
            target = self.landing(self.place.index, 0)
        elif len(self.full.shape) > len(self.own.shape):
            target = self.full.at[self.place.index]
        else:
            size = self.size * self.pieces
            target = self.full.at[pl.ds(pl.multiple_of(self.place.index * size, 16), size)]
        return pltpu.make_async_copy(self.own, target, self.here.at[0])

    def begin(self, piece):
        for step in range(1, self.place.major):
            self.along(piece, step).start()
        for across in range(1, self.place.minor):
            self.across(piece, 0, across).start()

    def forward(self, piece):
        for step in range(1, self.place.major):
            self.forward_step(piece, step)

    def forward_step(self, piece, step):
        self.along(piece, step).wait_recv()
        for across in range(1, self.place.minor):
            self.across(piece, step, across).start()

    def finish(self):
        for piece in range(self.pieces):
            for step in range(1, self.place.major):
                self.along(piece, step).wait_send()
            for step in range(self.place.major):
                for across in range(1, self.place.minor):
                    self.across(piece, step, across).wait()


class Reduce:
    def __init__(self, place, part, total, rows, pieces, scratch, loads=None):
        self.place, self.part, self.total, self.loads = place, part, total, loads
        self.size, self.pieces = rows // pieces, pieces
        self.got1, self.mine, self.got2, self.sends1, self.arrivals1, self.sends2, self.arrivals2 = (
            scratch
        )

    @staticmethod
    def scratch(place, rows, columns, pieces):
        dma = pltpu.SemaphoreType.DMA
        first = place.major * (place.minor - 1)
        second = max(place.major - 1, 1)
        return [
            pltpu.VMEM((first, rows, columns), BF16),
            pltpu.VMEM((second, rows, columns), BF16),
            pltpu.VMEM((second, rows, columns), BF16),
            dma((first * pieces,)),
            dma((first * pieces,)),
            dma((second * pieces,)),
            dma((second * pieces,)),
        ]

    def items(self):
        return [(piece, step) for step in self.steps() for piece in range(self.pieces)]

    def steps(self):
        return list(range(1, self.place.major)) + [0]

    def rows(self, piece):
        return pl.ds(piece * self.size, self.size)

    def part_rows(self, slot, rows_start, size):
        if len(self.part.shape) == 3:
            return slot, pl.ds(rows_start, size)
        start = slot * (self.size * self.pieces) + rows_start
        return (pl.ds(pl.multiple_of(start, 16), size),)

    def across(self, item, across):
        piece, step = item
        place = self.place
        slot = step * (place.minor - 1) + across - 1
        index = self.part_rows(place.slot(step, across), piece * self.size, self.size)
        return send(
            place,
            self.part.at[index],
            self.got1.at[slot, self.rows(piece)],
            place.slot(0, across),
            self.sends1,
            self.arrivals1,
            slot * self.pieces + piece,
        )

    def along(self, item):
        piece, step = item
        place = self.place
        return send(
            place,
            self.mine.at[step - 1, self.rows(piece)],
            self.got2.at[step - 1, self.rows(piece)],
            place.slot(step, 0),
            self.sends2,
            self.arrivals2,
            (step - 1) * self.pieces + piece,
        )

    def begin(self, item):
        for across in range(1, self.place.minor):
            self.across(item, across).start()
        if self.loads is not None:
            self.load(item[1]).start()

    def load(self, step):
        target = self.mine.at[step - 1] if step else self.total
        return pltpu.make_async_copy(
            self.part.at[self.place.slot(step, 0)], target, self.loads.at[step]
        )

    def own(self, step, rows):
        if self.loads is None:
            return self.part[self.part_rows(self.place.slot(step, 0), rows, 16)].astype(F32)
        source = self.mine.at[step - 1] if step else self.total
        return source[pl.ds(rows, 16)].astype(F32)

    def blocks(self, piece, body):
        def one(at, _):
            body(pl.multiple_of(piece * self.size + at * 16, 16))
            return 0

        lax.fori_loop(0, self.size // 16, one, 0)

    def handle(self, item):
        piece, step = item
        place = self.place
        for across in range(1, place.minor):
            self.across(item, across).wait_recv()
        if self.loads is not None:
            self.load(step).wait()
        if step == 0:
            return

        def body(start):
            value = self.own(step, start)
            rows = pl.ds(start, 16)
            for across in range(1, place.minor):
                slot = step * (place.minor - 1) + across - 1
                value = value + self.got1[slot, rows].astype(F32)
            self.mine[step - 1, rows] = value.astype(BF16)

        self.blocks(piece, body)
        self.along(item).start()

    def close(self, piece):
        place = self.place
        for step in range(1, place.major):
            self.along((piece, step)).wait_recv()

        def body(start):
            value = self.own(0, start)
            rows = pl.ds(start, 16)
            for across in range(1, place.minor):
                value = value + self.got1[across - 1, rows].astype(F32)
            for step in range(1, place.major):
                value = value + self.got2[step - 1, rows].astype(F32)
            self.total[rows] = value.astype(self.total.dtype)

        self.blocks(piece, body)

    def finish(self):
        for item in self.items():
            for across in range(1, self.place.minor):
                self.across(item, across).wait_send()
            if item[1]:
                self.along(item).wait_send()


WEIGHT_PIECES = 3
TOKEN_PIECES = 4
HBM = pl.BlockSpec(memory_space=pl.ANY)
VMEM = pl.BlockSpec(memory_space=pltpu.VMEM)


def comm_params(number):
    return pltpu.CompilerParams(
        collective_id=number, has_side_effects=True, vmem_limit_bytes=VMEM_BYTES
    )


def resident(x):
    return pl.BlockSpec(
        x.shape, lambda i: (0,) * len(x.shape), pipeline_mode=pl.Buffered(buffer_count=1)
    )


def run_forward(heads, tokens, cotangent, small, dt_weight, seg_pad, seg_row, spread, in_weight, out_weight):
    ring, seq = places()
    count, groups = lax.axis_size("fsdp"), lax.axis_size("seq")
    rows, own_rows = in_weight.shape[0], tokens.shape[0]
    length = own_rows * groups
    blocks = length // STRETCH
    wide = heads * HEAD
    edge = wide + 2 * STATE
    levels = levels_of("seq")
    shape = jax.ShapeDtypeStruct
    split = halved(rows, groups)
    own_shared = rows // groups if split else rows
    shared_shape = (count, groups, own_shared, SHARED) if split else (D, SHARED)

    def chunk(columns):
        return pl.BlockSpec((STRETCH, columns), lambda i: (i - i // blocks, 0))

    wholes = [tokens, cotangent, small, dt_weight, seg_pad, seg_row, spread]
    late = [
        shape((D, wide), BF16),
        shape((8, wide), F32),
        shape((8, edge), F32),
        shape((8, 128), F32),
        shape((8, wide), F32),
    ]
    dma = pltpu.SemaphoreType.DMA
    scratch = [
        pltpu.VMEM((own_shared, 2 * STATE), F32),
        pltpu.VMEM((rows, wide), BF16),
        pltpu.VMEM((rows, wide), BF16),
        pltpu.VMEM((rows, wide), BF16),
        pltpu.VMEM((own_shared, SHARED), BF16),
        pltpu.VMEM((own_rows, 2 * D), BF16),
        pltpu.VMEM((D, wide), BF16),
        pltpu.VMEM((D, wide), BF16),
        pltpu.VMEM((D, wide), BF16),
        pltpu.VMEM(shared_shape, BF16),
        pltpu.VMEM((count, own_shared, SHARED) if split else (16, 128), BF16),
        pltpu.VMEM((STRETCH, D), BF16),
        pltpu.VMEM((length, 2 * D), BF16),
        pltpu.VMEM((D, length), BF16),
        pltpu.VMEM((length, wide), F32),
        pltpu.VMEM((length, wide), BF16),
        pltpu.VMEM((length, wide), F32),
        pltpu.VMEM((STRETCH + 8, edge), F32),
        pltpu.VMEM((STATE, wide), F32),
        pltpu.VMEM((8, INNER + 128), F32),
        pltpu.VMEM((length, wide), BF16),
        pltpu.VMEM((length, wide), BF16),
        pltpu.VMEM((length, wide), BF16),
        pltpu.VMEM((D, length), BF16),
        pltpu.VMEM((D, wide), BF16),
        pltpu.VMEM((2 * (levels + 1), 8, length), F32),
        pltpu.VMEM((2 * levels, 8, length), F32),
        dma((12,)),
        dma((2 * levels,)),
        dma((2 * levels,)),
    ]
    scratch = scratch + Gather.scratch(ring, WEIGHT_PIECES) + Gather.scratch(ring, 1)
    scratch = scratch + Gather.scratch(ring, 1) + Gather.scratch(seq, TOKEN_PIECES)
    scratch = scratch + Gather.scratch(ring, 1) + Gather.scratch(seq, 1)
    return pl.pallas_call(
        partial(forward_kernel, heads),
        grid=(blocks + 1,),
        in_specs=[resident(x) for x in wholes] + [HBM, HBM],
        out_specs=[
            chunk(edge),
            chunk(edge),
            chunk(128),
            pl.BlockSpec((1, STATE, wide), lambda i: (i - i // blocks, 0, 0)),
        ]
        + [resident(x) for x in late]
        + [HBM] * 8,
        out_shape=[
            shape((length, edge), F32),
            shape((length, edge), BF16),
            shape((length, 128), F32),
            shape((blocks, STATE, wide), F32),
        ]
        + late
        + [shape((D, wide), BF16), shape((D, wide), BF16), shape(shared_shape, BF16)]
        + [shape((length, D), BF16), shape((length, wide), BF16), shape((length, wide), BF16)]
        + [shape((D, length), BF16), shape((D, wide), BF16)],
        scratch_shapes=scratch,
        compiler_params=pltpu.CompilerParams(
            collective_id=1,
            has_side_effects=True,
            vmem_limit_bytes=61 * 1024 * 1024,
            dimension_semantics=("arbitrary",),
        ),
        name="gather_and_forward",
    )(*wholes, in_weight, out_weight)


def backward_kernel(heads, *refs):
    chunk = refs[:5]
    packs = refs[5:12]
    d_z, w_z, w_x, w_s, normed_t, tokens, small, d_gain = refs[12:20]
    out_part, z_part, branch_part = refs[20:23]
    out_all, z_all, x_all, s_all, small_all, branch, d_normed, d_conv, d_head = refs[23:32]
    extended, d_state, d_rest, x_part, s_part, act_part, out_own, z_own, x_own, s_own, s_mid = refs[32:43]
    small_sums, small_got, small_sends, small_arrivals, out_loads, z_loads, branch_loads = refs[43:50]
    scratch = refs[50:]
    ring, seq = places()
    rows = x_own.shape[0]
    own_rows = act_part.shape[1]
    wide = heads * HEAD
    edge = wide + 2 * STATE
    groups = seq.major * seq.minor
    own_shared = s_own.shape[0]
    split = halved(rows, groups)
    levels = levels_of("fsdp")

    def stream(place, part, total, extent, pieces, at, loads=None):
        return Reduce(place, part, total, extent, pieces, scratch[7 * at : 7 * at + 7], loads)

    def spreading(own, full, pieces, at):
        return Gather(seq, own, full, own.shape[0], pieces, scratch[49 + 5 * at : 54 + 5 * at])

    out_sum = stream(ring, out_part, out_own, rows, 1, 0, out_loads)
    z_sum = stream(ring, z_part, z_own, rows, 1, 1, z_loads)
    x_sum = stream(ring, x_part, x_own, rows, WEIGHT_PIECES, 2)
    branch_sum = stream(seq, branch_part, branch, own_rows, 1, 3, branch_loads)
    d_normed_sum = stream(seq, act_part, d_normed, own_rows, 2, 4)
    if split:
        mid_sum = stream(seq, s_part, s_mid, s_mid.shape[0], 1, 5)
        s_sum = stream(ring, s_mid, s_own, own_shared, 1, 6)
    else:
        s_sum = stream(ring, s_part, s_own, rows, 1, 6)
    out_spread = spreading(out_own, out_all, 1, 0)
    z_spread = spreading(z_own, z_all, 1, 1)
    x_spread = spreading(x_own, x_all, WEIGHT_PIECES, 2)
    s_spread = spreading(s_own, s_all, 1, 3)
    small_spread = spreading(small_sums.at[levels], small_all, 1, 4)
    early = [(s, item) for s in (out_sum, z_sum) for item in s.items()]
    at_step = pl.program_id(0)
    blocks = d_rest.shape[0] // STRETCH

    def swap(level):
        return exchange(
            "fsdp",
            level,
            small_sums.at[level],
            small_got.at[level],
            small_sends.at[level],
            small_arrivals.at[level],
        )

    @pl.when(at_step == 0)
    def _():
        meet(ring, seq)
        for s, item in early:
            s.begin(item)
        for item in branch_sum.items():
            branch_sum.begin(item)

    backward_block(heads, *chunk, *packs, d_conv, d_head, extended, d_state, d_rest)

    for k in range(blocks):

        @pl.when(at_step == k)
        def _():
            s, item = early[k]
            s.handle(item)
            if k == blocks - 1:
                for item in branch_sum.items():
                    branch_sum.handle(item)
                branch_sum.close(0)
                branch_sum.finish()

    @pl.when(at_step == blocks - 1)
    def _():
        def x_block(slot):
            here = pl.ds(pl.multiple_of(slot * rows, 16), rows)

            def one(at, _):
                columns = pl.ds(pl.multiple_of(at * 384, 128), 384)
                x_part[slot, :, columns] = dot(normed_t[here, :], d_rest[:, columns]).astype(BF16)
                return 0

            lax.fori_loop(0, wide // 384, one, 0)

        def s_block(slot, _):
            here = pl.ds(pl.multiple_of(slot * rows, 16), rows)
            value = dot(normed_t[here, :], d_rest[:, wide:]).astype(BF16)
            if split:
                target = pl.ds(pl.multiple_of(slot * own_shared, 16), own_shared)
                for s in range(groups):
                    s_part[s, target, :] = value[s * own_shared : (s + 1) * own_shared]
            else:
                s_part[slot] = value
            return 0

        def normed_block(slot):
            here = pl.ds(pl.multiple_of(slot * own_rows, own_rows), own_rows)

            def one(at, _):
                columns = pl.ds(pl.multiple_of(at * 512, 128), 512)
                value = dot(d_z[here, :], w_z[columns, :], ((1,), (1,)))
                value = value + dot(d_rest[here, :wide], w_x[columns, :], ((1,), (1,)))
                value = value + dot(d_rest[here, wide:], w_s[columns, :], ((1,), (1,)))
                act_part[slot, :, columns] = value.astype(BF16)
                return 0

            lax.fori_loop(0, D // 512, one, 0)

        waiting = early[blocks:]

        def handle_early(amount=1):
            for _ in range(min(amount, len(waiting))):
                s, item = waiting.pop(0)
                s.handle(item)

        lax.fori_loop(0, ring.major * ring.minor, s_block, 0)
        if split:
            for item in mid_sum.items():
                mid_sum.begin(item)
        else:
            for item in s_sum.items():
                s_sum.begin(item)
        handle_early()
        for step in x_sum.steps():
            for across in range(1, ring.minor):
                x_block(ring.slot(step, across))
            for piece in range(WEIGHT_PIECES):
                x_sum.begin((piece, step))
        if split:
            for item in mid_sum.items():
                mid_sum.handle(item)
        handle_early()
        for step in d_normed_sum.steps():
            for across in range(1, seq.minor):
                normed_block(seq.slot(step, across))
            for piece in range(2):
                d_normed_sum.begin((piece, step))
        if split:
            mid_sum.close(0)
            for item in s_sum.items():
                s_sum.begin(item)
        handle_early()
        for step in x_sum.steps():
            x_block(ring.slot(step, 0))
        for step in d_normed_sum.steps():
            normed_block(seq.slot(step, 0))
        handle_early(len(waiting))
        out_sum.close(0)
        out_spread.begin(0)
        side = d_normed_sum.items() + [None] * (2 + levels)
        work = [(x_sum, item) for item in x_sum.items()] + [(s_sum, item) for item in s_sum.items()]

        def sideways(at):
            first = len(d_normed_sum.items())
            if at < first:
                d_normed_sum.handle(side[at])
                return
            if at == first:
                for piece in range(2):
                    d_normed_sum.close(piece)
                inputs = tokens[...].astype(F32)
                rms = lax.rsqrt(jnp.mean(inputs * inputs, axis=-1, keepdims=True) + NORM_EPS)
                small_sums[0] = jnp.zeros(small_sums.shape[1:], F32)
                small_sums[0, 0 : KERNEL + 1, :edge] = d_conv[0 : KERNEL + 1, :]
                small_sums[0, 5:6, :] = jnp.sum(
                    d_normed[...].astype(F32) * (inputs * rms), axis=0, keepdims=True
                )
                small_sums[0, 6:7, :wide] = d_gain[0:1, :]
                for k in range(3):
                    small_sums[0, 7:8, 128 * k : 128 * (k + 1)] = d_head[k : k + 1, :]
                swap(0).start()
                return
            level = at - first - 1
            if level < levels:
                swap(level).wait()
                small_sums[level + 1] = small_sums[level] + small_got[level]
                if level + 1 < levels:
                    swap(level + 1).start()
                else:
                    small_spread.begin(0)
                    small_spread.keep().start()

        done = 0
        for at, (s, item) in enumerate(work):
            s.handle(item)
            sideways(at)
            done = at + 1
            if at == WEIGHT_PIECES:
                z_sum.close(0)
                z_spread.begin(0)
                out_spread.forward(0)
        for at in range(done, len(side)):
            sideways(at)
        for piece in range(WEIGHT_PIECES):
            x_sum.close(piece)
            x_spread.begin(piece)
        s_sum.close(0)
        s_spread.begin(0)
        spreads = (out_spread, z_spread, x_spread, s_spread)
        for s in spreads:
            s.keep().start()
        z_spread.forward(0)
        small_spread.forward(0)
        for piece in range(WEIGHT_PIECES):
            x_spread.forward(piece)
        s_spread.forward(0)
        for s in (out_sum, z_sum, x_sum, s_sum, d_normed_sum):
            s.finish()
        if split:
            mid_sum.finish()
        for s in spreads + (small_spread,):
            s.finish()
            s.keep().wait()


def run_backward(
    heads, d_y, pre, conv, dt_pre, states, seg_pad, seg_row, packs, spread, d_z, weights, normed_t,
    tokens, small, d_gain, out_part, z_part, branch_part,
):
    length = d_y.shape[0]
    blocks = length // STRETCH
    wide = heads * HEAD
    edge = wide + 2 * STATE
    ring, seq = places()
    count, groups = lax.axis_size("fsdp"), lax.axis_size("seq")
    levels = levels_of("fsdp")

    def parted(x, by):
        return x.reshape(by, x.shape[0] // by, x.shape[1])

    out_part, z_part = parted(out_part, count), parted(z_part, count)
    branch_part = parted(branch_part, groups)
    rows, own_rows = out_part.shape[1], branch_part.shape[1]
    split = halved(rows, groups)
    own_shared = rows // groups if split else rows
    mid_rows = own_shared * count if split else 16
    wholes = [
        seg_pad, seg_row, *packs, spread, spread.T, d_z, *weights, normed_t, tokens, small, d_gain
    ]
    dma = pltpu.SemaphoreType.DMA
    scratch = [
        pltpu.VMEM((STRETCH + 8, edge), F32),
        pltpu.VMEM((STATE, wide), F32),
        pltpu.VMEM((length, wide + SHARED), BF16),
        pltpu.VMEM((count, rows, wide), BF16),
        pltpu.VMEM((groups, mid_rows, SHARED) if split else (count, rows, SHARED), BF16),
        pltpu.VMEM((groups, own_rows, D), BF16),
        pltpu.VMEM((rows, wide), BF16),
        pltpu.VMEM((rows, wide), BF16),
        pltpu.VMEM((rows, wide), BF16),
        pltpu.VMEM((own_shared, SHARED), BF16),
        pltpu.VMEM((mid_rows, SHARED), BF16),
        pltpu.VMEM((levels + 1, 8, D), F32),
        pltpu.VMEM((levels, 8, D), F32),
        dma((levels,)),
        dma((levels,)),
        dma((ring.major,)),
        dma((ring.major,)),
        dma((seq.major,)),
    ]
    scratch = scratch + Reduce.scratch(ring, rows, wide, 1) + Reduce.scratch(ring, rows, wide, 1)
    scratch = scratch + Reduce.scratch(ring, rows, wide, WEIGHT_PIECES)
    scratch = scratch + Reduce.scratch(seq, own_rows, D, 1) + Reduce.scratch(seq, own_rows, D, 2)
    scratch = scratch + Reduce.scratch(seq, mid_rows, SHARED, 1)
    scratch = scratch + Reduce.scratch(ring, own_shared, SHARED, 1)
    for pieces in (1, 1, WEIGHT_PIECES, 1, 1):
        scratch = scratch + Gather.scratch(seq, pieces)
    shape = jax.ShapeDtypeStruct
    gathered = [
        shape((groups, rows, wide), BF16),
        shape((groups, rows, wide), BF16),
        shape((groups, rows, wide), BF16),
        shape((groups, own_shared, SHARED), BF16),
        shape((groups, 8, D), F32),
    ]
    summed = [
        shape((own_rows, D), BF16),
        shape((own_rows, D), BF16),
        shape((8, edge), F32),
        shape((8, 128), F32),
    ]
    return pl.pallas_call(
        partial(backward_kernel, heads),
        grid=(blocks,),
        in_specs=[
            block(wide, blocks),
            block(edge, blocks),
            block(edge, blocks),
            block(128, blocks),
            pl.BlockSpec((1, STATE, wide), lambda i: (blocks - 1 - i, 0, 0)),
        ]
        + [resident(x) for x in wholes]
        + [HBM] * 3,
        out_specs=[HBM] * 5 + [resident(x) for x in summed],
        out_shape=gathered + summed,
        scratch_shapes=scratch,
        compiler_params=pltpu.CompilerParams(
            collective_id=2,
            has_side_effects=True,
            vmem_limit_bytes=61 * 1024 * 1024,
            dimension_semantics=("arbitrary",),
        ),
        name="backward_and_sums",
    )(d_y, pre, conv, dt_pre, states, *wholes, out_part, z_part, branch_part)


def exchange(place_axis, level, source, got, sends, arrivals):
    index = lax.axis_index(place_axis)
    other = partner(index, level)
    return pltpu.make_async_remote_copy(
        src_ref=source,
        dst_ref=got,
        send_sem=sends,
        recv_sem=arrivals,
        device_id={place_axis: other},
        device_id_type=pl.DeviceIdType.MESH,
    )


def partner(index, level):
    bit = 2**level
    return index + (1 - 2 * (index // bit % 2)) * bit


def levels_of(axis):
    return lax.axis_size(axis).bit_length() - 1


class Push:
    def __init__(self, axis, own, slots, sends, arrivals):
        self.axis, self.own, self.slots = axis, own, slots
        self.sends, self.arrivals = sends, arrivals
        self.count = lax.axis_size(axis)

    def copy(self, step):
        index = lax.axis_index(self.axis)
        return pltpu.make_async_remote_copy(
            src_ref=self.own,
            dst_ref=self.slots.at[index],
            send_sem=self.sends.at[step - 1],
            recv_sem=self.arrivals.at[step - 1],
            device_id={self.axis: (index + step) % self.count},
            device_id_type=pl.DeviceIdType.MESH,
        )

    def begin(self):
        for step in range(1, self.count):
            self.copy(step).start()

    def finish(self):
        for step in range(1, self.count):
            self.copy(step).wait()


def norm_kernel(sums, norms_out, own, slots, sends, arrivals):
    push = Push("fsdp", own, slots, sends, arrivals)
    index = lax.axis_index("fsdp")
    barrier = pltpu.get_barrier_semaphore()
    for step in range(1, push.count):
        other = (index + step) % push.count
        pl.semaphore_signal(
            barrier, inc=1, device_id={"fsdp": other}, device_id_type=pl.DeviceIdType.MESH
        )
    own[...] = jnp.broadcast_to(jnp.sum(sums[...], axis=1, keepdims=True), (8, 128))
    slots[index] = own[...]
    pl.semaphore_wait(barrier, push.count - 1)
    push.begin()
    push.finish()
    total = slots[0]
    for k in range(1, push.count):
        total = total + slots[k]
    norms_out[...] = jnp.sqrt(total)


def run_norms(sums):
    count = lax.axis_size("fsdp")
    dma = pltpu.SemaphoreType.DMA
    return pl.pallas_call(
        norm_kernel,
        in_specs=[VMEM],
        out_specs=VMEM,
        out_shape=jax.ShapeDtypeStruct((8, 128), F32),
        scratch_shapes=[
            pltpu.VMEM((8, 128), F32),
            pltpu.VMEM((count, 8, 128), F32),
            dma((count - 1,)),
            dma((count - 1,)),
        ],
        compiler_params=comm_params(3),
        name="norms",
    )(sums)


def small_update(groups, heads, small_all, small_w, small_m, small_v, outs, small_grad):
    wide = heads * HEAD
    edge = wide + 2 * STATE
    everyone = [small_all[s] for s in range(groups)]
    shared = everyone[0]
    for other in everyone[1:]:
        shared = shared + other
    small_grad[:, :D] = shared[5:6, :]
    for k in range(KERNEL + 1):
        base = D + k * CONV
        for s in range(groups):
            small_grad[:, base + s * wide : base + (s + 1) * wide] = everyone[s][k : k + 1, :wide]
        small_grad[:, base + INNER : base + CONV] = shared[k : k + 1, wide:edge]
    size = 3 * HEADS + INNER
    size = size + -size % 128
    lane = lax.broadcasted_iota(jnp.int32, (8, size), 1)
    rest = jnp.zeros((8, size), F32)
    gap = jnp.zeros((8, size - 128), F32)
    for s in range(groups):
        for k in range(3):
            part = jnp.broadcast_to(everyone[s][7:8, 128 * k : 128 * (k + 1)], (8, 128))
            part = jnp.concatenate([part, gap], axis=1)
            part = jnp.where(lane < heads, part, 0.0)
            move = k * HEADS + s * heads
            rest = rest + (pltpu.roll(part, move, 1) if move else part)
    gains = [jnp.broadcast_to(one[6:7, :wide], (8, wide)) for one in everyone]
    gains = gains + [jnp.zeros((8, size - INNER), F32)]
    rest = rest + pltpu.roll(jnp.concatenate(gains, axis=1), 3 * HEADS, 1)
    base = D + (KERNEL + 1) * CONV
    small_grad[:, base : base + size] = rest[0:1, :]
    gradient = small_grad[...]
    first, second, direction = adam_parts(gradient, small_m[...], small_v[...])
    values = (gradient, small_w[...] - LEARN_RATE * direction, first, second)
    for ref, value in zip(outs, values, strict=True):
        ref[...] = value[:, : ref.shape[1]]


def moments_kernel(groups, heads, *refs):
    z_piece, x_piece, tails, out_piece = refs[:4]
    small_all, small_w, small_m, small_v = refs[4:8]
    w_in, m_in, v_in, w_out, m_out, v_out = refs[8:14]
    g_in_new, m_in_new, v_in_new, u_in, g_out_new, m_out_new, v_out_new, u_out = refs[14:22]
    sums = refs[22]
    small_outs = refs[23:27]
    u_tail, small_grad = refs[27:29]
    wide = heads * HEAD

    @pl.when(pl.program_id(0) == 0)
    def _():
        sums[...] = jnp.zeros_like(sums)
        small_update(groups, heads, small_all, small_w, small_m, small_v, small_outs, small_grad)

    def update(gradient, start, w, m, v, g_new, m_new, v_new, u, at):
        size = min(gradient.shape[1], w.shape[1] - start)
        here = slice(start, start + size)
        gradient = gradient[:, :size]
        first, second, direction = adam_parts(gradient, m[:, here], v[:, here])
        weight = w[:, here]
        direction = direction + WEIGHT_DECAY * weight
        g_new[:, here] = gradient
        m_new[:, here] = first
        v_new[:, here] = second
        if u is None:
            u_tail[:, :size] = direction
        else:
            u[:, here] = direction.astype(BF16)
        sums[at : at + 1, :size] += jnp.sum(weight * weight, axis=0, keepdims=True)
        sums[at + 1 : at + 2, :size] += jnp.sum(direction * direction, axis=0, keepdims=True)

    inside = (w_in, m_in, v_in, g_in_new, m_in_new, v_in_new, u_in)
    outside = (w_out, m_out, v_out, g_out_new, m_out_new, v_out_new, u_out)
    for s in range(groups):
        update(z_piece[s].astype(F32), s * wide, *inside, 0)
        update(x_piece[s].astype(F32), INNER + s * wide, *inside, 0)
        update(out_piece[s].astype(F32), s * wide, *outside, 2)
    gradient = tails[0].astype(F32)
    for s in range(1, tails.shape[0]):
        gradient = gradient + tails[s].astype(F32)
    update(gradient, 2 * INNER, *inside[:-1], None, 0)


ROWS = 16


def by_rows(columns):
    return pl.BlockSpec((ROWS, columns), lambda i: (i, 0))


def run_moments(groups, heads, z_all, x_all, s_all, out_all, smalls, inside, outside):
    rows = inside[0].shape[0]
    wide = heads * HEAD
    piece = pl.BlockSpec((groups, ROWS, wide), lambda i: (0, i, 0))
    if s_all.shape[1] < rows:
        parts = s_all.shape[1] // ROWS
        tails = pl.BlockSpec((1, ROWS, SHARED), lambda i: (i // parts, i % parts, 0))
    else:
        tails = pl.BlockSpec((groups, ROWS, SHARED), lambda i: (0, i, 0))
    shape = jax.ShapeDtypeStruct
    extent = D + (KERNEL + 1) * CONV + 3 * HEADS + INNER
    small_out = [shape((1, extent), F32)] * 4
    in_like, out_like = shape(inside[0].shape, F32), shape(outside[0].shape, F32)
    in_spec, out_spec = by_rows(PROJ), by_rows(INNER)
    return pl.pallas_call(
        partial(moments_kernel, groups, heads),
        grid=(rows // ROWS,),
        in_specs=[piece, piece, tails, piece]
        + [resident(x) for x in smalls]
        + [in_spec] * 3
        + [out_spec] * 3,
        out_specs=[in_spec] * 3
        + [by_rows(2 * INNER)]
        + [out_spec] * 4
        + [pl.BlockSpec((8, wide), lambda i: (0, 0))]
        + [resident(x) for x in small_out]
        + [by_rows(SHARED)],
        out_shape=[in_like] * 3
        + [shape((rows, 2 * INNER), BF16)]
        + [out_like] * 3
        + [shape(out_like.shape, BF16), shape((8, wide), F32)]
        + small_out
        + [shape((rows, SHARED), F32)],
        scratch_shapes=[pltpu.VMEM(smalls[1].shape, F32)],
        compiler_params=compiler_params(),
        name="moments",
    )(z_all, x_all, s_all, out_all, *smalls, *inside, *outside)


def weights_kernel(norms, w_in, u_in, u_tail, w_out, u_out, in_new, out_new):
    in_rate, out_rate = [
        LEARN_RATE * (norms[at : at + 1, :1] / norms[at + 1 : at + 2, :1]) for at in (0, 2)
    ]
    edge = u_in.shape[1]
    rest = w_in.shape[1] - edge
    in_new[:, :edge] = w_in[:, :edge] - in_rate * u_in[...].astype(F32)
    in_new[:, edge:] = w_in[:, edge:] - in_rate * u_tail[:, :rest]
    out_new[...] = w_out[...] - out_rate * u_out[...].astype(F32)


def run_weights(norms, w_in, u_in, u_tail, w_out, u_out):
    in_spec, out_spec = by_rows(PROJ), by_rows(INNER)
    return pl.pallas_call(
        weights_kernel,
        grid=(w_in.shape[0] // ROWS,),
        in_specs=[
            resident(norms), in_spec, by_rows(2 * INNER), by_rows(SHARED), out_spec, out_spec
        ],
        out_specs=[in_spec, out_spec],
        out_shape=[
            jax.ShapeDtypeStruct(w_in.shape, F32),
            jax.ShapeDtypeStruct(w_out.shape, F32),
        ],
        compiler_params=compiler_params(),
        name="weights",
    )(norms, w_in, u_in, u_tail, w_out, u_out)


def adam_parts(gradient, first_old, second_old):
    first_new = FIRST_DECAY * first_old + (1.0 - FIRST_DECAY) * gradient
    second_new = SECOND_DECAY * second_old + (1.0 - SECOND_DECAY) * (gradient * gradient)
    first_scale = 1.0 / (1.0 - FIRST_DECAY**STEP)
    second_scale = 1.0 / (1.0 - SECOND_DECAY**STEP)
    direction = (first_new * first_scale) / (jnp.sqrt(second_new * second_scale) + ADAM_EPSILON)
    return (first_new, second_new, direction)


def wide_row(vector):
    return jnp.pad(vector, (0, -vector.shape[0] % 128))[None, :]


def shards(
    tokens,
    cotangent,
    segments,
    in_weight,
    out_weight,
    small_params,
    in_first,
    in_second,
    out_first,
    out_second,
    small_first,
    small_second,
):
    in_gain = small_params[:D]
    groups = lax.axis_size("seq")
    where_seq = lax.axis_index("seq")
    heads = HEADS // groups
    wide = INNER // groups
    segment_row = segments[0]

    def own(vector, axis=-1):
        size = vector.shape[axis] // groups
        return lax.dynamic_slice_in_dim(vector, where_seq * size, size, axis)

    inputs = tokens[0].astype(F32)
    in_rms = lax.rsqrt(jnp.mean(inputs * inputs, axis=-1, keepdims=True) + NORM_EPS)
    dt_weight = jnp.pad(
        in_weight[:, INNER + CONV :].astype(BF16), ((0, 0), (0, DT_PAD - HEADS))
    )
    small = wide_row(small_params)
    spread_heads = (
        jnp.arange(128)[:, None] == jnp.arange(wide)[None, :] // HEAD
    ).astype(BF16)
    seg_pad = jnp.pad(segment_row, (EDGE, EDGE), constant_values=-1)[:, None]
    (
        pre, conv_in, dt_pre, states, z_part, d_out_gain, conv_pack, head_pack, chan_pack,
        w_x, w_z, w_s, branch_part, d_y, d_z, normed_t, out_part,
    ) = run_forward(
        heads, tokens[0], cotangent[0], small, dt_weight, seg_pad, segments, spread_heads,
        in_weight, out_weight,
    )
    packs = (conv_pack, head_pack, chan_pack)
    out_all, z_all, x_all, s_all, small_all, branch, d_normed, _, _ = run_backward(
        heads, d_y, pre, conv_in, dt_pre, states, seg_pad, segments, packs, spread_heads, d_z,
        (w_z, w_x, w_s.reshape(D, SHARED)), normed_t, tokens[0], small, d_out_gain, out_part, z_part, branch_part,
    )
    output = (inputs + branch.astype(F32)).astype(BF16)[None]
    d_normed = d_normed.astype(F32)
    slope = d_normed * in_gain[None, :]
    d_inputs = slope * in_rms - inputs * (in_rms**3 / D) * jnp.sum(
        slope * inputs, axis=1, keepdims=True
    )
    input_grad = (cotangent[0].astype(F32) + d_inputs)[None]

    (
        in_grad, in_first_new, in_second_new, in_dir, out_grad, out_first_new, out_second_new, out_dir,
        squares, small_grad, small_new, small_first_new, small_second_new, in_tail,
    ) = run_moments(
        groups, heads, z_all, x_all, s_all, out_all,
        (small_all, small, wide_row(small_first), wide_row(small_second)),
        (in_weight, in_first, in_second), (out_weight, out_first, out_second),
    )
    norms = run_norms(squares)
    in_new, out_new = run_weights(norms, in_weight, in_dir, in_tail, out_weight, out_dir)
    small_grad, small_new, small_first_new, small_second_new = [
        x[0] for x in (small_grad, small_new, small_first_new, small_second_new)
    ]
    norms = norms[:4, 0]
    return (
        output,
        input_grad,
        in_grad,
        in_new,
        in_first_new,
        in_second_new,
        out_grad,
        out_new,
        out_first_new,
        out_second_new,
        small_grad,
        small_new,
        small_first_new,
        small_second_new,
        norms,
    )


def solution(mesh):
    matrix = P("fsdp", None)
    rows = P("fsdp", "seq", None)
    return jax.shard_map(
        shards,
        mesh=mesh,
        in_specs=(rows, rows, matrix, matrix, matrix, P(), matrix, matrix, matrix, matrix, P(), P()),
        out_specs=(rows, rows) + (matrix,) * 8 + (P(),) * 5,
        check_vma=False,
    )
```

```python
from functools import partial

import jax
import jax.numpy as jnp
from jax import lax
from jax.experimental import pallas as pl
from jax.experimental.pallas import tpu as pltpu
from jax.sharding import PartitionSpec as P

D = 1536
HEADS = 48
HEAD = 64
STATE = 128
KERNEL = 4
STRETCH = 256
STEP = 5
INNER = 3072
CONV = 3328
PROJ = 6448
DT_PAD = 128
SHARED = 2 * STATE + DT_PAD

NORM_EPS = 1e-05
FIRST_DECAY = 0.9
SECOND_DECAY = 0.999
ADAM_EPSILON = 1e-06
WEIGHT_DECAY = 0.01
LEARN_RATE = 0.5
F32 = jnp.float32
BF16 = jnp.bfloat16


def dot(a, b, dims=((1,), (0,))):
    return lax.dot_general(a, b, (dims, ((), ())), preferred_element_type=F32)


def split_dot(value, ones):
    high = value.astype(BF16)
    low = (value - high.astype(F32)).astype(BF16)
    return dot(high, ones) + dot(low, ones)


def tri_dot(ones, value):
    high = value.astype(BF16)
    rest = value - high.astype(F32)
    middle = rest.astype(BF16)
    low = (rest - middle.astype(F32)).astype(BF16)
    return dot(ones, high) + dot(ones, middle) + dot(ones, low)


def sigmoid(v):
    return 1.0 / (1.0 + jnp.exp(-v))


def softplus(v):
    return jnp.maximum(v, 0.0) + jnp.log1p(jnp.exp(-jnp.abs(v)))


def row_at_least():
    rows = lax.broadcasted_iota(jnp.int32, (STRETCH, STRETCH), 0)
    columns = lax.broadcasted_iota(jnp.int32, (STRETCH, STRETCH), 1)
    return rows >= columns


class Decays:
    def __init__(self, dt, rate, masks, spread):
        self.dt, self.spread = dt, spread
        lower = jnp.where(row_at_least(), 1.0, 0.0).astype(BF16)
        self.columns = dot(lower, dt) * rate
        self.rows = jnp.transpose(self.columns)
        last = self.columns[STRETCH - 1 :, :]
        self.into = jnp.exp(self.columns) * masks["carry"]
        self.out = jnp.exp(last - self.columns) * masks["tail"]
        self.through = jnp.broadcast_to(jnp.exp(last) * masks["keep"], (8, 128))
        self.bar = masks["bar"]

    def of(self, columns):
        ones = self.spread[:, columns]
        return (
            dot(self.dt, ones),
            split_dot(self.into, ones),
            split_dot(self.out, ones),
            split_dot(self.through, ones)[:1],
        )

    def between(self, head):
        return jnp.exp(self.columns[:, head : head + 1] - self.rows[head : head + 1, :] + self.bar)


EDGE = 8


def block_masks(seg_pad, seg_row, at):
    def rows(by, size=STRETCH):
        return seg_pad[pl.ds(at + EDGE + by, size), :]

    here = rows(0)
    first = jnp.where(at == 0, rows(0, 1), rows(-1, 1))
    last = rows(STRETCH - 1, 1)
    masks = {"carry": here == first, "tail": here == last, "keep": last == first}
    for by in range(1, KERNEL):
        masks[-by] = here == rows(-by)
        masks[by] = here == rows(by)
    masks = {key: jnp.where(value, 1.0, 0.0) for key, value in masks.items()}
    within = row_at_least() & (here == seg_row[:, pl.ds(at, STRETCH)])
    masks["bar"] = jnp.where(within, 0.0, -1e30)
    return masks


def forward_block(
    heads, at, normed, w_x, shared_columns, masks, packs, spread, outs, y_all, extended, state
):
    conv_pack, head_pack, chan_pack = packs
    pre_out, conv_out, dt_out, states_out = outs
    wide = heads * HEAD
    here = pl.ds(at, STRETCH)
    conv_low = jnp.concatenate([dot(normed, w_x[...]), dot(normed, shared_columns(0, 2 * STATE))], axis=1)
    conv_low = conv_low.astype(BF16)
    conv_out[...] = conv_low
    conv_in = conv_low.astype(F32)
    extended[8 : 8 + STRETCH, :] = conv_in
    pre = conv_pack[4:5, :] + conv_pack[3:4, :] * conv_in
    for by in range(1, KERNEL):
        pre = pre + conv_pack[3 - by : 4 - by, :] * (
            extended[8 - by : 8 - by + STRETCH, :] * masks[-by]
        )
    extended[0:8, :] = extended[STRETCH : STRETCH + 8, :]
    pre_out[...] = pre
    act = (pre * sigmoid(pre)).astype(BF16)
    b_mat = act[:, wide : wide + STATE]
    c_mat = act[:, wide + STATE :]
    lane = lax.broadcasted_iota(jnp.int32, (STRETCH, DT_PAD), 1)
    dt_pre = pltpu.roll(
        dot(normed, shared_columns(2 * STATE, DT_PAD)), DT_PAD - lax.axis_index("seq") * heads, 1
    )
    dt_pre = jnp.where(lane < heads, dt_pre, 0.0) + head_pack[0:1, :]
    dt_out[...] = dt_pre
    dt = softplus(dt_pre).astype(BF16)
    decay = Decays(dt, head_pack[1:2, :], masks, spread)
    scores = dot(c_mat, b_mat, ((1,), (1,)))
    first_half = lax.broadcasted_iota(jnp.int32, (STRETCH, 2 * HEAD), 1) < HEAD
    for pair in range(heads // 2):
        columns = slice(pair * 2 * HEAD, (pair + 1) * 2 * HEAD)
        steps, carry, tail, keep = decay.of(columns)
        xs = act[:, columns].astype(F32)
        scaled = xs * steps
        scaled_low = scaled.astype(BF16)
        old = state[:, columns]
        states_out[0, :, columns] = old
        y = dot(c_mat, old.astype(BF16)) * carry + chan_pack[0:1, columns] * xs
        state[:, columns] = old * keep + dot(b_mat, (scaled * tail).astype(BF16), ((0,), (0,)))
        halves = [
            dot((scores * decay.between(h)).astype(BF16), scaled_low)
            for h in (2 * pair, 2 * pair + 1)
        ]
        y_all[here, columns] = (y + jnp.where(first_half, halves[0], halves[1])).astype(BF16)


def fill_packs(heads, small, spread, packs, scratch_gain):
    conv_pack, head_pack, chan_pack = packs
    wide = heads * HEAD
    index = lax.axis_index("seq")
    start = pl.multiple_of(index * wide, 128)
    for ref in packs:
        ref[...] = jnp.zeros_like(ref)
    for k in range(KERNEL + 1):
        base = D + k * CONV
        conv_pack[k : k + 1, :wide] = small[:, pl.ds(base + start, wide)]
        conv_pack[k : k + 1, wide:] = small[:, base + INNER : base + CONV]
    base = D + (KERNEL + 1) * CONV
    window = jnp.broadcast_to(small[:, base : base + 256], (8, 256))
    lane = lax.broadcasted_iota(jnp.int32, (8, 256), 1)

    def own(k):
        moved = pltpu.roll(window, 256 - (k * HEADS + index * heads), 1)
        return jnp.where(lane < heads, moved, 0.0)[:, :128]

    head_pack[0:1, :] = own(0)[:1]
    rate = own(1)
    rate = jnp.where(lax.broadcasted_iota(jnp.int32, (8, 128), 1) < heads, -jnp.exp(rate), 0.0)
    head_pack[1:2, :] = rate[:1]
    chan_pack[0:1, :] = tri_spread(own(2), spread)[:1]
    base = base + 3 * HEADS
    shift = base % 128
    gain = jnp.broadcast_to(small[:, base - shift : base - shift + INNER + 128], (8, INNER + 128))
    scratch_gain[...] = pltpu.roll(gain, INNER + 128 - shift, 1)
    chan_pack[1:2, :] = scratch_gain[0:1, pl.ds(start, wide)]


def tri_spread(value, ones):
    high = value.astype(BF16)
    rest = value - high.astype(F32)
    middle = rest.astype(BF16)
    low = (rest - middle.astype(F32)).astype(BF16)
    return dot(high, ones) + dot(middle, ones) + dot(low, ones)


def as_row(column):
    lane = lax.broadcasted_iota(jnp.int32, (STRETCH, 128), 1)
    return jnp.transpose(jnp.where(lane == 0, column, 0.0))[0:8, :]


def as_column(rows):
    return jnp.transpose(jnp.concatenate([rows, jnp.zeros((120, STRETCH), F32)], axis=0))[:, 0:1]


def inverse_rms(squares):
    return lax.rsqrt(as_column(squares) / INNER + NORM_EPS)


def gate_gradients(y_low, z, d_mixed, gain, squares, products):
    rms = inverse_rms(squares)
    y = y_low.astype(F32)
    sig = sigmoid(z)
    silu = z * sig
    gated = y * silu
    unit = gated * rms
    d_gain = jnp.sum(d_mixed * unit, axis=0, keepdims=True)
    d_gated = d_mixed * gain * rms - unit * (rms * rms / INNER * as_column(products))
    d_z = d_gated * y * (sig * (1.0 + z * (1.0 - sig)))
    return (d_gated * silu).astype(BF16), d_z.astype(BF16), d_gain


def halved(rows, groups):
    return rows % (16 * groups) == 0


def forward_kernel(heads, *refs):
    tokens, cotangent, small, dt_weight, seg_pad, seg_row, spread_ref, in_weight, out_weight = refs[:9]
    outs = refs[9:13]
    z_part, d_gain = refs[13:15]
    packs = refs[15:18]
    w_x_out, w_z_out, w_s_out, branch_part, d_y_out, d_z_out, normed_t_out, out_part_out = refs[18:26]
    (
        stage_s, own_x, own_z, own_o, own_s, own_rows, w_x, w_z, w_o, w_s,
        shared_own, branch_stage, rows_all, returned_t, z_all, y_all, d_mixed_all, extended, state,
        scratch_gain, mixed_all, d_y, d_z, normed_t, out_part, sums, got, stage_sems, sum_sends, sum_arrivals,
    ) = refs[26:56]
    sems = refs[56:]
    ring, seq = places()
    wide = heads * HEAD
    edge = wide + 2 * STATE
    step = pl.program_id(0)
    blocks = pl.num_programs(0) - 1
    length = rows_all.shape[0]
    count = length // STRETCH
    rows = own_x.shape[0]
    split = halved(rows, seq.major * seq.minor)
    stage_x, stage_z, stage_o = [d_mixed_all.at[pl.ds(k * rows, rows)] for k in range(3)]

    def shared_columns(start, size):
        if split:
            return w_s[:, :, :, start : start + size].reshape(D, size)
        return w_s[:, start : start + size]

    get_x = Gather(ring, own_x, w_x, rows, WEIGHT_PIECES, sems[:5])
    get_z = Gather(ring, own_z, w_z, rows, 1, sems[5:10])
    get_o = Gather(ring, own_o, w_o, rows, 1, sems[10:15])
    get_rows = Gather(seq, own_rows, rows_all, own_rows.shape[0], TOKEN_PIECES, sems[15:20])
    if split:
        get_s = Gather(ring, own_s, shared_own, own_s.shape[0], 1, sems[20:25])
        pass_s = Gather(
            seq, shared_own, w_s, shared_own.shape[0], 1, sems[25:30],
            lambda slot, piece: w_s.at[:, slot],
        )
    else:
        get_s = Gather(ring, own_s, w_s, rows, 1, sems[20:25])
    saves = [
        pltpu.make_async_copy(source, target, stage_sems.at[4 + k])
        for k, (source, target) in enumerate(
            (
                (w_x, w_x_out),
                (w_z, w_z_out),
                (w_s, w_s_out),
                (normed_t, normed_t_out),
                (out_part, out_part_out),
                (d_y, d_y_out),
                (d_z, d_z_out),
            )
        )
    ]
    spread = spread_ref[...]
    at = pl.multiple_of(step * STRETCH, STRETCH)

    @pl.when(step == 0)
    def _():
        start = pl.multiple_of(seq.index * wide, 128)
        own_shared = own_s.shape[0]
        first_row = pl.multiple_of(seq.index * own_shared, 16) if split else 0
        sources = [
            (in_weight.at[pl.ds(first_row, own_shared), pl.ds(2 * INNER, 2 * STATE)], stage_s),
            (in_weight.at[:, pl.ds(INNER + start, wide)], stage_x),
            (in_weight.at[:, pl.ds(start, wide)], stage_z),
            (out_weight.at[:, pl.ds(start, wide)], stage_o),
        ]
        loads = [
            pltpu.make_async_copy(source, target, stage_sems.at[k])
            for k, (source, target) in enumerate(sources)
        ]
        for load in loads:
            load.start()
        meet(ring, seq)
        loads[0].wait()
        own_s[:, : 2 * STATE] = stage_s[...].astype(BF16)
        own_s[:, 2 * STATE :] = dt_weight[pl.ds(first_row, own_shared), :]
        get_s.begin(0)
        get_s.keep().start()
        loads[1].wait()
        own_x[...] = stage_x[...].astype(BF16)
        for piece in range(WEIGHT_PIECES):
            get_x.begin(piece)
        get_x.keep().start()
        inputs = tokens[...].astype(F32)
        rms = lax.rsqrt(jnp.mean(inputs * inputs, axis=-1, keepdims=True) + NORM_EPS)
        own_rows[:, :D] = (inputs * rms * small[:, :D]).astype(BF16)
        own_rows[:, D:] = cotangent[...]
        for piece in range(TOKEN_PIECES):
            get_rows.begin(piece)
        get_rows.keep().start()
        loads[2].wait()
        loads[3].wait()
        own_z[...] = stage_z[...].astype(BF16)
        own_o[...] = stage_o[...].astype(BF16)
        get_z.begin_across(0)
        get_o.begin_across(0)
        get_z.keep().start()
        get_o.keep().start()
        fill_packs(heads, small, spread, packs, scratch_gain)
        state[...] = jnp.zeros_like(state)
        extended[0:8, :] = jnp.zeros((8, edge), F32)
        d_gain[...] = jnp.zeros_like(d_gain)
        get_s.forward(0)
        get_rows.forward(0)
        get_x.forward(0)
        get_s.finish()
        get_s.keep().wait()
        if split:
            pass_s.begin(0)
            pass_s.keep().start()
        get_rows.forward(1)
        get_x.forward(1)
        get_z.begin_along(0)
        get_rows.forward(2)
        get_x.forward(2)
        get_o.begin_along(0)
        for piece in range(3, TOKEN_PIECES):
            get_rows.forward(piece)
        if split:
            pass_s.forward(0)
        get_rows.finish()
        get_rows.keep().wait()

        def turn(k, _):
            here = pl.ds(pl.multiple_of(k * STRETCH, STRETCH), STRETCH)
            normed_t[:, here] = jnp.transpose(rows_all[here, :D])
            returned_t[:, here] = jnp.transpose(rows_all[here, D:])
            return 0

        lax.fori_loop(0, count, turn, 0)
        if split:
            pass_s.finish()
            pass_s.keep().wait()
        get_x.finish()
        get_x.keep().wait()
        get_z.forward_step(0, 1)
        saves[0].start()
        saves[2].start()
        saves[3].start()

    @pl.when(step < blocks)
    def _():
        masks = block_masks(seg_pad, seg_row, at)
        forward_block(
            heads, at, rows_all[pl.ds(at, STRETCH), :D], w_x, shared_columns, masks, packs, spread, outs,
            y_all, extended, state,
        )

    forwards = [(stream, k) for stream in (get_z, get_o) for k in range(1, ring.major)][1:]
    ahead = min(count, len(forwards))
    for k in range(ahead):

        @pl.when(step == k)
        def _():
            stream, by = forwards[k]
            stream.forward_step(0, by)

    @pl.when(step == blocks)
    def _():
        later = list(forwards[ahead:])
        while later and later[0][0] is get_z:
            stream, by = later.pop(0)
            stream.forward_step(0, by)
        get_z.finish()
        get_z.keep().wait()
        saves[1].start()
        levels = levels_of("seq")
        gain = packs[2][1:2, :]

        def chunk_rows(k):
            return pl.ds(pl.multiple_of(k * STRETCH, STRETCH), STRETCH)

        def gated_at(here):
            z = z_all[here, :]
            return y_all[here, :].astype(F32) * (z * sigmoid(z))

        def summed(which):
            base = which * (levels + 1)
            for level in range(levels):
                at = which * levels + level
                copy = exchange(
                    "seq", level, sums.at[base + level], got.at[at], sum_sends.at[at], sum_arrivals.at[at]
                )
                copy.start()
                copy.wait()
                sums[base + level + 1] = sums[base + level] + got[at]
            return base + levels

        def gate(k, _):
            here = chunk_rows(k)
            z_all[here, :] = dot(rows_all[here, :D], w_z[...])
            gated = gated_at(here)
            sums[0, :, here] = as_row(jnp.sum(gated * gated, axis=1, keepdims=True))
            return 0

        lax.fori_loop(0, count, gate, 0)
        if later:
            stream, by = later.pop(0)
            stream.forward_step(0, by)
        squares = summed(0)

        def mix(k, _):
            here = chunk_rows(k)
            mixed_all[here, :] = (
                gated_at(here) * inverse_rms(sums[squares, :, here]) * gain
            ).astype(BF16)
            return 0

        lax.fori_loop(0, count, mix, 0)
        for stream, by in later:
            stream.forward_step(0, by)

        def contract_out(k, _):
            here = pl.ds(pl.multiple_of(k * 256, 256), 256)
            out_part[here, :] = dot(returned_t[here, :], mixed_all[...]).astype(BF16)
            return 0

        lax.fori_loop(0, D // 256, contract_out, 0)
        saves[4].start()
        get_o.finish()
        get_o.keep().wait()

        def measure(k, _):
            here = chunk_rows(k)
            d_mixed = dot(rows_all[here, D:], w_o[...])
            d_mixed_all[here, :] = d_mixed
            product = jnp.sum(d_mixed * gain * gated_at(here), axis=1, keepdims=True)
            sums[levels + 1, :, here] = as_row(product)
            return 0

        lax.fori_loop(0, count, measure, 0)
        products = summed(1)

        def differentiate(k, _):
            here = chunk_rows(k)
            d_y_block, d_z_block, d_gain_block = gate_gradients(
                y_all[here, :], z_all[here, :], d_mixed_all[here, :], gain,
                sums[squares, :, here], sums[products, :, here],
            )
            d_y[here, :] = d_y_block
            d_z[here, :] = d_z_block
            d_gain[0:1, :] += d_gain_block
            branch_stage[...] = dot(mixed_all[here, :], w_o[...], ((1,), (1,))).astype(BF16)
            out = pltpu.make_async_copy(branch_stage, branch_part.at[here], stage_sems.at[11])
            out.start()
            out.wait()
            return 0

        lax.fori_loop(0, count, differentiate, 0)
        saves[5].start()
        saves[6].start()

        def contract_z(k, _):
            here = pl.ds(pl.multiple_of(k * 256, 256), 256)
            z_part[here, :] = dot(normed_t[here, :], d_z[...]).astype(BF16)
            return 0

        lax.fori_loop(0, D // 256, contract_z, 0)
        for save in saves:
            save.wait()


def backward_block(
    heads,
    d_y_ref,
    pre_ref,
    conv_ref,
    dt_ref,
    states,
    seg_pad,
    seg_row,
    conv_pack,
    head_pack,
    chan_pack,
    spread_ref,
    gather_ref,
    d_conv_out,
    d_head_out,
    extended,
    d_state,
    d_rest,
):
    wide = heads * HEAD
    edge = wide + 2 * STATE

    @pl.when(pl.program_id(0) == 0)
    def _():
        d_state[...] = jnp.zeros_like(d_state)
        extended[STRETCH : STRETCH + 8, :] = jnp.zeros((8, edge), F32)
        d_conv_out[...] = jnp.zeros_like(d_conv_out)
        d_head_out[...] = jnp.zeros_like(d_head_out)

    at_row = pl.multiple_of((pl.num_programs(0) - 1 - pl.program_id(0)) * STRETCH, STRETCH)
    masks = block_masks(seg_pad, seg_row, at_row)
    spread = spread_ref[...]
    gather = gather_ref[...]
    pre = pre_ref[...]
    act = (pre * sigmoid(pre)).astype(BF16)
    b_mat = act[:, wide : wide + STATE]
    c_mat = act[:, wide + STATE :]
    dt_pre = dt_ref[...]
    dt = softplus(dt_pre).astype(BF16)
    rate = head_pack[1:2, :]
    decay = Decays(dt, rate, masks, spread)
    scores = dot(c_mat, b_mat, ((1,), (1,)))
    lane = lax.broadcasted_iota(jnp.int32, (STRETCH, 128), 1)
    first_half = lane < HEAD
    d_b = jnp.zeros((STRETCH, STATE), F32)
    d_c = jnp.zeros((STRETCH, STATE), F32)
    d_scores = jnp.zeros((STRETCH, STRETCH), F32)
    d_cum = jnp.zeros((STRETCH, 128), F32)
    d_dt = jnp.zeros((STRETCH, 128), F32)
    d_last = jnp.zeros((1, 128), F32)
    column_sums = []
    for pair in range(heads // 2):
        columns = slice(pair * 2 * HEAD, (pair + 1) * 2 * HEAD)
        ones = gather[columns, :]
        steps, carry, tail, keep = decay.of(columns)
        xs = act[:, columns].astype(F32)
        scaled = xs * steps
        scaled_low = scaled.astype(BF16)
        old = states[0, :, columns]
        old_low = old.astype(BF16)
        d_new = d_state[:, columns]
        d_new_low = d_new.astype(BF16)
        d_y_low = d_y_ref[:, columns]
        d_y = d_y_low.astype(F32)
        d_carried = d_y * carry
        d_carried_low = d_carried.astype(BF16)
        d_c = d_c + dot(d_carried_low, old_low, ((1,), (1,)))
        d_cum = d_cum + split_dot(d_carried * dot(c_mat, old_low), ones)
        weighed = scaled * tail
        into = dot(b_mat, d_new_low)
        d_b = d_b + dot(weighed.astype(BF16), d_new_low, ((1,), (1,)))
        tail_part = split_dot(weighed * into, ones)
        d_cum = d_cum - tail_part
        kept = jnp.sum(d_new * old, axis=0, keepdims=True) * keep
        kept = split_dot(jnp.broadcast_to(kept, (8, 128)), ones)[:1]
        d_last = d_last + jnp.sum(tail_part, axis=0, keepdims=True) + kept
        d_state[:, columns] = d_new * keep + dot(c_mat, d_carried_low, ((0,), (0,)))
        halves = []
        for h in (2 * pair, 2 * pair + 1):
            between = decay.between(h)
            weights = scores * between
            halves.append(dot(weights.astype(BF16), d_y_low, ((0,), (0,))))
            d_y_head = jnp.where(first_half == (h % 2 == 0), d_y_low, jnp.zeros_like(d_y_low))
            d_weights = dot(d_y_head, scaled_low, ((1,), (1,)))
            d_scores = d_scores + d_weights * between
            product = d_weights * weights
            d_cum = d_cum + jnp.where(lane == h, jnp.sum(product, axis=1, keepdims=True), 0.0)
            column_sums.append(jnp.sum(product, axis=0, keepdims=True))
        d_scaled = into * tail + jnp.where(first_half, halves[0], halves[1])
        d_xs = d_scaled * steps + chan_pack[0:1, columns] * d_y
        extended[0:STRETCH, columns] = d_xs.astype(BF16).astype(F32)
        d_dt = d_dt + split_dot(d_scaled * xs, ones)
        d_skip = jnp.sum(d_y * xs, axis=0, keepdims=True)
        d_head_out[2:3, :] += split_dot(jnp.broadcast_to(d_skip, (8, 128)), ones)[:1]
    column_sums.append(jnp.zeros((128 - heads, STRETCH), F32))
    d_cum = d_cum - jnp.transpose(jnp.concatenate(column_sums, axis=0))
    row = lax.broadcasted_iota(jnp.int32, (STRETCH, 128), 0)
    d_cum = d_cum + jnp.where(row == STRETCH - 1, d_last, 0.0)
    d_scores_low = d_scores.astype(BF16)
    d_c = d_c + dot(d_scores_low, b_mat)
    d_b = d_b + dot(d_scores_low, c_mat, ((0,), (0,)))

    rows = lax.broadcasted_iota(jnp.int32, (STRETCH, STRETCH), 0)
    upper = jnp.where(rows <= lax.broadcasted_iota(jnp.int32, (STRETCH, STRETCH), 1), 1.0, 0.0)
    d_dt = d_dt + rate * tri_dot(upper.astype(BF16), d_cum)
    d_dt_raw = d_dt.astype(BF16).astype(F32) * sigmoid(dt_pre)
    d_head_out[0:1, :] += jnp.sum(d_dt_raw, axis=0, keepdims=True)
    d_head_out[1:2, :] += jnp.sum(d_cum * decay.columns, axis=0, keepdims=True)

    extended[0:STRETCH, wide : wide + STATE] = d_b
    extended[0:STRETCH, wide + STATE :] = d_c
    here = pl.ds(at_row, STRETCH)
    moved = pltpu.roll(jnp.where(lane < heads, d_dt_raw, 0.0), lax.axis_index("seq") * heads, 1)
    d_rest[here, edge:] = moved.astype(BF16)

    def convolve_back(at, _):
        columns = pl.ds(pl.multiple_of(at * 128, 128), 128)
        value = pre_ref[:, columns]
        gate = sigmoid(value)
        d_pre = extended[0:STRETCH, columns] * (gate * (1.0 + value * (1.0 - gate)))
        extended[0:STRETCH, columns] = d_pre
        conv_in = conv_ref[:, columns].astype(F32)
        d_conv_in = conv_pack[3:4, columns] * d_pre
        d_conv_out[3:4, columns] += jnp.sum(d_pre * conv_in, axis=0, keepdims=True)
        d_conv_out[4:5, columns] += jnp.sum(d_pre, axis=0, keepdims=True)
        for by in range(1, KERNEL):
            moved = extended[by : by + STRETCH, columns] * masks[by]
            d_conv_in = d_conv_in + conv_pack[3 - by : 4 - by, columns] * moved
            d_conv_out[3 - by : 4 - by, columns] += jnp.sum(moved * conv_in, axis=0, keepdims=True)
        extended[STRETCH : STRETCH + 8, columns] = extended[0:8, columns]
        d_rest[here, columns] = d_conv_in.astype(BF16)
        return 0

    lax.fori_loop(0, edge // 128, convolve_back, 0)


VMEM_BYTES = 56 * 1024 * 1024


def block(columns, reverse=0):
    if reverse:
        return pl.BlockSpec((STRETCH, columns), lambda i: (reverse - 1 - i, 0))
    return pl.BlockSpec((STRETCH, columns), lambda i: (i, 0))


def whole(*shape):
    return pl.BlockSpec(shape, lambda i: (0,) * len(shape))


def compiler_params():
    return pltpu.CompilerParams(
        vmem_limit_bytes=VMEM_BYTES, dimension_semantics=("arbitrary",)
    )


class Place:
    def __init__(self, axis, minor):
        self.axis = axis
        self.minor = minor
        self.major = lax.axis_size(axis) // minor
        index = lax.axis_index(axis)
        self.at_major = index // minor
        self.at_minor = index % minor
        self.index = index

    def slot(self, by_major, by_minor):
        return (self.at_major + by_major) % self.major * self.minor + (
            self.at_minor + by_minor
        ) % self.minor

    def others(self):
        along = [self.slot(step, 0) for step in range(1, self.major)]
        return along + [self.slot(0, step) for step in range(1, self.minor)]


def places():
    ring = lax.axis_size("fsdp")
    side = 1
    while 2 * side * 2 * side * 2 <= ring:
        side = 2 * side
    return Place("fsdp", side), Place("seq", 2)


def meet(*all_places):
    barrier = pltpu.get_barrier_semaphore()
    count = 0
    for place in all_places:
        for other in place.others():
            pl.semaphore_signal(
                barrier, inc=1, device_id={place.axis: other}, device_id_type=pl.DeviceIdType.MESH
            )
            count = count + 1
    pl.semaphore_wait(barrier, count)


def send(place, source, target, to, sends, arrivals, at):
    return pltpu.make_async_remote_copy(
        src_ref=source,
        dst_ref=target,
        send_sem=sends.at[at],
        recv_sem=arrivals.at[at],
        device_id={place.axis: to},
        device_id_type=pl.DeviceIdType.MESH,
    )


class Gather:
    def __init__(self, place, own, full, rows, pieces, sems, target=None):
        self.place, self.own, self.full, self.landing = place, own, full, target
        self.size, self.pieces = rows // pieces, pieces
        self.sends1, self.arrivals1, self.sends2, self.arrivals2, self.here = sems

    @staticmethod
    def scratch(place, pieces):
        first = max(place.major - 1, 1) * pieces
        second = place.major * (place.minor - 1) * pieces
        dma = pltpu.SemaphoreType.DMA
        return [dma((first,)), dma((first,)), dma((second,)), dma((second,)), dma((1,))]

    def rows(self, piece):
        return pl.ds(piece * self.size, self.size)

    def target(self, slot, piece):
        if self.landing is not None:
            return self.landing(slot, piece)
        if len(self.full.shape) > len(self.own.shape):
            return self.full.at[slot, self.rows(piece)]
        start = slot * (self.size * self.pieces) + piece * self.size
        return self.full.at[pl.ds(pl.multiple_of(start, 16), self.size)]

    def along(self, piece, step):
        place = self.place
        return send(
            place,
            self.own.at[self.rows(piece)],
            self.target(place.index, piece),
            place.slot(step, 0),
            self.sends1,
            self.arrivals1,
            piece * (place.major - 1) + step - 1,
        )

    def across(self, piece, step, across):
        place = self.place
        slot = place.slot(-step, 0)
        target = self.target(slot, piece)
        source = self.own.at[self.rows(piece)] if step == 0 else target
        at = (piece * place.major + step) * (place.minor - 1) + across - 1
        return send(
            place, source, target, place.slot(0, across), self.sends2, self.arrivals2, at
        )

    def keep(self):
        if self.landing is not None:
            target = self.landing(self.place.index, 0)
        elif len(self.full.shape) > len(self.own.shape):
            target = self.full.at[self.place.index]
        else:
            size = self.size * self.pieces
            target = self.full.at[pl.ds(pl.multiple_of(self.place.index * size, 16), size)]
        return pltpu.make_async_copy(self.own, target, self.here.at[0])

    def begin(self, piece):
        self.begin_along(piece)
        self.begin_across(piece)

    def begin_along(self, piece):
        for step in range(1, self.place.major):
            self.along(piece, step).start()

    def begin_across(self, piece):
        for across in range(1, self.place.minor):
            self.across(piece, 0, across).start()

    def forward(self, piece):
        for step in range(1, self.place.major):
            self.forward_step(piece, step)

    def forward_step(self, piece, step):
        self.along(piece, step).wait_recv()
        for across in range(1, self.place.minor):
            self.across(piece, step, across).start()

    def finish(self):
        for piece in range(self.pieces):
            for step in range(1, self.place.major):
                self.along(piece, step).wait_send()
            for step in range(self.place.major):
                for across in range(1, self.place.minor):
                    self.across(piece, step, across).wait()


class Reduce:
    def __init__(self, place, part, total, rows, pieces, scratch, loads=None):
        self.place, self.part, self.total, self.loads = place, part, total, loads
        self.size, self.pieces = rows // pieces, pieces
        self.got1, self.mine, self.got2, self.sends1, self.arrivals1, self.sends2, self.arrivals2 = (
            scratch
        )

    @staticmethod
    def scratch(place, rows, columns, pieces):
        dma = pltpu.SemaphoreType.DMA
        first = place.major * (place.minor - 1)
        second = max(place.major - 1, 1)
        return [
            pltpu.VMEM((first, rows, columns), BF16),
            pltpu.VMEM((second, rows, columns), BF16),
            pltpu.VMEM((second, rows, columns), BF16),
            dma((first * pieces,)),
            dma((first * pieces,)),
            dma((second * pieces,)),
            dma((second * pieces,)),
        ]

    def items(self):
        return [(piece, step) for step in self.steps() for piece in range(self.pieces)]

    def steps(self):
        return list(range(1, self.place.major)) + [0]

    def rows(self, piece):
        return pl.ds(piece * self.size, self.size)

    def part_rows(self, slot, rows_start, size):
        if len(self.part.shape) == 3:
            return slot, pl.ds(rows_start, size)
        start = slot * (self.size * self.pieces) + rows_start
        return (pl.ds(pl.multiple_of(start, 16), size),)

    def across(self, item, across):
        piece, step = item
        place = self.place
        slot = step * (place.minor - 1) + across - 1
        index = self.part_rows(place.slot(step, across), piece * self.size, self.size)
        return send(
            place,
            self.part.at[index],
            self.got1.at[slot, self.rows(piece)],
            place.slot(0, across),
            self.sends1,
            self.arrivals1,
            slot * self.pieces + piece,
        )

    def along(self, item):
        piece, step = item
        place = self.place
        return send(
            place,
            self.mine.at[step - 1, self.rows(piece)],
            self.got2.at[step - 1, self.rows(piece)],
            place.slot(step, 0),
            self.sends2,
            self.arrivals2,
            (step - 1) * self.pieces + piece,
        )

    def begin(self, item):
        for across in range(1, self.place.minor):
            self.across(item, across).start()
        if self.loads is not None:
            self.load(item[1]).start()

    def load(self, step):
        target = self.mine.at[step - 1] if step else self.total
        return pltpu.make_async_copy(
            self.part.at[self.place.slot(step, 0)], target, self.loads.at[step]
        )

    def own(self, step, rows):
        if self.loads is None:
            return self.part[self.part_rows(self.place.slot(step, 0), rows, 16)].astype(F32)
        source = self.mine.at[step - 1] if step else self.total
        return source[pl.ds(rows, 16)].astype(F32)

    def blocks(self, piece, body):
        def one(at, _):
            body(pl.multiple_of(piece * self.size + at * 16, 16))
            return 0

        lax.fori_loop(0, self.size // 16, one, 0)

    def handle(self, item):
        piece, step = item
        place = self.place
        for across in range(1, place.minor):
            self.across(item, across).wait_recv()
        if self.loads is not None:
            self.load(step).wait()
        if step == 0:
            return

        def body(start):
            value = self.own(step, start)
            rows = pl.ds(start, 16)
            for across in range(1, place.minor):
                slot = step * (place.minor - 1) + across - 1
                value = value + self.got1[slot, rows].astype(F32)
            self.mine[step - 1, rows] = value.astype(BF16)

        self.blocks(piece, body)
        self.along(item).start()

    def close(self, piece):
        place = self.place
        for step in range(1, place.major):
            self.along((piece, step)).wait_recv()

        def body(start):
            value = self.own(0, start)
            rows = pl.ds(start, 16)
            for across in range(1, place.minor):
                value = value + self.got1[across - 1, rows].astype(F32)
            for step in range(1, place.major):
                value = value + self.got2[step - 1, rows].astype(F32)
            self.total[rows] = value.astype(self.total.dtype)

        self.blocks(piece, body)

    def finish(self):
        for item in self.items():
            for across in range(1, self.place.minor):
                self.across(item, across).wait_send()
            if item[1]:
                self.along(item).wait_send()


WEIGHT_PIECES = 3
TOKEN_PIECES = 4
HBM = pl.BlockSpec(memory_space=pl.ANY)
VMEM = pl.BlockSpec(memory_space=pltpu.VMEM)


def comm_params(number):
    return pltpu.CompilerParams(
        collective_id=number, has_side_effects=True, vmem_limit_bytes=VMEM_BYTES
    )


def resident(x):
    return pl.BlockSpec(
        x.shape, lambda i: (0,) * len(x.shape), pipeline_mode=pl.Buffered(buffer_count=1)
    )


def run_forward(heads, tokens, cotangent, small, dt_weight, seg_pad, seg_row, spread, in_weight, out_weight):
    ring, seq = places()
    count, groups = lax.axis_size("fsdp"), lax.axis_size("seq")
    rows, own_rows = in_weight.shape[0], tokens.shape[0]
    length = own_rows * groups
    blocks = length // STRETCH
    wide = heads * HEAD
    edge = wide + 2 * STATE
    levels = levels_of("seq")
    shape = jax.ShapeDtypeStruct
    split = halved(rows, groups)
    own_shared = rows // groups if split else rows
    shared_shape = (count, groups, own_shared, SHARED) if split else (D, SHARED)

    def chunk(columns):
        return pl.BlockSpec((STRETCH, columns), lambda i: (i - i // blocks, 0))

    wholes = [tokens, cotangent, small, dt_weight, seg_pad, seg_row, spread]
    late = [
        shape((D, wide), BF16),
        shape((8, wide), F32),
        shape((8, edge), F32),
        shape((8, 128), F32),
        shape((8, wide), F32),
    ]
    dma = pltpu.SemaphoreType.DMA
    scratch = [
        pltpu.VMEM((own_shared, 2 * STATE), F32),
        pltpu.VMEM((rows, wide), BF16),
        pltpu.VMEM((rows, wide), BF16),
        pltpu.VMEM((rows, wide), BF16),
        pltpu.VMEM((own_shared, SHARED), BF16),
        pltpu.VMEM((own_rows, 2 * D), BF16),
        pltpu.VMEM((D, wide), BF16),
        pltpu.VMEM((D, wide), BF16),
        pltpu.VMEM((D, wide), BF16),
        pltpu.VMEM(shared_shape, BF16),
        pltpu.VMEM((count, own_shared, SHARED) if split else (16, 128), BF16),
        pltpu.VMEM((STRETCH, D), BF16),
        pltpu.VMEM((length, 2 * D), BF16),
        pltpu.VMEM((D, length), BF16),
        pltpu.VMEM((length, wide), F32),
        pltpu.VMEM((length, wide), BF16),
        pltpu.VMEM((length, wide), F32),
        pltpu.VMEM((STRETCH + 8, edge), F32),
        pltpu.VMEM((STATE, wide), F32),
        pltpu.VMEM((8, INNER + 128), F32),
        pltpu.VMEM((length, wide), BF16),
        pltpu.VMEM((length, wide), BF16),
        pltpu.VMEM((length, wide), BF16),
        pltpu.VMEM((D, length), BF16),
        pltpu.VMEM((D, wide), BF16),
        pltpu.VMEM((2 * (levels + 1), 8, length), F32),
        pltpu.VMEM((2 * levels, 8, length), F32),
        dma((12,)),
        dma((2 * levels,)),
        dma((2 * levels,)),
    ]
    scratch = scratch + Gather.scratch(ring, WEIGHT_PIECES) + Gather.scratch(ring, 1)
    scratch = scratch + Gather.scratch(ring, 1) + Gather.scratch(seq, TOKEN_PIECES)
    scratch = scratch + Gather.scratch(ring, 1) + Gather.scratch(seq, 1)
    return pl.pallas_call(
        partial(forward_kernel, heads),
        grid=(blocks + 1,),
        in_specs=[resident(x) for x in wholes] + [HBM, HBM],
        out_specs=[
            chunk(edge),
            chunk(edge),
            chunk(128),
            pl.BlockSpec((1, STATE, wide), lambda i: (i - i // blocks, 0, 0)),
        ]
        + [resident(x) for x in late]
        + [HBM] * 8,
        out_shape=[
            shape((length, edge), F32),
            shape((length, edge), BF16),
            shape((length, 128), F32),
            shape((blocks, STATE, wide), F32),
        ]
        + late
        + [shape((D, wide), BF16), shape((D, wide), BF16), shape(shared_shape, BF16)]
        + [shape((length, D), BF16), shape((length, wide), BF16), shape((length, wide), BF16)]
        + [shape((D, length), BF16), shape((D, wide), BF16)],
        scratch_shapes=scratch,
        compiler_params=pltpu.CompilerParams(
            collective_id=1,
            has_side_effects=True,
            vmem_limit_bytes=61 * 1024 * 1024,
            dimension_semantics=("arbitrary",),
        ),
        name="gather_and_forward",
    )(*wholes, in_weight, out_weight)


def backward_kernel(heads, *refs):
    chunk = refs[:5]
    packs = refs[5:12]
    d_z, w_z, w_x, w_s, normed_t, tokens, small, d_gain = refs[12:20]
    out_part, z_part, branch_part = refs[20:23]
    out_all, z_all, x_all, s_all, small_all, branch, d_normed, d_conv, d_head = refs[23:32]
    extended, d_state, d_rest, x_part, s_part, act_part, out_own, z_own, x_own, s_own, s_mid = refs[32:43]
    small_sums, small_got, small_sends, small_arrivals, out_loads, z_loads, branch_loads = refs[43:50]
    scratch = refs[50:]
    ring, seq = places()
    rows = x_own.shape[0]
    own_rows = act_part.shape[1]
    wide = heads * HEAD
    edge = wide + 2 * STATE
    groups = seq.major * seq.minor
    own_shared = s_own.shape[0]
    split = halved(rows, groups)
    levels = levels_of("fsdp")

    def stream(place, part, total, extent, pieces, at, loads=None):
        return Reduce(place, part, total, extent, pieces, scratch[7 * at : 7 * at + 7], loads)

    def spreading(own, full, pieces, at):
        return Gather(seq, own, full, own.shape[0], pieces, scratch[49 + 5 * at : 54 + 5 * at])

    out_sum = stream(ring, out_part, out_own, rows, 1, 0, out_loads)
    z_sum = stream(ring, z_part, z_own, rows, 1, 1, z_loads)
    x_sum = stream(ring, x_part, x_own, rows, WEIGHT_PIECES, 2)
    branch_sum = stream(seq, branch_part, branch, own_rows, 1, 3, branch_loads)
    d_normed_sum = stream(seq, act_part, d_normed, own_rows, 2, 4)
    if split:
        mid_sum = stream(seq, s_part, s_mid, s_mid.shape[0], 1, 5)
        s_sum = stream(ring, s_mid, s_own, own_shared, 1, 6)
    else:
        s_sum = stream(ring, s_part, s_own, rows, 1, 6)
    out_spread = spreading(out_own, out_all, 1, 0)
    z_spread = spreading(z_own, z_all, 1, 1)
    x_spread = spreading(x_own, x_all, WEIGHT_PIECES, 2)
    s_spread = spreading(s_own, s_all, 1, 3)
    small_spread = spreading(small_sums.at[levels], small_all, 1, 4)
    early = [(s, item) for s in (out_sum, z_sum) for item in s.items()]
    at_step = pl.program_id(0)
    blocks = d_rest.shape[0] // STRETCH

    def swap(level):
        return exchange(
            "fsdp",
            level,
            small_sums.at[level],
            small_got.at[level],
            small_sends.at[level],
            small_arrivals.at[level],
        )

    @pl.when(at_step == 0)
    def _():
        meet(ring, seq)
        for s, item in early:
            s.begin(item)
        for item in branch_sum.items():
            branch_sum.begin(item)

    backward_block(heads, *chunk, *packs, d_conv, d_head, extended, d_state, d_rest)

    for k in range(blocks):

        @pl.when(at_step == k)
        def _():
            s, item = early[k]
            s.handle(item)
            if k == blocks - 1:
                for item in branch_sum.items():
                    branch_sum.handle(item)
                branch_sum.close(0)
                branch_sum.finish()

    @pl.when(at_step == blocks - 1)
    def _():
        def x_block(slot):
            here = pl.ds(pl.multiple_of(slot * rows, 16), rows)

            def one(at, _):
                columns = pl.ds(pl.multiple_of(at * 384, 128), 384)
                x_part[slot, :, columns] = dot(normed_t[here, :], d_rest[:, columns]).astype(BF16)
                return 0

            lax.fori_loop(0, wide // 384, one, 0)

        def s_block(slot, _):
            here = pl.ds(pl.multiple_of(slot * rows, 16), rows)
            value = dot(normed_t[here, :], d_rest[:, wide:]).astype(BF16)
            if split:
                target = pl.ds(pl.multiple_of(slot * own_shared, 16), own_shared)
                for s in range(groups):
                    s_part[s, target, :] = value[s * own_shared : (s + 1) * own_shared]
            else:
                s_part[slot] = value
            return 0

        def normed_block(slot):
            here = pl.ds(pl.multiple_of(slot * own_rows, own_rows), own_rows)

            def one(at, _):
                columns = pl.ds(pl.multiple_of(at * 512, 128), 512)
                value = dot(d_z[here, :], w_z[columns, :], ((1,), (1,)))
                value = value + dot(d_rest[here, :wide], w_x[columns, :], ((1,), (1,)))
                value = value + dot(d_rest[here, wide:], w_s[columns, :], ((1,), (1,)))
                act_part[slot, :, columns] = value.astype(BF16)
                return 0

            lax.fori_loop(0, D // 512, one, 0)

        waiting = early[blocks:]

        def handle_early(amount=1):
            for _ in range(min(amount, len(waiting))):
                s, item = waiting.pop(0)
                s.handle(item)

        lax.fori_loop(0, ring.major * ring.minor, s_block, 0)
        if split:
            for item in mid_sum.items():
                mid_sum.begin(item)
        else:
            for item in s_sum.items():
                s_sum.begin(item)
        handle_early()
        for step in x_sum.steps():
            for across in range(1, ring.minor):
                x_block(ring.slot(step, across))
            for piece in range(WEIGHT_PIECES):
                x_sum.begin((piece, step))
        if split:
            for item in mid_sum.items():
                mid_sum.handle(item)
        handle_early()
        for step in d_normed_sum.steps():
            for across in range(1, seq.minor):
                normed_block(seq.slot(step, across))
            for piece in range(2):
                d_normed_sum.begin((piece, step))
        if split:
            mid_sum.close(0)
            for item in s_sum.items():
                s_sum.begin(item)
        handle_early()
        for step in x_sum.steps():
            x_block(ring.slot(step, 0))
        for step in d_normed_sum.steps():
            normed_block(seq.slot(step, 0))
        handle_early(len(waiting))
        out_sum.close(0)
        out_spread.begin(0)
        side = d_normed_sum.items() + [None] * (2 + levels)
        work = [(x_sum, item) for item in x_sum.items()] + [(s_sum, item) for item in s_sum.items()]

        def sideways(at):
            first = len(d_normed_sum.items())
            if at < first:
                d_normed_sum.handle(side[at])
                return
            if at == first:
                for piece in range(2):
                    d_normed_sum.close(piece)
                inputs = tokens[...].astype(F32)
                rms = lax.rsqrt(jnp.mean(inputs * inputs, axis=-1, keepdims=True) + NORM_EPS)
                small_sums[0] = jnp.zeros(small_sums.shape[1:], F32)
                small_sums[0, 0 : KERNEL + 1, :edge] = d_conv[0 : KERNEL + 1, :]
                small_sums[0, 5:6, :] = jnp.sum(
                    d_normed[...].astype(F32) * (inputs * rms), axis=0, keepdims=True
                )
                small_sums[0, 6:7, :wide] = d_gain[0:1, :]
                for k in range(3):
                    small_sums[0, 7:8, 128 * k : 128 * (k + 1)] = d_head[k : k + 1, :]
                swap(0).start()
                return
            level = at - first - 1
            if level < levels:
                swap(level).wait()
                small_sums[level + 1] = small_sums[level] + small_got[level]
                if level + 1 < levels:
                    swap(level + 1).start()
                else:
                    small_spread.begin(0)
                    small_spread.keep().start()

        done = 0
        for at, (s, item) in enumerate(work):
            s.handle(item)
            sideways(at)
            done = at + 1
            if at == WEIGHT_PIECES:
                z_sum.close(0)
                z_spread.begin(0)
                out_spread.forward(0)
        for at in range(done, len(side)):
            sideways(at)
        for piece in range(WEIGHT_PIECES):
            x_sum.close(piece)
            x_spread.begin(piece)
        s_sum.close(0)
        s_spread.begin(0)
        spreads = (out_spread, z_spread, x_spread, s_spread)
        for s in spreads:
            s.keep().start()
        z_spread.forward(0)
        small_spread.forward(0)
        for piece in range(WEIGHT_PIECES):
            x_spread.forward(piece)
        s_spread.forward(0)
        for s in (out_sum, z_sum, x_sum, s_sum, d_normed_sum):
            s.finish()
        if split:
            mid_sum.finish()
        for s in spreads + (small_spread,):
            s.finish()
            s.keep().wait()


def run_backward(
    heads, d_y, pre, conv, dt_pre, states, seg_pad, seg_row, packs, spread, d_z, weights, normed_t,
    tokens, small, d_gain, out_part, z_part, branch_part,
):
    length = d_y.shape[0]
    blocks = length // STRETCH
    wide = heads * HEAD
    edge = wide + 2 * STATE
    ring, seq = places()
    count, groups = lax.axis_size("fsdp"), lax.axis_size("seq")
    levels = levels_of("fsdp")

    def parted(x, by):
        return x.reshape(by, x.shape[0] // by, x.shape[1])

    out_part, z_part = parted(out_part, count), parted(z_part, count)
    branch_part = parted(branch_part, groups)
    rows, own_rows = out_part.shape[1], branch_part.shape[1]
    split = halved(rows, groups)
    own_shared = rows // groups if split else rows
    mid_rows = own_shared * count if split else 16
    wholes = [
        seg_pad, seg_row, *packs, spread, spread.T, d_z, *weights, normed_t, tokens, small, d_gain
    ]
    dma = pltpu.SemaphoreType.DMA
    scratch = [
        pltpu.VMEM((STRETCH + 8, edge), F32),
        pltpu.VMEM((STATE, wide), F32),
        pltpu.VMEM((length, wide + SHARED), BF16),
        pltpu.VMEM((count, rows, wide), BF16),
        pltpu.VMEM((groups, mid_rows, SHARED) if split else (count, rows, SHARED), BF16),
        pltpu.VMEM((groups, own_rows, D), BF16),
        pltpu.VMEM((rows, wide), BF16),
        pltpu.VMEM((rows, wide), BF16),
        pltpu.VMEM((rows, wide), BF16),
        pltpu.VMEM((own_shared, SHARED), BF16),
        pltpu.VMEM((mid_rows, SHARED), BF16),
        pltpu.VMEM((levels + 1, 8, D), F32),
        pltpu.VMEM((levels, 8, D), F32),
        dma((levels,)),
        dma((levels,)),
        dma((ring.major,)),
        dma((ring.major,)),
        dma((seq.major,)),
    ]
    scratch = scratch + Reduce.scratch(ring, rows, wide, 1) + Reduce.scratch(ring, rows, wide, 1)
    scratch = scratch + Reduce.scratch(ring, rows, wide, WEIGHT_PIECES)
    scratch = scratch + Reduce.scratch(seq, own_rows, D, 1) + Reduce.scratch(seq, own_rows, D, 2)
    scratch = scratch + Reduce.scratch(seq, mid_rows, SHARED, 1)
    scratch = scratch + Reduce.scratch(ring, own_shared, SHARED, 1)
    for pieces in (1, 1, WEIGHT_PIECES, 1, 1):
        scratch = scratch + Gather.scratch(seq, pieces)
    shape = jax.ShapeDtypeStruct
    gathered = [
        shape((groups, rows, wide), BF16),
        shape((groups, rows, wide), BF16),
        shape((groups, rows, wide), BF16),
        shape((groups, own_shared, SHARED), BF16),
        shape((groups, 8, D), F32),
    ]
    summed = [
        shape((own_rows, D), BF16),
        shape((own_rows, D), BF16),
        shape((8, edge), F32),
        shape((8, 128), F32),
    ]
    return pl.pallas_call(
        partial(backward_kernel, heads),
        grid=(blocks,),
        in_specs=[
            block(wide, blocks),
            block(edge, blocks),
            block(edge, blocks),
            block(128, blocks),
            pl.BlockSpec((1, STATE, wide), lambda i: (blocks - 1 - i, 0, 0)),
        ]
        + [resident(x) for x in wholes]
        + [HBM] * 3,
        out_specs=[HBM] * 5 + [resident(x) for x in summed],
        out_shape=gathered + summed,
        scratch_shapes=scratch,
        compiler_params=pltpu.CompilerParams(
            collective_id=2,
            has_side_effects=True,
            vmem_limit_bytes=61 * 1024 * 1024,
            dimension_semantics=("arbitrary",),
        ),
        name="backward_and_sums",
    )(d_y, pre, conv, dt_pre, states, *wholes, out_part, z_part, branch_part)


def exchange(place_axis, level, source, got, sends, arrivals):
    index = lax.axis_index(place_axis)
    other = partner(index, level)
    return pltpu.make_async_remote_copy(
        src_ref=source,
        dst_ref=got,
        send_sem=sends,
        recv_sem=arrivals,
        device_id={place_axis: other},
        device_id_type=pl.DeviceIdType.MESH,
    )


def partner(index, level):
    bit = 2**level
    return index + (1 - 2 * (index // bit % 2)) * bit


def levels_of(axis):
    return lax.axis_size(axis).bit_length() - 1


class Push:
    def __init__(self, axis, own, slots, sends, arrivals):
        self.axis, self.own, self.slots = axis, own, slots
        self.sends, self.arrivals = sends, arrivals
        self.count = lax.axis_size(axis)

    def copy(self, step):
        index = lax.axis_index(self.axis)
        return pltpu.make_async_remote_copy(
            src_ref=self.own,
            dst_ref=self.slots.at[index],
            send_sem=self.sends.at[step - 1],
            recv_sem=self.arrivals.at[step - 1],
            device_id={self.axis: (index + step) % self.count},
            device_id_type=pl.DeviceIdType.MESH,
        )

    def begin(self):
        for step in range(1, self.count):
            self.copy(step).start()

    def finish(self):
        for step in range(1, self.count):
            self.copy(step).wait()


def norm_kernel(sums, norms_out, own, slots, sends, arrivals):
    push = Push("fsdp", own, slots, sends, arrivals)
    index = lax.axis_index("fsdp")
    barrier = pltpu.get_barrier_semaphore()
    for step in range(1, push.count):
        other = (index + step) % push.count
        pl.semaphore_signal(
            barrier, inc=1, device_id={"fsdp": other}, device_id_type=pl.DeviceIdType.MESH
        )
    own[...] = jnp.broadcast_to(jnp.sum(sums[...], axis=1, keepdims=True), (8, 128))
    slots[index] = own[...]
    pl.semaphore_wait(barrier, push.count - 1)
    push.begin()
    push.finish()
    total = slots[0]
    for k in range(1, push.count):
        total = total + slots[k]
    norms_out[...] = jnp.sqrt(total)


def run_norms(sums):
    count = lax.axis_size("fsdp")
    dma = pltpu.SemaphoreType.DMA
    return pl.pallas_call(
        norm_kernel,
        in_specs=[VMEM],
        out_specs=VMEM,
        out_shape=jax.ShapeDtypeStruct((8, 128), F32),
        scratch_shapes=[
            pltpu.VMEM((8, 128), F32),
            pltpu.VMEM((count, 8, 128), F32),
            dma((count - 1,)),
            dma((count - 1,)),
        ],
        compiler_params=comm_params(3),
        name="norms",
    )(sums)


def small_update(groups, heads, small_all, small_w, small_m, small_v, outs, small_grad):
    wide = heads * HEAD
    edge = wide + 2 * STATE
    everyone = [small_all[s] for s in range(groups)]
    shared = everyone[0]
    for other in everyone[1:]:
        shared = shared + other
    small_grad[:, :D] = shared[5:6, :]
    for k in range(KERNEL + 1):
        base = D + k * CONV
        for s in range(groups):
            small_grad[:, base + s * wide : base + (s + 1) * wide] = everyone[s][k : k + 1, :wide]
        small_grad[:, base + INNER : base + CONV] = shared[k : k + 1, wide:edge]
    size = 3 * HEADS + INNER
    size = size + -size % 128
    lane = lax.broadcasted_iota(jnp.int32, (8, size), 1)
    rest = jnp.zeros((8, size), F32)
    gap = jnp.zeros((8, size - 128), F32)
    for s in range(groups):
        for k in range(3):
            part = jnp.broadcast_to(everyone[s][7:8, 128 * k : 128 * (k + 1)], (8, 128))
            part = jnp.concatenate([part, gap], axis=1)
            part = jnp.where(lane < heads, part, 0.0)
            move = k * HEADS + s * heads
            rest = rest + (pltpu.roll(part, move, 1) if move else part)
    gains = [jnp.broadcast_to(one[6:7, :wide], (8, wide)) for one in everyone]
    gains = gains + [jnp.zeros((8, size - INNER), F32)]
    rest = rest + pltpu.roll(jnp.concatenate(gains, axis=1), 3 * HEADS, 1)
    base = D + (KERNEL + 1) * CONV
    small_grad[:, base : base + size] = rest[0:1, :]
    gradient = small_grad[...]
    first, second, direction = adam_parts(gradient, small_m[...], small_v[...])
    values = (gradient, small_w[...] - LEARN_RATE * direction, first, second)
    for ref, value in zip(outs, values, strict=True):
        ref[...] = value[:, : ref.shape[1]]


def moments_kernel(groups, heads, *refs):
    z_piece, x_piece, tails, out_piece = refs[:4]
    small_all, small_w, small_m, small_v = refs[4:8]
    w_in, m_in, v_in, w_out, m_out, v_out = refs[8:14]
    g_in_new, m_in_new, v_in_new, u_in, g_out_new, m_out_new, v_out_new, u_out = refs[14:22]
    sums = refs[22]
    small_outs = refs[23:27]
    u_tail, small_grad = refs[27:29]
    wide = heads * HEAD

    @pl.when(pl.program_id(0) == 0)
    def _():
        sums[...] = jnp.zeros_like(sums)
        small_update(groups, heads, small_all, small_w, small_m, small_v, small_outs, small_grad)

    def update(gradient, start, w, m, v, g_new, m_new, v_new, u, at):
        size = min(gradient.shape[1], w.shape[1] - start)
        here = slice(start, start + size)
        gradient = gradient[:, :size]
        first, second, direction = adam_parts(gradient, m[:, here], v[:, here])
        weight = w[:, here]
        direction = direction + WEIGHT_DECAY * weight
        g_new[:, here] = gradient
        m_new[:, here] = first
        v_new[:, here] = second
        if u is None:
            u_tail[:, :size] = direction
        else:
            u[:, here] = direction.astype(BF16)
        sums[at : at + 1, :size] += jnp.sum(weight * weight, axis=0, keepdims=True)
        sums[at + 1 : at + 2, :size] += jnp.sum(direction * direction, axis=0, keepdims=True)

    inside = (w_in, m_in, v_in, g_in_new, m_in_new, v_in_new, u_in)
    outside = (w_out, m_out, v_out, g_out_new, m_out_new, v_out_new, u_out)
    for s in range(groups):
        update(z_piece[s].astype(F32), s * wide, *inside, 0)
        update(x_piece[s].astype(F32), INNER + s * wide, *inside, 0)
        update(out_piece[s].astype(F32), s * wide, *outside, 2)
    gradient = tails[0].astype(F32)
    for s in range(1, tails.shape[0]):
        gradient = gradient + tails[s].astype(F32)
    update(gradient, 2 * INNER, *inside[:-1], None, 0)


ROWS = 48


def by_rows(columns):
    return pl.BlockSpec((ROWS, columns), lambda i: (i, 0))


def run_moments(groups, heads, z_all, x_all, s_all, out_all, smalls, inside, outside):
    rows = inside[0].shape[0]
    wide = heads * HEAD
    piece = pl.BlockSpec((groups, ROWS, wide), lambda i: (0, i, 0))
    if s_all.shape[1] < rows:
        parts = s_all.shape[1] // ROWS
        tails = pl.BlockSpec((1, ROWS, SHARED), lambda i: (i // parts, i % parts, 0))
    else:
        tails = pl.BlockSpec((groups, ROWS, SHARED), lambda i: (0, i, 0))
    shape = jax.ShapeDtypeStruct
    extent = D + (KERNEL + 1) * CONV + 3 * HEADS + INNER
    small_out = [shape((1, extent), F32)] * 4
    in_like, out_like = shape(inside[0].shape, F32), shape(outside[0].shape, F32)
    in_spec, out_spec = by_rows(PROJ), by_rows(INNER)
    return pl.pallas_call(
        partial(moments_kernel, groups, heads),
        grid=(rows // ROWS,),
        in_specs=[piece, piece, tails, piece]
        + [resident(x) for x in smalls]
        + [in_spec] * 3
        + [out_spec] * 3,
        out_specs=[in_spec] * 3
        + [by_rows(2 * INNER)]
        + [out_spec] * 4
        + [pl.BlockSpec((8, wide), lambda i: (0, 0))]
        + [resident(x) for x in small_out]
        + [by_rows(SHARED)],
        out_shape=[in_like] * 3
        + [shape((rows, 2 * INNER), BF16)]
        + [out_like] * 3
        + [shape(out_like.shape, BF16), shape((8, wide), F32)]
        + small_out
        + [shape((rows, SHARED), F32)],
        scratch_shapes=[pltpu.VMEM(smalls[1].shape, F32)],
        compiler_params=compiler_params(),
        name="moments",
    )(z_all, x_all, s_all, out_all, *smalls, *inside, *outside)


def weights_kernel(norms, w_in, u_in, u_tail, w_out, u_out, in_new, out_new):
    in_rate, out_rate = [
        LEARN_RATE * (norms[at : at + 1, :1] / norms[at + 1 : at + 2, :1]) for at in (0, 2)
    ]
    edge = u_in.shape[1]
    rest = w_in.shape[1] - edge
    in_new[:, :edge] = w_in[:, :edge] - in_rate * u_in[...].astype(F32)
    in_new[:, edge:] = w_in[:, edge:] - in_rate * u_tail[:, :rest]
    out_new[...] = w_out[...] - out_rate * u_out[...].astype(F32)


def run_weights(norms, w_in, u_in, u_tail, w_out, u_out):
    in_spec, out_spec = by_rows(PROJ), by_rows(INNER)
    return pl.pallas_call(
        weights_kernel,
        grid=(w_in.shape[0] // ROWS,),
        in_specs=[
            resident(norms), in_spec, by_rows(2 * INNER), by_rows(SHARED), out_spec, out_spec
        ],
        out_specs=[in_spec, out_spec],
        out_shape=[
            jax.ShapeDtypeStruct(w_in.shape, F32),
            jax.ShapeDtypeStruct(w_out.shape, F32),
        ],
        compiler_params=compiler_params(),
        name="weights",
    )(norms, w_in, u_in, u_tail, w_out, u_out)


def adam_parts(gradient, first_old, second_old):
    first_new = FIRST_DECAY * first_old + (1.0 - FIRST_DECAY) * gradient
    second_new = SECOND_DECAY * second_old + (1.0 - SECOND_DECAY) * (gradient * gradient)
    first_scale = 1.0 / (1.0 - FIRST_DECAY**STEP)
    second_scale = 1.0 / (1.0 - SECOND_DECAY**STEP)
    direction = (first_new * first_scale) / (jnp.sqrt(second_new * second_scale) + ADAM_EPSILON)
    return (first_new, second_new, direction)


def wide_row(vector):
    return jnp.pad(vector, (0, -vector.shape[0] % 128))[None, :]


def shards(
    tokens,
    cotangent,
    segments,
    in_weight,
    out_weight,
    small_params,
    in_first,
    in_second,
    out_first,
    out_second,
    small_first,
    small_second,
):
    in_gain = small_params[:D]
    groups = lax.axis_size("seq")
    where_seq = lax.axis_index("seq")
    heads = HEADS // groups
    wide = INNER // groups
    segment_row = segments[0]

    def own(vector, axis=-1):
        size = vector.shape[axis] // groups
        return lax.dynamic_slice_in_dim(vector, where_seq * size, size, axis)

    inputs = tokens[0].astype(F32)
    in_rms = lax.rsqrt(jnp.mean(inputs * inputs, axis=-1, keepdims=True) + NORM_EPS)
    dt_weight = jnp.pad(
        in_weight[:, INNER + CONV :].astype(BF16), ((0, 0), (0, DT_PAD - HEADS))
    )
    small = wide_row(small_params)
    spread_heads = (
        jnp.arange(128)[:, None] == jnp.arange(wide)[None, :] // HEAD
    ).astype(BF16)
    seg_pad = jnp.pad(segment_row, (EDGE, EDGE), constant_values=-1)[:, None]
    (
        pre, conv_in, dt_pre, states, z_part, d_out_gain, conv_pack, head_pack, chan_pack,
        w_x, w_z, w_s, branch_part, d_y, d_z, normed_t, out_part,
    ) = run_forward(
        heads, tokens[0], cotangent[0], small, dt_weight, seg_pad, segments, spread_heads,
        in_weight, out_weight,
    )
    packs = (conv_pack, head_pack, chan_pack)
    out_all, z_all, x_all, s_all, small_all, branch, d_normed, _, _ = run_backward(
        heads, d_y, pre, conv_in, dt_pre, states, seg_pad, segments, packs, spread_heads, d_z,
        (w_z, w_x, w_s.reshape(D, SHARED)), normed_t, tokens[0], small, d_out_gain, out_part, z_part, branch_part,
    )
    output = (inputs + branch.astype(F32)).astype(BF16)[None]
    d_normed = d_normed.astype(F32)
    slope = d_normed * in_gain[None, :]
    d_inputs = slope * in_rms - inputs * (in_rms**3 / D) * jnp.sum(
        slope * inputs, axis=1, keepdims=True
    )
    input_grad = (cotangent[0].astype(F32) + d_inputs)[None]

    (
        in_grad, in_first_new, in_second_new, in_dir, out_grad, out_first_new, out_second_new, out_dir,
        squares, small_grad, small_new, small_first_new, small_second_new, in_tail,
    ) = run_moments(
        groups, heads, z_all, x_all, s_all, out_all,
        (small_all, small, wide_row(small_first), wide_row(small_second)),
        (in_weight, in_first, in_second), (out_weight, out_first, out_second),
    )
    norms = run_norms(squares)
    in_new, out_new = run_weights(norms, in_weight, in_dir, in_tail, out_weight, out_dir)
    small_grad, small_new, small_first_new, small_second_new = [
        x[0] for x in (small_grad, small_new, small_first_new, small_second_new)
    ]
    norms = norms[:4, 0]
    return (
        output,
        input_grad,
        in_grad,
        in_new,
        in_first_new,
        in_second_new,
        out_grad,
        out_new,
        out_first_new,
        out_second_new,
        small_grad,
        small_new,
        small_first_new,
        small_second_new,
        norms,
    )


def solution(mesh):
    matrix = P("fsdp", None)
    rows = P("fsdp", "seq", None)
    return jax.shard_map(
        shards,
        mesh=mesh,
        in_specs=(rows, rows, matrix, matrix, matrix, P(), matrix, matrix, matrix, matrix, P(), P()),
        out_specs=(rows, rows) + (matrix,) * 8 + (P(),) * 5,
        check_vma=False,
    )
```

```python
from functools import partial

import jax
import jax.numpy as jnp
from jax import lax
from jax.experimental import pallas as pl
from jax.experimental.pallas import tpu as pltpu
from jax.sharding import PartitionSpec as P

D = 1536
HEADS = 48
HEAD = 64
STATE = 128
KERNEL = 4
STRETCH = 256
STEP = 5
INNER = 3072
CONV = 3328
PROJ = 6448
DT_PAD = 128
SHARED = 2 * STATE + DT_PAD

NORM_EPS = 1e-05
FIRST_DECAY = 0.9
SECOND_DECAY = 0.999
ADAM_EPSILON = 1e-06
WEIGHT_DECAY = 0.01
LEARN_RATE = 0.5
F32 = jnp.float32
BF16 = jnp.bfloat16


def dot(a, b, dims=((1,), (0,))):
    return lax.dot_general(a, b, (dims, ((), ())), preferred_element_type=F32)


def split_dot(value, ones):
    high = value.astype(BF16)
    low = (value - high.astype(F32)).astype(BF16)
    return dot(high, ones) + dot(low, ones)


def tri_dot(ones, value):
    high = value.astype(BF16)
    rest = value - high.astype(F32)
    middle = rest.astype(BF16)
    low = (rest - middle.astype(F32)).astype(BF16)
    return dot(ones, high) + dot(ones, middle) + dot(ones, low)


def sigmoid(v):
    return 1.0 / (1.0 + jnp.exp(-v))


def softplus(v):
    return jnp.maximum(v, 0.0) + jnp.log1p(jnp.exp(-jnp.abs(v)))


def row_at_least():
    rows = lax.broadcasted_iota(jnp.int32, (STRETCH, STRETCH), 0)
    columns = lax.broadcasted_iota(jnp.int32, (STRETCH, STRETCH), 1)
    return rows >= columns


class Decays:
    def __init__(self, dt, rate, masks, spread):
        self.dt, self.spread = dt, spread
        lower = jnp.where(row_at_least(), 1.0, 0.0).astype(BF16)
        self.columns = dot(lower, dt) * rate
        self.rows = jnp.transpose(self.columns)
        last = self.columns[STRETCH - 1 :, :]
        self.into = jnp.exp(self.columns) * masks["carry"]
        self.out = jnp.exp(last - self.columns) * masks["tail"]
        self.through = jnp.broadcast_to(jnp.exp(last) * masks["keep"], (8, 128))
        self.bar = masks["bar"]

    def of(self, columns):
        ones = self.spread[:, columns]
        return (
            dot(self.dt, ones),
            split_dot(self.into, ones),
            split_dot(self.out, ones),
            split_dot(self.through, ones)[:1],
        )

    def between(self, head):
        return jnp.exp(self.columns[:, head : head + 1] - self.rows[head : head + 1, :] + self.bar)


EDGE = 8


def block_masks(seg_pad, seg_row, at):
    def rows(by, size=STRETCH):
        return seg_pad[pl.ds(at + EDGE + by, size), :]

    here = rows(0)
    first = jnp.where(at == 0, rows(0, 1), rows(-1, 1))
    last = rows(STRETCH - 1, 1)
    masks = {"carry": here == first, "tail": here == last, "keep": last == first}
    for by in range(1, KERNEL):
        masks[-by] = here == rows(-by)
        masks[by] = here == rows(by)
    masks = {key: jnp.where(value, 1.0, 0.0) for key, value in masks.items()}
    within = row_at_least() & (here == seg_row[:, pl.ds(at, STRETCH)])
    masks["bar"] = jnp.where(within, 0.0, -1e30)
    return masks


def forward_block(
    heads, at, normed, w_x, shared_columns, masks, packs, spread, outs, y_all, extended, state
):
    conv_pack, head_pack, chan_pack = packs
    pre_out, conv_out, dt_out, states_out = outs
    wide = heads * HEAD
    here = pl.ds(at, STRETCH)
    conv_low = jnp.concatenate([dot(normed, w_x[...]), dot(normed, shared_columns(0, 2 * STATE))], axis=1)
    conv_low = conv_low.astype(BF16)
    conv_out[...] = conv_low
    conv_in = conv_low.astype(F32)
    extended[8 : 8 + STRETCH, :] = conv_in
    pre = conv_pack[4:5, :] + conv_pack[3:4, :] * conv_in
    for by in range(1, KERNEL):
        pre = pre + conv_pack[3 - by : 4 - by, :] * (
            extended[8 - by : 8 - by + STRETCH, :] * masks[-by]
        )
    extended[0:8, :] = extended[STRETCH : STRETCH + 8, :]
    pre_out[...] = pre
    act = (pre * sigmoid(pre)).astype(BF16)
    b_mat = act[:, wide : wide + STATE]
    c_mat = act[:, wide + STATE :]
    lane = lax.broadcasted_iota(jnp.int32, (STRETCH, DT_PAD), 1)
    dt_pre = pltpu.roll(
        dot(normed, shared_columns(2 * STATE, DT_PAD)), DT_PAD - lax.axis_index("seq") * heads, 1
    )
    dt_pre = jnp.where(lane < heads, dt_pre, 0.0) + head_pack[0:1, :]
    dt_out[...] = dt_pre
    dt = softplus(dt_pre).astype(BF16)
    decay = Decays(dt, head_pack[1:2, :], masks, spread)
    scores = dot(c_mat, b_mat, ((1,), (1,)))
    first_half = lax.broadcasted_iota(jnp.int32, (STRETCH, 2 * HEAD), 1) < HEAD
    for pair in range(heads // 2):
        columns = slice(pair * 2 * HEAD, (pair + 1) * 2 * HEAD)
        steps, carry, tail, keep = decay.of(columns)
        xs = act[:, columns].astype(F32)
        scaled = xs * steps
        scaled_low = scaled.astype(BF16)
        old = state[:, columns]
        states_out[0, :, columns] = old
        y = dot(c_mat, old.astype(BF16)) * carry + chan_pack[0:1, columns] * xs
        state[:, columns] = old * keep + dot(b_mat, (scaled * tail).astype(BF16), ((0,), (0,)))
        halves = [
            dot((scores * decay.between(h)).astype(BF16), scaled_low)
            for h in (2 * pair, 2 * pair + 1)
        ]
        y_all[here, columns] = (y + jnp.where(first_half, halves[0], halves[1])).astype(BF16)


def fill_packs(heads, small, spread, packs, scratch_gain):
    conv_pack, head_pack, chan_pack = packs
    wide = heads * HEAD
    index = lax.axis_index("seq")
    start = pl.multiple_of(index * wide, 128)
    for ref in packs:
        ref[...] = jnp.zeros_like(ref)
    for k in range(KERNEL + 1):
        base = D + k * CONV
        conv_pack[k : k + 1, :wide] = small[:, pl.ds(base + start, wide)]
        conv_pack[k : k + 1, wide:] = small[:, base + INNER : base + CONV]
    base = D + (KERNEL + 1) * CONV
    window = jnp.broadcast_to(small[:, base : base + 256], (8, 256))
    lane = lax.broadcasted_iota(jnp.int32, (8, 256), 1)

    def own(k):
        moved = pltpu.roll(window, 256 - (k * HEADS + index * heads), 1)
        return jnp.where(lane < heads, moved, 0.0)[:, :128]

    head_pack[0:1, :] = own(0)[:1]
    rate = own(1)
    rate = jnp.where(lax.broadcasted_iota(jnp.int32, (8, 128), 1) < heads, -jnp.exp(rate), 0.0)
    head_pack[1:2, :] = rate[:1]
    chan_pack[0:1, :] = tri_spread(own(2), spread)[:1]
    base = base + 3 * HEADS
    shift = base % 128
    gain = jnp.broadcast_to(small[:, base - shift : base - shift + INNER + 128], (8, INNER + 128))
    scratch_gain[...] = pltpu.roll(gain, INNER + 128 - shift, 1)
    chan_pack[1:2, :] = scratch_gain[0:1, pl.ds(start, wide)]


def tri_spread(value, ones):
    high = value.astype(BF16)
    rest = value - high.astype(F32)
    middle = rest.astype(BF16)
    low = (rest - middle.astype(F32)).astype(BF16)
    return dot(high, ones) + dot(middle, ones) + dot(low, ones)


def as_row(column):
    lane = lax.broadcasted_iota(jnp.int32, (STRETCH, 128), 1)
    return jnp.transpose(jnp.where(lane == 0, column, 0.0))[0:8, :]


def as_column(rows):
    return jnp.transpose(jnp.concatenate([rows, jnp.zeros((120, STRETCH), F32)], axis=0))[:, 0:1]


def inverse_rms(squares):
    return lax.rsqrt(as_column(squares) / INNER + NORM_EPS)


def gate_gradients(y_low, z, d_mixed, gain, squares, products):
    rms = inverse_rms(squares)
    y = y_low.astype(F32)
    sig = sigmoid(z)
    silu = z * sig
    gated = y * silu
    unit = gated * rms
    d_gain = jnp.sum(d_mixed * unit, axis=0, keepdims=True)
    d_gated = d_mixed * gain * rms - unit * (rms * rms / INNER * as_column(products))
    d_z = d_gated * y * (sig * (1.0 + z * (1.0 - sig)))
    return (d_gated * silu).astype(BF16), d_z.astype(BF16), d_gain


def halved(rows, groups):
    return rows % (16 * groups) == 0


def forward_kernel(heads, *refs):
    tokens, cotangent, small, dt_weight, seg_pad, seg_row, spread_ref, in_weight, out_weight = refs[:9]
    outs = refs[9:13]
    z_part, d_gain = refs[13:15]
    packs = refs[15:18]
    w_x_out, w_z_out, w_s_out, branch_part, d_y_out, d_z_out, normed_t_out, out_part_out = refs[18:26]
    (
        stage_s, own_x, own_z, own_o, own_s, own_rows, w_x, w_z, w_o, w_s,
        shared_own, branch_stage, rows_all, returned_t, z_all, y_all, d_mixed_all, extended, state,
        scratch_gain, mixed_all, d_y, d_z, normed_t, out_part, sums, got, stage_sems, sum_sends, sum_arrivals,
    ) = refs[26:56]
    sems = refs[56:]
    ring, seq = places()
    wide = heads * HEAD
    edge = wide + 2 * STATE
    step = pl.program_id(0)
    blocks = pl.num_programs(0) - 1
    length = rows_all.shape[0]
    count = length // STRETCH
    rows = own_x.shape[0]
    split = halved(rows, seq.major * seq.minor)
    stage_x, stage_z, stage_o = [d_mixed_all.at[pl.ds(k * rows, rows)] for k in range(3)]

    def shared_columns(start, size):
        if split:
            return w_s[:, :, :, start : start + size].reshape(D, size)
        return w_s[:, start : start + size]

    get_x = Gather(ring, own_x, w_x, rows, WEIGHT_PIECES, sems[:5])
    get_z = Gather(ring, own_z, w_z, rows, 1, sems[5:10])
    get_o = Gather(ring, own_o, w_o, rows, 1, sems[10:15])
    get_rows = Gather(seq, own_rows, rows_all, own_rows.shape[0], TOKEN_PIECES, sems[15:20])
    if split:
        get_s = Gather(ring, own_s, shared_own, own_s.shape[0], 1, sems[20:25])
        pass_s = Gather(
            seq, shared_own, w_s, shared_own.shape[0], 1, sems[25:30],
            lambda slot, piece: w_s.at[:, slot],
        )
    else:
        get_s = Gather(ring, own_s, w_s, rows, 1, sems[20:25])
    saves = [
        pltpu.make_async_copy(source, target, stage_sems.at[4 + k])
        for k, (source, target) in enumerate(
            (
                (w_x, w_x_out),
                (w_z, w_z_out),
                (w_s, w_s_out),
                (normed_t, normed_t_out),
                (out_part, out_part_out),
                (d_y, d_y_out),
                (d_z, d_z_out),
                (rows_all.at[:, D:], branch_part),
            )
        )
    ]
    spread = spread_ref[...]
    at = pl.multiple_of(step * STRETCH, STRETCH)

    @pl.when(step == 0)
    def _():
        start = pl.multiple_of(seq.index * wide, 128)
        own_shared = own_s.shape[0]
        first_row = pl.multiple_of(seq.index * own_shared, 16) if split else 0
        sources = [
            (in_weight.at[pl.ds(first_row, own_shared), pl.ds(2 * INNER, 2 * STATE)], stage_s),
            (in_weight.at[:, pl.ds(INNER + start, wide)], stage_x),
            (in_weight.at[:, pl.ds(start, wide)], stage_z),
            (out_weight.at[:, pl.ds(start, wide)], stage_o),
        ]
        loads = [
            pltpu.make_async_copy(source, target, stage_sems.at[k])
            for k, (source, target) in enumerate(sources)
        ]
        for load in loads:
            load.start()
        meet(ring, seq)
        loads[0].wait()
        own_s[:, : 2 * STATE] = stage_s[...].astype(BF16)
        own_s[:, 2 * STATE :] = dt_weight[pl.ds(first_row, own_shared), :]
        get_s.begin(0)
        get_s.keep().start()
        loads[1].wait()
        own_x[...] = stage_x[...].astype(BF16)
        for piece in range(WEIGHT_PIECES):
            get_x.begin(piece)
        get_x.keep().start()
        inputs = tokens[...].astype(F32)
        rms = lax.rsqrt(jnp.mean(inputs * inputs, axis=-1, keepdims=True) + NORM_EPS)
        own_rows[:, :D] = (inputs * rms * small[:, :D]).astype(BF16)
        own_rows[:, D:] = cotangent[...]
        for piece in range(TOKEN_PIECES):
            get_rows.begin(piece)
        get_rows.keep().start()
        loads[2].wait()
        loads[3].wait()
        own_z[...] = stage_z[...].astype(BF16)
        own_o[...] = stage_o[...].astype(BF16)
        get_z.begin_across(0)
        get_o.begin_across(0)
        get_z.keep().start()
        get_o.keep().start()
        fill_packs(heads, small, spread, packs, scratch_gain)
        state[...] = jnp.zeros_like(state)
        extended[0:8, :] = jnp.zeros((8, edge), F32)
        d_gain[...] = jnp.zeros_like(d_gain)
        get_s.forward(0)
        get_rows.forward(0)
        get_x.forward(0)
        get_s.finish()
        get_s.keep().wait()
        if split:
            pass_s.begin(0)
            pass_s.keep().start()
        get_rows.forward(1)
        get_x.forward(1)
        get_z.begin_along(0)
        get_rows.forward(2)
        get_x.forward(2)
        get_o.begin_along(0)
        for piece in range(3, TOKEN_PIECES):
            get_rows.forward(piece)
        if split:
            pass_s.forward(0)
        get_rows.finish()
        get_rows.keep().wait()

        def turn(k, _):
            here = pl.ds(pl.multiple_of(k * STRETCH, STRETCH), STRETCH)
            normed_t[:, here] = jnp.transpose(rows_all[here, :D])
            returned_t[:, here] = jnp.transpose(rows_all[here, D:])
            return 0

        lax.fori_loop(0, count, turn, 0)
        if split:
            pass_s.finish()
            pass_s.keep().wait()
        get_x.finish()
        get_x.keep().wait()
        get_z.forward_step(0, 1)
        saves[0].start()
        saves[2].start()
        saves[3].start()

    @pl.when(step < blocks)
    def _():
        masks = block_masks(seg_pad, seg_row, at)
        forward_block(
            heads, at, rows_all[pl.ds(at, STRETCH), :D], w_x, shared_columns, masks, packs, spread, outs,
            y_all, extended, state,
        )

    forwards = [(stream, k) for stream in (get_z, get_o) for k in range(1, ring.major)][1:]
    ahead = min(count, len(forwards))
    for k in range(ahead):

        @pl.when(step == k)
        def _():
            stream, by = forwards[k]
            stream.forward_step(0, by)

    @pl.when(step == blocks)
    def _():
        later = list(forwards[ahead:])
        while later and later[0][0] is get_z:
            stream, by = later.pop(0)
            stream.forward_step(0, by)
        get_z.finish()
        get_z.keep().wait()
        saves[1].start()
        levels = levels_of("seq")
        gain = packs[2][1:2, :]

        def chunk_rows(k):
            return pl.ds(pl.multiple_of(k * STRETCH, STRETCH), STRETCH)

        def gated_at(here):
            z = z_all[here, :]
            return y_all[here, :].astype(F32) * (z * sigmoid(z))

        def summed(which):
            base = which * (levels + 1)
            for level in range(levels):
                at = which * levels + level
                copy = exchange(
                    "seq", level, sums.at[base + level], got.at[at], sum_sends.at[at], sum_arrivals.at[at]
                )
                copy.start()
                copy.wait()
                sums[base + level + 1] = sums[base + level] + got[at]
            return base + levels

        def gate(k, _):
            here = chunk_rows(k)
            z_all[here, :] = dot(rows_all[here, :D], w_z[...])
            gated = gated_at(here)
            sums[0, :, here] = as_row(jnp.sum(gated * gated, axis=1, keepdims=True))
            return 0

        lax.fori_loop(0, count, gate, 0)
        if later:
            stream, by = later.pop(0)
            stream.forward_step(0, by)
        squares = summed(0)

        def mix(k, _):
            here = chunk_rows(k)
            mixed_all[here, :] = (
                gated_at(here) * inverse_rms(sums[squares, :, here]) * gain
            ).astype(BF16)
            return 0

        lax.fori_loop(0, count, mix, 0)
        for stream, by in later:
            stream.forward_step(0, by)

        def contract_out(k, _):
            here = pl.ds(pl.multiple_of(k * 256, 256), 256)
            out_part[here, :] = dot(returned_t[here, :], mixed_all[...]).astype(BF16)
            return 0

        lax.fori_loop(0, D // 256, contract_out, 0)
        saves[4].start()
        get_o.finish()
        get_o.keep().wait()

        def measure(k, _):
            here = chunk_rows(k)
            d_mixed = dot(rows_all[here, D:], w_o[...])
            d_mixed_all[here, :] = d_mixed
            product = jnp.sum(d_mixed * gain * gated_at(here), axis=1, keepdims=True)
            sums[levels + 1, :, here] = as_row(product)
            return 0

        lax.fori_loop(0, count, measure, 0)
        products = summed(1)

        def differentiate(k, _):
            here = chunk_rows(k)
            d_y_block, d_z_block, d_gain_block = gate_gradients(
                y_all[here, :], z_all[here, :], d_mixed_all[here, :], gain,
                sums[squares, :, here], sums[products, :, here],
            )
            d_y[here, :] = d_y_block
            d_z[here, :] = d_z_block
            d_gain[0:1, :] += d_gain_block
            rows_all[here, D:] = dot(mixed_all[here, :], w_o[...], ((1,), (1,))).astype(BF16)
            return 0

        lax.fori_loop(0, count, differentiate, 0)
        saves[5].start()
        saves[6].start()
        saves[7].start()

        def contract_z(k, _):
            here = pl.ds(pl.multiple_of(k * 256, 256), 256)
            z_part[here, :] = dot(normed_t[here, :], d_z[...]).astype(BF16)
            return 0

        lax.fori_loop(0, D // 256, contract_z, 0)
        for save in saves:
            save.wait()


def backward_block(
    heads,
    d_y_ref,
    pre_ref,
    conv_ref,
    dt_ref,
    states,
    seg_pad,
    seg_row,
    conv_pack,
    head_pack,
    chan_pack,
    spread_ref,
    gather_ref,
    d_conv_out,
    d_head_out,
    extended,
    d_state,
    d_rest,
):
    wide = heads * HEAD
    edge = wide + 2 * STATE

    @pl.when(pl.program_id(0) == 0)
    def _():
        d_state[...] = jnp.zeros_like(d_state)
        extended[STRETCH : STRETCH + 8, :] = jnp.zeros((8, edge), F32)
        d_conv_out[...] = jnp.zeros_like(d_conv_out)
        d_head_out[...] = jnp.zeros_like(d_head_out)

    at_row = pl.multiple_of((pl.num_programs(0) - 1 - pl.program_id(0)) * STRETCH, STRETCH)
    masks = block_masks(seg_pad, seg_row, at_row)
    spread = spread_ref[...]
    gather = gather_ref[...]
    pre = pre_ref[...]
    act = (pre * sigmoid(pre)).astype(BF16)
    b_mat = act[:, wide : wide + STATE]
    c_mat = act[:, wide + STATE :]
    dt_pre = dt_ref[...]
    dt = softplus(dt_pre).astype(BF16)
    rate = head_pack[1:2, :]
    decay = Decays(dt, rate, masks, spread)
    scores = dot(c_mat, b_mat, ((1,), (1,)))
    lane = lax.broadcasted_iota(jnp.int32, (STRETCH, 128), 1)
    first_half = lane < HEAD
    d_b = jnp.zeros((STRETCH, STATE), F32)
    d_c = jnp.zeros((STRETCH, STATE), F32)
    d_scores = jnp.zeros((STRETCH, STRETCH), F32)
    d_cum = jnp.zeros((STRETCH, 128), F32)
    d_dt = jnp.zeros((STRETCH, 128), F32)
    d_last = jnp.zeros((1, 128), F32)
    column_sums = []
    for pair in range(heads // 2):
        columns = slice(pair * 2 * HEAD, (pair + 1) * 2 * HEAD)
        ones = gather[columns, :]
        steps, carry, tail, keep = decay.of(columns)
        xs = act[:, columns].astype(F32)
        scaled = xs * steps
        scaled_low = scaled.astype(BF16)
        old = states[0, :, columns]
        old_low = old.astype(BF16)
        d_new = d_state[:, columns]
        d_new_low = d_new.astype(BF16)
        d_y_low = d_y_ref[:, columns]
        d_y = d_y_low.astype(F32)
        d_carried = d_y * carry
        d_carried_low = d_carried.astype(BF16)
        d_c = d_c + dot(d_carried_low, old_low, ((1,), (1,)))
        d_cum = d_cum + split_dot(d_carried * dot(c_mat, old_low), ones)
        weighed = scaled * tail
        into = dot(b_mat, d_new_low)
        d_b = d_b + dot(weighed.astype(BF16), d_new_low, ((1,), (1,)))
        tail_part = split_dot(weighed * into, ones)
        d_cum = d_cum - tail_part
        kept = jnp.sum(d_new * old, axis=0, keepdims=True) * keep
        kept = split_dot(jnp.broadcast_to(kept, (8, 128)), ones)[:1]
        d_last = d_last + jnp.sum(tail_part, axis=0, keepdims=True) + kept
        d_state[:, columns] = d_new * keep + dot(c_mat, d_carried_low, ((0,), (0,)))
        halves = []
        for h in (2 * pair, 2 * pair + 1):
            between = decay.between(h)
            weights = scores * between
            halves.append(dot(weights.astype(BF16), d_y_low, ((0,), (0,))))
            d_y_head = jnp.where(first_half == (h % 2 == 0), d_y_low, jnp.zeros_like(d_y_low))
            d_weights = dot(d_y_head, scaled_low, ((1,), (1,)))
            d_scores = d_scores + d_weights * between
            product = d_weights * weights
            d_cum = d_cum + jnp.where(lane == h, jnp.sum(product, axis=1, keepdims=True), 0.0)
            column_sums.append(jnp.sum(product, axis=0, keepdims=True))
        d_scaled = into * tail + jnp.where(first_half, halves[0], halves[1])
        d_xs = d_scaled * steps + chan_pack[0:1, columns] * d_y
        extended[0:STRETCH, columns] = d_xs.astype(BF16).astype(F32)
        d_dt = d_dt + split_dot(d_scaled * xs, ones)
        d_skip = jnp.sum(d_y * xs, axis=0, keepdims=True)
        d_head_out[2:3, :] += split_dot(jnp.broadcast_to(d_skip, (8, 128)), ones)[:1]
    column_sums.append(jnp.zeros((128 - heads, STRETCH), F32))
    d_cum = d_cum - jnp.transpose(jnp.concatenate(column_sums, axis=0))
    row = lax.broadcasted_iota(jnp.int32, (STRETCH, 128), 0)
    d_cum = d_cum + jnp.where(row == STRETCH - 1, d_last, 0.0)
    d_scores_low = d_scores.astype(BF16)
    d_c = d_c + dot(d_scores_low, b_mat)
    d_b = d_b + dot(d_scores_low, c_mat, ((0,), (0,)))

    rows = lax.broadcasted_iota(jnp.int32, (STRETCH, STRETCH), 0)
    upper = jnp.where(rows <= lax.broadcasted_iota(jnp.int32, (STRETCH, STRETCH), 1), 1.0, 0.0)
    d_dt = d_dt + rate * tri_dot(upper.astype(BF16), d_cum)
    d_dt_raw = d_dt.astype(BF16).astype(F32) * sigmoid(dt_pre)
    d_head_out[0:1, :] += jnp.sum(d_dt_raw, axis=0, keepdims=True)
    d_head_out[1:2, :] += jnp.sum(d_cum * decay.columns, axis=0, keepdims=True)

    extended[0:STRETCH, wide : wide + STATE] = d_b
    extended[0:STRETCH, wide + STATE :] = d_c
    here = pl.ds(at_row, STRETCH)
    moved = pltpu.roll(jnp.where(lane < heads, d_dt_raw, 0.0), lax.axis_index("seq") * heads, 1)
    d_rest[here, edge:] = moved.astype(BF16)

    def convolve_back(at, _):
        columns = pl.ds(pl.multiple_of(at * 128, 128), 128)
        value = pre_ref[:, columns]
        gate = sigmoid(value)
        d_pre = extended[0:STRETCH, columns] * (gate * (1.0 + value * (1.0 - gate)))
        extended[0:STRETCH, columns] = d_pre
        conv_in = conv_ref[:, columns].astype(F32)
        d_conv_in = conv_pack[3:4, columns] * d_pre
        d_conv_out[3:4, columns] += jnp.sum(d_pre * conv_in, axis=0, keepdims=True)
        d_conv_out[4:5, columns] += jnp.sum(d_pre, axis=0, keepdims=True)
        for by in range(1, KERNEL):
            moved = extended[by : by + STRETCH, columns] * masks[by]
            d_conv_in = d_conv_in + conv_pack[3 - by : 4 - by, columns] * moved
            d_conv_out[3 - by : 4 - by, columns] += jnp.sum(moved * conv_in, axis=0, keepdims=True)
        extended[STRETCH : STRETCH + 8, columns] = extended[0:8, columns]
        d_rest[here, columns] = d_conv_in.astype(BF16)
        return 0

    lax.fori_loop(0, edge // 128, convolve_back, 0)


VMEM_BYTES = 56 * 1024 * 1024


def block(columns, reverse=0):
    if reverse:
        return pl.BlockSpec((STRETCH, columns), lambda i: (reverse - 1 - i, 0))
    return pl.BlockSpec((STRETCH, columns), lambda i: (i, 0))


def whole(*shape):
    return pl.BlockSpec(shape, lambda i: (0,) * len(shape))


def compiler_params():
    return pltpu.CompilerParams(
        vmem_limit_bytes=VMEM_BYTES, dimension_semantics=("arbitrary",)
    )


class Place:
    def __init__(self, axis, minor):
        self.axis = axis
        self.minor = minor
        self.major = lax.axis_size(axis) // minor
        index = lax.axis_index(axis)
        self.at_major = index // minor
        self.at_minor = index % minor
        self.index = index

    def slot(self, by_major, by_minor):
        return (self.at_major + by_major) % self.major * self.minor + (
            self.at_minor + by_minor
        ) % self.minor

    def others(self):
        along = [self.slot(step, 0) for step in range(1, self.major)]
        return along + [self.slot(0, step) for step in range(1, self.minor)]


def places():
    ring = lax.axis_size("fsdp")
    side = 1
    while 2 * side * 2 * side * 2 <= ring:
        side = 2 * side
    return Place("fsdp", side), Place("seq", 2)


def meet(*all_places):
    barrier = pltpu.get_barrier_semaphore()
    count = 0
    for place in all_places:
        for other in place.others():
            pl.semaphore_signal(
                barrier, inc=1, device_id={place.axis: other}, device_id_type=pl.DeviceIdType.MESH
            )
            count = count + 1
    pl.semaphore_wait(barrier, count)


def send(place, source, target, to, sends, arrivals, at):
    return pltpu.make_async_remote_copy(
        src_ref=source,
        dst_ref=target,
        send_sem=sends.at[at],
        recv_sem=arrivals.at[at],
        device_id={place.axis: to},
        device_id_type=pl.DeviceIdType.MESH,
    )


class Gather:
    def __init__(self, place, own, full, rows, pieces, sems, target=None):
        self.place, self.own, self.full, self.landing = place, own, full, target
        self.size, self.pieces = rows // pieces, pieces
        self.sends1, self.arrivals1, self.sends2, self.arrivals2, self.here = sems

    @staticmethod
    def scratch(place, pieces):
        first = max(place.major - 1, 1) * pieces
        second = place.major * (place.minor - 1) * pieces
        dma = pltpu.SemaphoreType.DMA
        return [dma((first,)), dma((first,)), dma((second,)), dma((second,)), dma((1,))]

    def rows(self, piece):
        return pl.ds(piece * self.size, self.size)

    def target(self, slot, piece):
        if self.landing is not None:
            return self.landing(slot, piece)
        if len(self.full.shape) > len(self.own.shape):
            return self.full.at[slot, self.rows(piece)]
        start = slot * (self.size * self.pieces) + piece * self.size
        return self.full.at[pl.ds(pl.multiple_of(start, 16), self.size)]

    def along(self, piece, step):
        place = self.place
        return send(
            place,
            self.own.at[self.rows(piece)],
            self.target(place.index, piece),
            place.slot(step, 0),
            self.sends1,
            self.arrivals1,
            piece * (place.major - 1) + step - 1,
        )

    def across(self, piece, step, across):
        place = self.place
        slot = place.slot(-step, 0)
        target = self.target(slot, piece)
        source = self.own.at[self.rows(piece)] if step == 0 else target
        at = (piece * place.major + step) * (place.minor - 1) + across - 1
        return send(
            place, source, target, place.slot(0, across), self.sends2, self.arrivals2, at
        )

    def keep(self):
        if self.landing is not None:
            target = self.landing(self.place.index, 0)
        elif len(self.full.shape) > len(self.own.shape):
            target = self.full.at[self.place.index]
        else:
            size = self.size * self.pieces
            target = self.full.at[pl.ds(pl.multiple_of(self.place.index * size, 16), size)]
        return pltpu.make_async_copy(self.own, target, self.here.at[0])

    def begin(self, piece):
        self.begin_along(piece)
        self.begin_across(piece)

    def begin_along(self, piece):
        for step in range(1, self.place.major):
            self.along(piece, step).start()

    def begin_across(self, piece):
        for across in range(1, self.place.minor):
            self.across(piece, 0, across).start()

    def forward(self, piece):
        for step in range(1, self.place.major):
            self.forward_step(piece, step)

    def forward_step(self, piece, step):
        self.along(piece, step).wait_recv()
        for across in range(1, self.place.minor):
            self.across(piece, step, across).start()

    def finish(self):
        for piece in range(self.pieces):
            for step in range(1, self.place.major):
                self.along(piece, step).wait_send()
            for step in range(self.place.major):
                for across in range(1, self.place.minor):
                    self.across(piece, step, across).wait()


class Reduce:
    def __init__(self, place, part, total, rows, pieces, scratch, loads=None):
        self.place, self.part, self.total, self.loads = place, part, total, loads
        self.size, self.pieces = rows // pieces, pieces
        self.got1, self.mine, self.got2, self.sends1, self.arrivals1, self.sends2, self.arrivals2 = (
            scratch
        )

    @staticmethod
    def scratch(place, rows, columns, pieces):
        dma = pltpu.SemaphoreType.DMA
        first = place.major * (place.minor - 1)
        second = max(place.major - 1, 1)
        return [
            pltpu.VMEM((first, rows, columns), BF16),
            pltpu.VMEM((second, rows, columns), BF16),
            pltpu.VMEM((second, rows, columns), BF16),
            dma((first * pieces,)),
            dma((first * pieces,)),
            dma((second * pieces,)),
            dma((second * pieces,)),
        ]

    def items(self):
        return [(piece, step) for step in self.steps() for piece in range(self.pieces)]

    def steps(self):
        return list(range(1, self.place.major)) + [0]

    def rows(self, piece):
        return pl.ds(piece * self.size, self.size)

    def part_rows(self, slot, rows_start, size):
        if len(self.part.shape) == 3:
            return slot, pl.ds(rows_start, size)
        start = slot * (self.size * self.pieces) + rows_start
        return (pl.ds(pl.multiple_of(start, 16), size),)

    def across(self, item, across):
        piece, step = item
        place = self.place
        slot = step * (place.minor - 1) + across - 1
        index = self.part_rows(place.slot(step, across), piece * self.size, self.size)
        return send(
            place,
            self.part.at[index],
            self.got1.at[slot, self.rows(piece)],
            place.slot(0, across),
            self.sends1,
            self.arrivals1,
            slot * self.pieces + piece,
        )

    def along(self, item):
        piece, step = item
        place = self.place
        return send(
            place,
            self.mine.at[step - 1, self.rows(piece)],
            self.got2.at[step - 1, self.rows(piece)],
            place.slot(step, 0),
            self.sends2,
            self.arrivals2,
            (step - 1) * self.pieces + piece,
        )

    def begin(self, item):
        for across in range(1, self.place.minor):
            self.across(item, across).start()
        if self.loads is not None:
            self.load(item[1]).start()

    def load(self, step):
        target = self.mine.at[step - 1] if step else self.total
        return pltpu.make_async_copy(
            self.part.at[self.place.slot(step, 0)], target, self.loads.at[step]
        )

    def own(self, step, rows):
        if self.loads is None:
            return self.part[self.part_rows(self.place.slot(step, 0), rows, 16)].astype(F32)
        source = self.mine.at[step - 1] if step else self.total
        return source[pl.ds(rows, 16)].astype(F32)

    def blocks(self, piece, body):
        def one(at, _):
            body(pl.multiple_of(piece * self.size + at * 16, 16))
            return 0

        lax.fori_loop(0, self.size // 16, one, 0)

    def handle(self, item):
        piece, step = item
        place = self.place
        for across in range(1, place.minor):
            self.across(item, across).wait_recv()
        if self.loads is not None:
            self.load(step).wait()
        if step == 0:
            return

        def body(start):
            value = self.own(step, start)
            rows = pl.ds(start, 16)
            for across in range(1, place.minor):
                slot = step * (place.minor - 1) + across - 1
                value = value + self.got1[slot, rows].astype(F32)
            self.mine[step - 1, rows] = value.astype(BF16)

        self.blocks(piece, body)
        self.along(item).start()

    def close(self, piece):
        place = self.place
        for step in range(1, place.major):
            self.along((piece, step)).wait_recv()

        def body(start):
            value = self.own(0, start)
            rows = pl.ds(start, 16)
            for across in range(1, place.minor):
                value = value + self.got1[across - 1, rows].astype(F32)
            for step in range(1, place.major):
                value = value + self.got2[step - 1, rows].astype(F32)
            self.total[rows] = value.astype(self.total.dtype)

        self.blocks(piece, body)

    def finish(self):
        for item in self.items():
            for across in range(1, self.place.minor):
                self.across(item, across).wait_send()
            if item[1]:
                self.along(item).wait_send()


WEIGHT_PIECES = 3
TOKEN_PIECES = 4
HBM = pl.BlockSpec(memory_space=pl.ANY)
VMEM = pl.BlockSpec(memory_space=pltpu.VMEM)


def comm_params(number):
    return pltpu.CompilerParams(
        collective_id=number, has_side_effects=True, vmem_limit_bytes=VMEM_BYTES
    )


def resident(x):
    return pl.BlockSpec(
        x.shape, lambda i: (0,) * len(x.shape), pipeline_mode=pl.Buffered(buffer_count=1)
    )


def run_forward(heads, tokens, cotangent, small, dt_weight, seg_pad, seg_row, spread, in_weight, out_weight):
    ring, seq = places()
    count, groups = lax.axis_size("fsdp"), lax.axis_size("seq")
    rows, own_rows = in_weight.shape[0], tokens.shape[0]
    length = own_rows * groups
    blocks = length // STRETCH
    wide = heads * HEAD
    edge = wide + 2 * STATE
    levels = levels_of("seq")
    shape = jax.ShapeDtypeStruct
    split = halved(rows, groups)
    own_shared = rows // groups if split else rows
    shared_shape = (count, groups, own_shared, SHARED) if split else (D, SHARED)

    def chunk(columns):
        return pl.BlockSpec((STRETCH, columns), lambda i: (i - i // blocks, 0))

    wholes = [tokens, cotangent, small, dt_weight, seg_pad, seg_row, spread]
    late = [
        shape((D, wide), BF16),
        shape((8, wide), F32),
        shape((8, edge), F32),
        shape((8, 128), F32),
        shape((8, wide), F32),
    ]
    dma = pltpu.SemaphoreType.DMA
    scratch = [
        pltpu.VMEM((own_shared, 2 * STATE), F32),
        pltpu.VMEM((rows, wide), BF16),
        pltpu.VMEM((rows, wide), BF16),
        pltpu.VMEM((rows, wide), BF16),
        pltpu.VMEM((own_shared, SHARED), BF16),
        pltpu.VMEM((own_rows, 2 * D), BF16),
        pltpu.VMEM((D, wide), BF16),
        pltpu.VMEM((D, wide), BF16),
        pltpu.VMEM((D, wide), BF16),
        pltpu.VMEM(shared_shape, BF16),
        pltpu.VMEM((count, own_shared, SHARED) if split else (16, 128), BF16),
        pltpu.VMEM((STRETCH, D), BF16),
        pltpu.VMEM((length, 2 * D), BF16),
        pltpu.VMEM((D, length), BF16),
        pltpu.VMEM((length, wide), F32),
        pltpu.VMEM((length, wide), BF16),
        pltpu.VMEM((length, wide), F32),
        pltpu.VMEM((STRETCH + 8, edge), F32),
        pltpu.VMEM((STATE, wide), F32),
        pltpu.VMEM((8, INNER + 128), F32),
        pltpu.VMEM((length, wide), BF16),
        pltpu.VMEM((length, wide), BF16),
        pltpu.VMEM((length, wide), BF16),
        pltpu.VMEM((D, length), BF16),
        pltpu.VMEM((D, wide), BF16),
        pltpu.VMEM((2 * (levels + 1), 8, length), F32),
        pltpu.VMEM((2 * levels, 8, length), F32),
        dma((12,)),
        dma((2 * levels,)),
        dma((2 * levels,)),
    ]
    scratch = scratch + Gather.scratch(ring, WEIGHT_PIECES) + Gather.scratch(ring, 1)
    scratch = scratch + Gather.scratch(ring, 1) + Gather.scratch(seq, TOKEN_PIECES)
    scratch = scratch + Gather.scratch(ring, 1) + Gather.scratch(seq, 1)
    return pl.pallas_call(
        partial(forward_kernel, heads),
        grid=(blocks + 1,),
        in_specs=[resident(x) for x in wholes] + [HBM, HBM],
        out_specs=[
            chunk(edge),
            chunk(edge),
            chunk(128),
            pl.BlockSpec((1, STATE, wide), lambda i: (i - i // blocks, 0, 0)),
        ]
        + [resident(x) for x in late]
        + [HBM] * 8,
        out_shape=[
            shape((length, edge), F32),
            shape((length, edge), BF16),
            shape((length, 128), F32),
            shape((blocks, STATE, wide), F32),
        ]
        + late
        + [shape((D, wide), BF16), shape((D, wide), BF16), shape(shared_shape, BF16)]
        + [shape((length, D), BF16), shape((length, wide), BF16), shape((length, wide), BF16)]
        + [shape((D, length), BF16), shape((D, wide), BF16)],
        scratch_shapes=scratch,
        compiler_params=pltpu.CompilerParams(
            collective_id=1,
            has_side_effects=True,
            vmem_limit_bytes=61 * 1024 * 1024,
            dimension_semantics=("arbitrary",),
        ),
        name="gather_and_forward",
    )(*wholes, in_weight, out_weight)


def backward_kernel(heads, *refs):
    chunk = refs[:5]
    packs = refs[5:12]
    d_z, w_z, w_x, w_s, normed_t, tokens, small, d_gain = refs[12:20]
    out_part, z_part, branch_part = refs[20:23]
    out_all, z_all, x_all, s_all, small_all, branch, d_normed, d_conv, d_head = refs[23:32]
    extended, d_state, d_rest, x_part, s_part, act_part, out_own, z_own, x_own, s_own, s_mid = refs[32:43]
    small_sums, small_got, small_sends, small_arrivals, out_loads, z_loads, branch_loads = refs[43:50]
    scratch = refs[50:]
    ring, seq = places()
    rows = x_own.shape[0]
    own_rows = act_part.shape[1]
    wide = heads * HEAD
    edge = wide + 2 * STATE
    groups = seq.major * seq.minor
    own_shared = s_own.shape[0]
    split = halved(rows, groups)
    levels = levels_of("fsdp")

    def stream(place, part, total, extent, pieces, at, loads=None):
        return Reduce(place, part, total, extent, pieces, scratch[7 * at : 7 * at + 7], loads)

    def spreading(own, full, pieces, at):
        return Gather(seq, own, full, own.shape[0], pieces, scratch[49 + 5 * at : 54 + 5 * at])

    out_sum = stream(ring, out_part, out_own, rows, 1, 0, out_loads)
    z_sum = stream(ring, z_part, z_own, rows, 1, 1, z_loads)
    x_sum = stream(ring, x_part, x_own, rows, WEIGHT_PIECES, 2)
    branch_sum = stream(seq, branch_part, branch, own_rows, 1, 3, branch_loads)
    d_normed_sum = stream(seq, act_part, d_normed, own_rows, 2, 4)
    if split:
        mid_sum = stream(seq, s_part, s_mid, s_mid.shape[0], 1, 5)
        s_sum = stream(ring, s_mid, s_own, own_shared, 1, 6)
    else:
        s_sum = stream(ring, s_part, s_own, rows, 1, 6)
    out_spread = spreading(out_own, out_all, 1, 0)
    z_spread = spreading(z_own, z_all, 1, 1)
    x_spread = spreading(x_own, x_all, WEIGHT_PIECES, 2)
    s_spread = spreading(s_own, s_all, 1, 3)
    small_spread = spreading(small_sums.at[levels], small_all, 1, 4)
    early = [(s, item) for s in (out_sum, z_sum) for item in s.items()]
    at_step = pl.program_id(0)
    blocks = d_rest.shape[0] // STRETCH

    def swap(level):
        return exchange(
            "fsdp",
            level,
            small_sums.at[level],
            small_got.at[level],
            small_sends.at[level],
            small_arrivals.at[level],
        )

    @pl.when(at_step == 0)
    def _():
        meet(ring, seq)
        for s, item in early:
            s.begin(item)
        for item in branch_sum.items():
            branch_sum.begin(item)

    backward_block(heads, *chunk, *packs, d_conv, d_head, extended, d_state, d_rest)

    for k in range(blocks):

        @pl.when(at_step == k)
        def _():
            s, item = early[k]
            s.handle(item)
            if k == blocks - 1:
                for item in branch_sum.items():
                    branch_sum.handle(item)
                branch_sum.close(0)
                branch_sum.finish()

    @pl.when(at_step == blocks - 1)
    def _():
        def x_block(slot):
            here = pl.ds(pl.multiple_of(slot * rows, 16), rows)

            def one(at, _):
                columns = pl.ds(pl.multiple_of(at * 384, 128), 384)
                x_part[slot, :, columns] = dot(normed_t[here, :], d_rest[:, columns]).astype(BF16)
                return 0

            lax.fori_loop(0, wide // 384, one, 0)

        def s_block(slot, _):
            here = pl.ds(pl.multiple_of(slot * rows, 16), rows)
            value = dot(normed_t[here, :], d_rest[:, wide:]).astype(BF16)
            if split:
                target = pl.ds(pl.multiple_of(slot * own_shared, 16), own_shared)
                for s in range(groups):
                    s_part[s, target, :] = value[s * own_shared : (s + 1) * own_shared]
            else:
                s_part[slot] = value
            return 0

        def normed_block(slot):
            here = pl.ds(pl.multiple_of(slot * own_rows, own_rows), own_rows)

            def one(at, _):
                columns = pl.ds(pl.multiple_of(at * 512, 128), 512)
                value = dot(d_z[here, :], w_z[columns, :], ((1,), (1,)))
                value = value + dot(d_rest[here, :wide], w_x[columns, :], ((1,), (1,)))
                value = value + dot(d_rest[here, wide:], w_s[columns, :], ((1,), (1,)))
                act_part[slot, :, columns] = value.astype(BF16)
                return 0

            lax.fori_loop(0, D // 512, one, 0)

        waiting = early[blocks:]

        def handle_early(amount=1):
            for _ in range(min(amount, len(waiting))):
                s, item = waiting.pop(0)
                s.handle(item)

        lax.fori_loop(0, ring.major * ring.minor, s_block, 0)
        if split:
            for item in mid_sum.items():
                mid_sum.begin(item)
        else:
            for item in s_sum.items():
                s_sum.begin(item)
        handle_early()
        for step in x_sum.steps():
            for across in range(1, ring.minor):
                x_block(ring.slot(step, across))
            for piece in range(WEIGHT_PIECES):
                x_sum.begin((piece, step))
        if split:
            for item in mid_sum.items():
                mid_sum.handle(item)
        handle_early()
        for step in d_normed_sum.steps():
            for across in range(1, seq.minor):
                normed_block(seq.slot(step, across))
            for piece in range(2):
                d_normed_sum.begin((piece, step))
        if split:
            mid_sum.close(0)
            for item in s_sum.items():
                s_sum.begin(item)
        handle_early()
        for step in x_sum.steps():
            x_block(ring.slot(step, 0))
        for step in d_normed_sum.steps():
            normed_block(seq.slot(step, 0))
        handle_early(len(waiting))
        out_sum.close(0)
        out_spread.begin(0)
        side = d_normed_sum.items() + [None] * (2 + levels)
        work = [(x_sum, item) for item in x_sum.items()] + [(s_sum, item) for item in s_sum.items()]

        def sideways(at):
            first = len(d_normed_sum.items())
            if at < first:
                d_normed_sum.handle(side[at])
                return
            if at == first:
                for piece in range(2):
                    d_normed_sum.close(piece)
                inputs = tokens[...].astype(F32)
                rms = lax.rsqrt(jnp.mean(inputs * inputs, axis=-1, keepdims=True) + NORM_EPS)
                small_sums[0] = jnp.zeros(small_sums.shape[1:], F32)
                small_sums[0, 0 : KERNEL + 1, :edge] = d_conv[0 : KERNEL + 1, :]
                small_sums[0, 5:6, :] = jnp.sum(
                    d_normed[...].astype(F32) * (inputs * rms), axis=0, keepdims=True
                )
                small_sums[0, 6:7, :wide] = d_gain[0:1, :]
                for k in range(3):
                    small_sums[0, 7:8, 128 * k : 128 * (k + 1)] = d_head[k : k + 1, :]
                swap(0).start()
                return
            level = at - first - 1
            if level < levels:
                swap(level).wait()
                small_sums[level + 1] = small_sums[level] + small_got[level]
                if level + 1 < levels:
                    swap(level + 1).start()
                else:
                    small_spread.begin(0)
                    small_spread.keep().start()

        done = 0
        for at, (s, item) in enumerate(work):
            s.handle(item)
            sideways(at)
            done = at + 1
            if at == WEIGHT_PIECES:
                z_sum.close(0)
                z_spread.begin(0)
                out_spread.forward(0)
        for at in range(done, len(side)):
            sideways(at)
        for piece in range(WEIGHT_PIECES):
            x_sum.close(piece)
            x_spread.begin(piece)
        s_sum.close(0)
        s_spread.begin(0)
        spreads = (out_spread, z_spread, x_spread, s_spread)
        for s in spreads:
            s.keep().start()
        z_spread.forward(0)
        small_spread.forward(0)
        for piece in range(WEIGHT_PIECES):
            x_spread.forward(piece)
        s_spread.forward(0)
        for s in (out_sum, z_sum, x_sum, s_sum, d_normed_sum):
            s.finish()
        if split:
            mid_sum.finish()
        for s in spreads + (small_spread,):
            s.finish()
            s.keep().wait()


def run_backward(
    heads, d_y, pre, conv, dt_pre, states, seg_pad, seg_row, packs, spread, d_z, weights, normed_t,
    tokens, small, d_gain, out_part, z_part, branch_part,
):
    length = d_y.shape[0]
    blocks = length // STRETCH
    wide = heads * HEAD
    edge = wide + 2 * STATE
    ring, seq = places()
    count, groups = lax.axis_size("fsdp"), lax.axis_size("seq")
    levels = levels_of("fsdp")

    def parted(x, by):
        return x.reshape(by, x.shape[0] // by, x.shape[1])

    out_part, z_part = parted(out_part, count), parted(z_part, count)
    branch_part = parted(branch_part, groups)
    rows, own_rows = out_part.shape[1], branch_part.shape[1]
    split = halved(rows, groups)
    own_shared = rows // groups if split else rows
    mid_rows = own_shared * count if split else 16
    wholes = [
        seg_pad, seg_row, *packs, spread, spread.T, d_z, *weights, normed_t, tokens, small, d_gain
    ]
    dma = pltpu.SemaphoreType.DMA
    scratch = [
        pltpu.VMEM((STRETCH + 8, edge), F32),
        pltpu.VMEM((STATE, wide), F32),
        pltpu.VMEM((length, wide + SHARED), BF16),
        pltpu.VMEM((count, rows, wide), BF16),
        pltpu.VMEM((groups, mid_rows, SHARED) if split else (count, rows, SHARED), BF16),
        pltpu.VMEM((groups, own_rows, D), BF16),
        pltpu.VMEM((rows, wide), BF16),
        pltpu.VMEM((rows, wide), BF16),
        pltpu.VMEM((rows, wide), BF16),
        pltpu.VMEM((own_shared, SHARED), BF16),
        pltpu.VMEM((mid_rows, SHARED), BF16),
        pltpu.VMEM((levels + 1, 8, D), F32),
        pltpu.VMEM((levels, 8, D), F32),
        dma((levels,)),
        dma((levels,)),
        dma((ring.major,)),
        dma((ring.major,)),
        dma((seq.major,)),
    ]
    scratch = scratch + Reduce.scratch(ring, rows, wide, 1) + Reduce.scratch(ring, rows, wide, 1)
    scratch = scratch + Reduce.scratch(ring, rows, wide, WEIGHT_PIECES)
    scratch = scratch + Reduce.scratch(seq, own_rows, D, 1) + Reduce.scratch(seq, own_rows, D, 2)
    scratch = scratch + Reduce.scratch(seq, mid_rows, SHARED, 1)
    scratch = scratch + Reduce.scratch(ring, own_shared, SHARED, 1)
    for pieces in (1, 1, WEIGHT_PIECES, 1, 1):
        scratch = scratch + Gather.scratch(seq, pieces)
    shape = jax.ShapeDtypeStruct
    gathered = [
        shape((groups, rows, wide), BF16),
        shape((groups, rows, wide), BF16),
        shape((groups, rows, wide), BF16),
        shape((groups, own_shared, SHARED), BF16),
        shape((groups, 8, D), F32),
    ]
    summed = [
        shape((own_rows, D), BF16),
        shape((own_rows, D), BF16),
        shape((8, edge), F32),
        shape((8, 128), F32),
    ]
    return pl.pallas_call(
        partial(backward_kernel, heads),
        grid=(blocks,),
        in_specs=[
            block(wide, blocks),
            block(edge, blocks),
            block(edge, blocks),
            block(128, blocks),
            pl.BlockSpec((1, STATE, wide), lambda i: (blocks - 1 - i, 0, 0)),
        ]
        + [resident(x) for x in wholes]
        + [HBM] * 3,
        out_specs=[HBM] * 5 + [resident(x) for x in summed],
        out_shape=gathered + summed,
        scratch_shapes=scratch,
        compiler_params=pltpu.CompilerParams(
            collective_id=2,
            has_side_effects=True,
            vmem_limit_bytes=61 * 1024 * 1024,
            dimension_semantics=("arbitrary",),
        ),
        name="backward_and_sums",
    )(d_y, pre, conv, dt_pre, states, *wholes, out_part, z_part, branch_part)


def exchange(place_axis, level, source, got, sends, arrivals):
    index = lax.axis_index(place_axis)
    other = partner(index, level)
    return pltpu.make_async_remote_copy(
        src_ref=source,
        dst_ref=got,
        send_sem=sends,
        recv_sem=arrivals,
        device_id={place_axis: other},
        device_id_type=pl.DeviceIdType.MESH,
    )


def partner(index, level):
    bit = 2**level
    return index + (1 - 2 * (index // bit % 2)) * bit


def levels_of(axis):
    return lax.axis_size(axis).bit_length() - 1


class Push:
    def __init__(self, axis, own, slots, sends, arrivals):
        self.axis, self.own, self.slots = axis, own, slots
        self.sends, self.arrivals = sends, arrivals
        self.count = lax.axis_size(axis)

    def copy(self, step):
        index = lax.axis_index(self.axis)
        return pltpu.make_async_remote_copy(
            src_ref=self.own,
            dst_ref=self.slots.at[index],
            send_sem=self.sends.at[step - 1],
            recv_sem=self.arrivals.at[step - 1],
            device_id={self.axis: (index + step) % self.count},
            device_id_type=pl.DeviceIdType.MESH,
        )

    def begin(self):
        for step in range(1, self.count):
            self.copy(step).start()

    def finish(self):
        for step in range(1, self.count):
            self.copy(step).wait()


def norm_kernel(sums, norms_out, own, slots, sends, arrivals):
    push = Push("fsdp", own, slots, sends, arrivals)
    index = lax.axis_index("fsdp")
    barrier = pltpu.get_barrier_semaphore()
    for step in range(1, push.count):
        other = (index + step) % push.count
        pl.semaphore_signal(
            barrier, inc=1, device_id={"fsdp": other}, device_id_type=pl.DeviceIdType.MESH
        )
    own[...] = jnp.broadcast_to(jnp.sum(sums[...], axis=1, keepdims=True), (8, 128))
    slots[index] = own[...]
    pl.semaphore_wait(barrier, push.count - 1)
    push.begin()
    push.finish()
    total = slots[0]
    for k in range(1, push.count):
        total = total + slots[k]
    norms_out[...] = jnp.sqrt(total)


def run_norms(sums):
    count = lax.axis_size("fsdp")
    dma = pltpu.SemaphoreType.DMA
    return pl.pallas_call(
        norm_kernel,
        in_specs=[VMEM],
        out_specs=VMEM,
        out_shape=jax.ShapeDtypeStruct((8, 128), F32),
        scratch_shapes=[
            pltpu.VMEM((8, 128), F32),
            pltpu.VMEM((count, 8, 128), F32),
            dma((count - 1,)),
            dma((count - 1,)),
        ],
        compiler_params=comm_params(3),
        name="norms",
    )(sums)


def small_update(groups, heads, small_all, small_w, small_m, small_v, outs, small_grad):
    wide = heads * HEAD
    edge = wide + 2 * STATE
    everyone = [small_all[s] for s in range(groups)]
    shared = everyone[0]
    for other in everyone[1:]:
        shared = shared + other
    small_grad[:, :D] = shared[5:6, :]
    for k in range(KERNEL + 1):
        base = D + k * CONV
        for s in range(groups):
            small_grad[:, base + s * wide : base + (s + 1) * wide] = everyone[s][k : k + 1, :wide]
        small_grad[:, base + INNER : base + CONV] = shared[k : k + 1, wide:edge]
    size = 3 * HEADS + INNER
    size = size + -size % 128
    lane = lax.broadcasted_iota(jnp.int32, (8, size), 1)
    rest = jnp.zeros((8, size), F32)
    gap = jnp.zeros((8, size - 128), F32)
    for s in range(groups):
        for k in range(3):
            part = jnp.broadcast_to(everyone[s][7:8, 128 * k : 128 * (k + 1)], (8, 128))
            part = jnp.concatenate([part, gap], axis=1)
            part = jnp.where(lane < heads, part, 0.0)
            move = k * HEADS + s * heads
            rest = rest + (pltpu.roll(part, move, 1) if move else part)
    gains = [jnp.broadcast_to(one[6:7, :wide], (8, wide)) for one in everyone]
    gains = gains + [jnp.zeros((8, size - INNER), F32)]
    rest = rest + pltpu.roll(jnp.concatenate(gains, axis=1), 3 * HEADS, 1)
    base = D + (KERNEL + 1) * CONV
    small_grad[:, base : base + size] = rest[0:1, :]
    gradient = small_grad[...]
    first, second, direction = adam_parts(gradient, small_m[...], small_v[...])
    values = (gradient, small_w[...] - LEARN_RATE * direction, first, second)
    for ref, value in zip(outs, values, strict=True):
        ref[...] = value[:, : ref.shape[1]]


def moments_kernel(groups, heads, *refs):
    z_piece, x_piece, tails, out_piece = refs[:4]
    small_all, small_w, small_m, small_v = refs[4:8]
    w_in, m_in, v_in, w_out, m_out, v_out = refs[8:14]
    g_in_new, m_in_new, v_in_new, u_in, g_out_new, m_out_new, v_out_new, u_out = refs[14:22]
    sums = refs[22]
    small_outs = refs[23:27]
    u_tail, small_grad = refs[27:29]
    wide = heads * HEAD

    @pl.when(pl.program_id(0) == 0)
    def _():
        sums[...] = jnp.zeros_like(sums)
        small_update(groups, heads, small_all, small_w, small_m, small_v, small_outs, small_grad)

    def update(gradient, start, w, m, v, g_new, m_new, v_new, u, at):
        size = min(gradient.shape[1], w.shape[1] - start)
        here = slice(start, start + size)
        gradient = gradient[:, :size]
        first, second, direction = adam_parts(gradient, m[:, here], v[:, here])
        weight = w[:, here]
        direction = direction + WEIGHT_DECAY * weight
        g_new[:, here] = gradient
        m_new[:, here] = first
        v_new[:, here] = second
        if u is None:
            u_tail[:, :size] = direction
        else:
            u[:, here] = direction.astype(BF16)
        sums[at : at + 1, :size] += jnp.sum(weight * weight, axis=0, keepdims=True)
        sums[at + 1 : at + 2, :size] += jnp.sum(direction * direction, axis=0, keepdims=True)

    inside = (w_in, m_in, v_in, g_in_new, m_in_new, v_in_new, u_in)
    outside = (w_out, m_out, v_out, g_out_new, m_out_new, v_out_new, u_out)
    for s in range(groups):
        update(z_piece[s].astype(F32), s * wide, *inside, 0)
        update(x_piece[s].astype(F32), INNER + s * wide, *inside, 0)
        update(out_piece[s].astype(F32), s * wide, *outside, 2)
    gradient = tails[0].astype(F32)
    for s in range(1, tails.shape[0]):
        gradient = gradient + tails[s].astype(F32)
    update(gradient, 2 * INNER, *inside[:-1], None, 0)


ROWS = 48


def by_rows(columns):
    return pl.BlockSpec((ROWS, columns), lambda i: (i, 0))


def run_moments(groups, heads, z_all, x_all, s_all, out_all, smalls, inside, outside):
    rows = inside[0].shape[0]
    wide = heads * HEAD
    piece = pl.BlockSpec((groups, ROWS, wide), lambda i: (0, i, 0))
    if s_all.shape[1] < rows:
        parts = s_all.shape[1] // ROWS
        tails = pl.BlockSpec((1, ROWS, SHARED), lambda i: (i // parts, i % parts, 0))
    else:
        tails = pl.BlockSpec((groups, ROWS, SHARED), lambda i: (0, i, 0))
    shape = jax.ShapeDtypeStruct
    extent = D + (KERNEL + 1) * CONV + 3 * HEADS + INNER
    small_out = [shape((1, extent), F32)] * 4
    in_like, out_like = shape(inside[0].shape, F32), shape(outside[0].shape, F32)
    in_spec, out_spec = by_rows(PROJ), by_rows(INNER)
    return pl.pallas_call(
        partial(moments_kernel, groups, heads),
        grid=(rows // ROWS,),
        in_specs=[piece, piece, tails, piece]
        + [resident(x) for x in smalls]
        + [in_spec] * 3
        + [out_spec] * 3,
        out_specs=[in_spec] * 3
        + [by_rows(2 * INNER)]
        + [out_spec] * 4
        + [pl.BlockSpec((8, wide), lambda i: (0, 0))]
        + [resident(x) for x in small_out]
        + [by_rows(SHARED)],
        out_shape=[in_like] * 3
        + [shape((rows, 2 * INNER), BF16)]
        + [out_like] * 3
        + [shape(out_like.shape, BF16), shape((8, wide), F32)]
        + small_out
        + [shape((rows, SHARED), F32)],
        scratch_shapes=[pltpu.VMEM(smalls[1].shape, F32)],
        compiler_params=compiler_params(),
        name="moments",
    )(z_all, x_all, s_all, out_all, *smalls, *inside, *outside)


def weights_kernel(norms, w_in, u_in, u_tail, w_out, u_out, in_new, out_new):
    in_rate, out_rate = [
        LEARN_RATE * (norms[at : at + 1, :1] / norms[at + 1 : at + 2, :1]) for at in (0, 2)
    ]
    edge = u_in.shape[1]
    rest = w_in.shape[1] - edge
    in_new[:, :edge] = w_in[:, :edge] - in_rate * u_in[...].astype(F32)
    in_new[:, edge:] = w_in[:, edge:] - in_rate * u_tail[:, :rest]
    out_new[...] = w_out[...] - out_rate * u_out[...].astype(F32)


def run_weights(norms, w_in, u_in, u_tail, w_out, u_out):
    in_spec, out_spec = by_rows(PROJ), by_rows(INNER)
    return pl.pallas_call(
        weights_kernel,
        grid=(w_in.shape[0] // ROWS,),
        in_specs=[
            resident(norms), in_spec, by_rows(2 * INNER), by_rows(SHARED), out_spec, out_spec
        ],
        out_specs=[in_spec, out_spec],
        out_shape=[
            jax.ShapeDtypeStruct(w_in.shape, F32),
            jax.ShapeDtypeStruct(w_out.shape, F32),
        ],
        compiler_params=compiler_params(),
        name="weights",
    )(norms, w_in, u_in, u_tail, w_out, u_out)


def adam_parts(gradient, first_old, second_old):
    first_new = FIRST_DECAY * first_old + (1.0 - FIRST_DECAY) * gradient
    second_new = SECOND_DECAY * second_old + (1.0 - SECOND_DECAY) * (gradient * gradient)
    first_scale = 1.0 / (1.0 - FIRST_DECAY**STEP)
    second_scale = 1.0 / (1.0 - SECOND_DECAY**STEP)
    direction = (first_new * first_scale) / (jnp.sqrt(second_new * second_scale) + ADAM_EPSILON)
    return (first_new, second_new, direction)


def wide_row(vector):
    return jnp.pad(vector, (0, -vector.shape[0] % 128))[None, :]


def shards(
    tokens,
    cotangent,
    segments,
    in_weight,
    out_weight,
    small_params,
    in_first,
    in_second,
    out_first,
    out_second,
    small_first,
    small_second,
):
    in_gain = small_params[:D]
    groups = lax.axis_size("seq")
    where_seq = lax.axis_index("seq")
    heads = HEADS // groups
    wide = INNER // groups
    segment_row = segments[0]

    def own(vector, axis=-1):
        size = vector.shape[axis] // groups
        return lax.dynamic_slice_in_dim(vector, where_seq * size, size, axis)

    inputs = tokens[0].astype(F32)
    in_rms = lax.rsqrt(jnp.mean(inputs * inputs, axis=-1, keepdims=True) + NORM_EPS)
    dt_weight = jnp.pad(
        in_weight[:, INNER + CONV :].astype(BF16), ((0, 0), (0, DT_PAD - HEADS))
    )
    small = wide_row(small_params)
    spread_heads = (
        jnp.arange(128)[:, None] == jnp.arange(wide)[None, :] // HEAD
    ).astype(BF16)
    seg_pad = jnp.pad(segment_row, (EDGE, EDGE), constant_values=-1)[:, None]
    (
        pre, conv_in, dt_pre, states, z_part, d_out_gain, conv_pack, head_pack, chan_pack,
        w_x, w_z, w_s, branch_part, d_y, d_z, normed_t, out_part,
    ) = run_forward(
        heads, tokens[0], cotangent[0], small, dt_weight, seg_pad, segments, spread_heads,
        in_weight, out_weight,
    )
    packs = (conv_pack, head_pack, chan_pack)
    out_all, z_all, x_all, s_all, small_all, branch, d_normed, _, _ = run_backward(
        heads, d_y, pre, conv_in, dt_pre, states, seg_pad, segments, packs, spread_heads, d_z,
        (w_z, w_x, w_s.reshape(D, SHARED)), normed_t, tokens[0], small, d_out_gain, out_part, z_part, branch_part,
    )
    output = (inputs + branch.astype(F32)).astype(BF16)[None]
    d_normed = d_normed.astype(F32)
    slope = d_normed * in_gain[None, :]
    d_inputs = slope * in_rms - inputs * (in_rms**3 / D) * jnp.sum(
        slope * inputs, axis=1, keepdims=True
    )
    input_grad = (cotangent[0].astype(F32) + d_inputs)[None]

    (
        in_grad, in_first_new, in_second_new, in_dir, out_grad, out_first_new, out_second_new, out_dir,
        squares, small_grad, small_new, small_first_new, small_second_new, in_tail,
    ) = run_moments(
        groups, heads, z_all, x_all, s_all, out_all,
        (small_all, small, wide_row(small_first), wide_row(small_second)),
        (in_weight, in_first, in_second), (out_weight, out_first, out_second),
    )
    norms = run_norms(squares)
    in_new, out_new = run_weights(norms, in_weight, in_dir, in_tail, out_weight, out_dir)
    small_grad, small_new, small_first_new, small_second_new = [
        x[0] for x in (small_grad, small_new, small_first_new, small_second_new)
    ]
    norms = norms[:4, 0]
    return (
        output,
        input_grad,
        in_grad,
        in_new,
        in_first_new,
        in_second_new,
        out_grad,
        out_new,
        out_first_new,
        out_second_new,
        small_grad,
        small_new,
        small_first_new,
        small_second_new,
        norms,
    )


def solution(mesh):
    matrix = P("fsdp", None)
    rows = P("fsdp", "seq", None)
    return jax.shard_map(
        shards,
        mesh=mesh,
        in_specs=(rows, rows, matrix, matrix, matrix, P(), matrix, matrix, matrix, matrix, P(), P()),
        out_specs=(rows, rows) + (matrix,) * 8 + (P(),) * 5,
        check_vma=False,
    )
```
